32 devices in a mesh: dp: 8 (over y, x, core), mp: 4 (over z).
Axes of the slice: x: 2, y: 2, z: 4, core: 2. Of those that a mesh axis runs over, the one named last changes fastest.
Arguments:
- tokens: bfloat16 [4096, 2048], P(('dp', 'mp')), may hold values from -6 to 6
- cotangent: bfloat16 [4096, 2048], P(('dp', 'mp')), may hold values from -6 to 6
- lengths: int32 [16], replicated, may hold values from 1 to 2048, 4096 in all
- mix_state: float32 [3, 4, 2048, 2048], P(None, None, 'dp', 'mp'), as said below
- out_state: float32 [3, 2048, 2048], P(None, 'mp', 'dp')
- key_state: float32 [3, 2048, 7168], P(None, 'dp', 'mp')
- value_state: float32 [3, 7168, 2048], P(None, 'mp', 'dp')
- gate_state: float32 [3, 2048, 2048], P(None, 'dp', 'mp')
- down_state: float32 [3, 2048, 224], P(None, ('dp', 'mp'))
- up_state: float32 [3, 224, 2048], P(None, None, ('dp', 'mp'))
- vector_state: float32 [3, 16, 2048], P(None, None, ('dp', 'mp'))
Outputs:
- mixed: bfloat16 [4096, 2048], P(('dp', 'mp'))
- grad_tokens: float32 [4096, 2048], P(('dp', 'mp'))
- mix_update: float32 [3, 4, 2048, 2048], P(None, None, 'dp', 'mp')
- out_update: float32 [3, 2048, 2048], P(None, 'mp', 'dp')
- key_update: float32 [3, 2048, 7168], P(None, 'dp', 'mp')
- value_update: float32 [3, 7168, 2048], P(None, 'mp', 'dp')
- gate_update: float32 [3, 2048, 2048], P(None, 'dp', 'mp')
- down_update: float32 [3, 2048, 224], P(None, ('dp', 'mp'))
- up_update: float32 [3, 224, 2048], P(None, None, ('dp', 'mp'))
- vector_update: float32 [3, 16, 2048], P(None, None, ('dp', 'mp'))
The draws below stay inside these ranges and needn't reach their ends.
Inputs may be any that keep to these rules, and one draw needn't show every extreme that they name: `lengths`: lengths sum to 4096; the largest is exactly 2048. `mix_state`: index 0 is a weight of order fan-in to the minus one half, index 1 a velocity of both signs, index 2 an average of the weight's order.
All inputs are finite; a program needn't handle non-finite values.
Results may differ from the reference program's by a relative error of at most 0.018.
The reference program's roundings to bfloat16 on the way count: a program that leaves them out, or rounds other values in their place, can miss the bound.
Values may be sent and summed in bfloat16 or wider, within the bound.
A program may use at most 448 MiB of HBM per device.

```python
import math
import jax
import jax.numpy as jnp
import numpy as np
from jax import lax

MODEL_WIDTH = 2048
HEADS = 32
LANE_SPAN = 64
FF = 7168
TM_RANK = 32
DECAY_RANK = 64
DOWN_COLUMNS = 224
BLOCK = 16
TOK_DEV = 128
TOKENS = 4096
LONGEST = 2048
SEQS = 16
N_MP = 4


def bounded_normal(key, shape):
    return jnp.clip(jax.random.normal(key, shape, jnp.float32), -4.0, 4.0)


def moment_draw(key, shape, step_size):
    first, second = jax.random.split(key)
    magnitude = jnp.exp(jax.random.uniform(first, shape, jnp.float32, -0.693, 0.693))
    signs = jnp.where(jax.random.uniform(second, shape, jnp.float32) < 0.5, -1.0, 1.0)
    return 0.111 * step_size * magnitude * signs


def state_pile(key, shape, scale_factor, step_size):
    first, second, third = jax.random.split(key, 3)
    weight = scale_factor * bounded_normal(first, shape)
    moment = moment_draw(second, shape, step_size)
    average = scale_factor * bounded_normal(third, shape)
    return jnp.stack([weight, moment, average]).astype(jnp.float32)


def draw_mix_state(key, part):
    return state_pile(jax.random.fold_in(key, 11), (4, MODEL_WIDTH, MODEL_WIDTH), MODEL_WIDTH ** (-0.5), MODEL_WIDTH ** (-0.5))


def draw_out_state(key, part):
    return state_pile(jax.random.fold_in(key, 12), (MODEL_WIDTH, MODEL_WIDTH), MODEL_WIDTH ** (-0.5), MODEL_WIDTH ** (-0.5))


def draw_key_state(key, part):
    return state_pile(jax.random.fold_in(key, 13), (MODEL_WIDTH, FF), MODEL_WIDTH ** (-0.5), MODEL_WIDTH ** (-0.5))


def draw_value_state(key, part):
    return state_pile(jax.random.fold_in(key, 14), (FF, MODEL_WIDTH), FF ** (-0.5), FF ** (-0.5))


def draw_gate_state(key, part):
    return state_pile(jax.random.fold_in(key, 15), (MODEL_WIDTH, MODEL_WIDTH), MODEL_WIDTH ** (-0.5), MODEL_WIDTH ** (-0.5))


def draw_down_state(key, part):
    return state_pile(jax.random.fold_in(key, 16), (MODEL_WIDTH, DOWN_COLUMNS), MODEL_WIDTH ** (-0.5), MODEL_WIDTH ** (-0.5))


def draw_up_state(key, part):
    row_indices = jnp.arange(DOWN_COLUMNS)[:, None]
    scale_factor = jnp.where(row_indices < 5 * TM_RANK, 0.5 * TM_RANK ** (-0.5), 0.5 * DECAY_RANK ** (-0.5))
    return state_pile(jax.random.fold_in(key, 17), (DOWN_COLUMNS, MODEL_WIDTH), scale_factor, TM_RANK ** (-0.5))


def vector_rows(key):
    first, second, third = jax.random.split(key, 3)
    uniform = jax.random.uniform(first, (16, MODEL_WIDTH), jnp.float32)
    normal = bounded_normal(second, (16, MODEL_WIDTH))
    rate_draw = jax.random.uniform(third, (MODEL_WIDTH,), jnp.float32)
    gains = 1.0 + 0.4 * (uniform - 0.5)
    small = 0.2 * normal
    rate_low = 0.25 / LONGEST
    rate_high = 0.05
    log_rate = jnp.log(rate_low) + rate_draw * (jnp.log(rate_high) - jnp.log(rate_low))
    rows = [gains[0], small[1], uniform[2], uniform[3], uniform[4], uniform[5], uniform[6], uniform[7], log_rate, 0.5 * normal[9], gains[10], small[11], gains[12], small[13], uniform[14], uniform[15]]
    return jnp.stack(rows)


def draw_vector_state(key, part):
    first, second, third = jax.random.split(jax.random.fold_in(key, 18), 3)
    weight = vector_rows(first)
    moment = moment_draw(second, (16, MODEL_WIDTH), 2.0)
    average = vector_rows(third)
    return jnp.stack([weight, moment, average]).astype(jnp.float32)


def steps_of(key, extent, shards, low, high):
    def one(axis_at, blocks):
        steps = jax.random.uniform(jax.random.fold_in(jax.random.fold_in(key, 6), axis_at), (blocks,), jnp.float32, low / len(shards), high / len(shards))
        return jnp.repeat(jnp.exp(steps), extent[axis_at] // blocks).reshape((-1,) + (1,) * (len(extent) - axis_at - 1))

    factor_of = one(*shards[0])
    for cut in shards[1:]:
        factor_of = factor_of * one(*cut)
    return factor_of


def split_up(amount, total, most, slope):
    loads = [(1 << 20) // math.isqrt(standing ** slope) + 1 for standing in range(2, amount + 1)]
    spare, counts = total - most - (amount - 1), [1] * (amount - 1)
    while spare > 0:
        movable = [i for i in range(amount - 1) if counts[i] < most]
        whole, budget = sum([loads[i] for i in movable]), spare
        for i in movable:
            extra = min(most - counts[i], max(1, budget * loads[i] // whole), spare)
            counts[i] = counts[i] + extra
            spare = spare - extra
    return np.array([most] + counts)


def ragged_sizes(key, number_of, total, bound, skew):
    if number_of == 2:
        one = jax.random.randint(key, (), max(1, total - bound), min(bound, total - 1) + 1)
        return jnp.stack([one, total - one])
    sizes = jnp.asarray(split_up(number_of, total, bound, skew), jnp.int32)
    pairs = (number_of - 1) // 2
    donor, taker = sizes[1:1 + 2 * pairs:2], sizes[2:2 + 2 * pairs:2]
    room = jnp.minimum(donor - 1, bound - taker)
    moved = jax.random.randint(jax.random.fold_in(key, 1), (pairs,), 0, 1 << 20) % (room + 1)
    sizes = sizes.at[1:1 + 2 * pairs:2].set(donor - moved).at[2:2 + 2 * pairs:2].set(taker + moved)
    return sizes[jax.random.permutation(jax.random.fold_in(key, 2), number_of)]


def noise(rng, dims, deviation, limit, shards=(), kind=jnp.bfloat16):
    entries = deviation * jax.random.normal(rng, dims, jnp.float32)
    if shards:
        entries = entries * steps_of(rng, dims, shards, -0.22, 0.18)
    return jnp.clip(entries, -limit, limit).astype(kind)


def setup_inputs(seed: int = 0) -> dict:
    keys = jax.random.split(jax.random.key(seed), 12)
    return {
        "tokens": noise(keys[0], (TOKENS, MODEL_WIDTH), 1.0, 6.0, ((0, 32),)),
        "cotangent": noise(keys[1], (TOKENS, MODEL_WIDTH), 1.0, 6.0, ((0, 32),)),
        "lengths": ragged_sizes(keys[2], SEQS, TOKENS, LONGEST, 2).astype(jnp.int32),
        "mix_state": draw_mix_state(jax.random.fold_in(keys[11], 71), 0),
        "out_state": draw_out_state(jax.random.fold_in(keys[11], 71), 0),
        "key_state": draw_key_state(jax.random.fold_in(keys[11], 71), 0),
        "value_state": draw_value_state(jax.random.fold_in(keys[11], 71), 0),
        "gate_state": draw_gate_state(jax.random.fold_in(keys[11], 71), 0),
        "down_state": draw_down_state(jax.random.fold_in(keys[11], 71), 0),
        "up_state": draw_up_state(jax.random.fold_in(keys[11], 71), 0),
        "vector_state": draw_vector_state(jax.random.fold_in(keys[11], 71), 0),
    }


@jax.custom_vjp
def low(v):
    return lax.optimization_barrier(v.astype(jnp.bfloat16)).astype(jnp.float32)

@jax.custom_vjp
def low_back(v):
    return v

def low_keep(v):
    return (low(v), None)

def low_pass(kept, grad):
    return (grad,)

def back_keep(v):
    return (v, None)

def back_low(kept, grad):
    return (low(grad),)
low.defvjp(low_keep, low_pass)
low_back.defvjp(back_keep, back_low)
precise = lax.Precision.HIGHEST
momentum_rate = 0.9
average_rate = 0.9
norm_epsilon = 1e-05
group_epsilon = 0.00064

def product(left, right):
    return jnp.dot(left, right, precision=precise)

def layer_norm(value, gain, bias, epsilon):
    centre = value - lax.optimization_barrier(jnp.mean(value, -1, keepdims=True))
    spread = lax.optimization_barrier(jnp.mean(centre * centre, -1, keepdims=True))
    return centre * lax.rsqrt(spread + epsilon) * gain + bias

def shift_rows(value, keep_rows):
    return jnp.concatenate([jnp.zeros_like(value[:1]), value[:-1]], 0) * keep_rows[:, None]

def combine(earlier, later):
    return (earlier[0] * later[0], later[0][..., None] * earlier[1] + later[1])

def stretch_prefix(lookup_piece, payload_piece, fading_piece, stretch_piece, marker_piece):
    cumul = jnp.cumsum(fading_piece, 1)
    final = cumul[:, -1]
    tail = jnp.exp(final[:, None] - cumul)
    ending = (stretch_piece == stretch_piece[:, -1:]).astype(jnp.float32)
    stretch_b = jnp.einsum('njhc,njhe->nhce', lookup_piece * tail * ending[:, :, None, None], payload_piece, precision=precise)
    valid = 1.0 - jnp.minimum(jnp.cumsum(marker_piece, 1), 1.0)
    stretch_a = jnp.exp(final) * valid[:, -1][:, None, None]
    inc_a, inc_b = lax.associative_scan(combine, (stretch_a, stretch_b))
    swap_toward_lower = jnp.concatenate([jnp.ones_like(inc_a[:1]), inc_a[:-1]], 0)
    swap_toward_higher = jnp.concatenate([jnp.zeros_like(inc_b[:1]), inc_b[:-1]], 0)
    return (swap_toward_lower, swap_toward_higher, inc_a[-1], inc_b[-1])

def padded_result(acceptor_piece, lookup_piece, payload_piece, fading_piece, initial_reward, stretch_piece, marker_piece, swap_toward_lower, swap_toward_higher, carried_memory):
    cumul = jnp.cumsum(fading_piece, 1)
    before = cumul - fading_piece
    order = jnp.arange(fading_piece.shape[1])
    lower = order[:, None] > order[None, :]
    same = (stretch_piece[:, :, None] == stretch_piece[:, None, :]) & lower[None]
    masked = same[:, :, :, None, None]
    spacing = jnp.where(masked, before[:, :, None] - cumul[:, None, :], 0.0)
    factor = jnp.where(masked, jnp.exp(spacing), 0.0)
    scores = jnp.einsum('ntjhc,nthc,njhc->nthj', factor, acceptor_piece, lookup_piece, precision=precise)
    inner = jnp.einsum('nthj,njhe->nthe', scores, payload_piece, precision=precise)
    current_memory = lax.optimization_barrier(jnp.sum(acceptor_piece * initial_reward * lookup_piece, -1, keepdims=True)) * payload_piece
    valid = 1.0 - jnp.minimum(jnp.cumsum(marker_piece, 1), 1.0)
    start_state = swap_toward_higher + swap_toward_lower[..., None] * carried_memory[None]
    carried = jnp.einsum('nthc,nhce->nthe', acceptor_piece * jnp.exp(before), start_state, precision=precise)
    return inner + current_memory + carried * valid[:, :, None, None]

def traverse_linear_memory(acceptor_entries, lookup_tensor, payload_tensor, log_fading_rate, initial_reward, stretch_ordinal, opening_marker):
    span = TOK_DEV * N_MP
    count = TOKENS // span

    def blocked(value):
        return value.reshape((count, span // BLOCK, BLOCK) + value.shape[1:])

    def advance(carried_memory, pieces):
        acceptor_piece, lookup_piece, payload_piece, fading_piece, stretch_piece, marker_piece = pieces
        swap_toward_lower, swap_toward_higher, last_a, last_b = stretch_prefix(lookup_piece, payload_piece, fading_piece, stretch_piece, marker_piece)
        prefix_combination_result = padded_result(acceptor_piece, lookup_piece, payload_piece, fading_piece, initial_reward, stretch_piece, marker_piece, swap_toward_lower, swap_toward_higher, carried_memory)
        return (last_b + last_a[..., None] * carried_memory, prefix_combination_result)
    initial = jnp.zeros((HEADS, LANE_SPAN, LANE_SPAN), jnp.float32)
    pieces = (blocked(acceptor_entries), blocked(lookup_tensor), blocked(payload_tensor), blocked(log_fading_rate), blocked(stretch_ordinal), blocked(opening_marker))
    unused, results = lax.scan(jax.checkpoint(advance), initial, pieces)
    return results.reshape(TOKENS, HEADS, LANE_SPAN)

def block_forward(tokens, mix, out_weight, key_weight, value_weight, gate_weight, down, upper, vectors, stretch_ordinal, opening_marker):
    keep_rows = 1.0 - opening_marker
    width = tokens.shape[1]
    maa_cols = 5 * TM_RANK
    hidden = layer_norm(tokens, vectors[0], vectors[1], norm_epsilon)
    delta = shift_rows(hidden, keep_rows) - hidden
    base = low(hidden + delta * vectors[2])
    low_down = low(down)
    low_up = low(upper)
    mix_act = low(jnp.tanh(product(base, low_down[:, :maa_cols])))
    mixes = jnp.einsum('tir,ird->itd', mix_act.reshape(-1, 5, TM_RANK), low_up[:maa_cols].reshape(5, TM_RANK, width), precision=precise)
    inputs = [low(hidden + delta * (vectors[3 + number] + mixes[number])) for number in range(5)]
    decay_act = low(jnp.tanh(product(inputs[0], low_down[:, maa_cols:])))
    log_fading_rate = -jnp.exp(vectors[8] + product(decay_act, low_up[maa_cols:]))
    low_mix = low(mix)
    acceptor_entries = low_back(product(inputs[3], low_mix[0]))
    lookup_tensor = low_back(product(inputs[1], low_mix[1]))
    payload_tensor = low_back(product(inputs[2], low_mix[2]))
    gate = jax.nn.silu(low_back(product(inputs[4], low_mix[3])))
    heads_shape = (-1, HEADS, LANE_SPAN)
    wkv = traverse_linear_memory(acceptor_entries.reshape(heads_shape), lookup_tensor.reshape(heads_shape), payload_tensor.reshape(heads_shape), log_fading_rate.reshape(heads_shape), vectors[9].reshape(HEADS, LANE_SPAN), stretch_ordinal, opening_marker)
    centre = wkv - lax.optimization_barrier(jnp.mean(wkv, -1, keepdims=True))
    spread = lax.optimization_barrier(jnp.mean(centre * centre, -1, keepdims=True))
    normed = (centre * lax.rsqrt(spread + group_epsilon)).reshape(-1, width) * vectors[10] + vectors[11]
    attention = low_back(product(low(normed * gate), low(out_weight)))
    residual = tokens + attention
    hidden_two = layer_norm(low(residual), vectors[12], vectors[13], norm_epsilon)
    delta_two = shift_rows(hidden_two, keep_rows) - hidden_two
    key_pre = low_back(product(low(hidden_two + delta_two * vectors[14]), low(key_weight)))
    key_act = jnp.square(jnp.maximum(key_pre, 0.0))
    channel_sum = low_back(product(low(key_act), low(value_weight)))
    recv_gate = jax.nn.sigmoid(low_back(product(low(hidden_two + delta_two * vectors[15]), low(gate_weight))))
    return residual + recv_gate * channel_sum

def update(carried_memory, grad, fan):
    rate = (TOKENS * fan) ** (-0.5)
    scaled = rate * grad
    velocity = momentum_rate * carried_memory[1] + scaled
    weight = carried_memory[0] - (scaled + momentum_rate * velocity)
    average = average_rate * carried_memory[2] + (1.0 - average_rate) * weight
    return jnp.stack([velocity, weight, average])

def reference(tokens, cotangent, lengths, mix_state, out_state, key_state, value_state, gate_state, down_state, up_state, vector_state):
    seq_ends = jnp.cumsum(lengths).astype(jnp.int32)
    offsets = (seq_ends - lengths).astype(jnp.int32)
    positions = jnp.arange(TOKENS, dtype=jnp.int32)
    opening_marker = jnp.any(positions[:, None] == offsets[None, :], 1).astype(jnp.float32)
    stretch_ordinal = lax.optimization_barrier(jnp.sum((offsets[None, :] <= positions[:, None]).astype(jnp.int32), 1)).astype(jnp.int32)

    def forward(*params):
        return block_forward(*params, stretch_ordinal, opening_marker)
    params = (tokens.astype(jnp.float32), mix_state[0], out_state[0], key_state[0], value_state[0], gate_state[0], down_state[0], up_state[0], vector_state[0])
    output, pullback = jax.vjp(forward, *params)
    grads = pullback(cotangent.astype(jnp.float32))
    return (output.astype(jnp.bfloat16), grads[0], update(mix_state, grads[1], MODEL_WIDTH), update(out_state, grads[2], MODEL_WIDTH), update(key_state, grads[3], MODEL_WIDTH), update(value_state, grads[4], FF), update(gate_state, grads[5], MODEL_WIDTH), update(down_state, grads[6], MODEL_WIDTH), update(up_state, grads[7], TM_RANK), update(vector_state, grads[8], 1))
```

```python
import functools

import jax
import jax.numpy as jnp
import numpy as np
from jax import lax
from jax.experimental import pallas as pl
from jax.experimental.pallas import tpu as pltpu
from jax.sharding import PartitionSpec as P

LANE_SPAN = 64
FF = 7168
TM_RANK = 32
DECAY_RANK = 64


momentum_rate = 0.9
average_rate = 0.9
norm_epsilon = 1e-05
group_epsilon = 0.00064
CHUNK = 128
LEVELS = 7
PAIR = 2 * LANE_SPAN
MESH = pl.DeviceIdType.MESH


def from_behind(block, axis, distance):
    devices = range(lax.axis_size(axis))
    route = [(i - distance, i) for i in devices if i - distance in devices]
    return lax.ppermute(block, axis, route)


def half_dot(left, right):
    return jnp.dot(left, right, preferred_element_type=jnp.float32)


def half_left(left, right):
    return lax.dot_general(
        left, right, (((0,), (0,)), ((), ())), preferred_element_type=jnp.float32
    )


def half_right(left, right):
    return lax.dot_general(
        left, right, (((1,), (1,)), ((), ())), preferred_element_type=jnp.float32
    )


def split_pair(value):
    upper_part = value.astype(jnp.bfloat16)
    lower_part = (value - upper_part.astype(jnp.float32)).astype(jnp.bfloat16)
    return (upper_part, lower_part)


def norm_forward(value, gain, bias, epsilon):
    centre = value - jnp.mean(value, -1, keepdims=True)
    inverse = lax.rsqrt(jnp.mean(centre * centre, -1, keepdims=True) + epsilon)
    normal_hat = centre * inverse
    return (normal_hat * gain + bias, normal_hat, inverse)


def norm_backward(grad_out, normal_hat, inverse, gain):
    scaled = grad_out * gain
    return inverse * (
        scaled
        - jnp.mean(scaled, -1, keepdims=True)
        - normal_hat * jnp.mean(scaled * normal_hat, -1, keepdims=True)
    )


def level_tables():
    row = np.arange(CHUNK)
    later, earlier = row[:, None], row[None, :]
    level = np.full((CHUNK, CHUNK), -1.0, np.float32)
    sums = []
    for bit in range(LEVELS):
        block = (later >> (bit + 1)) == (earlier >> (bit + 1))
        level[block & ((later >> bit) % 2 == 1) & ((earlier >> bit) % 2 == 0)] = bit
        middle = ((later >> (bit + 1)) << (bit + 1)) + (1 << bit)
        upper = (later >> bit) % 2 == 1
        between = np.where(
            upper, (earlier >= middle) & (earlier < later), (earlier > later) & (earlier < middle)
        )
        if bit:
            sums.append(between)
    sums += [earlier < later, earlier > later]
    sums = np.concatenate(sums, 0).astype(np.float32)
    return np.concatenate([level, level], 1), np.concatenate([sums, sums], 1), sums.T


def dot_nn(left, right):
    return lax.dot_general(
        left, right, (((1,), (0,)), ((), ())), preferred_element_type=jnp.float32
    )


def dot_nt(left, right):
    return lax.dot_general(
        left, right, (((1,), (1,)), ((), ())), preferred_element_type=jnp.float32
    )


def dot_tn(left, right):
    return lax.dot_general(
        left, right, (((0,), (0,)), ((), ())), preferred_element_type=jnp.float32
    )


def first_head(shape):
    return lax.broadcasted_iota(jnp.int32, shape, len(shape) - 1) < LANE_SPAN


def stack_heads(value):
    first = first_head(value.shape)
    none = jnp.zeros_like(value)
    return jnp.concatenate([jnp.where(first, value, none), jnp.where(first, none, value)], 0)


def merge_heads(value):
    half = value.shape[0] // 2
    return jnp.where(first_head((half, value.shape[1])), value[:half], value[half:])


def own_blocks(value):
    upper = lax.broadcasted_iota(jnp.int32, value.shape, 0) < LANE_SPAN
    return jnp.where(upper == first_head(value.shape), value, 0.0)


def head_mean(value):
    row = lax.broadcasted_iota(jnp.int32, (PAIR, PAIR), 0) < LANE_SPAN
    ones = jnp.where(row == first_head((PAIR, PAIR)), 1.0 / LANE_SPAN, 0.0).astype(jnp.bfloat16)
    upper, lower = split_pair(value)
    return dot_nn(upper, ones) + dot_nn(lower, ones)


def head_sum(value):
    return head_mean(value) * float(LANE_SPAN)


def exact_pieces(left, right, axis_left, axis_right):
    upper, lower = split_pair(left)
    right_upper, right_lower = split_pair(right)
    return (
        jnp.concatenate([upper, lower, upper], axis_left),
        jnp.concatenate([right_upper, right_upper, right_lower], axis_right),
    )


def exact_nn(left, right):
    return dot_nn(*exact_pieces(left, right, 1, 0))


def exact_nt(left, right):
    return dot_nt(*exact_pieces(left, right, 1, 1))


def exact_tn(left, right):
    return dot_tn(*exact_pieces(left, right, 0, 0))


def packed_state(state):
    return jnp.concatenate(split_pair(state[:LANE_SPAN] + state[LANE_SPAN:]), 0)


def unpacked_state(piece):
    piece = piece.astype(jnp.float32)
    return piece[:LANE_SPAN] + piece[LANE_SPAN:]


def rows_of(chunk):
    return pl.ds(pl.multiple_of(chunk * CHUNK, CHUNK), CHUNK)


def lanes_of(pair):
    return pl.ds(pl.multiple_of(pair * PAIR, PAIR), PAIR)


def marks_of(chunk):
    return pl.ds(pl.multiple_of(chunk * 8, 8), 8)


def greet(count):
    me, mine = lax.axis_index("dp"), lax.axis_index("mp")
    barrier = pltpu.get_barrier_semaphore()
    for step in range(1, count):
        pl.semaphore_signal(
            barrier, inc=1, device_id=(lax.rem(me + step, count), mine), device_id_type=MESH
        )
    pl.semaphore_wait(barrier, count - 1)


def state_copies(other, me, sends, lands, send_sems, recv_sems, to):
    return [
        pltpu.make_async_remote_copy(
            src_ref=send,
            dst_ref=land.at[me],
            send_sem=send_sems.at[number, other],
            recv_sem=recv_sems.at[number, me],
            device_id=(to, lax.axis_index("mp")),
            device_id_type=MESH,
        )
        for number, (send, land) in enumerate(zip(sends, lands))
    ]


def send_states(count, sends, lands, send_sems, recv_sems, ahead):
    me = lax.axis_index("dp")
    for other in range(count):

        @pl.when((other > me) if ahead else (other < me))
        def _():
            for copy in state_copies(other, me, sends, lands, send_sems, recv_sems, other):
                copy.start()


def wait_states(count, sends, lands, send_sems, recv_sems, ahead):
    me = lax.axis_index("dp")
    for other in range(count):

        @pl.when((other > me) if ahead else (other < me))
        def _():
            for copy in state_copies(other, me, sends, lands, send_sems, recv_sems, other):
                copy.wait_send()

        @pl.when((other < me) if ahead else (other > me))
        def _():
            for copy in state_copies(other, other, sends, lands, send_sems, recv_sems, me):
                copy.wait_recv()


def decay_factors(fading, sums):
    upper, lower = split_pair(fading)
    return jnp.exp(dot_nn(sums, jnp.concatenate([upper, lower], 0)))


def table(at):
    return slice(at * CHUNK, (at + 1) * CHUNK)


def level_inputs(level, acceptor, lookup, factors):
    if level == 0:
        return None, acceptor, lookup
    factor = factors[table(level - 1), :]
    return factor, acceptor * factor, lookup * factor


def recurrence_forward(
    count, chunks, pairs,
    rec, key, val, gpre, logw, vec, seg_col, seg_row, valid, ending, whole, level, sums,
    gated, wkv, states, kept,
    factors, pre_a, pre_b, start_b, send_a, send_b, land_a, land_b, send_sems, recv_sems,
):
    bfloat = jnp.bfloat16
    greet(count)

    def summary(pair, carry):
        lanes = lanes_of(pair)

        def step(chunk, before):
            before_a, before_b = before
            rows, slot = rows_of(chunk), pair * chunks + chunk
            fading = logw[rows, lanes]
            factor = decay_factors(fading, sums[...])
            factors[slot] = factor
            faded = key[rows, lanes] * factor[table(LEVELS)] * ending[rows, :]
            chunk_b = own_blocks(exact_tn(val[rows, lanes], faded))
            chunk_a = jnp.exp(jnp.sum(fading, 0, keepdims=True)) * whole[marks_of(chunk), :][:1]
            pre_a[slot] = jnp.broadcast_to(before_a, (8, PAIR))
            pre_b[slot] = before_b
            return before_a * chunk_a, before_b * chunk_a + chunk_b

        last_a, last_b = lax.fori_loop(
            0, chunks, step, (jnp.ones((1, PAIR), jnp.float32), jnp.zeros((PAIR, PAIR), jnp.float32))
        )
        send_a[:, lanes] = jnp.broadcast_to(last_a, (8, PAIR))
        send_b[:, lanes] = packed_state(last_b)
        return carry

    lax.fori_loop(0, pairs, summary, 0)
    exchange = (count, (send_a, send_b), (land_a, land_b), send_sems, recv_sems, True)
    send_states(*exchange)

    def inside(slot, carry):
        pair, chunk = slot // chunks, slot % chunks
        rows, lanes = rows_of(chunk), lanes_of(pair)
        acceptor, lookup, payload = rec[rows, lanes], key[rows, lanes], val[rows, lanes]
        place = jnp.where(seg_col[rows, :] == seg_row[marks_of(chunk), :][:1], level[...], -1.0)
        scores = jnp.zeros((CHUNK, 2 * CHUNK), jnp.float32)
        for at in range(LEVELS):
            _, left, right = level_inputs(at, acceptor, lookup, factors.at[slot])
            part = exact_nt(left, stack_heads(right))
            scores = jnp.where(place == float(at), part, scores)
        bonus = head_sum(acceptor * vec[0:1, lanes] * lookup) * payload
        wkv[rows, lanes] = bonus + exact_nn(scores, stack_heads(payload))
        kept[slot] = scores.astype(bfloat)
        return carry

    lax.fori_loop(0, pairs * chunks, inside, 0)
    wait_states(*exchange)
    start_b[...] = lax.fori_loop(
        0,
        lax.axis_index("dp"),
        lambda other, state: state * land_a[other][:1] + unpacked_state(land_b[other]),
        jnp.zeros(start_b.shape, jnp.float32),
    )

    def finish(slot, carry):
        pair, chunk = slot // chunks, slot % chunks
        rows, lanes = rows_of(chunk), lanes_of(pair)
        state = pre_b[slot] + pre_a[slot][:1] * stack_heads(start_b[:, lanes])
        states[slot] = state
        reader = rec[rows, lanes] * factors[slot, table(LEVELS - 1), :] * valid[rows, :]
        out = wkv[rows, lanes] + exact_nt(reader, state)
        wkv[rows, lanes] = out
        centre = out - head_mean(out)
        inverse = lax.rsqrt(head_mean(centre * centre) + group_epsilon)
        normed = centre * inverse * vec[1:2, lanes] + vec[2:3, lanes]
        pre = gpre[rows, lanes]
        gated[rows, lanes] = (normed * pre * jax.nn.sigmoid(pre)).astype(bfloat)
        return carry

    lax.fori_loop(0, pairs * chunks, finish, 0)


def recurrence_backward(
    count, chunks, pairs,
    dgated, wkv, states, kept, rec, key, val, gpre, logw, vec, seg_col, seg_row, valid, ending, whole,
    level, sums, sums_back,
    drec, dkey, dval, dgpre, draw, dvec,
    factors, local, end_b, dout, drec_part, dkey_part, dval_part, dlog_part, steps,
    send_a, send_b, land_a, land_b, send_sems, recv_sems,
):
    bfloat = jnp.bfloat16
    greet(count)
    dvec[...] = jnp.zeros(dvec.shape, jnp.float32)

    def chunk_decay(chunk, lanes):
        fading = logw[rows_of(chunk), lanes]
        return jnp.exp(jnp.sum(fading, 0, keepdims=True)) * whole[marks_of(chunk), :][:1]

    def summary(pair, carry):
        lanes = lanes_of(pair)

        def step(back, after):
            after_a, after_b = after
            chunk = chunks - 1 - back
            rows, slot = rows_of(chunk), pair * chunks + chunk
            factor = decay_factors(logw[rows, lanes], sums[...])
            factors[slot] = factor
            out = wkv[rows, lanes]
            centre = out - head_mean(out)
            inverse = lax.rsqrt(head_mean(centre * centre) + group_epsilon)
            hat = centre * inverse
            gain = vec[1:2, lanes]
            normed = hat * gain + vec[2:3, lanes]
            pre = gpre[rows, lanes]
            sig = jax.nn.sigmoid(pre)
            grad = dgated[rows, lanes]
            grad_normed = grad * pre * sig
            dgpre[rows, lanes] = (grad * normed * sig * (1.0 + pre * (1.0 - sig))).astype(bfloat)
            dvec[2:3, lanes] += jnp.sum(grad_normed * hat, 0, keepdims=True)
            dvec[3:4, lanes] += jnp.sum(grad_normed, 0, keepdims=True)
            scaled = grad_normed * gain
            grad_out = inverse * (scaled - head_mean(scaled) - hat * head_mean(scaled * hat))
            dout[rows, lanes] = grad_out
            reader = rec[rows, lanes] * factor[table(LEVELS - 1)] * valid[rows, :]
            inner = own_blocks(exact_tn(grad_out, reader))
            local[slot] = inner
            chunk_a = chunk_decay(chunk, lanes)
            return after_a * chunk_a, after_b * chunk_a + inner

        last_a, last_b = lax.fori_loop(
            0, chunks, step, (jnp.ones((1, PAIR), jnp.float32), jnp.zeros((PAIR, PAIR), jnp.float32))
        )
        send_a[:, lanes] = jnp.broadcast_to(last_a, (8, PAIR))
        send_b[:, lanes] = packed_state(last_b)
        return carry

    lax.fori_loop(0, pairs, summary, 0)
    exchange = (count, (send_a, send_b), (land_a, land_b), send_sems, recv_sems, False)
    send_states(*exchange)

    def inside(slot, carry):
        pair, chunk = slot // chunks, slot % chunks
        rows, lanes = rows_of(chunk), lanes_of(pair)
        acceptor, lookup, payload = rec[rows, lanes], key[rows, lanes], val[rows, lanes]
        reward = vec[0:1, lanes]
        grad_exact = dout[rows, lanes]
        grad_out = grad_exact.astype(bfloat)
        place = jnp.where(seg_col[rows, :] == seg_row[marks_of(chunk), :][:1], level[...], -1.0)
        grad_scores = exact_nt(grad_exact, stack_heads(payload))
        grad_bonus = head_sum(grad_exact * payload)
        dvec[1:2, lanes] += jnp.sum(acceptor * lookup * grad_bonus, 0, keepdims=True)
        grad_acceptor = reward * lookup * grad_bonus
        grad_lookup = reward * acceptor * grad_bonus
        for at in range(LEVELS):
            factor, left, right = level_inputs(at, acceptor, lookup, factors.at[slot])
            left_low, right_low = left.astype(bfloat), stack_heads(right.astype(bfloat))
            here = place == float(at)
            grad_part = jnp.where(here, grad_scores, 0.0).astype(bfloat)
            grad_left = dot_nn(grad_part, right_low)
            grad_right = merge_heads(dot_tn(grad_part, left_low))
            if at:
                grad_left = grad_left * factor
                grad_right = grad_right * factor
                steps[table(at - 1), :] = acceptor * grad_left + lookup * grad_right
            grad_acceptor += grad_left
            grad_lookup += grad_right
        drec_part[rows, lanes] = grad_acceptor
        dkey_part[rows, lanes] = grad_lookup
        bonus = head_sum(acceptor * reward * lookup)
        dval_part[rows, lanes] = bonus * grad_exact + merge_heads(
            dot_tn(kept[slot], grad_out)
        )
        inner = (LEVELS - 1) * CHUNK
        dlog_part[rows, lanes] = dot_nn(sums_back[:, :inner], steps[...].astype(bfloat))
        return carry

    lax.fori_loop(0, pairs * chunks, inside, 0)
    wait_states(*exchange)
    me = lax.axis_index("dp")

    def later(step, state):
        other = count - 1 - step
        return state * land_a[other][:1] + unpacked_state(land_b[other])

    end_b[...] = lax.fori_loop(0, count - 1 - me, later, jnp.zeros(end_b.shape, jnp.float32))

    def finish(pair, carry):
        lanes = lanes_of(pair)

        def step(back, after):
            chunk = chunks - 1 - back
            rows, slot = rows_of(chunk), pair * chunks + chunk
            state = states[slot]
            after_low = after.astype(bfloat)
            reach = factors[slot, table(LEVELS - 1), :] * valid[rows, :]
            tail = factors[slot, table(LEVELS), :] * ending[rows, :]
            acceptor, lookup = rec[rows, lanes], key[rows, lanes]
            grad_reader = exact_nn(dout[rows, lanes], state) * reach
            grad_faded = exact_nn(val[rows, lanes], after) * tail
            faded = (lookup * tail).astype(bfloat)
            chunk_a = chunk_decay(chunk, lanes)
            total = chunk_a * jnp.sum(after * state, 0, keepdims=True)
            drec[rows, lanes] = (drec_part[rows, lanes] + grad_reader).astype(bfloat)
            dkey[rows, lanes] = (dkey_part[rows, lanes] + grad_faded).astype(bfloat)
            dval[rows, lanes] = (dval_part[rows, lanes] + dot_nt(faded, after_low)).astype(bfloat)
            inner = (LEVELS - 1) * CHUNK
            moves = jnp.concatenate([acceptor * grad_reader, lookup * grad_faded], 0)
            grad_log = dlog_part[rows, lanes] + total + dot_nn(
                sums_back[:, inner:], moves.astype(bfloat)
            )
            raw = grad_log * logw[rows, lanes]
            draw[rows, lanes] = raw
            dvec[0:1, lanes] += jnp.sum(raw, 0, keepdims=True)
            return after * chunk_a + local[slot]

        lax.fori_loop(0, chunks, step, stack_heads(end_b[:, lanes]))
        return carry

    lax.fori_loop(0, pairs, finish, 0)


def exchange_scratch(count, features):
    return [
        pltpu.VMEM((8, features), jnp.float32),
        pltpu.VMEM((2 * LANE_SPAN, features), jnp.bfloat16),
        pltpu.VMEM((count, 8, features), jnp.float32),
        pltpu.VMEM((count, 2 * LANE_SPAN, features), jnp.bfloat16),
        pltpu.SemaphoreType.DMA((2, count)),
        pltpu.SemaphoreType.DMA((2, count)),
    ]


def run_forward(count, rec, key, val, gpre, logw, vec, marks, tables):
    rows, features = rec.shape
    chunks, pairs = rows // CHUNK, features // PAIR
    slots = chunks * pairs
    whole_array = pl.BlockSpec(memory_space=pltpu.VMEM)
    level, sums, _ = tables
    return pl.pallas_call(
        functools.partial(recurrence_forward, count, chunks, pairs),
        out_shape=(
            jax.ShapeDtypeStruct((rows, features), jnp.bfloat16),
            jax.ShapeDtypeStruct((rows, features), jnp.float32),
            jax.ShapeDtypeStruct((slots, PAIR, PAIR), jnp.float32),
            jax.ShapeDtypeStruct((slots, CHUNK, 2 * CHUNK), jnp.bfloat16),
        ),
        in_specs=[whole_array] * 13,
        out_specs=(whole_array,) * 4,
        scratch_shapes=[
            pltpu.VMEM((slots, sums.shape[0], PAIR), jnp.float32),
            pltpu.VMEM((slots, 8, PAIR), jnp.float32),
            pltpu.VMEM((slots, PAIR, PAIR), jnp.float32),
            pltpu.VMEM((LANE_SPAN, features), jnp.float32),
        ]
        + exchange_scratch(count, features),
        compiler_params=pltpu.CompilerParams(
            collective_id=1, has_side_effects=True, vmem_limit_bytes=48 << 20
        ),
        name="recurrence_forward",
    )(rec, key, val, gpre, logw, vec, *marks, level, sums)


def run_backward(count, dgated, wkv, states, kept, rec, key, val, gpre, logw, vec, marks, tables):
    rows, features = rec.shape
    chunks, pairs = rows // CHUNK, features // PAIR
    slots = chunks * pairs
    whole_array = pl.BlockSpec(memory_space=pltpu.VMEM)
    level, sums, sums_back = tables
    low = jax.ShapeDtypeStruct((rows, features), jnp.bfloat16)
    full = pltpu.VMEM((rows, features), jnp.float32)
    return pl.pallas_call(
        functools.partial(recurrence_backward, count, chunks, pairs),
        out_shape=(
            low,
            low,
            low,
            low,
            jax.ShapeDtypeStruct((rows, features), jnp.float32),
            jax.ShapeDtypeStruct((8, features), jnp.float32),
        ),
        in_specs=[whole_array] * 18,
        out_specs=(whole_array,) * 6,
        scratch_shapes=[
            pltpu.VMEM((slots, sums.shape[0], PAIR), jnp.float32),
            pltpu.VMEM((slots, PAIR, PAIR), jnp.float32),
            pltpu.VMEM((LANE_SPAN, features), jnp.float32),
            full,
            full,
            full,
            full,
            full,
            pltpu.VMEM(((LEVELS - 1) * CHUNK, PAIR), jnp.float32),
        ]
        + exchange_scratch(count, features),
        compiler_params=pltpu.CompilerParams(
            collective_id=2, has_side_effects=True, vmem_limit_bytes=52 << 20
        ),
        name="recurrence_backward",
    )(dgated, wkv, states, kept, rec, key, val, gpre, logw, vec, *marks, level, sums, sums_back)


def gather_rows(value):
    return lax.all_gather(value, "mp", axis=0, tiled=True)


def sum_rows(value):
    return lax.psum_scatter(
        value.astype(jnp.bfloat16), "mp", scatter_dimension=0, tiled=True
    ).astype(jnp.float32)


def update(carried_memory, grad, fan, total_tokens):
    rate = (total_tokens * fan) ** (-0.5)
    scaled = rate * grad
    velocity = momentum_rate * carried_memory[1] + scaled
    weight = carried_memory[0] - (scaled + momentum_rate * velocity)
    average = average_rate * carried_memory[2] + (1.0 - average_rate) * weight
    return jnp.stack([velocity, weight, average])


def split_three(value):
    pieces = []
    for _ in range(3):
        pieces.append(lax.reduce_precision(value, 8, 7))
        value = value - pieces[-1]
    return [piece.astype(jnp.bfloat16) for piece in pieces]


def swap_columns(value):
    count = lax.axis_size("mp")
    rows, width = value.shape
    pieces = value.reshape(rows, count, width // count).transpose(1, 0, 2)
    mixed = lax.all_to_all(pieces, "mp", 0, 0, tiled=True)
    return mixed.reshape(count * rows, width // count)


def swap_rows(value):
    count = lax.axis_size("mp")
    rows, width = value.shape
    mixed = lax.all_to_all(
        value.reshape(count, rows // count, width), "mp", 0, 0, tiled=True
    )
    return mixed.transpose(1, 0, 2).reshape(rows // count, count * width)


def shifted(value, before, keep):
    return jnp.concatenate([before, value[:-1]], 0) * keep[:, None] - value


def shifted_back(value):
    return jnp.concatenate([value[1:], jnp.zeros((1, value.shape[1]), value.dtype)], 0)


def add_last(value, arriving):
    return jnp.concatenate([value[:-1], value[-1:] + arriving], 0)


def body(
    tokens,
    cotangent,
    lengths,
    mix_state,
    out_state,
    key_state,
    value_state,
    gate_state,
    down_state,
    up_state,
    vector_state,
):
    bfloat = jnp.bfloat16
    single = jnp.float32
    dp_count = lax.axis_size("dp")
    mp_count = lax.axis_size("mp")
    dp_index = lax.axis_index("dp")
    mp_index = lax.axis_index("mp")
    own_rows = tokens.shape[0]
    width = tokens.shape[1]
    group_rows = own_rows * mp_count
    total_tokens = group_rows * dp_count
    features = mix_state.shape[3]
    maa_cols = 5 * TM_RANK
    down_cols = maa_cols + DECAY_RANK
    col_start = mp_index * features
    row_start = mp_index * own_rows
    own_width = down_state.shape[1]

    pack = jnp.concatenate(
        [down_state[0].astype(bfloat), up_state[0].T.astype(bfloat)]
        + split_three(vector_state[0].T),
        1,
    )
    pack = jnp.pad(pack, ((0, 0), (0, -pack.shape[1] % 128)))
    small = lax.all_gather(lax.all_gather(pack, "mp", axis=0, tiled=True), "dp", axis=0, tiled=True)
    tokens_all = gather_rows(tokens)
    mix_weight, out_weight, gate_weight, key_weight, value_weight = (
        lax.all_gather(mix_state[0].astype(bfloat), "dp", axis=1, tiled=True),
        lax.all_gather(out_state[0].astype(bfloat), "dp", axis=1, tiled=True),
        lax.all_gather(gate_state[0].astype(bfloat), "dp", axis=0, tiled=True),
        lax.all_gather(key_state[0].astype(bfloat), "dp", axis=0, tiled=True),
        lax.all_gather(value_state[0].astype(bfloat), "dp", axis=1, tiled=True),
    )
    cotangent_cols = swap_columns(cotangent).astype(single)
    down_weight = small[:, :down_cols]
    up_weight = small[:, down_cols : 2 * down_cols]
    vectors = sum(
        small[:, 2 * down_cols + 16 * part : 2 * down_cols + 16 * part + 16].astype(single)
        for part in range(3)
    ).T

    seq_ends = jnp.cumsum(lengths)
    offsets = seq_ends - lengths
    positions = dp_index * group_rows + jnp.arange(group_rows, dtype=jnp.int32)
    opening = jnp.any(positions[:, None] == offsets[None, :], 1).astype(single)
    segment = jnp.sum((offsets[None, :] <= positions[:, None]).astype(single), 1)
    keep = 1.0 - opening
    chunks = group_rows // CHUNK
    parts = segment.reshape(chunks, CHUNK)
    first = parts[:, :1] - opening.reshape(chunks, CHUNK)[:, :1]

    def spread(value, lanes):
        return jnp.broadcast_to(value.astype(single).reshape(-1, 1), (value.size, lanes))

    marks = (
        spread(parts, 2 * CHUNK),
        jnp.repeat(jnp.concatenate([parts, parts], 1), 8, 0),
        spread(parts == first, PAIR),
        spread(parts == parts[:, -1:], PAIR),
        spread(jnp.repeat(parts[:, -1:] == first, 8, 0), PAIR),
    )
    level, sums, sums_back = level_tables()
    tables = (jnp.asarray(level), jnp.asarray(sums, bfloat), jnp.asarray(sums_back, bfloat))

    def local_share(row_number):
        return lax.dynamic_slice_in_dim(vectors[row_number], col_start, features, 0)

    def own_part(value):
        return lax.dynamic_slice_in_dim(value, row_start, own_rows, 0)

    before_first = from_behind(tokens_all[-1:], "dp", 1)
    hidden_one, hat_one, inv_one = norm_forward(
        tokens_all.astype(single), vectors[0], vectors[1], norm_epsilon
    )
    before_one = norm_forward(before_first.astype(single), vectors[0], vectors[1], norm_epsilon)[0]
    delta_one = shifted(hidden_one, before_one, keep)
    base_low = (hidden_one + delta_one * vectors[2]).astype(bfloat)
    mix_act = jnp.tanh(half_dot(base_low, down_weight[:, :maa_cols]))
    mix_act_low = mix_act.astype(bfloat)
    act_blocks = [mix_act_low[:, TM_RANK * n : TM_RANK * (n + 1)] for n in range(5)]
    up_blocks = [up_weight[:, TM_RANK * n : TM_RANK * (n + 1)] for n in range(5)]
    scales = [vectors[3 + n] + half_right(act_blocks[n], up_blocks[n]) for n in range(5)]
    inputs_low = [(hidden_one + delta_one * scales[n]).astype(bfloat) for n in range(5)]
    decay_act = jnp.tanh(half_dot(inputs_low[0], down_weight[:, maa_cols:]))
    decay_low = decay_act.astype(bfloat)
    decay_up = lax.dynamic_slice_in_dim(up_weight[:, maa_cols:], col_start, features, 0)
    log_fading_rate = -jnp.exp(local_share(8) + half_right(decay_low, decay_up))
    acceptor_entries = half_dot(inputs_low[3], mix_weight[0])
    lookup_tensor = half_dot(inputs_low[1], mix_weight[1])
    payload_tensor = half_dot(inputs_low[2], mix_weight[2])
    gate_pre = half_dot(inputs_low[4], mix_weight[3])
    local_vectors = jnp.concatenate(
        [jnp.stack([local_share(9), local_share(10), local_share(11)]), jnp.zeros((5, features))], 0
    )
    branch = (acceptor_entries, lookup_tensor, payload_tensor, gate_pre, log_fading_rate)
    gated_low, wkv, states, kept = run_forward(dp_count, *branch, local_vectors, marks, tables)

    attention = sum_rows(half_dot(gated_low, out_weight))
    residual = tokens.astype(single) + attention
    residual_all = gather_rows(residual.astype(bfloat))
    before_second = from_behind(residual_all[-1:], "dp", 1)
    hidden_two, hat_two, inv_two = norm_forward(
        residual_all.astype(single), vectors[12], vectors[13], norm_epsilon
    )
    before_two = norm_forward(before_second.astype(single), vectors[12], vectors[13], norm_epsilon)[
        0
    ]
    delta_two = shifted(hidden_two, before_two, keep)
    key_in_low = (hidden_two + delta_two * vectors[14]).astype(bfloat)
    recv_in_low = (hidden_two + delta_two * vectors[15]).astype(bfloat)
    key_pre = half_dot(key_in_low, key_weight)
    key_act_low = jnp.square(jnp.maximum(key_pre, 0.0)).astype(bfloat)
    recv_gate = jax.nn.sigmoid(half_dot(recv_in_low, gate_weight))
    channel_part = half_dot(key_act_low, value_weight).astype(bfloat)
    channel_part = channel_part.reshape(group_rows, mp_count, features).transpose(1, 0, 2)
    channel_sum = lax.psum_scatter(
        channel_part, "mp", scatter_dimension=0, tiled=True
    )[0].astype(single)
    gated_sum = recv_gate * channel_sum
    mixed = (residual + swap_rows(gated_sum.astype(bfloat)).astype(single)).astype(bfloat)

    grad_kv = (cotangent_cols * recv_gate).astype(bfloat)
    grad_recv_pre = (cotangent_cols * gated_sum * (1.0 - recv_gate)).astype(bfloat)
    grad_kv_all = (
        lax.all_gather(grad_kv, "mp", axis=0, tiled=False)
        .transpose(1, 0, 2)
        .reshape(group_rows, width)
    )
    grad_key_act = half_right(grad_kv_all, value_weight)
    grad_key_pre = (grad_key_act * 2.0 * jnp.maximum(key_pre, 0.0)).astype(bfloat)
    grad_key_in = half_right(grad_key_pre, key_weight)
    grad_recv_in = half_right(grad_recv_pre, gate_weight)
    grad_value_weight = half_left(key_act_low, grad_kv_all)
    grad_key_weight = half_left(key_in_low, grad_key_pre)
    grad_gate_weight = half_left(recv_in_low, grad_recv_pre)
    grad_delta_two = grad_key_in * vectors[14] + grad_recv_in * vectors[15]
    grad_key_mix = jnp.sum(grad_key_in * delta_two, 0)
    grad_recv_mix = jnp.sum(grad_recv_in * delta_two, 0)
    shifted_grad_two = grad_delta_two * keep[:, None]
    arriving_two = from_behind(shifted_grad_two[:1], "dp", -1)
    grad_hidden_two = add_last(
        grad_key_in + grad_recv_in - grad_delta_two + shifted_back(shifted_grad_two), arriving_two
    )
    grad_gain_two = jnp.sum(grad_hidden_two * hat_two, 0)
    grad_bias_two = jnp.sum(grad_hidden_two, 0)
    grad_residual = cotangent.astype(single) + norm_backward(
        sum_rows(grad_hidden_two), own_part(hat_two), own_part(inv_two), vectors[12]
    )
    grad_attn_all = gather_rows(grad_residual.astype(bfloat))
    grad_out_weight = half_left(gated_low, grad_attn_all)
    grad_gated = half_right(grad_attn_all, out_weight)
    grad_recept, grad_keys, grad_values, grad_gate_pre, grad_raw, grad_local = run_backward(
        dp_count, grad_gated, wkv, states, kept, *branch, local_vectors, marks, tables
    )

    raw_low = grad_raw.astype(bfloat)
    grad_up_decay = half_left(raw_low, decay_low)
    grad_decay_act = (half_dot(raw_low, decay_up) * (1.0 - decay_act * decay_act)).astype(bfloat)
    grad_down_decay = half_left(inputs_low[0], grad_decay_act)
    grad_inputs = [
        half_right(grad_decay_act, down_weight[:, maa_cols:]),
        half_right(grad_keys, mix_weight[1]),
        half_right(grad_values, mix_weight[2]),
        half_right(grad_recept, mix_weight[0]),
        half_right(grad_gate_pre, mix_weight[3]),
    ]
    grad_mix_weight = jnp.stack(
        [
            half_left(inputs_low[3], grad_recept),
            half_left(inputs_low[1], grad_keys),
            half_left(inputs_low[2], grad_values),
            half_left(inputs_low[4], grad_gate_pre),
        ]
    )
    grad_mixes = [grad_inputs[n] * delta_one for n in range(5)]
    mixes_low = [value.astype(bfloat) for value in grad_mixes]
    grad_up_mix = [half_left(mixes_low[n], act_blocks[n]) for n in range(5)]
    grad_mix_act = jnp.concatenate([half_dot(mixes_low[n], up_blocks[n]) for n in range(5)], 1)
    grad_mix_pre = (grad_mix_act * (1.0 - mix_act * mix_act)).astype(bfloat)
    grad_down_mix = half_left(base_low, grad_mix_pre)
    grad_base = half_right(grad_mix_pre, down_weight[:, :maa_cols])
    grad_delta_one = grad_base * vectors[2]
    grad_hidden_one = grad_base
    for number in range(5):
        grad_delta_one = grad_delta_one + grad_inputs[number] * scales[number]
        grad_hidden_one = grad_hidden_one + grad_inputs[number]
    shifted_grad_one = grad_delta_one * keep[:, None]
    arriving_one = from_behind(shifted_grad_one[:1], "dp", -1)
    grad_hidden_one = add_last(
        grad_hidden_one - grad_delta_one + shifted_back(shifted_grad_one), arriving_one
    )
    grad_tokens = grad_residual + norm_backward(
        sum_rows(grad_hidden_one), own_part(hat_one), own_part(inv_one), vectors[0]
    )

    def positioned(value):
        return lax.dynamic_update_slice_in_dim(
            jnp.zeros((width,) + value.shape[1:], single), value, col_start, 0
        )

    grad_vectors = jnp.concatenate(
        [
            jnp.stack(
                [
                    jnp.sum(grad_hidden_one * hat_one, 0),
                    jnp.sum(grad_hidden_one, 0),
                    jnp.sum(grad_base * delta_one, 0),
                ]
                + [jnp.sum(value, 0) for value in grad_mixes]
            ).T,
            positioned(grad_local[:4].T),
            jnp.stack([grad_gain_two, grad_bias_two, grad_key_mix, grad_recv_mix]).T,
        ],
        1,
    )
    grad_pack = jnp.concatenate(
        [grad_down_mix, grad_down_decay] + grad_up_mix + [positioned(grad_up_decay), grad_vectors],
        1,
    ).astype(bfloat)
    grad_pack = jnp.pad(grad_pack, ((0, 0), (0, -grad_pack.shape[1] % 128)))

    def summed(value, axis):
        return lax.psum_scatter(
            value.astype(bfloat), "dp", scatter_dimension=axis, tiled=True
        )

    value_sum = summed(grad_value_weight, 1).astype(single)
    key_sum = summed(grad_key_weight, 0).astype(single)
    gate_sum = summed(grad_gate_weight, 0).astype(single)
    out_sum = summed(grad_out_weight, 1).astype(single)
    mix_sum = summed(grad_mix_weight, 1).astype(single)
    small_sum = sum_rows(summed(grad_pack, 0))
    return (
        mixed,
        grad_tokens,
        update(mix_state, mix_sum, width, total_tokens),
        update(out_state, out_sum, width, total_tokens),
        update(key_state, key_sum, width, total_tokens),
        update(value_state, value_sum, FF, total_tokens),
        update(gate_state, gate_sum, width, total_tokens),
        update(down_state, small_sum[:, :down_cols], width, total_tokens),
        update(up_state, small_sum[:, down_cols : 2 * down_cols].T, TM_RANK, total_tokens),
        update(
            vector_state, small_sum[:, 2 * down_cols : 2 * down_cols + 16].T, 1, total_tokens
        ),
    )


def solution(mesh):
    return jax.shard_map(
        body,
        mesh=mesh,
        in_specs=(
            P(("dp", "mp"), None),
            P(("dp", "mp"), None),
            P(),
            P(None, None, "dp", "mp"),
            P(None, "mp", "dp"),
            P(None, "dp", "mp"),
            P(None, "mp", "dp"),
            P(None, "dp", "mp"),
            P(None, ("dp", "mp"), None),
            P(None, None, ("dp", "mp")),
            P(None, None, ("dp", "mp")),
        ),
        out_specs=(
            P(("dp", "mp"), None),
            P(("dp", "mp"), None),
            P(None, None, "dp", "mp"),
            P(None, "mp", "dp"),
            P(None, "dp", "mp"),
            P(None, "mp", "dp"),
            P(None, "dp", "mp"),
            P(None, ("dp", "mp"), None),
            P(None, None, ("dp", "mp")),
            P(None, None, ("dp", "mp")),
        ),
        check_vma=False,
    )
```

```python
import functools

import jax
import jax.numpy as jnp
import numpy as np
from jax import lax
from jax.experimental import pallas as pl
from jax.experimental.pallas import tpu as pltpu
from jax.sharding import PartitionSpec as P

LANE_SPAN = 64
FF = 7168
TM_RANK = 32
DECAY_RANK = 64


momentum_rate = 0.9
average_rate = 0.9
norm_epsilon = 1e-05
group_epsilon = 0.00064
CHUNK = 128
LEVELS = 7
PAIR = 2 * LANE_SPAN
MESH = pl.DeviceIdType.MESH
PIECES = 4


def from_behind(block, axis, distance):
    devices = range(lax.axis_size(axis))
    route = [(i - distance, i) for i in devices if i - distance in devices]
    return lax.ppermute(block, axis, route)


def half_dot(left, right):
    return jnp.dot(left, right, preferred_element_type=jnp.float32)


def half_left(left, right):
    return lax.dot_general(
        left, right, (((0,), (0,)), ((), ())), preferred_element_type=jnp.float32
    )


def half_right(left, right):
    return lax.dot_general(
        left, right, (((1,), (1,)), ((), ())), preferred_element_type=jnp.float32
    )


def split_pair(value):
    upper_part = value.astype(jnp.bfloat16)
    lower_part = (value - upper_part.astype(jnp.float32)).astype(jnp.bfloat16)
    return (upper_part, lower_part)


def norm_forward(value, gain, bias, epsilon):
    centre = value - jnp.mean(value, -1, keepdims=True)
    inverse = lax.rsqrt(jnp.mean(centre * centre, -1, keepdims=True) + epsilon)
    normal_hat = centre * inverse
    return (normal_hat * gain + bias, normal_hat, inverse)


def norm_backward(grad_out, normal_hat, inverse, gain):
    scaled = grad_out * gain
    return inverse * (
        scaled
        - jnp.mean(scaled, -1, keepdims=True)
        - normal_hat * jnp.mean(scaled * normal_hat, -1, keepdims=True)
    )


def level_tables():
    row = np.arange(CHUNK)
    later, earlier = row[:, None], row[None, :]
    level = np.full((CHUNK, CHUNK), -1.0, np.float32)
    sums = []
    for bit in range(LEVELS):
        block = (later >> (bit + 1)) == (earlier >> (bit + 1))
        level[block & ((later >> bit) % 2 == 1) & ((earlier >> bit) % 2 == 0)] = bit
        middle = ((later >> (bit + 1)) << (bit + 1)) + (1 << bit)
        upper = (later >> bit) % 2 == 1
        between = np.where(
            upper, (earlier >= middle) & (earlier < later), (earlier > later) & (earlier < middle)
        )
        if bit:
            sums.append(between)
    sums += [earlier < later, earlier > later]
    sums = np.concatenate(sums, 0).astype(np.float32)
    return np.concatenate([level, level], 1), np.concatenate([sums, sums], 1), sums.T


def dot_nn(left, right):
    return lax.dot_general(
        left, right, (((1,), (0,)), ((), ())), preferred_element_type=jnp.float32
    )


def dot_nt(left, right):
    return lax.dot_general(
        left, right, (((1,), (1,)), ((), ())), preferred_element_type=jnp.float32
    )


def dot_tn(left, right):
    return lax.dot_general(
        left, right, (((0,), (0,)), ((), ())), preferred_element_type=jnp.float32
    )


def first_head(shape):
    return lax.broadcasted_iota(jnp.int32, shape, len(shape) - 1) < LANE_SPAN


def stack_heads(value):
    first = first_head(value.shape)
    none = jnp.zeros_like(value)
    return jnp.concatenate([jnp.where(first, value, none), jnp.where(first, none, value)], 0)


def merge_heads(value):
    half = value.shape[0] // 2
    return jnp.where(first_head((half, value.shape[1])), value[:half], value[half:])


def own_blocks(value):
    upper = lax.broadcasted_iota(jnp.int32, value.shape, 0) < LANE_SPAN
    return jnp.where(upper == first_head(value.shape), value, 0.0)


def head_mean(value):
    row = lax.broadcasted_iota(jnp.int32, (PAIR, PAIR), 0) < LANE_SPAN
    ones = jnp.where(row == first_head((PAIR, PAIR)), 1.0 / LANE_SPAN, 0.0).astype(jnp.bfloat16)
    upper, lower = split_pair(value)
    return dot_nn(upper, ones) + dot_nn(lower, ones)


def head_sum(value):
    return head_mean(value) * float(LANE_SPAN)


def exact_pieces(left, right, axis_left, axis_right):
    upper, lower = split_pair(left)
    right_upper, right_lower = split_pair(right)
    return (
        jnp.concatenate([upper, lower, upper], axis_left),
        jnp.concatenate([right_upper, right_upper, right_lower], axis_right),
    )


def exact_nn(left, right):
    return dot_nn(*exact_pieces(left, right, 1, 0))


def exact_nt(left, right):
    return dot_nt(*exact_pieces(left, right, 1, 1))


def exact_tn(left, right):
    return dot_tn(*exact_pieces(left, right, 0, 0))


def packed_state(state):
    return jnp.concatenate(split_pair(state[:LANE_SPAN] + state[LANE_SPAN:]), 0)


def unpacked_state(piece):
    piece = piece.astype(jnp.float32)
    return piece[:LANE_SPAN] + piece[LANE_SPAN:]


def rows_of(chunk):
    return pl.ds(pl.multiple_of(chunk * CHUNK, CHUNK), CHUNK)


def lanes_of(pair):
    return pl.ds(pl.multiple_of(pair * PAIR, PAIR), PAIR)


def marks_of(chunk):
    return pl.ds(pl.multiple_of(chunk * 8, 8), 8)


def greet(count):
    me, mine = lax.axis_index("dp"), lax.axis_index("mp")
    barrier = pltpu.get_barrier_semaphore()
    for step in range(1, count):
        pl.semaphore_signal(
            barrier, inc=1, device_id=(lax.rem(me + step, count), mine), device_id_type=MESH
        )
    pl.semaphore_wait(barrier, count - 1)


def state_copies(other, me, sends, lands, send_sems, recv_sems, to):
    return [
        pltpu.make_async_remote_copy(
            src_ref=send,
            dst_ref=land.at[me],
            send_sem=send_sems.at[number, other],
            recv_sem=recv_sems.at[number, me],
            device_id=(to, lax.axis_index("mp")),
            device_id_type=MESH,
        )
        for number, (send, land) in enumerate(zip(sends, lands))
    ]


def send_states(count, sends, lands, send_sems, recv_sems, ahead):
    me = lax.axis_index("dp")
    for other in range(count):

        @pl.when((other > me) if ahead else (other < me))
        def _():
            for copy in state_copies(other, me, sends, lands, send_sems, recv_sems, other):
                copy.start()


def wait_states(count, sends, lands, send_sems, recv_sems, ahead):
    me = lax.axis_index("dp")
    for other in range(count):

        @pl.when((other > me) if ahead else (other < me))
        def _():
            for copy in state_copies(other, me, sends, lands, send_sems, recv_sems, other):
                copy.wait_send()

        @pl.when((other < me) if ahead else (other > me))
        def _():
            for copy in state_copies(other, other, sends, lands, send_sems, recv_sems, me):
                copy.wait_recv()


def decay_factors(fading, sums):
    upper, lower = split_pair(fading)
    return jnp.exp(dot_nn(sums, jnp.concatenate([upper, lower], 0)))


def table(at):
    return slice(at * CHUNK, (at + 1) * CHUNK)


def level_inputs(level, acceptor, lookup, factors):
    if level == 0:
        return None, acceptor, lookup
    factor = factors[table(level - 1), :]
    return factor, acceptor * factor, lookup * factor


def recurrence_forward(
    count, chunks, pairs,
    rec, key, val, gpre, logw, vec, seg_col, seg_row, valid, ending, whole, level, sums,
    gated, wkv, states, kept,
    factors, pre_a, pre_b, start_b, send_a, send_b, land_a, land_b, send_sems, recv_sems,
):
    bfloat = jnp.bfloat16
    greet(count)

    def summary(pair, carry):
        lanes = lanes_of(pair)

        def step(chunk, before):
            before_a, before_b = before
            rows, slot = rows_of(chunk), pair * chunks + chunk
            fading = logw[rows, lanes]
            factor = decay_factors(fading, sums[...])
            factors[slot] = factor
            faded = key[rows, lanes] * factor[table(LEVELS)] * ending[rows, :]
            chunk_b = own_blocks(exact_tn(val[rows, lanes], faded))
            chunk_a = jnp.exp(jnp.sum(fading, 0, keepdims=True)) * whole[marks_of(chunk), :][:1]
            pre_a[slot] = jnp.broadcast_to(before_a, (8, PAIR))
            pre_b[slot] = before_b
            return before_a * chunk_a, before_b * chunk_a + chunk_b

        last_a, last_b = lax.fori_loop(
            0, chunks, step, (jnp.ones((1, PAIR), jnp.float32), jnp.zeros((PAIR, PAIR), jnp.float32))
        )
        send_a[:, lanes] = jnp.broadcast_to(last_a, (8, PAIR))
        send_b[:, lanes] = packed_state(last_b)
        return carry

    lax.fori_loop(0, pairs, summary, 0)
    exchange = (count, (send_a, send_b), (land_a, land_b), send_sems, recv_sems, True)
    send_states(*exchange)

    def inside(slot, carry):
        pair, chunk = slot // chunks, slot % chunks
        rows, lanes = rows_of(chunk), lanes_of(pair)
        acceptor, lookup, payload = rec[rows, lanes], key[rows, lanes], val[rows, lanes]
        place = jnp.where(seg_col[rows, :] == seg_row[marks_of(chunk), :][:1], level[...], -1.0)
        scores = jnp.zeros((CHUNK, 2 * CHUNK), jnp.float32)
        for at in range(LEVELS):
            _, left, right = level_inputs(at, acceptor, lookup, factors.at[slot])
            part = exact_nt(left, stack_heads(right))
            scores = jnp.where(place == float(at), part, scores)
        bonus = head_sum(acceptor * vec[0:1, lanes] * lookup) * payload
        wkv[rows, lanes] = bonus + exact_nn(scores, stack_heads(payload))
        kept[slot] = scores.astype(bfloat)
        return carry

    lax.fori_loop(0, pairs * chunks, inside, 0)
    wait_states(*exchange)
    start_b[...] = lax.fori_loop(
        0,
        lax.axis_index("dp"),
        lambda other, state: state * land_a[other][:1] + unpacked_state(land_b[other]),
        jnp.zeros(start_b.shape, jnp.float32),
    )

    def finish(slot, carry):
        pair, chunk = slot // chunks, slot % chunks
        rows, lanes = rows_of(chunk), lanes_of(pair)
        state = pre_b[slot] + pre_a[slot][:1] * stack_heads(start_b[:, lanes])
        states[slot] = state
        reader = rec[rows, lanes] * factors[slot, table(LEVELS - 1), :] * valid[rows, :]
        out = wkv[rows, lanes] + exact_nt(reader, state)
        wkv[rows, lanes] = out
        centre = out - head_mean(out)
        inverse = lax.rsqrt(head_mean(centre * centre) + group_epsilon)
        normed = centre * inverse * vec[1:2, lanes] + vec[2:3, lanes]
        pre = gpre[rows, lanes]
        gated[rows, lanes] = (normed * pre * jax.nn.sigmoid(pre)).astype(bfloat)
        return carry

    lax.fori_loop(0, pairs * chunks, finish, 0)


def recurrence_backward(
    count, chunks, pairs,
    dgated, wkv, states, kept, rec, key, val, gpre, logw, vec, seg_col, seg_row, valid, ending, whole,
    level, sums, sums_back,
    drec, dkey, dval, dgpre, draw, dvec,
    factors, local, end_b, dout, drec_part, dkey_part, dval_part, dlog_part, steps,
    send_a, send_b, land_a, land_b, send_sems, recv_sems,
):
    bfloat = jnp.bfloat16
    greet(count)
    dvec[...] = jnp.zeros(dvec.shape, jnp.float32)

    def chunk_decay(chunk, lanes):
        fading = logw[rows_of(chunk), lanes]
        return jnp.exp(jnp.sum(fading, 0, keepdims=True)) * whole[marks_of(chunk), :][:1]

    def summary(pair, carry):
        lanes = lanes_of(pair)

        def step(back, after):
            after_a, after_b = after
            chunk = chunks - 1 - back
            rows, slot = rows_of(chunk), pair * chunks + chunk
            factor = decay_factors(logw[rows, lanes], sums[...])
            factors[slot] = factor
            out = wkv[rows, lanes]
            centre = out - head_mean(out)
            inverse = lax.rsqrt(head_mean(centre * centre) + group_epsilon)
            hat = centre * inverse
            gain = vec[1:2, lanes]
            normed = hat * gain + vec[2:3, lanes]
            pre = gpre[rows, lanes]
            sig = jax.nn.sigmoid(pre)
            grad = dgated[rows, lanes]
            grad_normed = grad * pre * sig
            dgpre[rows, lanes] = (grad * normed * sig * (1.0 + pre * (1.0 - sig))).astype(bfloat)
            dvec[2:3, lanes] += jnp.sum(grad_normed * hat, 0, keepdims=True)
            dvec[3:4, lanes] += jnp.sum(grad_normed, 0, keepdims=True)
            scaled = grad_normed * gain
            grad_out = inverse * (scaled - head_mean(scaled) - hat * head_mean(scaled * hat))
            dout[rows, lanes] = grad_out
            reader = rec[rows, lanes] * factor[table(LEVELS - 1)] * valid[rows, :]
            inner = own_blocks(exact_tn(grad_out, reader))
            local[slot] = inner
            chunk_a = chunk_decay(chunk, lanes)
            return after_a * chunk_a, after_b * chunk_a + inner

        last_a, last_b = lax.fori_loop(
            0, chunks, step, (jnp.ones((1, PAIR), jnp.float32), jnp.zeros((PAIR, PAIR), jnp.float32))
        )
        send_a[:, lanes] = jnp.broadcast_to(last_a, (8, PAIR))
        send_b[:, lanes] = packed_state(last_b)
        return carry

    lax.fori_loop(0, pairs, summary, 0)
    exchange = (count, (send_a, send_b), (land_a, land_b), send_sems, recv_sems, False)
    send_states(*exchange)

    def inside(slot, carry):
        pair, chunk = slot // chunks, slot % chunks
        rows, lanes = rows_of(chunk), lanes_of(pair)
        acceptor, lookup, payload = rec[rows, lanes], key[rows, lanes], val[rows, lanes]
        reward = vec[0:1, lanes]
        grad_exact = dout[rows, lanes]
        grad_out = grad_exact.astype(bfloat)
        place = jnp.where(seg_col[rows, :] == seg_row[marks_of(chunk), :][:1], level[...], -1.0)
        grad_scores = exact_nt(grad_exact, stack_heads(payload))
        grad_bonus = head_sum(grad_exact * payload)
        dvec[1:2, lanes] += jnp.sum(acceptor * lookup * grad_bonus, 0, keepdims=True)
        grad_acceptor = reward * lookup * grad_bonus
        grad_lookup = reward * acceptor * grad_bonus
        for at in range(LEVELS):
            factor, left, right = level_inputs(at, acceptor, lookup, factors.at[slot])
            left_low, right_low = left.astype(bfloat), stack_heads(right.astype(bfloat))
            here = place == float(at)
            grad_part = jnp.where(here, grad_scores, 0.0).astype(bfloat)
            grad_left = dot_nn(grad_part, right_low)
            grad_right = merge_heads(dot_tn(grad_part, left_low))
            if at:
                grad_left = grad_left * factor
                grad_right = grad_right * factor
                steps[table(at - 1), :] = acceptor * grad_left + lookup * grad_right
            grad_acceptor += grad_left
            grad_lookup += grad_right
        drec_part[rows, lanes] = grad_acceptor
        dkey_part[rows, lanes] = grad_lookup
        bonus = head_sum(acceptor * reward * lookup)
        dval_part[rows, lanes] = bonus * grad_exact + merge_heads(
            dot_tn(kept[slot], grad_out)
        )
        inner = (LEVELS - 1) * CHUNK
        dlog_part[rows, lanes] = dot_nn(sums_back[:, :inner], steps[...].astype(bfloat))
        return carry

    lax.fori_loop(0, pairs * chunks, inside, 0)
    wait_states(*exchange)
    me = lax.axis_index("dp")

    def later(step, state):
        other = count - 1 - step
        return state * land_a[other][:1] + unpacked_state(land_b[other])

    end_b[...] = lax.fori_loop(0, count - 1 - me, later, jnp.zeros(end_b.shape, jnp.float32))

    def finish(pair, carry):
        lanes = lanes_of(pair)

        def step(back, after):
            chunk = chunks - 1 - back
            rows, slot = rows_of(chunk), pair * chunks + chunk
            state = states[slot]
            after_low = after.astype(bfloat)
            reach = factors[slot, table(LEVELS - 1), :] * valid[rows, :]
            tail = factors[slot, table(LEVELS), :] * ending[rows, :]
            acceptor, lookup = rec[rows, lanes], key[rows, lanes]
            grad_reader = exact_nn(dout[rows, lanes], state) * reach
            grad_faded = exact_nn(val[rows, lanes], after) * tail
            faded = (lookup * tail).astype(bfloat)
            chunk_a = chunk_decay(chunk, lanes)
            total = chunk_a * jnp.sum(after * state, 0, keepdims=True)
            drec[rows, lanes] = (drec_part[rows, lanes] + grad_reader).astype(bfloat)
            dkey[rows, lanes] = (dkey_part[rows, lanes] + grad_faded).astype(bfloat)
            dval[rows, lanes] = (dval_part[rows, lanes] + dot_nt(faded, after_low)).astype(bfloat)
            inner = (LEVELS - 1) * CHUNK
            moves = jnp.concatenate([acceptor * grad_reader, lookup * grad_faded], 0)
            grad_log = dlog_part[rows, lanes] + total + dot_nn(
                sums_back[:, inner:], moves.astype(bfloat)
            )
            raw = grad_log * logw[rows, lanes]
            draw[rows, lanes] = raw
            dvec[0:1, lanes] += jnp.sum(raw, 0, keepdims=True)
            return after * chunk_a + local[slot]

        lax.fori_loop(0, chunks, step, stack_heads(end_b[:, lanes]))
        return carry

    lax.fori_loop(0, pairs, finish, 0)


def exchange_scratch(count, features):
    return [
        pltpu.VMEM((8, features), jnp.float32),
        pltpu.VMEM((2 * LANE_SPAN, features), jnp.bfloat16),
        pltpu.VMEM((count, 8, features), jnp.float32),
        pltpu.VMEM((count, 2 * LANE_SPAN, features), jnp.bfloat16),
        pltpu.SemaphoreType.DMA((2, count)),
        pltpu.SemaphoreType.DMA((2, count)),
    ]


def run_forward(count, rec, key, val, gpre, logw, vec, marks, tables):
    rows, features = rec.shape
    chunks, pairs = rows // CHUNK, features // PAIR
    slots = chunks * pairs
    whole_array = pl.BlockSpec(memory_space=pltpu.VMEM)
    level, sums, _ = tables
    return pl.pallas_call(
        functools.partial(recurrence_forward, count, chunks, pairs),
        out_shape=(
            jax.ShapeDtypeStruct((rows, features), jnp.bfloat16),
            jax.ShapeDtypeStruct((rows, features), jnp.float32),
            jax.ShapeDtypeStruct((slots, PAIR, PAIR), jnp.float32),
            jax.ShapeDtypeStruct((slots, CHUNK, 2 * CHUNK), jnp.bfloat16),
        ),
        in_specs=[whole_array] * 13,
        out_specs=(whole_array,) * 4,
        scratch_shapes=[
            pltpu.VMEM((slots, sums.shape[0], PAIR), jnp.float32),
            pltpu.VMEM((slots, 8, PAIR), jnp.float32),
            pltpu.VMEM((slots, PAIR, PAIR), jnp.float32),
            pltpu.VMEM((LANE_SPAN, features), jnp.float32),
        ]
        + exchange_scratch(count, features),
        compiler_params=pltpu.CompilerParams(
            collective_id=1, has_side_effects=True, vmem_limit_bytes=48 << 20
        ),
        name="recurrence_forward",
    )(rec, key, val, gpre, logw, vec, *marks, level, sums)


def run_backward(count, dgated, wkv, states, kept, rec, key, val, gpre, logw, vec, marks, tables):
    rows, features = rec.shape
    chunks, pairs = rows // CHUNK, features // PAIR
    slots = chunks * pairs
    whole_array = pl.BlockSpec(memory_space=pltpu.VMEM)
    level, sums, sums_back = tables
    low = jax.ShapeDtypeStruct((rows, features), jnp.bfloat16)
    full = pltpu.VMEM((rows, features), jnp.float32)
    return pl.pallas_call(
        functools.partial(recurrence_backward, count, chunks, pairs),
        out_shape=(
            low,
            low,
            low,
            low,
            jax.ShapeDtypeStruct((rows, features), jnp.float32),
            jax.ShapeDtypeStruct((8, features), jnp.float32),
        ),
        in_specs=[whole_array] * 18,
        out_specs=(whole_array,) * 6,
        scratch_shapes=[
            pltpu.VMEM((slots, sums.shape[0], PAIR), jnp.float32),
            pltpu.VMEM((slots, PAIR, PAIR), jnp.float32),
            pltpu.VMEM((LANE_SPAN, features), jnp.float32),
            full,
            full,
            full,
            full,
            full,
            pltpu.VMEM(((LEVELS - 1) * CHUNK, PAIR), jnp.float32),
        ]
        + exchange_scratch(count, features),
        compiler_params=pltpu.CompilerParams(
            collective_id=2, has_side_effects=True, vmem_limit_bytes=52 << 20
        ),
        name="recurrence_backward",
    )(dgated, wkv, states, kept, rec, key, val, gpre, logw, vec, *marks, level, sums, sums_back)


def flipped(index, mask):
    for bit in range(mask.bit_length()):
        size = 1 << bit
        if mask & size:
            index = index + size - 2 * size * lax.rem(index // size, 2)
    return index


def masks_over(bits):
    masks = [0]
    for bit in bits:
        masks = masks + [mask | (1 << bit) for mask in masks]
    return masks


def paths(count):
    higher = list(range(1, count.bit_length() - 1))
    return higher + [0], higher[::-1] + [0]


def remote(source, target, send_sem, recv_sem, dp, mp):
    return pltpu.make_async_remote_copy(
        src_ref=source,
        dst_ref=target,
        send_sem=send_sem,
        recv_sem=recv_sem,
        device_id=(dp, mp),
        device_id_type=MESH,
    )


def greet_all(partners):
    barrier = pltpu.get_barrier_semaphore()
    for dp, mp in partners:
        pl.semaphore_signal(barrier, inc=1, device_id=(dp, mp), device_id_type=MESH)
    pl.semaphore_wait(barrier, len(partners))


def line_partners(count):
    dp, mp = lax.axis_index("dp"), lax.axis_index("mp")
    return [(dp, lax.rem(mp + step, count)) for step in sorted({1, count - 1})]


def cube_partners(count):
    dp, mp = lax.axis_index("dp"), lax.axis_index("mp")
    return [(flipped(dp, 1 << bit), mp) for bit in range(count.bit_length() - 1)]


class Line:
    def __init__(self, count, rows, send_sems, recv_sems):
        self.count, self.rows = count, rows
        self.send_sems, self.recv_sems = send_sems, recv_sems
        self.dp, self.me = lax.axis_index("dp"), lax.axis_index("mp")
        self.piece = rows // PIECES

    def at(self, block, piece):
        return pl.ds(pl.multiple_of(block * self.rows + piece * self.piece, 16), self.piece)

    def copy(self, source, target, right, slot, piece):
        side = 0 if right else 1
        return remote(
            source,
            target,
            self.send_sems.at[side, slot, piece],
            self.recv_sems.at[side, slot, piece],
            self.dp,
            lax.rem(self.me + (1 if right else self.count - 1), self.count),
        )


class LineGather(Line):
    def hop(self, target, distance, piece, right):
        block = self.me - distance if right else self.me + distance
        ref = target.at[self.at(block, piece)]
        return self.copy(ref, ref, right, distance, piece)

    def holds(self, distance, right):
        return self.me >= distance if right else self.me + distance < self.count

    def passes(self, distance, right):
        onward = self.me < self.count - 1 if right else self.me > 0
        return jnp.logical_and(self.holds(distance, right), onward)

    def send(self, target, distance, piece):
        for right in (True, False):
            if distance:

                @pl.when(self.holds(distance, right))
                def _():
                    block = self.me - distance if right else self.me + distance
                    ref = target.at[self.at(block, piece)]
                    self.copy(ref, ref, right, distance - 1, piece).wait_recv()

            if distance < self.count - 1:

                @pl.when(self.passes(distance, right))
                def _():
                    self.hop(target, distance, piece, right).start()

    def finish(self, target):
        for distance in range(self.count - 1):
            for piece in range(PIECES):
                for right in (True, False):

                    @pl.when(self.passes(distance, right))
                    def _():
                        self.hop(target, distance, piece, right).wait_send()


class LineSum(Line):
    def hop(self, source, land, block, piece, right):
        return self.copy(
            source.at[self.at(block, piece)],
            land.at[0 if right else 1, self.at(block, piece)],
            right,
            block,
            piece,
        )

    def forward(self, part, moving, land, block, piece, right):
        side = 0 if right else 1
        at = self.at(block, piece)
        first = 0 if right else self.count - 1

        @pl.when(self.me < block if right else self.me > block)
        def _():
            @pl.when(self.me == first)
            def _():
                moving[at] = part[at]

            @pl.when(self.me != first)
            def _():
                self.hop(moving, land, block, piece, right).wait_recv()
                moving[at] = (
                    part[at].astype(jnp.float32) + land[side, at].astype(jnp.float32)
                ).astype(jnp.bfloat16)

            self.hop(moving, land, block, piece, right).start()

    def step(self, part, moving, land, number):
        for piece in range(PIECES):
            self.forward(part, moving, land, self.count - 1 - number, piece, True)
            self.forward(part, moving, land, number, piece, False)

    def total(self, part, moving, land, total, piece):
        at = self.at(self.me, piece)
        own = slice(piece * self.piece, (piece + 1) * self.piece)
        total[own] = part[at].astype(jnp.float32)
        for right in (True, False):

            @pl.when(self.me > 0 if right else self.me < self.count - 1)
            def _():
                self.hop(moving, land, self.me, piece, right).wait_recv()
                total[own] += land[0 if right else 1, at].astype(jnp.float32)

        return own

    def finish(self, moving, land):
        for number in range(self.count - 1):
            for piece in range(PIECES):
                for right in (True, False):
                    block = self.count - 1 - number if right else number

                    @pl.when(self.me < block if right else self.me > block)
                    def _():
                        self.hop(moving, land, block, piece, right).wait_send()


class Cube:
    def __init__(self, count, send_sems, recv_sems):
        self.count, self.send_sems, self.recv_sems = count, send_sems, recv_sems
        self.dp, self.mp = lax.axis_index("dp"), lax.axis_index("mp")
        self.stages = count.bit_length() - 1

    def copy(self, source, target, unit, mask, bit):
        return remote(
            source,
            target,
            self.send_sems.at[unit, mask],
            self.recv_sems.at[unit, mask],
            flipped(self.dp, 1 << bit),
            self.mp,
        )


class CubeGather(Cube):
    def stage(self, unit, path, view, stage):
        order = paths(self.count)[path]
        if stage:
            for mask in masks_over(order[: stage - 1]):
                got = mask | (1 << order[stage - 1])
                ref = view(flipped(self.dp, got))
                self.copy(ref, ref, unit, got, order[stage - 1]).wait_recv()
        if stage < self.stages:
            for mask in masks_over(order[:stage]):
                ref = view(flipped(self.dp, mask))
                self.copy(ref, ref, unit, mask | (1 << order[stage]), order[stage]).start()

    def finish(self, unit, path, view):
        order = paths(self.count)[path]
        for stage in range(self.stages):
            for mask in masks_over(order[:stage]):
                ref = view(flipped(self.dp, mask))
                self.copy(ref, ref, unit, mask | (1 << order[stage]), order[stage]).wait_send()


class CubeSum(Cube):
    def slot(self, order, stage, mask):
        base = self.count - (self.count >> stage)
        return base + masks_over(order[stage + 1 :]).index(mask)

    def source(self, unit, order, view, land, stage, mask):
        if stage == 0:
            return view(flipped(self.dp, mask))
        return land.at[self.slot(order, stage - 1, mask)]

    def sends(self, unit, path, view, land, stage):
        order = paths(self.count)[path][::-1]
        bit = order[stage]
        return [
            self.copy(
                self.source(unit, order, view, land, stage, mask | (1 << bit)),
                land.at[self.slot(order, stage, mask)],
                unit,
                mask | (1 << bit),
                bit,
            )
            for mask in masks_over(order[stage + 1 :])
        ]

    def start(self, unit, path, view, land, stage):
        for copy in self.sends(unit, path, view, land, stage):
            copy.start()

    def absorb(self, unit, path, view, land, stage, out=None):
        order = paths(self.count)[path][::-1]
        for copy, mask in zip(
            self.sends(unit, path, view, land, stage), masks_over(order[stage + 1 :])
        ):
            copy.wait_recv()
            before = self.source(unit, order, view, land, stage, mask)
            here = land.at[self.slot(order, stage, mask)]
            step = 16

            def add(number, carry):
                at = pl.ds(pl.multiple_of(number * step, step), step)
                both = before[at].astype(jnp.float32) + here[at].astype(jnp.float32)
                if out is None:
                    here[at] = both.astype(jnp.bfloat16)
                else:
                    out[at] = both
                return carry

            lax.fori_loop(0, here.shape[0] // step, add, 0)

    def finish(self, unit, path, view, land):
        for stage in range(self.stages):
            for copy in self.sends(unit, path, view, land, stage):
                copy.wait_send()


def line_sems(count):
    return [pltpu.SemaphoreType.DMA((2, count, PIECES)), pltpu.SemaphoreType.DMA((2, count, PIECES))]


def cube_sems(units, count):
    return [pltpu.SemaphoreType.DMA((units, count)), pltpu.SemaphoreType.DMA((units, count))]


def start_kernel(
    dp_count, mp_count, tokens, pack, mix,
    tokens_all, small, mix_all,
    own_sems, line_send, line_recv, pack_send, pack_recv, cube_send, cube_recv,
):
    dp, mp = lax.axis_index("dp"), lax.axis_index("mp")
    rows = tokens.shape[0]
    matrices, block = mix.shape[0], mix.shape[1]
    pack_rows, group = pack.shape[0], pack.shape[0] * mp_count
    half = group // 2
    others = [lax.rem(mp + step, mp_count) for step in range(1, mp_count)]
    greet_all([(dp, other) for other in others] + cube_partners(dp_count))
    line = LineGather(mp_count, rows, line_send, line_recv)
    cube = CubeGather(dp_count, cube_send, cube_recv)

    pack_at = small.at[pl.ds(pl.multiple_of(dp * group + mp * pack_rows, 16), pack_rows)]
    own = [
        pltpu.make_async_copy(pack, pack_at, own_sems.at[0]),
        pltpu.make_async_copy(
            tokens, tokens_all.at[pl.ds(pl.multiple_of(mp * rows, 16), rows)], own_sems.at[1]
        ),
    ] + [
        pltpu.make_async_copy(
            mix.at[number],
            mix_all.at[number, pl.ds(pl.multiple_of(dp * block, 16), block)],
            own_sems.at[2 + number],
        )
        for number in range(matrices)
    ]
    for copy in own:
        copy.start()
    pack_copies = [
        remote(pack, pack_at, pack_send.at[step], pack_recv.at[step], dp, other)
        for step, other in enumerate(others)
    ]
    for copy in pack_copies:
        copy.start()

    def small_view(part):
        def view(index):
            return small.at[pl.ds(pl.multiple_of(index * group + part * half, 16), half)]

        return view

    def mix_view(number):
        def view(index):
            return mix_all.at[number, pl.ds(pl.multiple_of(index * block, 16), block)]

        return view

    mix_units = [
        (2 + number, 0 if 2 * number < matrices else 1, mix_view(number))
        for number in range(matrices)
    ]
    small_units = [(part, part, small_view(part)) for part in range(2)]
    for copy in own:
        copy.wait()
    for piece in range(PIECES):
        line.send(tokens_all, 0, piece)
    for unit in mix_units:
        cube.stage(*unit, 0)
    for copy in pack_copies:
        copy.wait()
    for unit in small_units:
        cube.stage(*unit, 0)
    for distance in range(1, mp_count):
        for piece in range(PIECES):
            line.send(tokens_all, distance, piece)
        if distance < dp_count.bit_length() - 1:
            for unit in small_units + mix_units:
                cube.stage(*unit, distance)
    for stage in range(min(mp_count, dp_count.bit_length() - 1), dp_count.bit_length()):
        for unit in small_units + mix_units:
            cube.stage(*unit, stage)
    line.finish(tokens_all)
    for unit in small_units + mix_units:
        cube.finish(*unit)


def run_start(dp_count, mp_count, tokens, pack, mix):
    rows, width = tokens.shape
    matrices, block, features = mix.shape
    anywhere = pl.BlockSpec(memory_space=pl.ANY)
    return pl.pallas_call(
        functools.partial(start_kernel, dp_count, mp_count),
        out_shape=(
            jax.ShapeDtypeStruct((rows * mp_count, width), tokens.dtype),
            jax.ShapeDtypeStruct((pack.shape[0] * mp_count * dp_count, pack.shape[1]), pack.dtype),
            jax.ShapeDtypeStruct((matrices, block * dp_count, features), mix.dtype),
        ),
        in_specs=[anywhere] * 3,
        out_specs=(anywhere,) * 3,
        scratch_shapes=[
            pltpu.SemaphoreType.DMA((2 + matrices,)),
            *line_sems(mp_count),
            pltpu.SemaphoreType.DMA((mp_count - 1,)),
            pltpu.SemaphoreType.DMA((mp_count - 1,)),
            *cube_sems(2 + matrices, dp_count),
        ],
        compiler_params=pltpu.CompilerParams(collective_id=3, has_side_effects=True),
        name="gather_start",
    )(tokens, pack, mix)


def residual_rows(total, rows, tokens):
    return total + tokens[rows].astype(jnp.float32)


def backward_rows(total, rows, source, gain, skip):
    value = source[rows].astype(jnp.float32)
    centre = value - jnp.mean(value, -1, keepdims=True)
    inverse = lax.rsqrt(jnp.mean(centre * centre, -1, keepdims=True) + norm_epsilon)
    return skip[rows].astype(jnp.float32) + norm_backward(total, centre * inverse, inverse, gain[:1])


def exchange_kernel(count, epilogue, extras, part, *refs):
    extra, refs = refs[:extras], refs[extras:]
    own, gathered, moving, land, total = refs[:5]
    sum_send, sum_recv, line_send, line_recv = refs[5:]
    rows = own.shape[0]
    greet_all(line_partners(count))
    adder = LineSum(count, rows, sum_send, sum_recv)
    line = LineGather(count, rows, line_send, line_recv)
    for number in range(count - 1):
        adder.step(part, moving, land, number)
    for piece in range(PIECES):
        at = adder.total(part, moving, land, total, piece)
        value = epilogue(total[at], at, *extra)
        own[at] = value
        gathered[line.at(line.me, piece)] = value.astype(jnp.bfloat16)
        line.send(gathered, 0, piece)
    for distance in range(1, count):
        for piece in range(PIECES):
            line.send(gathered, distance, piece)
    adder.finish(moving, land)
    line.finish(gathered)


def run_exchange(count, number, epilogue, part, *extra):
    rows, width = part.shape[0] // count, part.shape[1]
    vmem = pl.BlockSpec(memory_space=pltpu.VMEM)
    return pl.pallas_call(
        functools.partial(exchange_kernel, count, epilogue, len(extra)),
        out_shape=(
            jax.ShapeDtypeStruct((rows, width), jnp.float32),
            jax.ShapeDtypeStruct(part.shape, jnp.bfloat16),
        ),
        in_specs=[vmem] * (1 + len(extra)),
        out_specs=(vmem, vmem),
        scratch_shapes=[
            pltpu.VMEM(part.shape, jnp.bfloat16),
            pltpu.VMEM((2,) + part.shape, jnp.bfloat16),
            pltpu.VMEM((rows, width), jnp.float32),
            *line_sems(count),
            *line_sems(count),
        ],
        compiler_params=pltpu.CompilerParams(
            collective_id=number, has_side_effects=True, vmem_limit_bytes=40 << 20
        ),
        name="sum_and_gather",
    )(part, *extra)


def end_kernel(
    dp_count, mp_count, part, source, gain, skip, mix, pack,
    own, mix_sum, pack_sum,
    moving, land, total, mix_land, pack_land, pack_own, pack_out, small_land,
    sum_send, sum_recv, cube_send, cube_recv, small_send, small_recv,
):
    dp, mp = lax.axis_index("dp"), lax.axis_index("mp")
    rows, matrices = own.shape[0], mix.shape[0]
    block, group = mix_sum.shape[1], pack_own.shape[0]
    half, pack_rows = group // 2, pack_sum.shape[0]
    others = [lax.rem(mp + step, mp_count) for step in range(1, mp_count)]
    greet_all([(dp, other) for other in others] + cube_partners(dp_count))
    adder = LineSum(mp_count, rows, sum_send, sum_recv)
    cube = CubeSum(dp_count, cube_send, cube_recv)

    def mix_view(number):
        def view(index):
            return mix.at[number, pl.ds(pl.multiple_of(index * block, 16), block)]

        return view

    def pack_view(side):
        def view(index):
            return pack.at[pl.ds(pl.multiple_of(index * group + side * half, 16), half)]

        return view

    units = [(side, side, pack_view(side), pack_land.at[side]) for side in range(2)] + [
        (2 + number, 0 if 2 * number < matrices else 1, mix_view(number), mix_land.at[number])
        for number in range(matrices)
    ]
    outs = [pack_own.at[pl.ds(side * half, half)] for side in range(2)] + [
        mix_sum.at[number] for number in range(matrices)
    ]
    for unit in units:
        cube.start(*unit, 0)
    last = cube.stages - 1
    adder.step(part, moving, land, 0)
    for stage in range(last):
        for unit in units:
            cube.absorb(*unit, stage)
            cube.start(*unit, stage + 1)
        if stage + 1 < mp_count - 1:
            adder.step(part, moving, land, stage + 1)
    for number in range(last + 1, mp_count - 1):
        adder.step(part, moving, land, number)
    for unit, out in zip(units[:2], outs[:2]):
        cube.absorb(*unit, last, out)
    pack_out[...] = pack_own[...].astype(jnp.bfloat16)
    small_copies = [
        remote(
            pack_out.at[pl.ds(pl.multiple_of(other * pack_rows, 16), pack_rows)],
            small_land.at[step],
            small_send.at[step],
            small_recv.at[step],
            dp,
            other,
        )
        for step, other in enumerate(others)
    ]
    for copy in small_copies:
        copy.start()
    for piece in range(PIECES):
        at = adder.total(part, moving, land, total, piece)
        own[at] = backward_rows(total[at], at, source, gain, skip)
    for unit, out in zip(units[2:], outs[2:]):
        cube.absorb(*unit, last, out)
    pack_sum[...] = pack_own[pl.ds(pl.multiple_of(mp * pack_rows, 16), pack_rows), :]
    for step, copy in enumerate(small_copies):
        copy.wait()
        pack_sum[...] += small_land[step].astype(jnp.float32)
    adder.finish(moving, land)
    for unit in units:
        cube.finish(*unit)


def run_end(dp_count, mp_count, part, source, gain, skip, mix, pack):
    rows, width = source.shape
    matrices, features = mix.shape[0], mix.shape[2]
    block, group = mix.shape[1] // dp_count, pack.shape[0] // dp_count
    lanes = pack.shape[1]
    vmem = pl.BlockSpec(memory_space=pltpu.VMEM)
    return pl.pallas_call(
        functools.partial(end_kernel, dp_count, mp_count),
        out_shape=(
            jax.ShapeDtypeStruct((rows, width), jnp.float32),
            jax.ShapeDtypeStruct((matrices, block, features), jnp.float32),
            jax.ShapeDtypeStruct((group // mp_count, lanes), jnp.float32),
        ),
        in_specs=[vmem] * 6,
        out_specs=(vmem,) * 3,
        scratch_shapes=[
            pltpu.VMEM(part.shape, jnp.bfloat16),
            pltpu.VMEM((2,) + part.shape, jnp.bfloat16),
            pltpu.VMEM((rows, width), jnp.float32),
            pltpu.VMEM((matrices, dp_count - 1, block, features), jnp.bfloat16),
            pltpu.VMEM((2, dp_count - 1, group // 2, lanes), jnp.bfloat16),
            pltpu.VMEM((group, lanes), jnp.float32),
            pltpu.VMEM((group, lanes), jnp.bfloat16),
            pltpu.VMEM((mp_count - 1, group // mp_count, lanes), jnp.bfloat16),
            *line_sems(mp_count),
            *cube_sems(2 + matrices, dp_count),
            pltpu.SemaphoreType.DMA((mp_count - 1,)),
            pltpu.SemaphoreType.DMA((mp_count - 1,)),
        ],
        compiler_params=pltpu.CompilerParams(
            collective_id=6, has_side_effects=True, vmem_limit_bytes=56 << 20
        ),
        name="sum_end",
    )(part, source, gain, skip, mix, pack)


def update(carried_memory, grad, fan, total_tokens):
    rate = (total_tokens * fan) ** (-0.5)
    scaled = rate * grad
    velocity = momentum_rate * carried_memory[1] + scaled
    weight = carried_memory[0] - (scaled + momentum_rate * velocity)
    average = average_rate * carried_memory[2] + (1.0 - average_rate) * weight
    return jnp.stack([velocity, weight, average])


def split_three(value):
    pieces = []
    for _ in range(3):
        pieces.append(lax.reduce_precision(value, 8, 7))
        value = value - pieces[-1]
    return [piece.astype(jnp.bfloat16) for piece in pieces]


def swap_columns(value):
    count = lax.axis_size("mp")
    rows, width = value.shape
    pieces = value.reshape(rows, count, width // count).transpose(1, 0, 2)
    mixed = lax.all_to_all(pieces, "mp", 0, 0, tiled=True)
    return mixed.reshape(count * rows, width // count)


def swap_rows(value):
    count = lax.axis_size("mp")
    rows, width = value.shape
    mixed = lax.all_to_all(
        value.reshape(count, rows // count, width), "mp", 0, 0, tiled=True
    )
    return mixed.transpose(1, 0, 2).reshape(rows // count, count * width)


def shifted(value, before, keep):
    return jnp.concatenate([before, value[:-1]], 0) * keep[:, None] - value


def shifted_back(value):
    return jnp.concatenate([value[1:], jnp.zeros((1, value.shape[1]), value.dtype)], 0)


def add_last(value, arriving):
    return jnp.concatenate([value[:-1], value[-1:] + arriving], 0)


def body(
    tokens,
    cotangent,
    lengths,
    mix_state,
    out_state,
    key_state,
    value_state,
    gate_state,
    down_state,
    up_state,
    vector_state,
):
    bfloat = jnp.bfloat16
    single = jnp.float32
    dp_count = lax.axis_size("dp")
    mp_count = lax.axis_size("mp")
    dp_index = lax.axis_index("dp")
    mp_index = lax.axis_index("mp")
    own_rows = tokens.shape[0]
    width = tokens.shape[1]
    group_rows = own_rows * mp_count
    total_tokens = group_rows * dp_count
    features = mix_state.shape[3]
    maa_cols = 5 * TM_RANK
    down_cols = maa_cols + DECAY_RANK
    col_start = mp_index * features

    pack = jnp.concatenate(
        [down_state[0].astype(bfloat), up_state[0].T.astype(bfloat)]
        + split_three(vector_state[0].T),
        1,
    )
    pack = jnp.pad(pack, ((0, 0), (0, -pack.shape[1] % 128)))
    tokens_all, small, mix_weight = run_start(
        dp_count, mp_count, tokens, pack, mix_state[0].astype(bfloat)
    )
    out_low, gate_low, key_low, value_low, tokens_all = lax.optimization_barrier(
        (
            out_state[0].astype(bfloat),
            gate_state[0].astype(bfloat),
            key_state[0].astype(bfloat),
            value_state[0].astype(bfloat),
            tokens_all,
        )
    )
    out_weight, gate_weight, key_weight, value_weight = (
        lax.all_gather(out_low, "dp", axis=1, tiled=True),
        lax.all_gather(gate_low, "dp", axis=0, tiled=True),
        lax.all_gather(key_low, "dp", axis=0, tiled=True),
        lax.all_gather(value_low, "dp", axis=1, tiled=True),
    )
    cotangent_cols = swap_columns(cotangent).astype(single)
    down_weight = small[:, :down_cols]
    up_weight = small[:, down_cols : 2 * down_cols]
    vectors = sum(
        small[:, 2 * down_cols + 16 * part : 2 * down_cols + 16 * part + 16].astype(single)
        for part in range(3)
    ).T

    seq_ends = jnp.cumsum(lengths)
    offsets = seq_ends - lengths
    positions = dp_index * group_rows + jnp.arange(group_rows, dtype=jnp.int32)
    opening = jnp.any(positions[:, None] == offsets[None, :], 1).astype(single)
    segment = jnp.sum((offsets[None, :] <= positions[:, None]).astype(single), 1)
    keep = 1.0 - opening
    chunks = group_rows // CHUNK
    parts = segment.reshape(chunks, CHUNK)
    first = parts[:, :1] - opening.reshape(chunks, CHUNK)[:, :1]

    def spread(value, lanes):
        return jnp.broadcast_to(value.astype(single).reshape(-1, 1), (value.size, lanes))

    marks = (
        spread(parts, 2 * CHUNK),
        jnp.repeat(jnp.concatenate([parts, parts], 1), 8, 0),
        spread(parts == first, PAIR),
        spread(parts == parts[:, -1:], PAIR),
        spread(jnp.repeat(parts[:, -1:] == first, 8, 0), PAIR),
    )
    level, sums, sums_back = level_tables()
    tables = (jnp.asarray(level), jnp.asarray(sums, bfloat), jnp.asarray(sums_back, bfloat))

    def local_share(row_number):
        return lax.dynamic_slice_in_dim(vectors[row_number], col_start, features, 0)

    def spread_row(value):
        return jnp.broadcast_to(value[None], (8, width))

    before_first = from_behind(tokens_all[-1:], "dp", 1)
    hidden_one, hat_one, inv_one = norm_forward(
        tokens_all.astype(single), vectors[0], vectors[1], norm_epsilon
    )
    before_one = norm_forward(before_first.astype(single), vectors[0], vectors[1], norm_epsilon)[0]
    delta_one = shifted(hidden_one, before_one, keep)
    base_low = (hidden_one + delta_one * vectors[2]).astype(bfloat)
    mix_act = jnp.tanh(half_dot(base_low, down_weight[:, :maa_cols]))
    mix_act_low = mix_act.astype(bfloat)
    act_blocks = [mix_act_low[:, TM_RANK * n : TM_RANK * (n + 1)] for n in range(5)]
    up_blocks = [up_weight[:, TM_RANK * n : TM_RANK * (n + 1)] for n in range(5)]
    scales = [vectors[3 + n] + half_right(act_blocks[n], up_blocks[n]) for n in range(5)]
    inputs_low = [(hidden_one + delta_one * scales[n]).astype(bfloat) for n in range(5)]
    decay_act = jnp.tanh(half_dot(inputs_low[0], down_weight[:, maa_cols:]))
    decay_low = decay_act.astype(bfloat)
    decay_up = lax.dynamic_slice_in_dim(up_weight[:, maa_cols:], col_start, features, 0)
    log_fading_rate = -jnp.exp(local_share(8) + half_right(decay_low, decay_up))
    acceptor_entries = half_dot(inputs_low[3], mix_weight[0])
    lookup_tensor = half_dot(inputs_low[1], mix_weight[1])
    payload_tensor = half_dot(inputs_low[2], mix_weight[2])
    gate_pre = half_dot(inputs_low[4], mix_weight[3])
    local_vectors = jnp.concatenate(
        [jnp.stack([local_share(9), local_share(10), local_share(11)]), jnp.zeros((5, features))], 0
    )
    branch = (acceptor_entries, lookup_tensor, payload_tensor, gate_pre, log_fading_rate)
    gated_low, wkv, states, kept = run_forward(dp_count, *branch, local_vectors, marks, tables)

    residual, residual_all = run_exchange(
        mp_count, 4, residual_rows, half_dot(gated_low, out_weight).astype(bfloat), tokens
    )
    before_second = from_behind(residual_all[-1:], "dp", 1)
    hidden_two, hat_two, inv_two = norm_forward(
        residual_all.astype(single), vectors[12], vectors[13], norm_epsilon
    )
    before_two = norm_forward(before_second.astype(single), vectors[12], vectors[13], norm_epsilon)[
        0
    ]
    delta_two = shifted(hidden_two, before_two, keep)
    key_in_low = (hidden_two + delta_two * vectors[14]).astype(bfloat)
    recv_in_low = (hidden_two + delta_two * vectors[15]).astype(bfloat)
    key_pre = half_dot(key_in_low, key_weight)
    key_act_low = jnp.square(jnp.maximum(key_pre, 0.0)).astype(bfloat)
    recv_gate = jax.nn.sigmoid(half_dot(recv_in_low, gate_weight))
    channel_part = half_dot(key_act_low, value_weight).astype(bfloat)
    channel_part = channel_part.reshape(group_rows, mp_count, features).transpose(1, 0, 2)
    channel_sum = lax.psum_scatter(
        channel_part, "mp", scatter_dimension=0, tiled=True
    )[0].astype(single)
    gated_sum = recv_gate * channel_sum
    mixed = (residual + swap_rows(gated_sum.astype(bfloat)).astype(single)).astype(bfloat)

    grad_kv = (cotangent_cols * recv_gate).astype(bfloat)
    grad_recv_pre = (cotangent_cols * gated_sum * (1.0 - recv_gate)).astype(bfloat)
    grad_kv_all = (
        lax.all_gather(grad_kv, "mp", axis=0, tiled=False)
        .transpose(1, 0, 2)
        .reshape(group_rows, width)
    )
    grad_key_act = half_right(grad_kv_all, value_weight)
    grad_key_pre = (grad_key_act * 2.0 * jnp.maximum(key_pre, 0.0)).astype(bfloat)
    grad_key_in = half_right(grad_key_pre, key_weight)
    grad_recv_in = half_right(grad_recv_pre, gate_weight)
    grad_value_weight = half_left(key_act_low, grad_kv_all)
    grad_key_weight = half_left(key_in_low, grad_key_pre)
    grad_gate_weight = half_left(recv_in_low, grad_recv_pre)
    grad_delta_two = grad_key_in * vectors[14] + grad_recv_in * vectors[15]
    grad_key_mix = jnp.sum(grad_key_in * delta_two, 0)
    grad_recv_mix = jnp.sum(grad_recv_in * delta_two, 0)
    shifted_grad_two = grad_delta_two * keep[:, None]
    arriving_two = from_behind(shifted_grad_two[:1], "dp", -1)
    grad_hidden_two = add_last(
        grad_key_in + grad_recv_in - grad_delta_two + shifted_back(shifted_grad_two), arriving_two
    )
    grad_gain_two = jnp.sum(grad_hidden_two * hat_two, 0)
    grad_bias_two = jnp.sum(grad_hidden_two, 0)
    grad_residual, grad_attn_all = run_exchange(
        mp_count,
        5,
        backward_rows,
        grad_hidden_two.astype(bfloat),
        residual.astype(bfloat),
        spread_row(vectors[12]),
        cotangent,
    )
    grad_out_weight = half_left(gated_low, grad_attn_all)
    grad_gated = half_right(grad_attn_all, out_weight)
    grad_recept, grad_keys, grad_values, grad_gate_pre, grad_raw, grad_local = run_backward(
        dp_count, grad_gated, wkv, states, kept, *branch, local_vectors, marks, tables
    )

    raw_low = grad_raw.astype(bfloat)
    grad_up_decay = half_left(raw_low, decay_low)
    grad_decay_act = (half_dot(raw_low, decay_up) * (1.0 - decay_act * decay_act)).astype(bfloat)
    grad_down_decay = half_left(inputs_low[0], grad_decay_act)
    grad_inputs = [
        half_right(grad_decay_act, down_weight[:, maa_cols:]),
        half_right(grad_keys, mix_weight[1]),
        half_right(grad_values, mix_weight[2]),
        half_right(grad_recept, mix_weight[0]),
        half_right(grad_gate_pre, mix_weight[3]),
    ]
    grad_mix_weight = jnp.stack(
        [
            half_left(inputs_low[3], grad_recept),
            half_left(inputs_low[1], grad_keys),
            half_left(inputs_low[2], grad_values),
            half_left(inputs_low[4], grad_gate_pre),
        ]
    )
    grad_mixes = [grad_inputs[n] * delta_one for n in range(5)]
    mixes_low = [value.astype(bfloat) for value in grad_mixes]
    grad_up_mix = [half_left(mixes_low[n], act_blocks[n]) for n in range(5)]
    grad_mix_act = jnp.concatenate([half_dot(mixes_low[n], up_blocks[n]) for n in range(5)], 1)
    grad_mix_pre = (grad_mix_act * (1.0 - mix_act * mix_act)).astype(bfloat)
    grad_down_mix = half_left(base_low, grad_mix_pre)
    grad_base = half_right(grad_mix_pre, down_weight[:, :maa_cols])
    grad_delta_one = grad_base * vectors[2]
    grad_hidden_one = grad_base
    for number in range(5):
        grad_delta_one = grad_delta_one + grad_inputs[number] * scales[number]
        grad_hidden_one = grad_hidden_one + grad_inputs[number]
    shifted_grad_one = grad_delta_one * keep[:, None]
    arriving_one = from_behind(shifted_grad_one[:1], "dp", -1)
    grad_hidden_one = add_last(
        grad_hidden_one - grad_delta_one + shifted_back(shifted_grad_one), arriving_one
    )
    def positioned(value):
        return lax.dynamic_update_slice_in_dim(
            jnp.zeros((width,) + value.shape[1:], single), value, col_start, 0
        )

    grad_vectors = jnp.concatenate(
        [
            jnp.stack(
                [
                    jnp.sum(grad_hidden_one * hat_one, 0),
                    jnp.sum(grad_hidden_one, 0),
                    jnp.sum(grad_base * delta_one, 0),
                ]
                + [jnp.sum(value, 0) for value in grad_mixes]
            ).T,
            positioned(grad_local[:4].T),
            jnp.stack([grad_gain_two, grad_bias_two, grad_key_mix, grad_recv_mix]).T,
        ],
        1,
    )
    grad_pack = jnp.concatenate(
        [grad_down_mix, grad_down_decay] + grad_up_mix + [positioned(grad_up_decay), grad_vectors],
        1,
    ).astype(bfloat)
    grad_pack = jnp.pad(grad_pack, ((0, 0), (0, -grad_pack.shape[1] % 128)))

    def summed(value, axis):
        return lax.psum_scatter(
            value.astype(bfloat), "dp", scatter_dimension=axis, tiled=True
        )

    value_sum = summed(grad_value_weight, 1).astype(single)
    key_sum = summed(grad_key_weight, 0).astype(single)
    gate_sum = summed(grad_gate_weight, 0).astype(single)
    out_sum = summed(grad_out_weight, 1).astype(single)
    grad_tokens, mix_sum, small_sum = run_end(
        dp_count,
        mp_count,
        grad_hidden_one.astype(bfloat),
        tokens,
        spread_row(vectors[0]),
        grad_residual,
        grad_mix_weight.astype(bfloat),
        grad_pack,
    )
    return (
        mixed,
        grad_tokens,
        update(mix_state, mix_sum, width, total_tokens),
        update(out_state, out_sum, width, total_tokens),
        update(key_state, key_sum, width, total_tokens),
        update(value_state, value_sum, FF, total_tokens),
        update(gate_state, gate_sum, width, total_tokens),
        update(down_state, small_sum[:, :down_cols], width, total_tokens),
        update(up_state, small_sum[:, down_cols : 2 * down_cols].T, TM_RANK, total_tokens),
        update(
            vector_state, small_sum[:, 2 * down_cols : 2 * down_cols + 16].T, 1, total_tokens
        ),
    )


def solution(mesh):
    return jax.shard_map(
        body,
        mesh=mesh,
        in_specs=(
            P(("dp", "mp"), None),
            P(("dp", "mp"), None),
            P(),
            P(None, None, "dp", "mp"),
            P(None, "mp", "dp"),
            P(None, "dp", "mp"),
            P(None, "mp", "dp"),
            P(None, "dp", "mp"),
            P(None, ("dp", "mp"), None),
            P(None, None, ("dp", "mp")),
            P(None, None, ("dp", "mp")),
        ),
        out_specs=(
            P(("dp", "mp"), None),
            P(("dp", "mp"), None),
            P(None, None, "dp", "mp"),
            P(None, "mp", "dp"),
            P(None, "dp", "mp"),
            P(None, "mp", "dp"),
            P(None, "dp", "mp"),
            P(None, ("dp", "mp"), None),
            P(None, None, ("dp", "mp")),
            P(None, None, ("dp", "mp")),
        ),
        check_vma=False,
    )
```

```python
import functools

import jax
import jax.numpy as jnp
import numpy as np
from jax import lax
from jax.experimental import pallas as pl
from jax.experimental.pallas import tpu as pltpu
from jax.sharding import PartitionSpec as P

LANE_SPAN = 64
FF = 7168
TM_RANK = 32
DECAY_RANK = 64


momentum_rate = 0.9
average_rate = 0.9
norm_epsilon = 1e-05
group_epsilon = 0.00064
CHUNK = 128
LEVELS = 7
PAIR = 2 * LANE_SPAN
MESH = pl.DeviceIdType.MESH
PIECES = 2
WINDOW = 256
ROW_BLOCK = 256


def from_behind(block, axis, distance):
    devices = range(lax.axis_size(axis))
    route = [(i - distance, i) for i in devices if i - distance in devices]
    return lax.ppermute(block, axis, route)


def half_dot(left, right):
    return jnp.dot(left, right, preferred_element_type=jnp.float32)


def half_left(left, right):
    return lax.dot_general(
        left, right, (((0,), (0,)), ((), ())), preferred_element_type=jnp.float32
    )


def half_right(left, right):
    return lax.dot_general(
        left, right, (((1,), (1,)), ((), ())), preferred_element_type=jnp.float32
    )


def split_pair(value):
    upper_part = value.astype(jnp.bfloat16)
    lower_part = (value - upper_part.astype(jnp.float32)).astype(jnp.bfloat16)
    return (upper_part, lower_part)


def norm_forward(value, gain, bias, epsilon):
    centre = value - jnp.mean(value, -1, keepdims=True)
    inverse = lax.rsqrt(jnp.mean(centre * centre, -1, keepdims=True) + epsilon)
    normal_hat = centre * inverse
    return (normal_hat * gain + bias, normal_hat, inverse)


def norm_backward(grad_out, normal_hat, inverse, gain):
    scaled = grad_out * gain
    return inverse * (
        scaled
        - jnp.mean(scaled, -1, keepdims=True)
        - normal_hat * jnp.mean(scaled * normal_hat, -1, keepdims=True)
    )


def level_tables():
    row = np.arange(CHUNK)
    later, earlier = row[:, None], row[None, :]
    level = np.full((CHUNK, CHUNK), -1.0, np.float32)
    sums = []
    for bit in range(LEVELS):
        block = (later >> (bit + 1)) == (earlier >> (bit + 1))
        level[block & ((later >> bit) % 2 == 1) & ((earlier >> bit) % 2 == 0)] = bit
        middle = ((later >> (bit + 1)) << (bit + 1)) + (1 << bit)
        upper = (later >> bit) % 2 == 1
        between = np.where(
            upper, (earlier >= middle) & (earlier < later), (earlier > later) & (earlier < middle)
        )
        if bit:
            sums.append(between)
    sums += [earlier < later, earlier > later]
    sums = np.concatenate(sums, 0).astype(np.float32)
    return np.concatenate([level, level], 1), np.concatenate([sums, sums], 1), sums.T


def dot_nn(left, right):
    return lax.dot_general(
        left, right, (((1,), (0,)), ((), ())), preferred_element_type=jnp.float32
    )


def dot_nt(left, right):
    return lax.dot_general(
        left, right, (((1,), (1,)), ((), ())), preferred_element_type=jnp.float32
    )


def dot_tn(left, right):
    return lax.dot_general(
        left, right, (((0,), (0,)), ((), ())), preferred_element_type=jnp.float32
    )


def first_head(shape):
    return lax.broadcasted_iota(jnp.int32, shape, len(shape) - 1) < LANE_SPAN


def stack_heads(value):
    first = first_head(value.shape)
    none = jnp.zeros_like(value)
    return jnp.concatenate([jnp.where(first, value, none), jnp.where(first, none, value)], 0)


def merge_heads(value):
    half = value.shape[0] // 2
    return jnp.where(first_head((half, value.shape[1])), value[:half], value[half:])


def own_blocks(value):
    upper = lax.broadcasted_iota(jnp.int32, value.shape, 0) < LANE_SPAN
    return jnp.where(upper == first_head(value.shape), value, 0.0)


def head_mean(value):
    row = lax.broadcasted_iota(jnp.int32, (PAIR, PAIR), 0) < LANE_SPAN
    ones = jnp.where(row == first_head((PAIR, PAIR)), 1.0 / LANE_SPAN, 0.0).astype(jnp.bfloat16)
    upper, lower = split_pair(value)
    return dot_nn(upper, ones) + dot_nn(lower, ones)


def head_sum(value):
    return head_mean(value) * float(LANE_SPAN)


def exact_pieces(left, right, axis_left, axis_right):
    upper, lower = split_pair(left)
    right_upper, right_lower = split_pair(right)
    return (
        jnp.concatenate([upper, lower, upper], axis_left),
        jnp.concatenate([right_upper, right_upper, right_lower], axis_right),
    )


def exact_nn(left, right):
    return dot_nn(*exact_pieces(left, right, 1, 0))


def exact_nt(left, right):
    return dot_nt(*exact_pieces(left, right, 1, 1))


def exact_tn(left, right):
    return dot_tn(*exact_pieces(left, right, 0, 0))


def packed_state(state):
    return jnp.concatenate(split_pair(state[:LANE_SPAN] + state[LANE_SPAN:]), 0)


def unpacked_state(piece):
    piece = piece.astype(jnp.float32)
    return piece[:LANE_SPAN] + piece[LANE_SPAN:]


def rows_of(chunk):
    return pl.ds(pl.multiple_of(chunk * CHUNK, CHUNK), CHUNK)


def lanes_of(pair):
    return pl.ds(pl.multiple_of(pair * PAIR, PAIR), PAIR)


def marks_of(chunk):
    return pl.ds(pl.multiple_of(chunk * 8, 8), 8)


def greet(dp_count, mp_count):
    me, mine = lax.axis_index("dp"), lax.axis_index("mp")
    barrier = pltpu.get_barrier_semaphore()
    for step in range(1, dp_count):
        pl.semaphore_signal(
            barrier, inc=1, device_id=(lax.rem(me + step, dp_count), mine), device_id_type=MESH
        )
    for step in range(1, mp_count):
        pl.semaphore_signal(
            barrier, inc=1, device_id=(me, lax.rem(mine + step, mp_count)), device_id_type=MESH
        )
    pl.semaphore_wait(barrier, dp_count + mp_count - 2)


def swap_copies(count, source, target, send_sems, recv_sems):
    me, mine = lax.axis_index("dp"), lax.axis_index("mp")
    copies = []
    for step in range(1, count):
        other = lax.rem(mine + step, count)
        copies.append(
            pltpu.make_async_remote_copy(
                src_ref=source(other),
                dst_ref=target(mine),
                send_sem=send_sems.at[step - 1],
                recv_sem=recv_sems.at[step - 1],
                device_id=(me, other),
                device_id_type=MESH,
            )
        )
    return copies


def state_copies(other, me, sends, lands, send_sems, recv_sems, to):
    return [
        pltpu.make_async_remote_copy(
            src_ref=send,
            dst_ref=land.at[me],
            send_sem=send_sems.at[number, other],
            recv_sem=recv_sems.at[number, me],
            device_id=(to, lax.axis_index("mp")),
            device_id_type=MESH,
        )
        for number, (send, land) in enumerate(zip(sends, lands))
    ]


def send_states(count, sends, lands, send_sems, recv_sems, ahead):
    me = lax.axis_index("dp")
    for other in range(count):

        @pl.when((other > me) if ahead else (other < me))
        def _():
            for copy in state_copies(other, me, sends, lands, send_sems, recv_sems, other):
                copy.start()


def wait_states(count, sends, lands, send_sems, recv_sems, ahead):
    me = lax.axis_index("dp")
    for other in range(count):

        @pl.when((other > me) if ahead else (other < me))
        def _():
            for copy in state_copies(other, me, sends, lands, send_sems, recv_sems, other):
                copy.wait_send()

        @pl.when((other < me) if ahead else (other > me))
        def _():
            for copy in state_copies(other, other, sends, lands, send_sems, recv_sems, me):
                copy.wait_recv()


def decay_factors(fading, sums):
    upper, lower = split_pair(fading)
    return jnp.exp(dot_nn(sums, jnp.concatenate([upper, lower], 0)))


def table(at):
    return slice(at * CHUNK, (at + 1) * CHUNK)


def level_inputs(level, acceptor, lookup, factors):
    if level == 0:
        return None, acceptor, lookup
    factor = factors[table(level - 1), :]
    return factor, acceptor * factor, lookup * factor


def recurrence_forward(
    count, mp_count, chunks, pairs,
    rec, key, val, gpre, logw, vec, seg_col, seg_row, valid, ending, whole, level, sums, cotangent,
    gated, wkv, states, kept, columns,
    factors, pre_a, pre_b, start_b, send_a, send_b, land_a, land_b, send_sems, recv_sems,
    swap_send, swap_recv,
):
    bfloat = jnp.bfloat16
    greet(count, mp_count)
    mine, own_rows, features = lax.axis_index("mp"), cotangent.shape[0], columns.shape[1]

    def own_columns(other):
        return cotangent.at[:, pl.ds(pl.multiple_of(other * features, 128), features)]

    def landing(other):
        return columns.at[pl.ds(pl.multiple_of(other * own_rows, 16), own_rows)]

    swaps = swap_copies(mp_count, own_columns, landing, swap_send, swap_recv)
    for copy in swaps:
        copy.start()
    landing(mine)[...] = own_columns(mine)[...]

    def summary(pair, carry):
        lanes = lanes_of(pair)

        def step(chunk, before):
            before_a, before_b = before
            rows, slot = rows_of(chunk), pair * chunks + chunk
            fading = logw[rows, lanes]
            factor = decay_factors(fading, sums[...])
            factors[slot] = factor
            faded = key[rows, lanes] * factor[table(LEVELS)] * ending[rows, :]
            chunk_b = own_blocks(exact_tn(val[rows, lanes], faded))
            chunk_a = jnp.exp(jnp.sum(fading, 0, keepdims=True)) * whole[marks_of(chunk), :][:1]
            pre_a[slot] = jnp.broadcast_to(before_a, (8, PAIR))
            pre_b[slot] = before_b
            return before_a * chunk_a, before_b * chunk_a + chunk_b

        last_a, last_b = lax.fori_loop(
            0, chunks, step, (jnp.ones((1, PAIR), jnp.float32), jnp.zeros((PAIR, PAIR), jnp.float32))
        )
        send_a[:, lanes] = jnp.broadcast_to(last_a, (8, PAIR))
        send_b[:, lanes] = packed_state(last_b)
        return carry

    lax.fori_loop(0, pairs, summary, 0)
    exchange = (count, (send_a, send_b), (land_a, land_b), send_sems, recv_sems, True)
    send_states(*exchange)

    def inside(slot, carry):
        pair, chunk = slot // chunks, slot % chunks
        rows, lanes = rows_of(chunk), lanes_of(pair)
        acceptor, lookup, payload = rec[rows, lanes], key[rows, lanes], val[rows, lanes]
        place = jnp.where(seg_col[rows, :] == seg_row[marks_of(chunk), :][:1], level[...], -1.0)
        scores = jnp.zeros((CHUNK, 2 * CHUNK), jnp.float32)
        for at in range(LEVELS):
            _, left, right = level_inputs(at, acceptor, lookup, factors.at[slot])
            part = exact_nt(left, stack_heads(right))
            scores = jnp.where(place == float(at), part, scores)
        bonus = head_sum(acceptor * vec[0:1, lanes] * lookup) * payload
        wkv[rows, lanes] = bonus + exact_nn(scores, stack_heads(payload))
        kept[slot] = scores.astype(bfloat)
        return carry

    lax.fori_loop(0, pairs * chunks, inside, 0)
    wait_states(*exchange)
    start_b[...] = lax.fori_loop(
        0,
        lax.axis_index("dp"),
        lambda other, state: state * land_a[other][:1] + unpacked_state(land_b[other]),
        jnp.zeros(start_b.shape, jnp.float32),
    )

    def finish(slot, carry):
        pair, chunk = slot // chunks, slot % chunks
        rows, lanes = rows_of(chunk), lanes_of(pair)
        state = pre_b[slot] + pre_a[slot][:1] * stack_heads(start_b[:, lanes])
        states[slot] = state
        reader = rec[rows, lanes] * factors[slot, table(LEVELS - 1), :] * valid[rows, :]
        out = wkv[rows, lanes] + exact_nt(reader, state)
        wkv[rows, lanes] = out
        centre = out - head_mean(out)
        inverse = lax.rsqrt(head_mean(centre * centre) + group_epsilon)
        normed = centre * inverse * vec[1:2, lanes] + vec[2:3, lanes]
        pre = gpre[rows, lanes]
        gated[rows, lanes] = (normed * pre * jax.nn.sigmoid(pre)).astype(bfloat)
        return carry

    lax.fori_loop(0, pairs * chunks, finish, 0)
    for copy in swaps:
        copy.wait()


def recurrence_backward(
    count, mp_count, chunks, pairs,
    dgated, wkv, states, kept, rec, key, val, gpre, logw, vec, seg_col, seg_row, valid, ending, whole,
    level, sums, sums_back, change, residual,
    drec, dkey, dval, dgpre, draw, dvec, mixed,
    factors, local, end_b, dout, drec_part, dkey_part, dval_part, dlog_part, steps,
    send_a, send_b, land_a, land_b, send_sems, recv_sems,
    swapped, swap_send, swap_recv,
):
    bfloat = jnp.bfloat16
    greet(count, mp_count)
    mine, own_rows, features = lax.axis_index("mp"), residual.shape[0], change.shape[1]

    def rows_for(other):
        return change.at[pl.ds(pl.multiple_of(other * own_rows, 16), own_rows)]

    swaps = swap_copies(mp_count, rows_for, lambda other: swapped.at[other], swap_send, swap_recv)
    for copy in swaps:
        copy.start()
    swapped[mine] = rows_for(mine)[...]
    dvec[...] = jnp.zeros(dvec.shape, jnp.float32)

    def chunk_decay(chunk, lanes):
        fading = logw[rows_of(chunk), lanes]
        return jnp.exp(jnp.sum(fading, 0, keepdims=True)) * whole[marks_of(chunk), :][:1]

    def summary(pair, carry):
        lanes = lanes_of(pair)

        def step(back, after):
            after_a, after_b = after
            chunk = chunks - 1 - back
            rows, slot = rows_of(chunk), pair * chunks + chunk
            factor = decay_factors(logw[rows, lanes], sums[...])
            factors[slot] = factor
            out = wkv[rows, lanes]
            centre = out - head_mean(out)
            inverse = lax.rsqrt(head_mean(centre * centre) + group_epsilon)
            hat = centre * inverse
            gain = vec[1:2, lanes]
            normed = hat * gain + vec[2:3, lanes]
            pre = gpre[rows, lanes]
            sig = jax.nn.sigmoid(pre)
            grad = dgated[rows, lanes]
            grad_normed = grad * pre * sig
            dgpre[rows, lanes] = (grad * normed * sig * (1.0 + pre * (1.0 - sig))).astype(bfloat)
            dvec[2:3, lanes] += jnp.sum(grad_normed * hat, 0, keepdims=True)
            dvec[3:4, lanes] += jnp.sum(grad_normed, 0, keepdims=True)
            scaled = grad_normed * gain
            grad_out = inverse * (scaled - head_mean(scaled) - hat * head_mean(scaled * hat))
            dout[rows, lanes] = grad_out
            reader = rec[rows, lanes] * factor[table(LEVELS - 1)] * valid[rows, :]
            inner = own_blocks(exact_tn(grad_out, reader))
            local[slot] = inner
            chunk_a = chunk_decay(chunk, lanes)
            return after_a * chunk_a, after_b * chunk_a + inner

        last_a, last_b = lax.fori_loop(
            0, chunks, step, (jnp.ones((1, PAIR), jnp.float32), jnp.zeros((PAIR, PAIR), jnp.float32))
        )
        send_a[:, lanes] = jnp.broadcast_to(last_a, (8, PAIR))
        send_b[:, lanes] = packed_state(last_b)
        return carry

    lax.fori_loop(0, pairs, summary, 0)
    exchange = (count, (send_a, send_b), (land_a, land_b), send_sems, recv_sems, False)
    send_states(*exchange)

    def inside(slot, carry):
        pair, chunk = slot // chunks, slot % chunks
        rows, lanes = rows_of(chunk), lanes_of(pair)
        acceptor, lookup, payload = rec[rows, lanes], key[rows, lanes], val[rows, lanes]
        reward = vec[0:1, lanes]
        grad_exact = dout[rows, lanes]
        grad_out = grad_exact.astype(bfloat)
        place = jnp.where(seg_col[rows, :] == seg_row[marks_of(chunk), :][:1], level[...], -1.0)
        grad_scores = exact_nt(grad_exact, stack_heads(payload))
        grad_bonus = head_sum(grad_exact * payload)
        dvec[1:2, lanes] += jnp.sum(acceptor * lookup * grad_bonus, 0, keepdims=True)
        grad_acceptor = reward * lookup * grad_bonus
        grad_lookup = reward * acceptor * grad_bonus
        for at in range(LEVELS):
            factor, left, right = level_inputs(at, acceptor, lookup, factors.at[slot])
            left_low, right_low = left.astype(bfloat), stack_heads(right.astype(bfloat))
            here = place == float(at)
            grad_part = jnp.where(here, grad_scores, 0.0).astype(bfloat)
            grad_left = dot_nn(grad_part, right_low)
            grad_right = merge_heads(dot_tn(grad_part, left_low))
            if at:
                grad_left = grad_left * factor
                grad_right = grad_right * factor
                steps[table(at - 1), :] = acceptor * grad_left + lookup * grad_right
            grad_acceptor += grad_left
            grad_lookup += grad_right
        drec_part[rows, lanes] = grad_acceptor
        dkey_part[rows, lanes] = grad_lookup
        bonus = head_sum(acceptor * reward * lookup)
        dval_part[rows, lanes] = bonus * grad_exact + merge_heads(
            dot_tn(kept[slot], grad_out)
        )
        inner = (LEVELS - 1) * CHUNK
        dlog_part[rows, lanes] = dot_nn(sums_back[:, :inner], steps[...].astype(bfloat))
        return carry

    lax.fori_loop(0, pairs * chunks, inside, 0)
    wait_states(*exchange)
    me = lax.axis_index("dp")

    def later(step, state):
        other = count - 1 - step
        return state * land_a[other][:1] + unpacked_state(land_b[other])

    end_b[...] = lax.fori_loop(0, count - 1 - me, later, jnp.zeros(end_b.shape, jnp.float32))

    def finish(pair, carry):
        lanes = lanes_of(pair)

        def step(back, after):
            chunk = chunks - 1 - back
            rows, slot = rows_of(chunk), pair * chunks + chunk
            state = states[slot]
            after_low = after.astype(bfloat)
            reach = factors[slot, table(LEVELS - 1), :] * valid[rows, :]
            tail = factors[slot, table(LEVELS), :] * ending[rows, :]
            acceptor, lookup = rec[rows, lanes], key[rows, lanes]
            grad_reader = exact_nn(dout[rows, lanes], state) * reach
            grad_faded = exact_nn(val[rows, lanes], after) * tail
            faded = (lookup * tail).astype(bfloat)
            chunk_a = chunk_decay(chunk, lanes)
            total = chunk_a * jnp.sum(after * state, 0, keepdims=True)
            drec[rows, lanes] = (drec_part[rows, lanes] + grad_reader).astype(bfloat)
            dkey[rows, lanes] = (dkey_part[rows, lanes] + grad_faded).astype(bfloat)
            dval[rows, lanes] = (dval_part[rows, lanes] + dot_nt(faded, after_low)).astype(bfloat)
            inner = (LEVELS - 1) * CHUNK
            moves = jnp.concatenate([acceptor * grad_reader, lookup * grad_faded], 0)
            grad_log = dlog_part[rows, lanes] + total + dot_nn(
                sums_back[:, inner:], moves.astype(bfloat)
            )
            raw = grad_log * logw[rows, lanes]
            draw[rows, lanes] = raw
            dvec[0:1, lanes] += jnp.sum(raw, 0, keepdims=True)
            return after * chunk_a + local[slot]

        lax.fori_loop(0, chunks, step, stack_heads(end_b[:, lanes]))
        return carry

    lax.fori_loop(0, pairs, finish, 0)
    for copy in swaps:
        copy.wait()
    for other in range(mp_count):
        lanes = slice(other * features, (other + 1) * features)
        mixed[:, lanes] = (residual[:, lanes] + swapped[other].astype(jnp.float32)).astype(bfloat)


def exchange_scratch(count, features):
    return [
        pltpu.VMEM((8, features), jnp.float32),
        pltpu.VMEM((2 * LANE_SPAN, features), jnp.bfloat16),
        pltpu.VMEM((count, 8, features), jnp.float32),
        pltpu.VMEM((count, 2 * LANE_SPAN, features), jnp.bfloat16),
        pltpu.SemaphoreType.DMA((2, count)),
        pltpu.SemaphoreType.DMA((2, count)),
    ]


def run_forward(count, mp_count, rec, key, val, gpre, logw, vec, marks, tables, cotangent):
    rows, features = rec.shape
    chunks, pairs = rows // CHUNK, features // PAIR
    slots = chunks * pairs
    whole_array = pl.BlockSpec(memory_space=pltpu.VMEM)
    level, sums, _ = tables
    return pl.pallas_call(
        functools.partial(recurrence_forward, count, mp_count, chunks, pairs),
        out_shape=(
            jax.ShapeDtypeStruct((rows, features), jnp.bfloat16),
            jax.ShapeDtypeStruct((rows, features), jnp.float32),
            jax.ShapeDtypeStruct((slots, PAIR, PAIR), jnp.float32),
            jax.ShapeDtypeStruct((slots, CHUNK, 2 * CHUNK), jnp.bfloat16),
            jax.ShapeDtypeStruct((rows, features), jnp.bfloat16),
        ),
        in_specs=[whole_array] * 14,
        out_specs=(whole_array,) * 5,
        scratch_shapes=[
            pltpu.VMEM((slots, sums.shape[0], PAIR), jnp.float32),
            pltpu.VMEM((slots, 8, PAIR), jnp.float32),
            pltpu.VMEM((slots, PAIR, PAIR), jnp.float32),
            pltpu.VMEM((LANE_SPAN, features), jnp.float32),
        ]
        + exchange_scratch(count, features)
        + [
            pltpu.SemaphoreType.DMA((mp_count - 1,)),
            pltpu.SemaphoreType.DMA((mp_count - 1,)),
        ],
        compiler_params=pltpu.CompilerParams(
            collective_id=1, has_side_effects=True, vmem_limit_bytes=48 << 20
        ),
        name="recurrence_forward",
    )(rec, key, val, gpre, logw, vec, *marks, level, sums, cotangent)


def run_backward(
    count, mp_count, dgated, wkv, states, kept, rec, key, val, gpre, logw, vec, marks, tables,
    change, residual,
):
    rows, features = rec.shape
    chunks, pairs = rows // CHUNK, features // PAIR
    slots = chunks * pairs
    whole_array = pl.BlockSpec(memory_space=pltpu.VMEM)
    level, sums, sums_back = tables
    low = jax.ShapeDtypeStruct((rows, features), jnp.bfloat16)
    full = pltpu.VMEM((rows, features), jnp.float32)
    return pl.pallas_call(
        functools.partial(recurrence_backward, count, mp_count, chunks, pairs),
        out_shape=(
            low,
            low,
            low,
            low,
            jax.ShapeDtypeStruct((rows, features), jnp.float32),
            jax.ShapeDtypeStruct((8, features), jnp.float32),
            jax.ShapeDtypeStruct(residual.shape, jnp.bfloat16),
        ),
        in_specs=[whole_array] * 20,
        out_specs=(whole_array,) * 7,
        scratch_shapes=[
            pltpu.VMEM((slots, sums.shape[0], PAIR), jnp.float32),
            pltpu.VMEM((slots, PAIR, PAIR), jnp.float32),
            pltpu.VMEM((LANE_SPAN, features), jnp.float32),
            full,
            full,
            full,
            full,
            full,
            pltpu.VMEM(((LEVELS - 1) * CHUNK, PAIR), jnp.float32),
        ]
        + exchange_scratch(count, features)
        + [pltpu.VMEM((mp_count,) + residual.shape[:1] + (features,), jnp.bfloat16)]
        + [
            pltpu.SemaphoreType.DMA((mp_count - 1,)),
            pltpu.SemaphoreType.DMA((mp_count - 1,)),
        ],
        compiler_params=pltpu.CompilerParams(
            collective_id=2, has_side_effects=True, vmem_limit_bytes=52 << 20
        ),
        name="recurrence_backward",
    )(
        dgated, wkv, states, kept, rec, key, val, gpre, logw, vec, *marks, level, sums, sums_back,
        change, residual,
    )


def flipped(index, mask):
    for bit in range(mask.bit_length()):
        size = 1 << bit
        if mask & size:
            index = index + size - 2 * size * lax.rem(index // size, 2)
    return index


def masks_over(bits):
    masks = [0]
    for bit in bits:
        masks = masks + [mask | (1 << bit) for mask in masks]
    return masks


def paths(count):
    higher = list(range(1, count.bit_length() - 1))
    return higher + [0], higher[::-1] + [0]


def remote(source, target, send_sem, recv_sem, dp, mp):
    return pltpu.make_async_remote_copy(
        src_ref=source,
        dst_ref=target,
        send_sem=send_sem,
        recv_sem=recv_sem,
        device_id=(dp, mp),
        device_id_type=MESH,
    )


def greet_all(partners):
    barrier = pltpu.get_barrier_semaphore()
    for dp, mp in partners:
        pl.semaphore_signal(barrier, inc=1, device_id=(dp, mp), device_id_type=MESH)
    pl.semaphore_wait(barrier, len(partners))


def line_partners(count):
    dp, mp = lax.axis_index("dp"), lax.axis_index("mp")
    return [(dp, lax.rem(mp + step, count)) for step in sorted({1, count - 1})]


def cube_partners(count):
    dp, mp = lax.axis_index("dp"), lax.axis_index("mp")
    return [(flipped(dp, 1 << bit), mp) for bit in range(count.bit_length() - 1)]


class Line:
    def __init__(self, count, rows, send_sems, recv_sems):
        self.count, self.rows = count, rows
        self.send_sems, self.recv_sems = send_sems, recv_sems
        self.dp, self.me = lax.axis_index("dp"), lax.axis_index("mp")
        self.piece = rows // PIECES

    def at(self, block, piece):
        return pl.ds(pl.multiple_of(block * self.rows + piece * self.piece, 16), self.piece)

    def copy(self, source, target, right, slot, piece):
        side = 0 if right else 1
        return remote(
            source,
            target,
            self.send_sems.at[side, slot, piece],
            self.recv_sems.at[side, slot, piece],
            self.dp,
            lax.rem(self.me + (1 if right else self.count - 1), self.count),
        )


class LineGather(Line):
    def hop(self, target, distance, piece, right):
        block = self.me - distance if right else self.me + distance
        ref = target.at[self.at(block, piece)]
        return self.copy(ref, ref, right, distance, piece)

    def holds(self, distance, right):
        return self.me >= distance if right else self.me + distance < self.count

    def passes(self, distance, right):
        onward = self.me < self.count - 1 if right else self.me > 0
        return jnp.logical_and(self.holds(distance, right), onward)

    def send(self, target, distance, piece):
        for right in (True, False):
            if distance:

                @pl.when(self.holds(distance, right))
                def _():
                    block = self.me - distance if right else self.me + distance
                    ref = target.at[self.at(block, piece)]
                    self.copy(ref, ref, right, distance - 1, piece).wait_recv()

            if distance < self.count - 1:

                @pl.when(self.passes(distance, right))
                def _():
                    self.hop(target, distance, piece, right).start()

    def finish(self, target):
        for distance in range(self.count - 1):
            for piece in range(PIECES):
                for right in (True, False):

                    @pl.when(self.passes(distance, right))
                    def _():
                        self.hop(target, distance, piece, right).wait_send()


class LineSum(Line):
    def hop(self, source, land, block, piece, right):
        return self.copy(
            source.at[self.at(block, piece)],
            land.at[0 if right else 1, self.at(block, piece)],
            right,
            block,
            piece,
        )

    def begin(self, part, moving, land):
        for number in range(self.count - 1):
            for piece in range(PIECES):
                for right in (True, False):
                    block = self.count - 1 - number if right else number
                    at = self.at(block, piece)

                    @pl.when(self.me == (0 if right else self.count - 1))
                    def _():
                        moving[at] = part[at]
                        self.hop(moving, land, block, piece, right).start()

    def forward(self, part, moving, land, block, piece, right):
        side = 0 if right else 1
        at = self.at(block, piece)
        inside = jnp.logical_and(self.me > 0, self.me < self.count - 1)

        @pl.when(jnp.logical_and(inside, self.me < block if right else self.me > block))
        def _():
            self.hop(moving, land, block, piece, right).wait_recv()
            moving[at] = (
                part[at].astype(jnp.float32) + land[side, at].astype(jnp.float32)
            ).astype(jnp.bfloat16)
            self.hop(moving, land, block, piece, right).start()

    def step(self, part, moving, land, number):
        for piece in range(PIECES):
            self.forward(part, moving, land, self.count - 1 - number, piece, True)
            self.forward(part, moving, land, number, piece, False)

    def total(self, part, moving, land, total, piece):
        at = self.at(self.me, piece)
        own = slice(piece * self.piece, (piece + 1) * self.piece)
        total[own] = part[at].astype(jnp.float32)
        for right in (True, False):

            @pl.when(self.me > 0 if right else self.me < self.count - 1)
            def _():
                self.hop(moving, land, self.me, piece, right).wait_recv()
                total[own] += land[0 if right else 1, at].astype(jnp.float32)

        return own

    def finish(self, moving, land):
        for number in range(self.count - 1):
            for piece in range(PIECES):
                for right in (True, False):
                    block = self.count - 1 - number if right else number

                    @pl.when(self.me < block if right else self.me > block)
                    def _():
                        self.hop(moving, land, block, piece, right).wait_send()


class Cube:
    def __init__(self, count, send_sems, recv_sems):
        self.count, self.send_sems, self.recv_sems = count, send_sems, recv_sems
        self.dp, self.mp = lax.axis_index("dp"), lax.axis_index("mp")
        self.stages = count.bit_length() - 1

    def copy(self, source, target, unit, mask, bit):
        return remote(
            source,
            target,
            self.send_sems.at[unit, mask],
            self.recv_sems.at[unit, mask],
            flipped(self.dp, 1 << bit),
            self.mp,
        )


class CubeGather(Cube):
    def stage(self, unit, path, view, stage):
        order = paths(self.count)[path]
        if stage:
            for mask in masks_over(order[: stage - 1]):
                got = mask | (1 << order[stage - 1])
                ref = view(flipped(self.dp, got))
                self.copy(ref, ref, unit, got, order[stage - 1]).wait_recv()
        if stage < self.stages:
            for mask in masks_over(order[:stage]):
                ref = view(flipped(self.dp, mask))
                self.copy(ref, ref, unit, mask | (1 << order[stage]), order[stage]).start()

    def finish(self, unit, path, view):
        order = paths(self.count)[path]
        for stage in range(self.stages):
            for mask in masks_over(order[:stage]):
                ref = view(flipped(self.dp, mask))
                self.copy(ref, ref, unit, mask | (1 << order[stage]), order[stage]).wait_send()


class CubeSum(Cube):
    def slot(self, order, stage, mask):
        base = self.count - (self.count >> stage)
        return base + masks_over(order[stage + 1 :]).index(mask)

    def source(self, unit, order, view, land, stage, mask):
        if stage == 0:
            return view(flipped(self.dp, mask))
        return land.at[self.slot(order, stage - 1, mask)]

    def sends(self, unit, path, view, land, stage):
        order = paths(self.count)[path][::-1]
        bit = order[stage]
        return [
            self.copy(
                self.source(unit, order, view, land, stage, mask | (1 << bit)),
                land.at[self.slot(order, stage, mask)],
                unit,
                mask | (1 << bit),
                bit,
            )
            for mask in masks_over(order[stage + 1 :])
        ]

    def start(self, unit, path, view, land, stage):
        for copy in self.sends(unit, path, view, land, stage):
            copy.start()

    def absorb(self, unit, path, view, land, stage, out=None):
        order = paths(self.count)[path][::-1]
        for copy, mask in zip(
            self.sends(unit, path, view, land, stage), masks_over(order[stage + 1 :])
        ):
            copy.wait_recv()
            before = self.source(unit, order, view, land, stage, mask)
            here = land.at[self.slot(order, stage, mask)]
            step = 16

            def add(number, carry):
                at = pl.ds(pl.multiple_of(number * step, step), step)
                both = before[at].astype(jnp.float32) + here[at].astype(jnp.float32)
                if out is None:
                    here[at] = both.astype(jnp.bfloat16)
                else:
                    out[at] = both
                return carry

            lax.fori_loop(0, here.shape[0] // step, add, 0)

    def finish(self, unit, path, view, land):
        for stage in range(self.stages):
            for copy in self.sends(unit, path, view, land, stage):
                copy.wait_send()


def line_sems(count):
    return [pltpu.SemaphoreType.DMA((2, count, PIECES)), pltpu.SemaphoreType.DMA((2, count, PIECES))]


def cube_sems(units, count):
    return [pltpu.SemaphoreType.DMA((units, count)), pltpu.SemaphoreType.DMA((units, count))]


def start_kernel(
    dp_count, mp_count, tokens, pack, mix_state, out_state, gate_state, key_state, value_state,
    tokens_all, small, mix_all, out_low, gate_low, key_low, value_low,
    mix, mix_full, out_full, gate_full, key_full, value_full,
    load_sems, own_sems, line_send, line_recv, pack_send, pack_recv, cube_send, cube_recv,
):
    dp, mp = lax.axis_index("dp"), lax.axis_index("mp")
    rows = tokens.shape[0]
    matrices, block = mix.shape[0], mix.shape[1]
    pack_rows, group = pack.shape[0], pack.shape[0] * mp_count
    half = group // 2
    states = (mix_state, out_state, gate_state, key_state, value_state)
    fulls = (mix_full, out_full, gate_full, key_full, value_full)
    loads = [
        pltpu.make_async_copy(state.at[0], full, load_sems.at[number])
        for number, (state, full) in enumerate(zip(states, fulls))
    ]
    for load in loads:
        load.start()
    others = [lax.rem(mp + step, mp_count) for step in range(1, mp_count)]
    greet_all([(dp, other) for other in others] + cube_partners(dp_count))
    line = LineGather(mp_count, rows, line_send, line_recv)
    cube = CubeGather(dp_count, cube_send, cube_recv)

    pack_at = small.at[pl.ds(pl.multiple_of(dp * group + mp * pack_rows, 16), pack_rows)]
    own = [
        pltpu.make_async_copy(pack, pack_at, own_sems.at[0]),
        pltpu.make_async_copy(
            tokens, tokens_all.at[pl.ds(pl.multiple_of(mp * rows, 16), rows)], own_sems.at[1]
        ),
    ]
    pack_copies = [
        remote(pack, pack_at, pack_send.at[step], pack_recv.at[step], dp, other)
        for step, other in enumerate(others)
    ]
    for copy in pack_copies + own:
        copy.start()
    loads[0].wait()
    for number in range(matrices):
        mix[number] = mix_full[number].astype(jnp.bfloat16)
    own_mix = [
        pltpu.make_async_copy(
            mix.at[number],
            mix_all.at[number, pl.ds(pl.multiple_of(dp * block, 16), block)],
            own_sems.at[2 + number],
        )
        for number in range(matrices)
    ]
    for copy in own_mix:
        copy.start()

    def small_view(part):
        def view(index):
            return small.at[pl.ds(pl.multiple_of(index * group + part * half, 16), half)]

        return view

    def mix_view(number):
        def view(index):
            return mix_all.at[number, pl.ds(pl.multiple_of(index * block, 16), block)]

        return view

    mix_units = [
        (2 + number, 0 if 2 * number < matrices else 1, mix_view(number))
        for number in range(matrices)
    ]
    small_units = [(part, part, small_view(part)) for part in range(2)]
    for copy in own + own_mix:
        copy.wait()
    for unit in mix_units:
        cube.stage(*unit, 0)
    for piece in range(PIECES):
        line.send(tokens_all, 0, piece)
    for load, full, low in zip(loads[1:], fulls[1:], (out_low, gate_low, key_low, value_low)):
        load.wait()
        step = 64

        def convert(number, carry):
            at = pl.ds(pl.multiple_of(number * step, step), step)
            low[at] = full[at].astype(jnp.bfloat16)
            return carry

        lax.fori_loop(0, full.shape[0] // step, convert, 0)
    for copy in pack_copies:
        copy.wait()
    for unit in small_units:
        cube.stage(*unit, 0)
    for distance in range(1, mp_count):
        for piece in range(PIECES):
            line.send(tokens_all, distance, piece)
        if distance < dp_count.bit_length() - 1:
            for unit in mix_units + small_units:
                cube.stage(*unit, distance)
    for stage in range(min(mp_count, dp_count.bit_length() - 1), dp_count.bit_length()):
        for unit in mix_units + small_units:
            cube.stage(*unit, stage)
    line.finish(tokens_all)
    for unit in mix_units + small_units:
        cube.finish(*unit)


def run_start(dp_count, mp_count, tokens, pack, states):
    rows, width = tokens.shape
    matrices, block, features = states[0].shape[1:]
    anywhere = pl.BlockSpec(memory_space=pl.ANY)
    vmem = pl.BlockSpec(memory_space=pltpu.VMEM)
    bfloat = jnp.bfloat16
    return pl.pallas_call(
        functools.partial(start_kernel, dp_count, mp_count),
        out_shape=(
            jax.ShapeDtypeStruct((rows * mp_count, width), bfloat),
            jax.ShapeDtypeStruct((pack.shape[0] * mp_count * dp_count, pack.shape[1]), bfloat),
            jax.ShapeDtypeStruct((matrices, block * dp_count, features), bfloat),
            *[jax.ShapeDtypeStruct(state.shape[1:], bfloat) for state in states[1:]],
        ),
        in_specs=[vmem, vmem] + [anywhere] * 5,
        out_specs=(anywhere,) * 3 + (vmem,) * 4,
        scratch_shapes=[
            pltpu.VMEM(states[0].shape[1:], bfloat),
            *[pltpu.VMEM(state.shape[1:], jnp.float32) for state in states],
            pltpu.SemaphoreType.DMA((5,)),
            pltpu.SemaphoreType.DMA((2 + matrices,)),
            *line_sems(mp_count),
            pltpu.SemaphoreType.DMA((mp_count - 1,)),
            pltpu.SemaphoreType.DMA((mp_count - 1,)),
            *cube_sems(2 + matrices, dp_count),
        ],
        compiler_params=pltpu.CompilerParams(
            collective_id=3, has_side_effects=True, vmem_limit_bytes=32 << 20
        ),
        name="gather_start",
    )(tokens, pack, *states)


def residual_rows(total, rows, tokens):
    return total + tokens[rows].astype(jnp.float32)


def backward_rows(total, rows, source, gain, skip):
    value = source[rows].astype(jnp.float32)
    centre = value - jnp.mean(value, -1, keepdims=True)
    inverse = lax.rsqrt(jnp.mean(centre * centre, -1, keepdims=True) + norm_epsilon)
    return skip[rows].astype(jnp.float32) + norm_backward(total, centre * inverse, inverse, gain[:1])


def exchange_kernel(count, epilogue, extras, part, *refs):
    extra, refs = refs[:extras], refs[extras:]
    own, gathered, moving, land, total = refs[:5]
    sum_send, sum_recv, line_send, line_recv = refs[5:]
    rows = own.shape[0]
    greet_all(line_partners(count))
    adder = LineSum(count, rows, sum_send, sum_recv)
    line = LineGather(count, rows, line_send, line_recv)
    adder.begin(part, moving, land)
    for number in range(count - 1):
        adder.step(part, moving, land, number)
    for piece in range(PIECES):
        at = adder.total(part, moving, land, total, piece)
        value = epilogue(total[at], at, *extra)
        own[at] = value
        gathered[line.at(line.me, piece)] = value.astype(jnp.bfloat16)
        line.send(gathered, 0, piece)
    for distance in range(1, count):
        for piece in range(PIECES):
            line.send(gathered, distance, piece)
    adder.finish(moving, land)
    line.finish(gathered)


def run_exchange(count, number, epilogue, part, *extra):
    rows, width = part.shape[0] // count, part.shape[1]
    vmem = pl.BlockSpec(memory_space=pltpu.VMEM)
    return pl.pallas_call(
        functools.partial(exchange_kernel, count, epilogue, len(extra)),
        out_shape=(
            jax.ShapeDtypeStruct((rows, width), jnp.float32),
            jax.ShapeDtypeStruct(part.shape, jnp.bfloat16),
        ),
        in_specs=[vmem] * (1 + len(extra)),
        out_specs=(vmem, vmem),
        scratch_shapes=[
            pltpu.VMEM(part.shape, jnp.bfloat16),
            pltpu.VMEM((2,) + part.shape, jnp.bfloat16),
            pltpu.VMEM((rows, width), jnp.float32),
            *line_sems(count),
            *line_sems(count),
        ],
        compiler_params=pltpu.CompilerParams(
            collective_id=number, has_side_effects=True, vmem_limit_bytes=40 << 20
        ),
        name="sum_and_gather",
    )(part, *extra)


def end_kernel(
    dp_count, mp_count, part, source, gain, skip, mix_a, mix_b, mix_c, mix_d, pack,
    own, mix_sum, pack_sum,
    moving, land, total, mix_land, pack_land, pack_own, pack_out, small_land,
    sum_send, sum_recv, cube_send, cube_recv, small_send, small_recv,
):
    dp, mp = lax.axis_index("dp"), lax.axis_index("mp")
    mix = (mix_a, mix_b, mix_c, mix_d)
    rows, matrices = own.shape[0], len(mix)
    block, group = mix_sum.shape[1], pack_own.shape[0]
    half, pack_rows = group // 2, pack_sum.shape[0]
    others = [lax.rem(mp + step, mp_count) for step in range(1, mp_count)]
    greet_all([(dp, other) for other in others] + cube_partners(dp_count))
    adder = LineSum(mp_count, rows, sum_send, sum_recv)
    cube = CubeSum(dp_count, cube_send, cube_recv)

    def mix_view(number):
        def view(index):
            return mix[number].at[pl.ds(pl.multiple_of(index * block, 16), block)]

        return view

    def pack_view(side):
        def view(index):
            return pack.at[pl.ds(pl.multiple_of(index * group + side * half, 16), half)]

        return view

    units = [(side, side, pack_view(side), pack_land.at[side]) for side in range(2)] + [
        (2 + number, 0 if 2 * number < matrices else 1, mix_view(number), mix_land.at[number])
        for number in range(matrices)
    ]
    outs = [pack_own.at[pl.ds(side * half, half)] for side in range(2)] + [
        mix_sum.at[number] for number in range(matrices)
    ]
    for unit in units:
        cube.start(*unit, 0)
    adder.begin(part, moving, land)
    last = cube.stages - 1
    for unit in units:
        cube.absorb(*unit, 0)
        cube.start(*unit, 1)
    for number in range(mp_count - 1):
        adder.step(part, moving, land, number)
    for piece in range(PIECES):
        at = adder.total(part, moving, land, total, piece)
        own[at] = backward_rows(total[at], at, source, gain, skip)
    for stage in range(1, last):
        for unit in units:
            cube.absorb(*unit, stage)
            cube.start(*unit, stage + 1)
    for unit, out in zip(units[:2], outs[:2]):
        cube.absorb(*unit, last, out)
    pack_out[...] = pack_own[...].astype(jnp.bfloat16)
    small_copies = [
        remote(
            pack_out.at[pl.ds(pl.multiple_of(other * pack_rows, 16), pack_rows)],
            small_land.at[step],
            small_send.at[step],
            small_recv.at[step],
            dp,
            other,
        )
        for step, other in enumerate(others)
    ]
    for copy in small_copies:
        copy.start()
    for unit, out in zip(units[2:], outs[2:]):
        cube.absorb(*unit, last, out)
    pack_sum[...] = pack_own[pl.ds(pl.multiple_of(mp * pack_rows, 16), pack_rows), :]
    for step, copy in enumerate(small_copies):
        copy.wait()
        pack_sum[...] += small_land[step].astype(jnp.float32)
    adder.finish(moving, land)
    for unit in units:
        cube.finish(*unit)


def run_end(dp_count, mp_count, part, source, gain, skip, mix, pack):
    rows, width = source.shape
    matrices, features = len(mix), mix[0].shape[1]
    block, group = mix[0].shape[0] // dp_count, pack.shape[0] // dp_count
    lanes = pack.shape[1]
    vmem = pl.BlockSpec(memory_space=pltpu.VMEM)
    return pl.pallas_call(
        functools.partial(end_kernel, dp_count, mp_count),
        out_shape=(
            jax.ShapeDtypeStruct((rows, width), jnp.float32),
            jax.ShapeDtypeStruct((matrices, block, features), jnp.float32),
            jax.ShapeDtypeStruct((group // mp_count, lanes), jnp.float32),
        ),
        in_specs=[vmem] * 9,
        out_specs=(vmem,) * 3,
        scratch_shapes=[
            pltpu.VMEM(part.shape, jnp.bfloat16),
            pltpu.VMEM((2,) + part.shape, jnp.bfloat16),
            pltpu.VMEM((rows, width), jnp.float32),
            pltpu.VMEM((matrices, dp_count - 1, block, features), jnp.bfloat16),
            pltpu.VMEM((2, dp_count - 1, group // 2, lanes), jnp.bfloat16),
            pltpu.VMEM((group, lanes), jnp.float32),
            pltpu.VMEM((group, lanes), jnp.bfloat16),
            pltpu.VMEM((mp_count - 1, group // mp_count, lanes), jnp.bfloat16),
            *line_sems(mp_count),
            *cube_sems(2 + matrices, dp_count),
            pltpu.SemaphoreType.DMA((mp_count - 1,)),
            pltpu.SemaphoreType.DMA((mp_count - 1,)),
        ],
        compiler_params=pltpu.CompilerParams(
            collective_id=6, has_side_effects=True, vmem_limit_bytes=56 << 20
        ),
        name="sum_end",
    )(part, source, gain, skip, *mix, pack)


def update_rows(rate, state, grad, new):
    scaled = rate * grad[...].astype(jnp.float32)
    velocity = momentum_rate * state[1] + scaled
    weight = state[0] - (scaled + momentum_rate * velocity)
    new[0] = velocity
    new[1] = weight
    new[2] = average_rate * state[2] + (1.0 - average_rate) * weight


def run_update(state, grad, fan, total_tokens):
    shape = state.shape
    lanes = shape[-1]
    flat = state.reshape(3, -1, lanes)
    grad = grad.reshape(-1, lanes)
    block = 128
    triple = pl.BlockSpec((3, block, lanes), lambda i: (0, i, 0))
    return pl.pallas_call(
        functools.partial(update_rows, (total_tokens * fan) ** (-0.5)),
        grid=(grad.shape[0] // block,),
        out_shape=jax.ShapeDtypeStruct(flat.shape, jnp.float32),
        in_specs=[triple, pl.BlockSpec((block, lanes), lambda i: (i, 0))],
        out_specs=triple,
        compiler_params=pltpu.CompilerParams(vmem_limit_bytes=32 << 20),
        name="momentum_update",
    )(flat, grad).reshape(shape)


def lane_mask(shape, low, high):
    lane = lax.broadcasted_iota(jnp.int32, shape, len(shape) - 1)
    return jnp.logical_and(lane >= low, lane < high)


def masked(value, low, high):
    return jnp.where(lane_mask(value.shape, low, high), value, jnp.zeros_like(value))


def block_norm(value, vectors):
    hidden, hat, _ = norm_forward(value.astype(jnp.float32), vectors[0:1], vectors[1:2], norm_epsilon)
    return hidden, hat


def block_delta(hidden, before, keep):
    row = lax.broadcasted_iota(jnp.int32, hidden.shape, 0)
    behind = jnp.where(row == 0, before, pltpu.roll(hidden, 1, 0))
    return behind * keep - hidden


def mixing_forward(
    tokens, heads, keep, small, vectors, decay_row, up_own, mix, inputs, rec, key, val, gpre, logw, acts
):
    bfloat = jnp.bfloat16
    maa_cols = 5 * TM_RANK
    down_cols = maa_cols + DECAY_RANK
    hidden, _ = block_norm(tokens[...], vectors)
    before, _ = block_norm(heads[0], vectors)
    delta = block_delta(hidden, before[:1], keep[:, :1])
    base = (hidden + delta * vectors[2:3]).astype(bfloat)
    act = jnp.tanh(dot_nn(base, small[:, :WINDOW]))
    act_low = act.astype(bfloat)
    for number in range(5):
        mine = masked(act_low, TM_RANK * number, TM_RANK * (number + 1))
        scale = vectors[3 + number : 4 + number] + dot_nt(mine, small[:, WINDOW:])
        value = (hidden + delta * scale).astype(bfloat)
        inputs[number] = value
        if number:
            place = {1: 1, 2: 2, 3: 0, 4: 3}[number]
            (rec, key, val, gpre)[place][...] = dot_nn(value, mix[place])
        else:
            decay = masked(jnp.tanh(dot_nn(value, small[:, :WINDOW])), maa_cols, down_cols)
            logw[...] = -jnp.exp(decay_row[:1] + dot_nt(decay.astype(bfloat), up_own[...]))
    acts[...] = masked(act, 0, maa_cols) + decay


def run_mixing_forward(tokens, heads, keep, small, vectors, decay_row, up_own, mix):
    rows, width = tokens.shape
    features = mix.shape[2]
    block = lambda lanes: pl.BlockSpec((ROW_BLOCK, lanes), lambda i: (i, 0))
    fixed = lambda value: pl.BlockSpec(
        value.shape, lambda i: (0,) * value.ndim, pipeline_mode=pl.Buffered(1)
    )
    stack = lambda count, lanes: pl.BlockSpec((count, ROW_BLOCK, lanes), lambda i: (0, i, 0))
    return pl.pallas_call(
        mixing_forward,
        grid=(rows // ROW_BLOCK,),
        out_shape=(
            jax.ShapeDtypeStruct((5, rows, width), jnp.bfloat16),
            *[jax.ShapeDtypeStruct((rows, features), jnp.float32)] * 5,
            jax.ShapeDtypeStruct((rows, WINDOW), jnp.float32),
        ),
        in_specs=[
            block(width),
            pl.BlockSpec((1,) + heads.shape[1:], lambda i: (i, 0, 0)),
            block(keep.shape[1]),
            fixed(small),
            fixed(vectors),
            fixed(decay_row),
            fixed(up_own),
            fixed(mix),
        ],
        out_specs=(stack(5, width), *[block(features)] * 5, block(WINDOW)),
        compiler_params=pltpu.CompilerParams(vmem_limit_bytes=58 << 20),
        name="mixing_forward",
    )(tokens, heads, keep, small, vectors, decay_row, up_own, mix)


def mixing_backward(
    tokens, heads, keep, acts, drec, dkey, dval, dgate, draw,
    small, vectors, up_own, mix, given,
    grad_hidden, grad_pack, first_row,
    grad_down, grad_up, grad_vec, carried,
):
    bfloat = jnp.bfloat16
    step, last = pl.program_id(0), pl.num_programs(0) - 1
    maa_cols = 5 * TM_RANK
    down_cols = maa_cols + DECAY_RANK
    features = mix.shape[2]
    col_start = pl.multiple_of(lax.axis_index("mp") * features, 128)

    @pl.when(step == 0)
    def _():
        grad_down[...] = jnp.zeros(grad_down.shape, jnp.float32)
        grad_up[...] = jnp.zeros(grad_up.shape, jnp.float32)
        grad_vec[...] = given[...]
        carried[...] = jnp.zeros(carried.shape, jnp.float32)

    down, upper = small.at[:, :WINDOW], small.at[:, WINDOW:]
    hidden, hat = block_norm(tokens[...], vectors)
    before, before_hat = block_norm(heads[0], vectors)
    delta = block_delta(hidden, before[:1], keep[:, :1])
    act = acts[...]
    act_low = act.astype(bfloat)
    slope = 1.0 - act * act
    raw = draw[...].astype(bfloat)
    grad_decay = masked(dot_nn(raw, up_own[...]) * slope, maa_cols, down_cols).astype(bfloat)
    grad_up[pl.ds(col_start, features), :] += dot_tn(raw, masked(act_low, maa_cols, down_cols))

    def add_row(row, value):
        grad_vec[row : row + 1, :] += jnp.sum(value, 0, keepdims=True)

    total = jnp.zeros(hidden.shape, jnp.float32)
    grad_delta = jnp.zeros(hidden.shape, jnp.float32)
    grad_act = jnp.zeros(act.shape, jnp.float32)
    for number in range(5):
        low, high = TM_RANK * number, TM_RANK * (number + 1)
        mine = masked(act_low, low, high)
        scale = vectors[3 + number : 4 + number] + dot_nt(mine, upper[...])
        if number:
            source = {1: dkey, 2: dval, 3: drec, 4: dgate}[number]
            grad_input = dot_nt(source[...], mix[{1: 1, 2: 2, 3: 0, 4: 3}[number]])
        else:
            grad_input = dot_nt(grad_decay, down[...])
            value = (hidden + delta * scale).astype(bfloat)
            grad_down[...] += dot_tn(value, grad_decay)
        moved = grad_input * delta
        add_row(3 + number, moved)
        moved_low = moved.astype(bfloat)
        grad_up[...] += dot_tn(moved_low, mine)
        grad_act += masked(dot_nn(moved_low, upper[...]), low, high)
        grad_delta += grad_input * scale
        total += grad_input
    grad_pre = (grad_act * slope).astype(bfloat)
    base = (hidden + delta * vectors[2:3]).astype(bfloat)
    grad_down[...] += dot_tn(base, grad_pre)
    grad_base = dot_nt(grad_pre, down[...])
    add_row(2, grad_base * delta)
    grad_delta += grad_base * vectors[2:3]
    shifted_grad = grad_delta * keep[:, :1]
    row = lax.broadcasted_iota(jnp.int32, hidden.shape, 0)
    back = jnp.where(
        row == ROW_BLOCK - 1, carried[:1], pltpu.roll(shifted_grad, ROW_BLOCK - 1, 0)
    )
    carried[...] = jnp.broadcast_to(shifted_grad[:1], carried.shape)
    total += grad_base - grad_delta + back
    add_row(0, total * hat)
    add_row(1, total)
    grad_hidden[...] = total.astype(bfloat)

    @pl.when(step == last)
    def _():
        first_row[...] = carried[...]
        add_row(0, carried[:1] * before_hat[:1])
        add_row(1, carried[:1])
        spot = lax.broadcasted_iota(jnp.int32, (16, WINDOW), 0) + down_cols
        lane = lax.broadcasted_iota(jnp.int32, (16, WINDOW), 1)
        one = jnp.where(spot == lane, 1.0, 0.0).astype(bfloat)
        placed = dot_tn(grad_vec[...].astype(bfloat), one)
        grad_pack[:, :WINDOW] = (grad_down[...] + placed).astype(bfloat)
        grad_pack[:, WINDOW:] = grad_up[...].astype(bfloat)


def run_mixing_backward(
    tokens, heads, keep, acts, drec, dkey, dval, dgate, draw, small, vectors, up_own, mix, given
):
    rows, width = tokens.shape
    features = mix.shape[2]
    count = rows // ROW_BLOCK
    block = lambda lanes: pl.BlockSpec((ROW_BLOCK, lanes), lambda i: (count - 1 - i, 0))
    fixed = lambda value: pl.BlockSpec(
        value.shape, lambda i: (0,) * len(value.shape), pipeline_mode=pl.Buffered(1)
    )
    first = jax.ShapeDtypeStruct((8, width), jnp.float32)
    pack = jax.ShapeDtypeStruct((width, 2 * WINDOW), jnp.bfloat16)
    return pl.pallas_call(
        mixing_backward,
        grid=(count,),
        out_shape=(jax.ShapeDtypeStruct((rows, width), jnp.bfloat16), pack, first),
        in_specs=[
            block(width),
            pl.BlockSpec((1,) + heads.shape[1:], lambda i: (count - 1 - i, 0, 0)),
            block(keep.shape[1]),
            block(WINDOW),
            block(features),
            block(features),
            block(features),
            block(features),
            block(features),
            fixed(small),
            fixed(vectors),
            fixed(up_own),
            fixed(mix),
            fixed(given),
        ],
        out_specs=(block(width), fixed(pack), fixed(first)),
        scratch_shapes=[
            pltpu.VMEM((width, WINDOW), jnp.float32),
            pltpu.VMEM((width, WINDOW), jnp.float32),
            pltpu.VMEM((16, width), jnp.float32),
            pltpu.VMEM((8, width), jnp.float32),
        ],
        compiler_params=pltpu.CompilerParams(vmem_limit_bytes=60 << 20),
        name="mixing_backward",
    )(tokens, heads, keep, acts, drec, dkey, dval, dgate, draw, small, vectors, up_own, mix, given)


def channel_backward(
    source, heads, keep, grad_key, grad_recv, vectors, gate,
    grad_hidden, sums, first_row,
    carried,
):
    step, last = pl.program_id(0), pl.num_programs(0) - 1

    @pl.when(step == 0)
    def _():
        sums[...] = jnp.zeros(sums.shape, jnp.float32)
        carried[...] = jnp.zeros(carried.shape, jnp.float32)

    def norm(value):
        return norm_forward(
            value.astype(jnp.float32), vectors[12:13], vectors[13:14], norm_epsilon
        )[:2]

    def add_row(row, value):
        sums[row : row + 1, :] += jnp.sum(value, 0, keepdims=True)

    hidden, hat = norm(source[...])
    before, before_hat = norm(heads[0])
    delta = block_delta(hidden, before[:1], keep[:, :1])
    grad_recv_in = dot_nt(grad_recv[...], gate[...])
    grad_key_in = grad_key[...]
    grad_delta = grad_key_in * vectors[14:15] + grad_recv_in * vectors[15:16]
    add_row(2, grad_key_in * delta)
    add_row(3, grad_recv_in * delta)
    shifted_grad = grad_delta * keep[:, :1]
    row = lax.broadcasted_iota(jnp.int32, hidden.shape, 0)
    back = jnp.where(
        row == ROW_BLOCK - 1, carried[:1], pltpu.roll(shifted_grad, ROW_BLOCK - 1, 0)
    )
    carried[...] = jnp.broadcast_to(shifted_grad[:1], carried.shape)
    total = grad_key_in + grad_recv_in - grad_delta + back
    add_row(0, total * hat)
    add_row(1, total)
    grad_hidden[...] = total.astype(jnp.bfloat16)

    @pl.when(step == last)
    def _():
        first_row[...] = carried[...]
        add_row(0, carried[:1] * before_hat[:1])
        add_row(1, carried[:1])


def run_channel_backward(source, heads, keep, grad_key, grad_recv, vectors, gate):
    rows, width = source.shape
    count = rows // ROW_BLOCK
    block = lambda lanes: pl.BlockSpec((ROW_BLOCK, lanes), lambda i: (count - 1 - i, 0))
    fixed = lambda value: pl.BlockSpec(
        value.shape, lambda i: (0,) * len(value.shape), pipeline_mode=pl.Buffered(1)
    )
    first = jax.ShapeDtypeStruct((8, width), jnp.float32)
    return pl.pallas_call(
        channel_backward,
        grid=(count,),
        out_shape=(jax.ShapeDtypeStruct((rows, width), jnp.bfloat16), first, first),
        in_specs=[
            block(width),
            pl.BlockSpec((1,) + heads.shape[1:], lambda i: (count - 1 - i, 0, 0)),
            block(keep.shape[1]),
            block(width),
            block(grad_recv.shape[1]),
            fixed(vectors),
            fixed(gate),
        ],
        out_specs=(block(width), fixed(first), fixed(first)),
        scratch_shapes=[pltpu.VMEM((8, width), jnp.float32)],
        compiler_params=pltpu.CompilerParams(vmem_limit_bytes=48 << 20),
        name="channel_backward",
    )(source, heads, keep, grad_key, grad_recv, vectors, gate)


def update(carried_memory, grad, fan, total_tokens):
    rate = (total_tokens * fan) ** (-0.5)
    scaled = rate * grad
    velocity = momentum_rate * carried_memory[1] + scaled
    weight = carried_memory[0] - (scaled + momentum_rate * velocity)
    average = average_rate * carried_memory[2] + (1.0 - average_rate) * weight
    return jnp.stack([velocity, weight, average])


def split_three(value):
    pieces = []
    for _ in range(3):
        pieces.append(lax.reduce_precision(value, 8, 7))
        value = value - pieces[-1]
    return [piece.astype(jnp.bfloat16) for piece in pieces]


def shifted(value, before, keep):
    return jnp.concatenate([before, value[:-1]], 0) * keep[:, None] - value


def add_last(value, arriving):
    last = (value[-1:].astype(jnp.float32) + arriving).astype(value.dtype)
    return value.at[-1:].set(last)


def block_heads(before, rows):
    width = rows.shape[1]
    ends = rows.reshape(-1, ROW_BLOCK, width)[:-1, -1]
    heads = jnp.concatenate([before, ends], 0)
    return jnp.broadcast_to(heads[:, None], (heads.shape[0], 16, width))


def body(
    tokens,
    cotangent,
    lengths,
    mix_state,
    out_state,
    key_state,
    value_state,
    gate_state,
    down_state,
    up_state,
    vector_state,
):
    bfloat = jnp.bfloat16
    single = jnp.float32
    dp_count = lax.axis_size("dp")
    mp_count = lax.axis_size("mp")
    dp_index = lax.axis_index("dp")
    mp_index = lax.axis_index("mp")
    own_rows = tokens.shape[0]
    width = tokens.shape[1]
    group_rows = own_rows * mp_count
    total_tokens = group_rows * dp_count
    features = mix_state.shape[3]
    maa_cols = 5 * TM_RANK
    down_cols = maa_cols + DECAY_RANK
    col_start = mp_index * features

    upper, middle, lower = split_three(vector_state[0].T)
    pack = jnp.concatenate(
        [
            down_state[0].astype(bfloat),
            upper,
            middle,
            up_state[0].T.astype(bfloat),
            lower,
            jnp.zeros_like(lower),
        ],
        1,
    )
    states = (mix_state, out_state, gate_state, key_state, value_state)
    tokens_all, small, mix_weight, out_low, gate_low, key_low, value_low = run_start(
        dp_count, mp_count, tokens, pack, states
    )
    out_weight = lax.all_gather(out_low, "dp", axis=1, tiled=True)
    gate_weight = lax.all_gather(gate_low, "dp", axis=0, tiled=True)
    vectors = sum(
        small[:, start : start + 16].astype(single)
        for start in (down_cols, down_cols + 16, WINDOW + down_cols)
    ).T

    seq_ends = jnp.cumsum(lengths)
    offsets = seq_ends - lengths
    positions = dp_index * group_rows + jnp.arange(group_rows, dtype=jnp.int32)
    opening = jnp.any(positions[:, None] == offsets[None, :], 1).astype(single)
    segment = jnp.sum((offsets[None, :] <= positions[:, None]).astype(single), 1)
    keep = 1.0 - opening
    chunks = group_rows // CHUNK
    parts = segment.reshape(chunks, CHUNK)
    first = parts[:, :1] - opening.reshape(chunks, CHUNK)[:, :1]

    def spread(value, lanes):
        return jnp.broadcast_to(value.astype(single).reshape(-1, 1), (value.size, lanes))

    marks = (
        spread(parts, 2 * CHUNK),
        jnp.repeat(jnp.concatenate([parts, parts], 1), 8, 0),
        spread(parts == first, PAIR),
        spread(parts == parts[:, -1:], PAIR),
        spread(jnp.repeat(parts[:, -1:] == first, 8, 0), PAIR),
    )
    level, sums, sums_back = level_tables()
    tables = (jnp.asarray(level), jnp.asarray(sums, bfloat), jnp.asarray(sums_back, bfloat))

    def local_share(row_number):
        return lax.dynamic_slice_in_dim(vectors[row_number], col_start, features, 0)

    def spread_row(value):
        return jnp.broadcast_to(value[None], (8, width))

    before_first = from_behind(tokens_all[-1:], "dp", 1)
    heads = block_heads(before_first, tokens_all)
    keep_lanes = spread(keep, PAIR)
    up_own = lax.dynamic_slice_in_dim(small[:, WINDOW:], col_start, features, 0)
    decay_row = jnp.broadcast_to(local_share(8)[None], (8, features))
    inputs_low, *branch, acts = run_mixing_forward(
        tokens_all, heads, keep_lanes, small, vectors, decay_row, up_own, mix_weight
    )
    key_low, value_low, branch = lax.optimization_barrier((key_low, value_low, branch))
    key_weight = lax.all_gather(key_low, "dp", axis=0, tiled=True)
    value_weight = lax.all_gather(value_low, "dp", axis=1, tiled=True)
    local_vectors = jnp.concatenate(
        [jnp.stack([local_share(9), local_share(10), local_share(11)]), jnp.zeros((5, features))], 0
    )
    gated_low, wkv, states, kept, cotangent_cols = run_forward(
        dp_count, mp_count, *branch, local_vectors, marks, tables, cotangent
    )
    cotangent_cols = cotangent_cols.astype(single)

    residual, residual_all = run_exchange(
        mp_count, 4, residual_rows, half_dot(gated_low, out_weight).astype(bfloat), tokens
    )
    before_second = from_behind(residual_all[-1:], "dp", 1)
    hidden_two, hat_two, inv_two = norm_forward(
        residual_all.astype(single), vectors[12], vectors[13], norm_epsilon
    )
    before_two = norm_forward(before_second.astype(single), vectors[12], vectors[13], norm_epsilon)[
        0
    ]
    delta_two = shifted(hidden_two, before_two, keep)
    key_in_low = (hidden_two + delta_two * vectors[14]).astype(bfloat)
    recv_in_low = (hidden_two + delta_two * vectors[15]).astype(bfloat)
    recv_gate = jax.nn.sigmoid(half_dot(recv_in_low, gate_weight))
    grad_kv = (cotangent_cols * recv_gate).astype(bfloat)
    grad_kv, key_in_low = lax.optimization_barrier((grad_kv, key_in_low))
    key_pre = half_dot(key_in_low, key_weight)
    key_act_low = jnp.square(jnp.maximum(key_pre, 0.0)).astype(bfloat)
    grad_kv_all = lax.all_gather(grad_kv, "mp", axis=1, tiled=True)
    channel_sum = lax.psum_scatter(
        half_dot(key_act_low, value_weight).astype(bfloat), "mp", scatter_dimension=1, tiled=True
    ).astype(single)
    gated_sum = recv_gate * channel_sum
    grad_recv_pre = (cotangent_cols * gated_sum * (1.0 - recv_gate)).astype(bfloat)
    grad_key_act = half_right(grad_kv_all, value_weight)
    grad_key_pre = (grad_key_act * 2.0 * jnp.maximum(key_pre, 0.0)).astype(bfloat)
    grad_key_in = half_right(grad_key_pre, key_weight)
    grad_value_weight = half_left(key_act_low, grad_kv_all).astype(bfloat)
    grad_key_weight = half_left(key_in_low, grad_key_pre).astype(bfloat)
    grad_gate_weight = half_left(recv_in_low, grad_recv_pre).astype(bfloat)
    grad_hidden_two, channel_sums, first_row_two = run_channel_backward(
        residual_all,
        block_heads(before_second, residual_all),
        keep_lanes,
        grad_key_in,
        grad_recv_pre,
        vectors,
        gate_weight,
    )
    grad_hidden_two = add_last(grad_hidden_two, from_behind(first_row_two[:1], "dp", -1))
    grad_hidden_low, grad_value_weight, grad_key_weight, grad_gate_weight = (
        lax.optimization_barrier(
            (
                grad_hidden_two,
                grad_value_weight,
                grad_key_weight,
                grad_gate_weight,
            )
        )
    )
    def summed(value, axis):
        return lax.psum_scatter(value, "dp", scatter_dimension=axis, tiled=True)

    value_sum = summed(grad_value_weight, 1)
    key_sum = summed(grad_key_weight, 0)
    gate_sum = summed(grad_gate_weight, 0)
    grad_residual, grad_attn_all = run_exchange(
        mp_count,
        5,
        backward_rows,
        grad_hidden_low,
        residual.astype(bfloat),
        spread_row(vectors[12]),
        cotangent,
    )
    grad_out_weight = half_left(gated_low, grad_attn_all)
    out_sum = summed(grad_out_weight.astype(bfloat), 1)
    grad_gated = half_right(grad_attn_all, out_weight)
    grad_recept, grad_keys, grad_values, grad_gate_pre, grad_raw, grad_local, mixed = run_backward(
        dp_count,
        mp_count,
        grad_gated,
        wkv,
        states,
        kept,
        *branch,
        local_vectors,
        marks,
        tables,
        gated_sum.astype(bfloat),
        residual,
    )

    value_sum, key_sum, grad_raw = lax.optimization_barrier((value_sum, key_sum, grad_raw))
    grad_mix_weight = [
        half_left(inputs_low[number], value).astype(bfloat)
        for number, value in (
            (3, grad_recept),
            (1, grad_keys),
            (2, grad_values),
            (4, grad_gate_pre),
        )
    ]
    given = jnp.concatenate(
        [
            jnp.zeros((8, width), single),
            lax.dynamic_update_slice_in_dim(
                jnp.zeros((4, width), single), grad_local[:4], col_start, 1
            ),
            channel_sums[:4],
        ],
        0,
    )
    grad_hidden_one, grad_pack, first_row = run_mixing_backward(
        tokens_all,
        heads,
        keep_lanes,
        acts,
        grad_recept,
        grad_keys,
        grad_values,
        grad_gate_pre,
        grad_raw,
        small,
        vectors,
        up_own,
        mix_weight,
        given,
    )
    arriving_one = from_behind(first_row[:1], "dp", -1)
    grad_hidden_one = add_last(grad_hidden_one, arriving_one)

    grad_tokens, mix_sum, small_sum = run_end(
        dp_count,
        mp_count,
        grad_hidden_one,
        tokens,
        spread_row(vectors[0]),
        grad_residual,
        grad_mix_weight,
        grad_pack,
    )
    gate_sum, out_sum, mix_sum = lax.optimization_barrier((gate_sum, out_sum, mix_sum))
    return (
        mixed,
        grad_tokens,
        run_update(mix_state, mix_sum, width, total_tokens),
        run_update(out_state, out_sum, width, total_tokens),
        run_update(key_state, key_sum, width, total_tokens),
        run_update(value_state, value_sum, FF, total_tokens),
        run_update(gate_state, gate_sum, width, total_tokens),
        update(down_state, small_sum[:, :down_cols], width, total_tokens),
        update(up_state, small_sum[:, WINDOW : WINDOW + down_cols].T, TM_RANK, total_tokens),
        update(vector_state, small_sum[:, down_cols : down_cols + 16].T, 1, total_tokens),
    )


def solution(mesh):
    return jax.shard_map(
        body,
        mesh=mesh,
        in_specs=(
            P(("dp", "mp"), None),
            P(("dp", "mp"), None),
            P(),
            P(None, None, "dp", "mp"),
            P(None, "mp", "dp"),
            P(None, "dp", "mp"),
            P(None, "mp", "dp"),
            P(None, "dp", "mp"),
            P(None, ("dp", "mp"), None),
            P(None, None, ("dp", "mp")),
            P(None, None, ("dp", "mp")),
        ),
        out_specs=(
            P(("dp", "mp"), None),
            P(("dp", "mp"), None),
            P(None, None, "dp", "mp"),
            P(None, "mp", "dp"),
            P(None, "dp", "mp"),
            P(None, "mp", "dp"),
            P(None, "dp", "mp"),
            P(None, ("dp", "mp"), None),
            P(None, None, ("dp", "mp")),
            P(None, None, ("dp", "mp")),
        ),
        check_vma=False,
    )
```

```python
import functools

import jax
import jax.numpy as jnp
import numpy as np
from jax import lax
from jax.experimental import pallas as pl
from jax.experimental.pallas import tpu as pltpu
from jax.sharding import PartitionSpec as P

LANE_SPAN = 64
FF = 7168
TM_RANK = 32
DECAY_RANK = 64


momentum_rate = 0.9
average_rate = 0.9
norm_epsilon = 1e-05
group_epsilon = 0.00064
CHUNK = 128
LEVELS = 7
PAIR = 2 * LANE_SPAN
MESH = pl.DeviceIdType.MESH
PIECES = 2
WINDOW = 256
ROW_BLOCK = 256


def half_dot(left, right):
    return jnp.dot(left, right, preferred_element_type=jnp.float32)


def half_left(left, right):
    return lax.dot_general(
        left, right, (((0,), (0,)), ((), ())), preferred_element_type=jnp.float32
    )


def half_right(left, right):
    return lax.dot_general(
        left, right, (((1,), (1,)), ((), ())), preferred_element_type=jnp.float32
    )


def split_pair(value):
    upper_part = value.astype(jnp.bfloat16)
    lower_part = (value - upper_part.astype(jnp.float32)).astype(jnp.bfloat16)
    return (upper_part, lower_part)


def norm_forward(value, gain, bias, epsilon):
    centre = value - jnp.mean(value, -1, keepdims=True)
    inverse = lax.rsqrt(jnp.mean(centre * centre, -1, keepdims=True) + epsilon)
    normal_hat = centre * inverse
    return (normal_hat * gain + bias, normal_hat, inverse)


def norm_backward(grad_out, normal_hat, inverse, gain):
    scaled = grad_out * gain
    return inverse * (
        scaled
        - jnp.mean(scaled, -1, keepdims=True)
        - normal_hat * jnp.mean(scaled * normal_hat, -1, keepdims=True)
    )


def level_tables():
    row = np.arange(CHUNK)
    later, earlier = row[:, None], row[None, :]
    level = np.full((CHUNK, CHUNK), -1.0, np.float32)
    sums = []
    for bit in range(LEVELS):
        block = (later >> (bit + 1)) == (earlier >> (bit + 1))
        level[block & ((later >> bit) % 2 == 1) & ((earlier >> bit) % 2 == 0)] = bit
        middle = ((later >> (bit + 1)) << (bit + 1)) + (1 << bit)
        upper = (later >> bit) % 2 == 1
        between = np.where(
            upper, (earlier >= middle) & (earlier < later), (earlier > later) & (earlier < middle)
        )
        if bit:
            sums.append(between)
    sums += [earlier < later, earlier > later]
    sums = np.concatenate(sums, 0).astype(np.float32)
    return np.concatenate([level, level], 1), np.concatenate([sums, sums], 1), sums.T


def dot_nn(left, right):
    return lax.dot_general(
        left, right, (((1,), (0,)), ((), ())), preferred_element_type=jnp.float32
    )


def dot_nt(left, right):
    return lax.dot_general(
        left, right, (((1,), (1,)), ((), ())), preferred_element_type=jnp.float32
    )


def dot_tn(left, right):
    return lax.dot_general(
        left, right, (((0,), (0,)), ((), ())), preferred_element_type=jnp.float32
    )


def first_head(shape):
    return lax.broadcasted_iota(jnp.int32, shape, len(shape) - 1) < LANE_SPAN


def stack_heads(value):
    first = first_head(value.shape)
    none = jnp.zeros_like(value)
    return jnp.concatenate([jnp.where(first, value, none), jnp.where(first, none, value)], 0)


def merge_heads(value):
    half = value.shape[0] // 2
    return jnp.where(first_head((half, value.shape[1])), value[:half], value[half:])


def own_blocks(value):
    upper = lax.broadcasted_iota(jnp.int32, value.shape, 0) < LANE_SPAN
    return jnp.where(upper == first_head(value.shape), value, 0.0)


def head_mean(value):
    row = lax.broadcasted_iota(jnp.int32, (PAIR, PAIR), 0) < LANE_SPAN
    ones = jnp.where(row == first_head((PAIR, PAIR)), 1.0 / LANE_SPAN, 0.0).astype(jnp.bfloat16)
    upper, lower = split_pair(value)
    return dot_nn(upper, ones) + dot_nn(lower, ones)


def head_sum(value):
    return head_mean(value) * float(LANE_SPAN)


def exact_pieces(left, right, axis_left, axis_right):
    upper, lower = split_pair(left)
    right_upper, right_lower = split_pair(right)
    return (
        jnp.concatenate([upper, lower, upper], axis_left),
        jnp.concatenate([right_upper, right_upper, right_lower], axis_right),
    )


def exact_nn(left, right):
    return dot_nn(*exact_pieces(left, right, 1, 0))


def exact_nt(left, right):
    return dot_nt(*exact_pieces(left, right, 1, 1))


def exact_tn(left, right):
    return dot_tn(*exact_pieces(left, right, 0, 0))


def packed_state(state):
    return jnp.concatenate(split_pair(state[:LANE_SPAN] + state[LANE_SPAN:]), 0)


def unpacked_state(piece):
    piece = piece.astype(jnp.float32)
    return piece[:LANE_SPAN] + piece[LANE_SPAN:]


def rows_of(chunk):
    return pl.ds(pl.multiple_of(chunk * CHUNK, CHUNK), CHUNK)


def lanes_of(pair):
    return pl.ds(pl.multiple_of(pair * PAIR, PAIR), PAIR)


def marks_of(chunk):
    return pl.ds(pl.multiple_of(chunk * 8, 8), 8)


def greet(dp_count, mp_count):
    me, mine = lax.axis_index("dp"), lax.axis_index("mp")
    barrier = pltpu.get_barrier_semaphore()
    for step in range(1, dp_count):
        pl.semaphore_signal(
            barrier, inc=1, device_id=(lax.rem(me + step, dp_count), mine), device_id_type=MESH
        )
    for step in range(1, mp_count):
        pl.semaphore_signal(
            barrier, inc=1, device_id=(me, lax.rem(mine + step, mp_count)), device_id_type=MESH
        )
    pl.semaphore_wait(barrier, dp_count + mp_count - 2)


def swap_copies(count, source, target, send_sems, recv_sems):
    me, mine = lax.axis_index("dp"), lax.axis_index("mp")
    copies = []
    for step in range(1, count):
        other = lax.rem(mine + step, count)
        copies.append(
            pltpu.make_async_remote_copy(
                src_ref=source(other),
                dst_ref=target(mine),
                send_sem=send_sems.at[step - 1],
                recv_sem=recv_sems.at[step - 1],
                device_id=(me, other),
                device_id_type=MESH,
            )
        )
    return copies


def state_copies(other, me, sends, lands, send_sems, recv_sems, to):
    return [
        pltpu.make_async_remote_copy(
            src_ref=send,
            dst_ref=land.at[me],
            send_sem=send_sems.at[number, other],
            recv_sem=recv_sems.at[number, me],
            device_id=(to, lax.axis_index("mp")),
            device_id_type=MESH,
        )
        for number, (send, land) in enumerate(zip(sends, lands))
    ]


def send_states(count, sends, lands, send_sems, recv_sems, ahead):
    me = lax.axis_index("dp")
    for other in range(count):

        @pl.when((other > me) if ahead else (other < me))
        def _():
            for copy in state_copies(other, me, sends, lands, send_sems, recv_sems, other):
                copy.start()


def wait_states(count, sends, lands, send_sems, recv_sems, ahead):
    me = lax.axis_index("dp")
    for other in range(count):

        @pl.when((other > me) if ahead else (other < me))
        def _():
            for copy in state_copies(other, me, sends, lands, send_sems, recv_sems, other):
                copy.wait_send()

        @pl.when((other < me) if ahead else (other > me))
        def _():
            for copy in state_copies(other, other, sends, lands, send_sems, recv_sems, me):
                copy.wait_recv()


def decay_factors(fading, sums):
    upper, lower = split_pair(fading)
    return jnp.exp(dot_nn(sums, jnp.concatenate([upper, lower], 0)))


def table(at):
    return slice(at * CHUNK, (at + 1) * CHUNK)


def level_inputs(level, acceptor, lookup, factors):
    if level == 0:
        return None, acceptor, lookup
    factor = factors[table(level - 1), :]
    return factor, acceptor * factor, lookup * factor


def recurrence_forward(
    count, mp_count, chunks, pairs,
    rec, key, val, gpre, logw, vec, seg_col, seg_row, valid, ending, whole, level, sums, cotangent,
    gated, wkv, states, kept, columns,
    factors, pre_a, pre_b, start_b, send_a, send_b, land_a, land_b, send_sems, recv_sems,
    swap_send, swap_recv,
):
    bfloat = jnp.bfloat16
    greet(count, mp_count)
    mine, own_rows, features = lax.axis_index("mp"), cotangent.shape[0], columns.shape[1]

    def own_columns(other):
        return cotangent.at[:, pl.ds(pl.multiple_of(other * features, 128), features)]

    def landing(other):
        return columns.at[pl.ds(pl.multiple_of(other * own_rows, 16), own_rows)]

    swaps = swap_copies(mp_count, own_columns, landing, swap_send, swap_recv)
    for copy in swaps:
        copy.start()
    landing(mine)[...] = own_columns(mine)[...]

    def summary(pair, carry):
        lanes = lanes_of(pair)

        def step(chunk, before):
            before_a, before_b = before
            rows, slot = rows_of(chunk), pair * chunks + chunk
            fading = logw[rows, lanes]
            factor = decay_factors(fading, sums[...])
            factors[slot] = factor
            faded = key[rows, lanes] * factor[table(LEVELS)] * ending[rows, :]
            chunk_b = own_blocks(exact_tn(val[rows, lanes], faded))
            chunk_a = jnp.exp(jnp.sum(fading, 0, keepdims=True)) * whole[marks_of(chunk), :][:1]
            pre_a[slot] = jnp.broadcast_to(before_a, (8, PAIR))
            pre_b[slot] = before_b
            return before_a * chunk_a, before_b * chunk_a + chunk_b

        last_a, last_b = lax.fori_loop(
            0, chunks, step, (jnp.ones((1, PAIR), jnp.float32), jnp.zeros((PAIR, PAIR), jnp.float32))
        )
        send_a[:, lanes] = jnp.broadcast_to(last_a, (8, PAIR))
        send_b[:, lanes] = packed_state(last_b)
        return carry

    lax.fori_loop(0, pairs, summary, 0)
    exchange = (count, (send_a, send_b), (land_a, land_b), send_sems, recv_sems, True)
    send_states(*exchange)

    def inside(slot, carry):
        pair, chunk = slot // chunks, slot % chunks
        rows, lanes = rows_of(chunk), lanes_of(pair)
        acceptor, lookup, payload = rec[rows, lanes], key[rows, lanes], val[rows, lanes]
        place = jnp.where(seg_col[rows, :] == seg_row[marks_of(chunk), :][:1], level[...], -1.0)
        scores = jnp.zeros((CHUNK, 2 * CHUNK), jnp.float32)
        for at in range(LEVELS):
            _, left, right = level_inputs(at, acceptor, lookup, factors.at[slot])
            part = exact_nt(left, stack_heads(right))
            scores = jnp.where(place == float(at), part, scores)
        bonus = head_sum(acceptor * vec[0:1, lanes] * lookup) * payload
        wkv[rows, lanes] = bonus + exact_nn(scores, stack_heads(payload))
        kept[slot] = scores.astype(bfloat)
        return carry

    lax.fori_loop(0, pairs * chunks, inside, 0)
    wait_states(*exchange)
    start_b[...] = lax.fori_loop(
        0,
        lax.axis_index("dp"),
        lambda other, state: state * land_a[other][:1] + unpacked_state(land_b[other]),
        jnp.zeros(start_b.shape, jnp.float32),
    )

    def finish(slot, carry):
        pair, chunk = slot // chunks, slot % chunks
        rows, lanes = rows_of(chunk), lanes_of(pair)
        state = pre_b[slot] + pre_a[slot][:1] * stack_heads(start_b[:, lanes])
        states[slot] = state
        reader = rec[rows, lanes] * factors[slot, table(LEVELS - 1), :] * valid[rows, :]
        out = wkv[rows, lanes] + exact_nt(reader, state)
        wkv[rows, lanes] = out
        centre = out - head_mean(out)
        inverse = lax.rsqrt(head_mean(centre * centre) + group_epsilon)
        normed = centre * inverse * vec[1:2, lanes] + vec[2:3, lanes]
        pre = gpre[rows, lanes]
        gated[rows, lanes] = (normed * pre * jax.nn.sigmoid(pre)).astype(bfloat)
        return carry

    lax.fori_loop(0, pairs * chunks, finish, 0)
    for copy in swaps:
        copy.wait()


def recurrence_backward(
    count, mp_count, chunks, pairs,
    dgated, wkv, states, kept, rec, key, val, gpre, logw, vec, seg_col, seg_row, valid, ending, whole,
    level, sums, sums_back, change, residual,
    drec, dkey, dval, dgpre, draw, dvec, mixed,
    factors, local, end_b, dout, drec_part, dkey_part, dval_part, dlog_part, steps,
    send_a, send_b, land_a, land_b, send_sems, recv_sems,
    swapped, swap_send, swap_recv,
):
    bfloat = jnp.bfloat16
    greet(count, mp_count)
    mine, own_rows, features = lax.axis_index("mp"), residual.shape[0], change.shape[1]

    def rows_for(other):
        return change.at[pl.ds(pl.multiple_of(other * own_rows, 16), own_rows)]

    swaps = swap_copies(mp_count, rows_for, lambda other: swapped.at[other], swap_send, swap_recv)
    for copy in swaps:
        copy.start()
    swapped[mine] = rows_for(mine)[...]
    dvec[...] = jnp.zeros(dvec.shape, jnp.float32)

    def chunk_decay(chunk, lanes):
        fading = logw[rows_of(chunk), lanes]
        return jnp.exp(jnp.sum(fading, 0, keepdims=True)) * whole[marks_of(chunk), :][:1]

    def summary(pair, carry):
        lanes = lanes_of(pair)

        def step(back, after):
            after_a, after_b = after
            chunk = chunks - 1 - back
            rows, slot = rows_of(chunk), pair * chunks + chunk
            factor = decay_factors(logw[rows, lanes], sums[...])
            factors[slot] = factor
            out = wkv[rows, lanes]
            centre = out - head_mean(out)
            inverse = lax.rsqrt(head_mean(centre * centre) + group_epsilon)
            hat = centre * inverse
            gain = vec[1:2, lanes]
            normed = hat * gain + vec[2:3, lanes]
            pre = gpre[rows, lanes]
            sig = jax.nn.sigmoid(pre)
            grad = dgated[rows, lanes]
            grad_normed = grad * pre * sig
            dgpre[rows, lanes] = (grad * normed * sig * (1.0 + pre * (1.0 - sig))).astype(bfloat)
            dvec[2:3, lanes] += jnp.sum(grad_normed * hat, 0, keepdims=True)
            dvec[3:4, lanes] += jnp.sum(grad_normed, 0, keepdims=True)
            scaled = grad_normed * gain
            grad_out = inverse * (scaled - head_mean(scaled) - hat * head_mean(scaled * hat))
            dout[rows, lanes] = grad_out
            reader = rec[rows, lanes] * factor[table(LEVELS - 1)] * valid[rows, :]
            inner = own_blocks(exact_tn(grad_out, reader))
            local[slot] = inner
            chunk_a = chunk_decay(chunk, lanes)
            return after_a * chunk_a, after_b * chunk_a + inner

        last_a, last_b = lax.fori_loop(
            0, chunks, step, (jnp.ones((1, PAIR), jnp.float32), jnp.zeros((PAIR, PAIR), jnp.float32))
        )
        send_a[:, lanes] = jnp.broadcast_to(last_a, (8, PAIR))
        send_b[:, lanes] = packed_state(last_b)
        return carry

    lax.fori_loop(0, pairs, summary, 0)
    exchange = (count, (send_a, send_b), (land_a, land_b), send_sems, recv_sems, False)
    send_states(*exchange)

    def inside(slot, carry):
        pair, chunk = slot // chunks, slot % chunks
        rows, lanes = rows_of(chunk), lanes_of(pair)
        acceptor, lookup, payload = rec[rows, lanes], key[rows, lanes], val[rows, lanes]
        reward = vec[0:1, lanes]
        grad_exact = dout[rows, lanes]
        grad_out = grad_exact.astype(bfloat)
        place = jnp.where(seg_col[rows, :] == seg_row[marks_of(chunk), :][:1], level[...], -1.0)
        grad_scores = exact_nt(grad_exact, stack_heads(payload))
        grad_bonus = head_sum(grad_exact * payload)
        dvec[1:2, lanes] += jnp.sum(acceptor * lookup * grad_bonus, 0, keepdims=True)
        grad_acceptor = reward * lookup * grad_bonus
        grad_lookup = reward * acceptor * grad_bonus
        for at in range(LEVELS):
            factor, left, right = level_inputs(at, acceptor, lookup, factors.at[slot])
            left_low, right_low = left.astype(bfloat), stack_heads(right.astype(bfloat))
            here = place == float(at)
            grad_part = jnp.where(here, grad_scores, 0.0).astype(bfloat)
            grad_left = dot_nn(grad_part, right_low)
            grad_right = merge_heads(dot_tn(grad_part, left_low))
            if at:
                grad_left = grad_left * factor
                grad_right = grad_right * factor
                steps[table(at - 1), :] = acceptor * grad_left + lookup * grad_right
            grad_acceptor += grad_left
            grad_lookup += grad_right
        drec_part[rows, lanes] = grad_acceptor
        dkey_part[rows, lanes] = grad_lookup
        bonus = head_sum(acceptor * reward * lookup)
        dval_part[rows, lanes] = bonus * grad_exact + merge_heads(
            dot_tn(kept[slot], grad_out)
        )
        inner = (LEVELS - 1) * CHUNK
        dlog_part[rows, lanes] = dot_nn(sums_back[:, :inner], steps[...].astype(bfloat))
        return carry

    lax.fori_loop(0, pairs * chunks, inside, 0)
    wait_states(*exchange)
    me = lax.axis_index("dp")

    def later(step, state):
        other = count - 1 - step
        return state * land_a[other][:1] + unpacked_state(land_b[other])

    end_b[...] = lax.fori_loop(0, count - 1 - me, later, jnp.zeros(end_b.shape, jnp.float32))

    def finish(pair, carry):
        lanes = lanes_of(pair)

        def step(back, after):
            chunk = chunks - 1 - back
            rows, slot = rows_of(chunk), pair * chunks + chunk
            state = states[slot]
            after_low = after.astype(bfloat)
            reach = factors[slot, table(LEVELS - 1), :] * valid[rows, :]
            tail = factors[slot, table(LEVELS), :] * ending[rows, :]
            acceptor, lookup = rec[rows, lanes], key[rows, lanes]
            grad_reader = exact_nn(dout[rows, lanes], state) * reach
            grad_faded = exact_nn(val[rows, lanes], after) * tail
            faded = (lookup * tail).astype(bfloat)
            chunk_a = chunk_decay(chunk, lanes)
            total = chunk_a * jnp.sum(after * state, 0, keepdims=True)
            drec[rows, lanes] = (drec_part[rows, lanes] + grad_reader).astype(bfloat)
            dkey[rows, lanes] = (dkey_part[rows, lanes] + grad_faded).astype(bfloat)
            dval[rows, lanes] = (dval_part[rows, lanes] + dot_nt(faded, after_low)).astype(bfloat)
            inner = (LEVELS - 1) * CHUNK
            moves = jnp.concatenate([acceptor * grad_reader, lookup * grad_faded], 0)
            grad_log = dlog_part[rows, lanes] + total + dot_nn(
                sums_back[:, inner:], moves.astype(bfloat)
            )
            raw = grad_log * logw[rows, lanes]
            draw[rows, lanes] = raw
            dvec[0:1, lanes] += jnp.sum(raw, 0, keepdims=True)
            return after * chunk_a + local[slot]

        lax.fori_loop(0, chunks, step, stack_heads(end_b[:, lanes]))
        return carry

    lax.fori_loop(0, pairs, finish, 0)
    for copy in swaps:
        copy.wait()
    for other in range(mp_count):
        lanes = slice(other * features, (other + 1) * features)
        mixed[:, lanes] = (residual[:, lanes] + swapped[other].astype(jnp.float32)).astype(bfloat)


def exchange_scratch(count, features):
    return [
        pltpu.VMEM((8, features), jnp.float32),
        pltpu.VMEM((2 * LANE_SPAN, features), jnp.bfloat16),
        pltpu.VMEM((count, 8, features), jnp.float32),
        pltpu.VMEM((count, 2 * LANE_SPAN, features), jnp.bfloat16),
        pltpu.SemaphoreType.DMA((2, count)),
        pltpu.SemaphoreType.DMA((2, count)),
    ]


def run_forward(count, mp_count, rec, key, val, gpre, logw, vec, marks, tables, cotangent):
    rows, features = rec.shape
    chunks, pairs = rows // CHUNK, features // PAIR
    slots = chunks * pairs
    whole_array = pl.BlockSpec(memory_space=pltpu.VMEM)
    level, sums, _ = tables
    return pl.pallas_call(
        functools.partial(recurrence_forward, count, mp_count, chunks, pairs),
        out_shape=(
            jax.ShapeDtypeStruct((rows, features), jnp.bfloat16),
            jax.ShapeDtypeStruct((rows, features), jnp.float32),
            jax.ShapeDtypeStruct((slots, PAIR, PAIR), jnp.float32),
            jax.ShapeDtypeStruct((slots, CHUNK, 2 * CHUNK), jnp.bfloat16),
            jax.ShapeDtypeStruct((rows, features), jnp.bfloat16),
        ),
        in_specs=[whole_array] * 14,
        out_specs=(whole_array,) * 5,
        scratch_shapes=[
            pltpu.VMEM((slots, sums.shape[0], PAIR), jnp.float32),
            pltpu.VMEM((slots, 8, PAIR), jnp.float32),
            pltpu.VMEM((slots, PAIR, PAIR), jnp.float32),
            pltpu.VMEM((LANE_SPAN, features), jnp.float32),
        ]
        + exchange_scratch(count, features)
        + [
            pltpu.SemaphoreType.DMA((mp_count - 1,)),
            pltpu.SemaphoreType.DMA((mp_count - 1,)),
        ],
        compiler_params=pltpu.CompilerParams(
            collective_id=1, has_side_effects=True, vmem_limit_bytes=48 << 20
        ),
        name="recurrence_forward",
    )(rec, key, val, gpre, logw, vec, *marks, level, sums, cotangent)


def run_backward(
    count, mp_count, dgated, wkv, states, kept, rec, key, val, gpre, logw, vec, marks, tables,
    change, residual,
):
    rows, features = rec.shape
    chunks, pairs = rows // CHUNK, features // PAIR
    slots = chunks * pairs
    whole_array = pl.BlockSpec(memory_space=pltpu.VMEM)
    level, sums, sums_back = tables
    low = jax.ShapeDtypeStruct((rows, features), jnp.bfloat16)
    full = pltpu.VMEM((rows, features), jnp.float32)
    return pl.pallas_call(
        functools.partial(recurrence_backward, count, mp_count, chunks, pairs),
        out_shape=(
            low,
            low,
            low,
            low,
            jax.ShapeDtypeStruct((rows, features), jnp.float32),
            jax.ShapeDtypeStruct((8, features), jnp.float32),
            jax.ShapeDtypeStruct(residual.shape, jnp.bfloat16),
        ),
        in_specs=[whole_array] * 20,
        out_specs=(whole_array,) * 7,
        scratch_shapes=[
            pltpu.VMEM((slots, sums.shape[0], PAIR), jnp.float32),
            pltpu.VMEM((slots, PAIR, PAIR), jnp.float32),
            pltpu.VMEM((LANE_SPAN, features), jnp.float32),
            full,
            full,
            full,
            full,
            full,
            pltpu.VMEM(((LEVELS - 1) * CHUNK, PAIR), jnp.float32),
        ]
        + exchange_scratch(count, features)
        + [pltpu.VMEM((mp_count,) + residual.shape[:1] + (features,), jnp.bfloat16)]
        + [
            pltpu.SemaphoreType.DMA((mp_count - 1,)),
            pltpu.SemaphoreType.DMA((mp_count - 1,)),
        ],
        compiler_params=pltpu.CompilerParams(
            collective_id=2, has_side_effects=True, vmem_limit_bytes=52 << 20
        ),
        name="recurrence_backward",
    )(
        dgated, wkv, states, kept, rec, key, val, gpre, logw, vec, *marks, level, sums, sums_back,
        change, residual,
    )


def flipped(index, mask):
    for bit in range(mask.bit_length()):
        size = 1 << bit
        if mask & size:
            index = index + size - 2 * size * lax.rem(index // size, 2)
    return index


def masks_over(bits):
    masks = [0]
    for bit in bits:
        masks = masks + [mask | (1 << bit) for mask in masks]
    return masks


def paths(count):
    higher = list(range(1, count.bit_length() - 1))
    return higher + [0], higher[::-1] + [0]


def remote(source, target, send_sem, recv_sem, dp, mp):
    return pltpu.make_async_remote_copy(
        src_ref=source,
        dst_ref=target,
        send_sem=send_sem,
        recv_sem=recv_sem,
        device_id=(dp, mp),
        device_id_type=MESH,
    )


def greet_all(partners, some=()):
    barrier = pltpu.get_barrier_semaphore()
    count = len(partners)
    for dp, mp in partners:
        pl.semaphore_signal(barrier, inc=1, device_id=(dp, mp), device_id_type=MESH)
    for present, dp, mp in some:

        @pl.when(present)
        def _():
            pl.semaphore_signal(barrier, inc=1, device_id=(dp, mp), device_id_type=MESH)

        count = count + jnp.where(present, 1, 0)
    pl.semaphore_wait(barrier, count)


class Halo:
    def __init__(self, dp_count, mp_count, send_sems, recv_sem):
        self.dp, self.mp = lax.axis_index("dp"), lax.axis_index("mp")
        self.count, self.lines = dp_count, mp_count
        self.send_sems, self.recv_sem = send_sems, recv_sem
        self.after = lax.rem(self.dp + 1, dp_count)
        self.previous = lax.rem(self.dp + dp_count - 1, dp_count)
        self.takes = self.dp > 0
        self.gives = jnp.logical_and(self.mp == mp_count - 1, self.dp < dp_count - 1)

    def partners(self):
        return [(self.takes, self.previous, self.lines - 1)] + [
            (self.gives, self.after, line) for line in range(self.lines)
        ]

    def copy(self, source, target, line):
        return remote(source, target, self.send_sems.at[line], self.recv_sem, self.after, line)

    def start(self, source, target):
        @pl.when(self.dp == 0)
        def _():
            target[...] = jnp.zeros(target.shape, target.dtype)

        @pl.when(self.gives)
        def _():
            for line in range(self.lines):
                self.copy(source, target, line).start()

    def finish(self, source, target):
        @pl.when(self.takes)
        def _():
            self.copy(source, target, 0).wait_recv()

        @pl.when(self.gives)
        def _():
            for line in range(self.lines):
                self.copy(source, target, line).wait_send()


class Arrival:
    def __init__(self, dp_count, send_sem, recv_sem):
        self.dp, self.mp = lax.axis_index("dp"), lax.axis_index("mp")
        self.send_sem, self.recv_sem = send_sem, recv_sem
        self.after = lax.rem(self.dp + 1, dp_count)
        self.previous = lax.rem(self.dp + dp_count - 1, dp_count)
        self.gives, self.takes = self.dp > 0, self.dp < dp_count - 1

    def partners(self):
        return [(self.gives, self.previous, self.mp), (self.takes, self.after, self.mp)]

    def copy(self, row, land):
        return remote(row, land, self.send_sem, self.recv_sem, self.previous, self.mp)

    def start(self, row, land):
        @pl.when(self.gives)
        def _():
            self.copy(row, land).start()

        @pl.when(jnp.logical_not(self.takes))
        def _():
            land[...] = jnp.zeros(land.shape, land.dtype)

    def wait(self, row, land):
        @pl.when(self.takes)
        def _():
            self.copy(row, land).wait_recv()

    def finish(self, row, land):
        @pl.when(self.gives)
        def _():
            self.copy(row, land).wait_send()


def line_partners(count):
    dp, mp = lax.axis_index("dp"), lax.axis_index("mp")
    return [(dp, lax.rem(mp + step, count)) for step in sorted({1, count - 1})]


def cube_partners(count):
    dp, mp = lax.axis_index("dp"), lax.axis_index("mp")
    return [(flipped(dp, 1 << bit), mp) for bit in range(count.bit_length() - 1)]


class Line:
    def __init__(self, count, rows, send_sems, recv_sems):
        self.count, self.rows = count, rows
        self.send_sems, self.recv_sems = send_sems, recv_sems
        self.dp, self.me = lax.axis_index("dp"), lax.axis_index("mp")
        self.piece = rows // PIECES

    def at(self, block, piece):
        return pl.ds(pl.multiple_of(block * self.rows + piece * self.piece, 16), self.piece)

    def copy(self, source, target, right, slot, piece):
        side = 0 if right else 1
        return remote(
            source,
            target,
            self.send_sems.at[side, slot, piece],
            self.recv_sems.at[side, slot, piece],
            self.dp,
            lax.rem(self.me + (1 if right else self.count - 1), self.count),
        )


class LineGather(Line):
    def hop(self, target, distance, piece, right):
        block = self.me - distance if right else self.me + distance
        ref = target.at[self.at(block, piece)]
        return self.copy(ref, ref, right, distance, piece)

    def holds(self, distance, right):
        return self.me >= distance if right else self.me + distance < self.count

    def passes(self, distance, right):
        onward = self.me < self.count - 1 if right else self.me > 0
        return jnp.logical_and(self.holds(distance, right), onward)

    def send(self, target, distance, piece):
        for right in (True, False):
            if distance:

                @pl.when(self.holds(distance, right))
                def _():
                    block = self.me - distance if right else self.me + distance
                    ref = target.at[self.at(block, piece)]
                    self.copy(ref, ref, right, distance - 1, piece).wait_recv()

            if distance < self.count - 1:

                @pl.when(self.passes(distance, right))
                def _():
                    self.hop(target, distance, piece, right).start()

    def finish(self, target):
        for distance in range(self.count - 1):
            for piece in range(PIECES):
                for right in (True, False):

                    @pl.when(self.passes(distance, right))
                    def _():
                        self.hop(target, distance, piece, right).wait_send()


class LineSum(Line):
    def hop(self, source, land, block, piece, right):
        return self.copy(
            source.at[self.at(block, piece)],
            land.at[0 if right else 1, self.at(block, piece)],
            right,
            block,
            piece,
        )

    def own(self, part, extra, block, piece):
        value = part[self.at(block, piece)].astype(jnp.float32)
        if extra is not None and piece == PIECES - 1:
            row = lax.broadcasted_iota(jnp.int32, value.shape, 0)
            last = jnp.logical_and(row == self.piece - 1, block == self.count - 1)
            value = value + jnp.where(last, extra[:1], 0.0)
        return value

    def begin(self, part, extra, moving, land, number, ready=None):
        for piece in range(PIECES):
            if ready is not None and piece == PIECES - 1:
                ready()
            for right in (True, False):
                block = self.count - 1 - number if right else number
                at = self.at(block, piece)

                @pl.when(self.me == (0 if right else self.count - 1))
                def _():
                    moving[at] = self.own(part, extra, block, piece).astype(jnp.bfloat16)
                    if number:
                        before = block + 1 if right else block - 1
                        self.hop(moving, land, before, piece, right).wait_send()
                    self.hop(moving, land, block, piece, right).start()

    def forward(self, part, extra, moving, land, block, piece, right):
        side = 0 if right else 1
        at = self.at(block, piece)
        inside = jnp.logical_and(self.me > 0, self.me < self.count - 1)

        @pl.when(jnp.logical_and(inside, self.me < block if right else self.me > block))
        def _():
            self.hop(moving, land, block, piece, right).wait_recv()
            moving[at] = (
                self.own(part, extra, block, piece) + land[side, at].astype(jnp.float32)
            ).astype(jnp.bfloat16)
            self.hop(moving, land, block, piece, right).start()

    def step(self, part, extra, moving, land, number):
        for piece in range(PIECES):
            self.forward(part, extra, moving, land, self.count - 1 - number, piece, True)
            self.forward(part, extra, moving, land, number, piece, False)

    def total(self, part, extra, moving, land, total, piece):
        at = self.at(self.me, piece)
        own = slice(piece * self.piece, (piece + 1) * self.piece)
        total[own] = self.own(part, extra, self.me, piece)
        for right in (True, False):

            @pl.when(self.me > 0 if right else self.me < self.count - 1)
            def _():
                self.hop(moving, land, self.me, piece, right).wait_recv()
                total[own] += land[0 if right else 1, at].astype(jnp.float32)

        return own

    def finish(self, moving, land):
        inside = jnp.logical_and(self.me > 0, self.me < self.count - 1)
        for number in range(self.count - 1):
            for piece in range(PIECES):
                for right in (True, False):
                    block = self.count - 1 - number if right else number
                    sent = jnp.logical_and(inside, self.me < block if right else self.me > block)
                    if number == self.count - 2:
                        sent = jnp.logical_or(sent, self.me == (0 if right else self.count - 1))

                    @pl.when(sent)
                    def _():
                        self.hop(moving, land, block, piece, right).wait_send()


class Cube:
    def __init__(self, count, send_sems, recv_sems):
        self.count, self.send_sems, self.recv_sems = count, send_sems, recv_sems
        self.dp, self.mp = lax.axis_index("dp"), lax.axis_index("mp")
        self.stages = count.bit_length() - 1

    def copy(self, source, target, unit, mask, bit):
        return remote(
            source,
            target,
            self.send_sems.at[unit, mask],
            self.recv_sems.at[unit, mask],
            flipped(self.dp, 1 << bit),
            self.mp,
        )


class CubeGather(Cube):
    def stage(self, unit, path, view, stage):
        order = paths(self.count)[path]
        if stage:
            for mask in masks_over(order[: stage - 1]):
                got = mask | (1 << order[stage - 1])
                ref = view(flipped(self.dp, got))
                self.copy(ref, ref, unit, got, order[stage - 1]).wait_recv()
        if stage < self.stages:
            for mask in masks_over(order[:stage]):
                ref = view(flipped(self.dp, mask))
                self.copy(ref, ref, unit, mask | (1 << order[stage]), order[stage]).start()

    def finish(self, unit, path, view):
        order = paths(self.count)[path]
        for stage in range(self.stages):
            for mask in masks_over(order[:stage]):
                ref = view(flipped(self.dp, mask))
                self.copy(ref, ref, unit, mask | (1 << order[stage]), order[stage]).wait_send()


class CubeSum(Cube):
    def slot(self, order, stage, mask):
        base = self.count - (self.count >> stage)
        return base + masks_over(order[stage + 1 :]).index(mask)

    def source(self, unit, order, view, land, stage, mask):
        if stage == 0:
            return view(flipped(self.dp, mask))
        return land.at[self.slot(order, stage - 1, mask)]

    def sends(self, unit, path, view, land, stage):
        order = paths(self.count)[path][::-1]
        bit = order[stage]
        return [
            self.copy(
                self.source(unit, order, view, land, stage, mask | (1 << bit)),
                land.at[self.slot(order, stage, mask)],
                unit,
                mask | (1 << bit),
                bit,
            )
            for mask in masks_over(order[stage + 1 :])
        ]

    def start(self, unit, path, view, land, stage):
        for copy in self.sends(unit, path, view, land, stage):
            copy.start()

    def absorb(self, unit, path, view, land, stage, out=None):
        order = paths(self.count)[path][::-1]
        for copy, mask in zip(
            self.sends(unit, path, view, land, stage), masks_over(order[stage + 1 :])
        ):
            copy.wait_recv()
            before = self.source(unit, order, view, land, stage, mask)
            here = land.at[self.slot(order, stage, mask)]
            step = 16

            def add(number, carry):
                at = pl.ds(pl.multiple_of(number * step, step), step)
                both = before[at].astype(jnp.float32) + here[at].astype(jnp.float32)
                if out is None:
                    here[at] = both.astype(jnp.bfloat16)
                else:
                    out[at] = both
                return carry

            lax.fori_loop(0, here.shape[0] // step, add, 0)

    def finish(self, unit, path, view, land):
        for stage in range(self.stages):
            for copy in self.sends(unit, path, view, land, stage):
                copy.wait_send()


def line_sems(count):
    return [pltpu.SemaphoreType.DMA((2, count, PIECES)), pltpu.SemaphoreType.DMA((2, count, PIECES))]


def cube_sems(units, count):
    return [pltpu.SemaphoreType.DMA((units, count)), pltpu.SemaphoreType.DMA((units, count))]


def start_kernel(
    dp_count, mp_count, tokens, pack, mix_state, out_state, gate_state, key_state, value_state,
    tokens_all, small, mix_all, out_low, gate_low, key_low, value_low, before,
    mix, mix_full, out_full, gate_full, key_full, value_full,
    load_sems, own_sems, line_send, line_recv, pack_send, pack_recv, cube_send, cube_recv,
    halo_send, halo_recv,
):
    dp, mp = lax.axis_index("dp"), lax.axis_index("mp")
    rows = tokens.shape[0]
    halo = Halo(dp_count, mp_count, halo_send, halo_recv)
    edge = tokens.at[pl.ds(rows - 16, 16)]
    matrices, block = mix.shape[0], mix.shape[1]
    pack_rows, group = pack.shape[0], pack.shape[0] * mp_count
    half = group // 2
    states = (mix_state, out_state, gate_state, key_state, value_state)
    fulls = (mix_full, out_full, gate_full, key_full, value_full)
    loads = [
        pltpu.make_async_copy(state.at[0], full, load_sems.at[number])
        for number, (state, full) in enumerate(zip(states, fulls))
    ]
    for load in loads:
        load.start()
    others = [lax.rem(mp + step, mp_count) for step in range(1, mp_count)]
    greet_all([(dp, other) for other in others] + cube_partners(dp_count), halo.partners())
    halo.start(edge, before)
    line = LineGather(mp_count, rows, line_send, line_recv)
    cube = CubeGather(dp_count, cube_send, cube_recv)

    pack_at = small.at[pl.ds(pl.multiple_of(dp * group + mp * pack_rows, 16), pack_rows)]
    own = [
        pltpu.make_async_copy(pack, pack_at, own_sems.at[0]),
        pltpu.make_async_copy(
            tokens, tokens_all.at[pl.ds(pl.multiple_of(mp * rows, 16), rows)], own_sems.at[1]
        ),
    ]
    pack_copies = [
        remote(pack, pack_at, pack_send.at[step], pack_recv.at[step], dp, other)
        for step, other in enumerate(others)
    ]
    for copy in pack_copies + own:
        copy.start()
    loads[0].wait()
    for number in range(matrices):
        mix[number] = mix_full[number].astype(jnp.bfloat16)
    own_mix = [
        pltpu.make_async_copy(
            mix.at[number],
            mix_all.at[number, pl.ds(pl.multiple_of(dp * block, 16), block)],
            own_sems.at[2 + number],
        )
        for number in range(matrices)
    ]
    for copy in own_mix:
        copy.start()

    def small_view(part):
        def view(index):
            return small.at[pl.ds(pl.multiple_of(index * group + part * half, 16), half)]

        return view

    def mix_view(number):
        def view(index):
            return mix_all.at[number, pl.ds(pl.multiple_of(index * block, 16), block)]

        return view

    mix_units = [
        (2 + number, 0 if 2 * number < matrices else 1, mix_view(number))
        for number in range(matrices)
    ]
    small_units = [(part, part, small_view(part)) for part in range(2)]
    for copy in own + own_mix:
        copy.wait()
    for unit in mix_units:
        cube.stage(*unit, 0)
    for piece in range(PIECES):
        line.send(tokens_all, 0, piece)
    for load, full, low in zip(loads[1:], fulls[1:], (out_low, gate_low, key_low, value_low)):
        load.wait()
        step = 64

        def convert(number, carry):
            at = pl.ds(pl.multiple_of(number * step, step), step)
            low[at] = full[at].astype(jnp.bfloat16)
            return carry

        lax.fori_loop(0, full.shape[0] // step, convert, 0)
    for copy in pack_copies:
        copy.wait()
    for unit in small_units:
        cube.stage(*unit, 0)
    for distance in range(1, mp_count):
        for piece in range(PIECES):
            line.send(tokens_all, distance, piece)
        if distance < dp_count.bit_length() - 1:
            for unit in mix_units + small_units:
                cube.stage(*unit, distance)
    for stage in range(min(mp_count, dp_count.bit_length() - 1), dp_count.bit_length()):
        for unit in mix_units + small_units:
            cube.stage(*unit, stage)
    line.finish(tokens_all)
    halo.finish(edge, before)
    for unit in mix_units + small_units:
        cube.finish(*unit)


def run_start(dp_count, mp_count, tokens, pack, states):
    rows, width = tokens.shape
    matrices, block, features = states[0].shape[1:]
    anywhere = pl.BlockSpec(memory_space=pl.ANY)
    vmem = pl.BlockSpec(memory_space=pltpu.VMEM)
    bfloat = jnp.bfloat16
    return pl.pallas_call(
        functools.partial(start_kernel, dp_count, mp_count),
        out_shape=(
            jax.ShapeDtypeStruct((rows * mp_count, width), bfloat),
            jax.ShapeDtypeStruct((pack.shape[0] * mp_count * dp_count, pack.shape[1]), bfloat),
            jax.ShapeDtypeStruct((matrices, block * dp_count, features), bfloat),
            *[jax.ShapeDtypeStruct(state.shape[1:], bfloat) for state in states[1:]],
            jax.ShapeDtypeStruct((16, width), bfloat),
        ),
        in_specs=[vmem, vmem] + [anywhere] * 5,
        out_specs=(anywhere,) * 3 + (vmem,) * 5,
        scratch_shapes=[
            pltpu.VMEM(states[0].shape[1:], bfloat),
            *[pltpu.VMEM(state.shape[1:], jnp.float32) for state in states],
            pltpu.SemaphoreType.DMA((5,)),
            pltpu.SemaphoreType.DMA((2 + matrices,)),
            *line_sems(mp_count),
            pltpu.SemaphoreType.DMA((mp_count - 1,)),
            pltpu.SemaphoreType.DMA((mp_count - 1,)),
            *cube_sems(2 + matrices, dp_count),
            pltpu.SemaphoreType.DMA((mp_count,)),
            pltpu.SemaphoreType.DMA,
        ],
        compiler_params=pltpu.CompilerParams(
            collective_id=3, has_side_effects=True, vmem_limit_bytes=60 << 20
        ),
        name="gather_start",
    )(tokens, pack, *states)


def residual_rows(total, rows, tokens):
    return total + tokens[rows].astype(jnp.float32)


def backward_rows(total, rows, source, gain, skip):
    value = source[rows].astype(jnp.float32)
    centre = value - jnp.mean(value, -1, keepdims=True)
    inverse = lax.rsqrt(jnp.mean(centre * centre, -1, keepdims=True) + norm_epsilon)
    return skip[rows].astype(jnp.float32) + norm_backward(total, centre * inverse, inverse, gain[:1])


def exchange_kernel(dp_count, count, epilogue, forward, extras, part, *refs):
    extra, refs = refs[:extras], refs[extras:]
    own, gathered = refs[:2]
    moving, land, total, edge, sum_send, sum_recv, line_send, line_recv, row_send, row_recv = refs[-10:]
    rows = own.shape[0]
    if forward:
        halo = Halo(dp_count, count, row_send, row_recv)
        before, first, ready = refs[2], None, None
        greet_all(line_partners(count), halo.partners())
        edge_at = gathered.at[pl.ds(count * rows - 16, 16)]
    else:
        arrival = Arrival(dp_count, row_send.at[0], row_recv)
        first, extra = extra[0], extra[1:]
        greet_all(line_partners(count), arrival.partners())
        arrival.start(first, edge)
        ready = lambda: arrival.wait(first, edge)
    arriving = None if forward else edge
    adder = LineSum(count, rows, sum_send, sum_recv)
    line = LineGather(count, rows, line_send, line_recv)
    for number in range(count - 1):
        adder.begin(part, arriving, moving, land, number, None if number else ready)
        adder.step(part, arriving, moving, land, number)
    for piece in range(PIECES):
        at = adder.total(part, arriving, moving, land, total, piece)
        value = epilogue(total[at], at, *extra)
        own[at] = value
        gathered[line.at(line.me, piece)] = value.astype(jnp.bfloat16)
        line.send(gathered, 0, piece)
    if forward:
        halo.start(edge_at, before)
    for distance in range(1, count):
        for piece in range(PIECES):
            line.send(gathered, distance, piece)
    adder.finish(moving, land)
    line.finish(gathered)
    if forward:
        halo.finish(edge_at, before)
    else:
        arrival.finish(first, edge)


def run_exchange(dp_count, count, number, epilogue, forward, part, *extra):
    rows, width = part.shape[0] // count, part.shape[1]
    vmem = pl.BlockSpec(memory_space=pltpu.VMEM)
    out_shape = [
        jax.ShapeDtypeStruct((rows, width), jnp.float32),
        jax.ShapeDtypeStruct(part.shape, jnp.bfloat16),
    ]
    if forward:
        out_shape.append(jax.ShapeDtypeStruct((16, width), jnp.bfloat16))
    return pl.pallas_call(
        functools.partial(exchange_kernel, dp_count, count, epilogue, forward, len(extra)),
        out_shape=out_shape,
        in_specs=[vmem] * (1 + len(extra)),
        out_specs=[vmem] * len(out_shape),
        scratch_shapes=[
            pltpu.VMEM(part.shape, jnp.bfloat16),
            pltpu.VMEM((2,) + part.shape, jnp.bfloat16),
            pltpu.VMEM((rows, width), jnp.float32),
            pltpu.VMEM((8, width), jnp.float32),
            *line_sems(count),
            *line_sems(count),
            pltpu.SemaphoreType.DMA((count,)),
            pltpu.SemaphoreType.DMA,
        ],
        compiler_params=pltpu.CompilerParams(
            collective_id=number, has_side_effects=True, vmem_limit_bytes=40 << 20
        ),
        name="sum_and_gather",
    )(part, *extra)


def end_kernel(
    dp_count, mp_count, part, first, source, gain, skip, mix_a, mix_b, mix_c, mix_d, pack,
    own, mix_sum, pack_sum,
    moving, land, total, mix_land, pack_land, pack_own, pack_out, small_land,
    edge, sum_send, sum_recv, cube_send, cube_recv, small_send, small_recv, row_send, row_recv,
):
    dp, mp = lax.axis_index("dp"), lax.axis_index("mp")
    mix = (mix_a, mix_b, mix_c, mix_d)
    rows, matrices = own.shape[0], len(mix)
    block, group = mix_sum.shape[1], pack_own.shape[0]
    half, pack_rows = group // 2, pack_sum.shape[0]
    others = [lax.rem(mp + step, mp_count) for step in range(1, mp_count)]
    arrival = Arrival(dp_count, row_send, row_recv)
    greet_all([(dp, other) for other in others] + cube_partners(dp_count), arrival.partners())
    arrival.start(first, edge)
    adder = LineSum(mp_count, rows, sum_send, sum_recv)
    cube = CubeSum(dp_count, cube_send, cube_recv)

    def mix_view(number):
        def view(index):
            return mix[number].at[pl.ds(pl.multiple_of(index * block, 16), block)]

        return view

    def pack_view(side):
        def view(index):
            return pack.at[pl.ds(pl.multiple_of(index * group + side * half, 16), half)]

        return view

    units = [(side, side, pack_view(side), pack_land.at[side]) for side in range(2)] + [
        (2 + number, 0 if 2 * number < matrices else 1, mix_view(number), mix_land.at[number])
        for number in range(matrices)
    ]
    outs = [pack_own.at[pl.ds(side * half, half)] for side in range(2)] + [
        mix_sum.at[number] for number in range(matrices)
    ]
    for unit in units:
        cube.start(*unit, 0)
    adder.begin(part, edge, moving, land, 0, lambda: arrival.wait(first, edge))
    last = cube.stages - 1
    for unit in units:
        cube.absorb(*unit, 0)
        cube.start(*unit, 1)
    for number in range(1, mp_count - 1):
        adder.begin(part, edge, moving, land, number)
        adder.step(part, edge, moving, land, number - 1)
    adder.step(part, edge, moving, land, mp_count - 2)
    for piece in range(PIECES):
        at = adder.total(part, edge, moving, land, total, piece)
        own[at] = backward_rows(total[at], at, source, gain, skip)
    for stage in range(1, last):
        for unit in units:
            cube.absorb(*unit, stage)
            cube.start(*unit, stage + 1)
    for unit, out in zip(units[:2], outs[:2]):
        cube.absorb(*unit, last, out)
    pack_out[...] = pack_own[...].astype(jnp.bfloat16)
    small_copies = [
        remote(
            pack_out.at[pl.ds(pl.multiple_of(other * pack_rows, 16), pack_rows)],
            small_land.at[step],
            small_send.at[step],
            small_recv.at[step],
            dp,
            other,
        )
        for step, other in enumerate(others)
    ]
    for copy in small_copies:
        copy.start()
    for unit, out in zip(units[2:], outs[2:]):
        cube.absorb(*unit, last, out)
    pack_sum[...] = pack_own[pl.ds(pl.multiple_of(mp * pack_rows, 16), pack_rows), :]
    for step, copy in enumerate(small_copies):
        copy.wait()
        pack_sum[...] += small_land[step].astype(jnp.float32)
    adder.finish(moving, land)
    arrival.finish(first, edge)
    for unit in units:
        cube.finish(*unit)


def run_end(dp_count, mp_count, part, first, source, gain, skip, mix, pack):
    rows, width = source.shape
    matrices, features = len(mix), mix[0].shape[1]
    block, group = mix[0].shape[0] // dp_count, pack.shape[0] // dp_count
    lanes = pack.shape[1]
    vmem = pl.BlockSpec(memory_space=pltpu.VMEM)
    return pl.pallas_call(
        functools.partial(end_kernel, dp_count, mp_count),
        out_shape=(
            jax.ShapeDtypeStruct((rows, width), jnp.float32),
            jax.ShapeDtypeStruct((matrices, block, features), jnp.float32),
            jax.ShapeDtypeStruct((group // mp_count, lanes), jnp.float32),
        ),
        in_specs=[vmem] * 10,
        out_specs=(vmem,) * 3,
        scratch_shapes=[
            pltpu.VMEM(part.shape, jnp.bfloat16),
            pltpu.VMEM((2,) + part.shape, jnp.bfloat16),
            pltpu.VMEM((rows, width), jnp.float32),
            pltpu.VMEM((matrices, dp_count - 1, block, features), jnp.bfloat16),
            pltpu.VMEM((2, dp_count - 1, group // 2, lanes), jnp.bfloat16),
            pltpu.VMEM((group, lanes), jnp.float32),
            pltpu.VMEM((group, lanes), jnp.bfloat16),
            pltpu.VMEM((mp_count - 1, group // mp_count, lanes), jnp.bfloat16),
            pltpu.VMEM((8, width), jnp.float32),
            *line_sems(mp_count),
            *cube_sems(2 + matrices, dp_count),
            pltpu.SemaphoreType.DMA((mp_count - 1,)),
            pltpu.SemaphoreType.DMA((mp_count - 1,)),
            pltpu.SemaphoreType.DMA,
            pltpu.SemaphoreType.DMA,
        ],
        compiler_params=pltpu.CompilerParams(
            collective_id=6, has_side_effects=True, vmem_limit_bytes=56 << 20
        ),
        name="sum_end",
    )(part, first, source, gain, skip, *mix, pack)


def update_rows(rate, state, grad, new):
    scaled = rate * grad[...].astype(jnp.float32)
    velocity = momentum_rate * state[1] + scaled
    weight = state[0] - (scaled + momentum_rate * velocity)
    new[0] = velocity
    new[1] = weight
    new[2] = average_rate * state[2] + (1.0 - average_rate) * weight


def run_update(state, grad, fan, total_tokens):
    shape = state.shape
    lanes = shape[-1]
    flat = state.reshape(3, -1, lanes)
    grad = grad.reshape(-1, lanes)
    block = 128
    while grad.shape[0] % (2 * block) == 0 and 2 * block * lanes <= 1 << 18:
        block *= 2
    triple = pl.BlockSpec((3, block, lanes), lambda i: (0, i, 0))
    return pl.pallas_call(
        functools.partial(update_rows, (total_tokens * fan) ** (-0.5)),
        grid=(grad.shape[0] // block,),
        out_shape=jax.ShapeDtypeStruct(flat.shape, jnp.float32),
        in_specs=[triple, pl.BlockSpec((block, lanes), lambda i: (i, 0))],
        out_specs=triple,
        compiler_params=pltpu.CompilerParams(vmem_limit_bytes=24 << 20),
        name="momentum_update",
    )(flat, grad).reshape(shape)


def lane_mask(shape, low, high):
    lane = lax.broadcasted_iota(jnp.int32, shape, len(shape) - 1)
    return jnp.logical_and(lane >= low, lane < high)


def masked(value, low, high):
    return jnp.where(lane_mask(value.shape, low, high), value, jnp.zeros_like(value))


def block_norm(value, vectors):
    hidden, hat, _ = norm_forward(value.astype(jnp.float32), vectors[0:1], vectors[1:2], norm_epsilon)
    return hidden, hat


def block_delta(hidden, before, keep):
    row = lax.broadcasted_iota(jnp.int32, hidden.shape, 0)
    behind = jnp.where(row == 0, before, pltpu.roll(hidden, 1, 0))
    return behind * keep - hidden


def mixing_forward(
    tokens, heads, keep, small, vectors, decay_row, up_own, mix, inputs, rec, key, val, gpre, logw, acts
):
    bfloat = jnp.bfloat16
    maa_cols = 5 * TM_RANK
    down_cols = maa_cols + DECAY_RANK
    hidden, _ = block_norm(tokens[...], vectors)
    before, _ = block_norm(heads[0], vectors)
    delta = block_delta(hidden, before[:1], keep[:, :1])
    base = (hidden + delta * vectors[2:3]).astype(bfloat)
    act = jnp.tanh(dot_nn(base, small[:, :WINDOW]))
    act_low = act.astype(bfloat)
    for number in range(5):
        mine = masked(act_low, TM_RANK * number, TM_RANK * (number + 1))
        scale = vectors[3 + number : 4 + number] + dot_nt(mine, small[:, WINDOW:])
        value = (hidden + delta * scale).astype(bfloat)
        inputs[number] = value
        if number:
            place = {1: 1, 2: 2, 3: 0, 4: 3}[number]
            (rec, key, val, gpre)[place][...] = dot_nn(value, mix[place])
        else:
            decay = masked(jnp.tanh(dot_nn(value, small[:, :WINDOW])), maa_cols, down_cols)
            logw[...] = -jnp.exp(decay_row[:1] + dot_nt(decay.astype(bfloat), up_own[...]))
    acts[...] = masked(act, 0, maa_cols) + decay


def run_mixing_forward(tokens, heads, keep, small, vectors, decay_row, up_own, mix):
    rows, width = tokens.shape
    features = mix.shape[2]
    block = lambda lanes: pl.BlockSpec((ROW_BLOCK, lanes), lambda i: (i, 0))
    fixed = lambda value: pl.BlockSpec(
        value.shape, lambda i: (0,) * value.ndim, pipeline_mode=pl.Buffered(1)
    )
    stack = lambda count, lanes: pl.BlockSpec((count, ROW_BLOCK, lanes), lambda i: (0, i, 0))
    return pl.pallas_call(
        mixing_forward,
        grid=(rows // ROW_BLOCK,),
        out_shape=(
            jax.ShapeDtypeStruct((5, rows, width), jnp.bfloat16),
            *[jax.ShapeDtypeStruct((rows, features), jnp.float32)] * 5,
            jax.ShapeDtypeStruct((rows, WINDOW), jnp.float32),
        ),
        in_specs=[
            block(width),
            pl.BlockSpec((1,) + heads.shape[1:], lambda i: (i, 0, 0)),
            block(keep.shape[1]),
            fixed(small),
            fixed(vectors),
            fixed(decay_row),
            fixed(up_own),
            fixed(mix),
        ],
        out_specs=(stack(5, width), *[block(features)] * 5, block(WINDOW)),
        compiler_params=pltpu.CompilerParams(vmem_limit_bytes=58 << 20),
        name="mixing_forward",
    )(tokens, heads, keep, small, vectors, decay_row, up_own, mix)


def mixing_backward(
    tokens, heads, keep, acts, drec, dkey, dval, dgate, draw,
    small, vectors, up_own, mix, given,
    grad_hidden, grad_pack, first_row,
    grad_down, grad_up, grad_vec, carried,
):
    bfloat = jnp.bfloat16
    step, last = pl.program_id(0), pl.num_programs(0) - 1
    maa_cols = 5 * TM_RANK
    down_cols = maa_cols + DECAY_RANK
    features = mix.shape[2]
    col_start = pl.multiple_of(lax.axis_index("mp") * features, 128)

    @pl.when(step == 0)
    def _():
        grad_down[...] = jnp.zeros(grad_down.shape, jnp.float32)
        grad_up[...] = jnp.zeros(grad_up.shape, jnp.float32)
        grad_vec[...] = given[...]
        carried[...] = jnp.zeros(carried.shape, jnp.float32)

    down, upper = small.at[:, :WINDOW], small.at[:, WINDOW:]
    hidden, hat = block_norm(tokens[...], vectors)
    before, before_hat = block_norm(heads[0], vectors)
    delta = block_delta(hidden, before[:1], keep[:, :1])
    act = acts[...]
    act_low = act.astype(bfloat)
    slope = 1.0 - act * act
    raw = draw[...].astype(bfloat)
    grad_decay = masked(dot_nn(raw, up_own[...]) * slope, maa_cols, down_cols).astype(bfloat)
    grad_up[pl.ds(col_start, features), :] += dot_tn(raw, masked(act_low, maa_cols, down_cols))

    def add_row(row, value):
        grad_vec[row : row + 1, :] += jnp.sum(value, 0, keepdims=True)

    total = jnp.zeros(hidden.shape, jnp.float32)
    grad_delta = jnp.zeros(hidden.shape, jnp.float32)
    grad_act = jnp.zeros(act.shape, jnp.float32)
    for number in range(5):
        low, high = TM_RANK * number, TM_RANK * (number + 1)
        mine = masked(act_low, low, high)
        scale = vectors[3 + number : 4 + number] + dot_nt(mine, upper[...])
        if number:
            source = {1: dkey, 2: dval, 3: drec, 4: dgate}[number]
            grad_input = dot_nt(source[...], mix[{1: 1, 2: 2, 3: 0, 4: 3}[number]])
        else:
            grad_input = dot_nt(grad_decay, down[...])
            value = (hidden + delta * scale).astype(bfloat)
            grad_down[...] += dot_tn(value, grad_decay)
        moved = grad_input * delta
        add_row(3 + number, moved)
        moved_low = moved.astype(bfloat)
        grad_up[...] += dot_tn(moved_low, mine)
        grad_act += masked(dot_nn(moved_low, upper[...]), low, high)
        grad_delta += grad_input * scale
        total += grad_input
    grad_pre = (grad_act * slope).astype(bfloat)
    base = (hidden + delta * vectors[2:3]).astype(bfloat)
    grad_down[...] += dot_tn(base, grad_pre)
    grad_base = dot_nt(grad_pre, down[...])
    add_row(2, grad_base * delta)
    grad_delta += grad_base * vectors[2:3]
    shifted_grad = grad_delta * keep[:, :1]
    row = lax.broadcasted_iota(jnp.int32, hidden.shape, 0)
    back = jnp.where(
        row == ROW_BLOCK - 1, carried[:1], pltpu.roll(shifted_grad, ROW_BLOCK - 1, 0)
    )
    carried[...] = jnp.broadcast_to(shifted_grad[:1], carried.shape)
    total += grad_base - grad_delta + back
    add_row(0, total * hat)
    add_row(1, total)
    grad_hidden[...] = total.astype(bfloat)

    @pl.when(step == last)
    def _():
        first_row[...] = carried[...]
        add_row(0, carried[:1] * before_hat[:1])
        add_row(1, carried[:1])
        spot = lax.broadcasted_iota(jnp.int32, (16, WINDOW), 0) + down_cols
        lane = lax.broadcasted_iota(jnp.int32, (16, WINDOW), 1)
        one = jnp.where(spot == lane, 1.0, 0.0).astype(bfloat)
        placed = dot_tn(grad_vec[...].astype(bfloat), one)
        grad_pack[:, :WINDOW] = (grad_down[...] + placed).astype(bfloat)
        grad_pack[:, WINDOW:] = grad_up[...].astype(bfloat)


def run_mixing_backward(
    tokens, heads, keep, acts, drec, dkey, dval, dgate, draw, small, vectors, up_own, mix, given
):
    rows, width = tokens.shape
    features = mix.shape[2]
    count = rows // ROW_BLOCK
    block = lambda lanes: pl.BlockSpec((ROW_BLOCK, lanes), lambda i: (count - 1 - i, 0))
    fixed = lambda value: pl.BlockSpec(
        value.shape, lambda i: (0,) * len(value.shape), pipeline_mode=pl.Buffered(1)
    )
    first = jax.ShapeDtypeStruct((8, width), jnp.float32)
    pack = jax.ShapeDtypeStruct((width, 2 * WINDOW), jnp.bfloat16)
    return pl.pallas_call(
        mixing_backward,
        grid=(count,),
        out_shape=(jax.ShapeDtypeStruct((rows, width), jnp.bfloat16), pack, first),
        in_specs=[
            block(width),
            pl.BlockSpec((1,) + heads.shape[1:], lambda i: (count - 1 - i, 0, 0)),
            block(keep.shape[1]),
            block(WINDOW),
            block(features),
            block(features),
            block(features),
            block(features),
            block(features),
            fixed(small),
            fixed(vectors),
            fixed(up_own),
            fixed(mix),
            fixed(given),
        ],
        out_specs=(block(width), fixed(pack), fixed(first)),
        scratch_shapes=[
            pltpu.VMEM((width, WINDOW), jnp.float32),
            pltpu.VMEM((width, WINDOW), jnp.float32),
            pltpu.VMEM((16, width), jnp.float32),
            pltpu.VMEM((8, width), jnp.float32),
        ],
        compiler_params=pltpu.CompilerParams(vmem_limit_bytes=60 << 20),
        name="mixing_backward",
    )(tokens, heads, keep, acts, drec, dkey, dval, dgate, draw, small, vectors, up_own, mix, given)


def channel_backward(
    source, heads, keep, grad_key, grad_recv, vectors, gate,
    grad_hidden, sums, first_row,
    carried,
):
    step, last = pl.program_id(0), pl.num_programs(0) - 1

    @pl.when(step == 0)
    def _():
        sums[...] = jnp.zeros(sums.shape, jnp.float32)
        carried[...] = jnp.zeros(carried.shape, jnp.float32)

    def norm(value):
        return norm_forward(
            value.astype(jnp.float32), vectors[12:13], vectors[13:14], norm_epsilon
        )[:2]

    def add_row(row, value):
        sums[row : row + 1, :] += jnp.sum(value, 0, keepdims=True)

    hidden, hat = norm(source[...])
    before, before_hat = norm(heads[0])
    delta = block_delta(hidden, before[:1], keep[:, :1])
    grad_recv_in = dot_nt(grad_recv[...], gate[...])
    grad_key_in = grad_key[...]
    grad_delta = grad_key_in * vectors[14:15] + grad_recv_in * vectors[15:16]
    add_row(2, grad_key_in * delta)
    add_row(3, grad_recv_in * delta)
    shifted_grad = grad_delta * keep[:, :1]
    row = lax.broadcasted_iota(jnp.int32, hidden.shape, 0)
    back = jnp.where(
        row == ROW_BLOCK - 1, carried[:1], pltpu.roll(shifted_grad, ROW_BLOCK - 1, 0)
    )
    carried[...] = jnp.broadcast_to(shifted_grad[:1], carried.shape)
    total = grad_key_in + grad_recv_in - grad_delta + back
    add_row(0, total * hat)
    add_row(1, total)
    grad_hidden[...] = total.astype(jnp.bfloat16)

    @pl.when(step == last)
    def _():
        first_row[...] = carried[...]
        add_row(0, carried[:1] * before_hat[:1])
        add_row(1, carried[:1])


def run_channel_backward(source, heads, keep, grad_key, grad_recv, vectors, gate):
    rows, width = source.shape
    count = rows // ROW_BLOCK
    block = lambda lanes: pl.BlockSpec((ROW_BLOCK, lanes), lambda i: (count - 1 - i, 0))
    fixed = lambda value: pl.BlockSpec(
        value.shape, lambda i: (0,) * len(value.shape), pipeline_mode=pl.Buffered(1)
    )
    first = jax.ShapeDtypeStruct((8, width), jnp.float32)
    return pl.pallas_call(
        channel_backward,
        grid=(count,),
        out_shape=(jax.ShapeDtypeStruct((rows, width), jnp.bfloat16), first, first),
        in_specs=[
            block(width),
            pl.BlockSpec((1,) + heads.shape[1:], lambda i: (count - 1 - i, 0, 0)),
            block(keep.shape[1]),
            block(width),
            block(grad_recv.shape[1]),
            fixed(vectors),
            fixed(gate),
        ],
        out_specs=(block(width), fixed(first), fixed(first)),
        scratch_shapes=[pltpu.VMEM((8, width), jnp.float32)],
        compiler_params=pltpu.CompilerParams(vmem_limit_bytes=48 << 20),
        name="channel_backward",
    )(source, heads, keep, grad_key, grad_recv, vectors, gate)


def update(carried_memory, grad, fan, total_tokens):
    rate = (total_tokens * fan) ** (-0.5)
    scaled = rate * grad
    velocity = momentum_rate * carried_memory[1] + scaled
    weight = carried_memory[0] - (scaled + momentum_rate * velocity)
    average = average_rate * carried_memory[2] + (1.0 - average_rate) * weight
    return jnp.stack([velocity, weight, average])


def split_three(value):
    pieces = []
    for _ in range(3):
        pieces.append(lax.reduce_precision(value, 8, 7))
        value = value - pieces[-1]
    return [piece.astype(jnp.bfloat16) for piece in pieces]


def shifted(value, before, keep):
    return jnp.concatenate([before, value[:-1]], 0) * keep[:, None] - value


def block_heads(before, rows):
    width = rows.shape[1]
    ends = rows.reshape(-1, ROW_BLOCK, width)[:-1, -1]
    heads = jnp.concatenate([before, ends], 0)
    return jnp.broadcast_to(heads[:, None], (heads.shape[0], 16, width))


def body(
    tokens,
    cotangent,
    lengths,
    mix_state,
    out_state,
    key_state,
    value_state,
    gate_state,
    down_state,
    up_state,
    vector_state,
):
    bfloat = jnp.bfloat16
    single = jnp.float32
    dp_count = lax.axis_size("dp")
    mp_count = lax.axis_size("mp")
    dp_index = lax.axis_index("dp")
    mp_index = lax.axis_index("mp")
    own_rows = tokens.shape[0]
    width = tokens.shape[1]
    group_rows = own_rows * mp_count
    total_tokens = group_rows * dp_count
    features = mix_state.shape[3]
    maa_cols = 5 * TM_RANK
    down_cols = maa_cols + DECAY_RANK
    col_start = mp_index * features

    upper, middle, lower = split_three(vector_state[0].T)
    pack = jnp.concatenate(
        [
            down_state[0].astype(bfloat),
            upper,
            middle,
            up_state[0].T.astype(bfloat),
            lower,
            jnp.zeros_like(lower),
        ],
        1,
    )
    states = (mix_state, out_state, gate_state, key_state, value_state)
    tokens_all, small, mix_weight, out_low, gate_low, key_low, value_low, before_one = run_start(
        dp_count, mp_count, tokens, pack, states
    )
    out_weight = lax.all_gather(out_low, "dp", axis=1, tiled=True)
    gate_weight = lax.all_gather(gate_low, "dp", axis=0, tiled=True)
    vectors = sum(
        small[:, start : start + 16].astype(single)
        for start in (down_cols, down_cols + 16, WINDOW + down_cols)
    ).T

    seq_ends = jnp.cumsum(lengths)
    offsets = seq_ends - lengths
    positions = dp_index * group_rows + jnp.arange(group_rows, dtype=jnp.int32)
    opening = jnp.any(positions[:, None] == offsets[None, :], 1).astype(single)
    segment = jnp.sum((offsets[None, :] <= positions[:, None]).astype(single), 1)
    keep = 1.0 - opening
    chunks = group_rows // CHUNK
    parts = segment.reshape(chunks, CHUNK)
    first = parts[:, :1] - opening.reshape(chunks, CHUNK)[:, :1]

    def spread(value, lanes):
        return jnp.broadcast_to(value.astype(single).reshape(-1, 1), (value.size, lanes))

    marks = (
        spread(parts, 2 * CHUNK),
        jnp.repeat(jnp.concatenate([parts, parts], 1), 8, 0),
        spread(parts == first, PAIR),
        spread(parts == parts[:, -1:], PAIR),
        spread(jnp.repeat(parts[:, -1:] == first, 8, 0), PAIR),
    )
    level, sums, sums_back = level_tables()
    tables = (jnp.asarray(level), jnp.asarray(sums, bfloat), jnp.asarray(sums_back, bfloat))

    def local_share(row_number):
        return lax.dynamic_slice_in_dim(vectors[row_number], col_start, features, 0)

    def spread_row(value):
        return jnp.broadcast_to(value[None], (8, width))

    heads = block_heads(before_one[-1:], tokens_all)
    keep_lanes = spread(keep, PAIR)
    up_own = lax.dynamic_slice_in_dim(small[:, WINDOW:], col_start, features, 0)
    decay_row = jnp.broadcast_to(local_share(8)[None], (8, features))
    inputs_low, *branch, acts = run_mixing_forward(
        tokens_all, heads, keep_lanes, small, vectors, decay_row, up_own, mix_weight
    )
    key_low, value_low, branch = lax.optimization_barrier((key_low, value_low, branch))
    key_weight = lax.all_gather(key_low, "dp", axis=0, tiled=True)
    value_weight = lax.all_gather(value_low, "dp", axis=1, tiled=True)
    local_vectors = jnp.concatenate(
        [jnp.stack([local_share(9), local_share(10), local_share(11)]), jnp.zeros((5, features))], 0
    )
    gated_low, wkv, states, kept, cotangent_cols = run_forward(
        dp_count, mp_count, *branch, local_vectors, marks, tables, cotangent
    )
    cotangent_cols = cotangent_cols.astype(single)

    residual, residual_all, before_second = run_exchange(
        dp_count,
        mp_count,
        4,
        residual_rows,
        True,
        half_dot(gated_low, out_weight).astype(bfloat),
        tokens,
    )
    before_second = before_second[-1:]
    hidden_two, hat_two, inv_two = norm_forward(
        residual_all.astype(single), vectors[12], vectors[13], norm_epsilon
    )
    before_two = norm_forward(before_second.astype(single), vectors[12], vectors[13], norm_epsilon)[
        0
    ]
    delta_two = shifted(hidden_two, before_two, keep)
    key_in_low = (hidden_two + delta_two * vectors[14]).astype(bfloat)
    recv_in_low = (hidden_two + delta_two * vectors[15]).astype(bfloat)
    recv_gate = jax.nn.sigmoid(half_dot(recv_in_low, gate_weight))
    grad_kv = (cotangent_cols * recv_gate).astype(bfloat)
    grad_kv, key_in_low = lax.optimization_barrier((grad_kv, key_in_low))
    key_pre = half_dot(key_in_low, key_weight)
    key_act_low = jnp.square(jnp.maximum(key_pre, 0.0)).astype(bfloat)
    grad_kv_all = lax.all_gather(grad_kv, "mp", axis=1, tiled=True)
    channel_sum = lax.psum_scatter(
        half_dot(key_act_low, value_weight).astype(bfloat), "mp", scatter_dimension=1, tiled=True
    ).astype(single)
    gated_sum = recv_gate * channel_sum
    grad_recv_pre = (cotangent_cols * gated_sum * (1.0 - recv_gate)).astype(bfloat)
    grad_key_act = half_right(grad_kv_all, value_weight)
    grad_key_pre = (grad_key_act * 2.0 * jnp.maximum(key_pre, 0.0)).astype(bfloat)
    grad_key_in = half_right(grad_key_pre, key_weight)
    grad_value_weight = half_left(key_act_low, grad_kv_all).astype(bfloat)
    grad_key_weight = half_left(key_in_low, grad_key_pre).astype(bfloat)
    grad_gate_weight = half_left(recv_in_low, grad_recv_pre).astype(bfloat)
    grad_hidden_two, channel_sums, first_row_two = run_channel_backward(
        residual_all,
        block_heads(before_second, residual_all),
        keep_lanes,
        grad_key_in,
        grad_recv_pre,
        vectors,
        gate_weight,
    )
    def summed(value, axis):
        return lax.psum_scatter(value, "dp", scatter_dimension=axis, tiled=True)

    value_sum = summed(grad_value_weight, 1)
    key_sum = summed(grad_key_weight, 0)
    gate_sum = summed(grad_gate_weight, 0)
    grad_residual, grad_attn_all = run_exchange(
        dp_count,
        mp_count,
        5,
        backward_rows,
        False,
        grad_hidden_two,
        first_row_two,
        residual.astype(bfloat),
        spread_row(vectors[12]),
        cotangent,
    )
    grad_out_weight = half_left(gated_low, grad_attn_all)
    out_sum = summed(grad_out_weight.astype(bfloat), 1)
    grad_gated = half_right(grad_attn_all, out_weight)
    grad_recept, grad_keys, grad_values, grad_gate_pre, grad_raw, grad_local, mixed = run_backward(
        dp_count,
        mp_count,
        grad_gated,
        wkv,
        states,
        kept,
        *branch,
        local_vectors,
        marks,
        tables,
        gated_sum.astype(bfloat),
        residual,
    )

    value_sum, key_sum, grad_raw = lax.optimization_barrier((value_sum, key_sum, grad_raw))
    grad_mix_weight = [
        half_left(inputs_low[number], value).astype(bfloat)
        for number, value in (
            (3, grad_recept),
            (1, grad_keys),
            (2, grad_values),
            (4, grad_gate_pre),
        )
    ]
    given = jnp.concatenate(
        [
            jnp.zeros((8, width), single),
            lax.dynamic_update_slice_in_dim(
                jnp.zeros((4, width), single), grad_local[:4], col_start, 1
            ),
            channel_sums[:4],
        ],
        0,
    )
    grad_hidden_one, grad_pack, first_row = run_mixing_backward(
        tokens_all,
        heads,
        keep_lanes,
        acts,
        grad_recept,
        grad_keys,
        grad_values,
        grad_gate_pre,
        grad_raw,
        small,
        vectors,
        up_own,
        mix_weight,
        given,
    )
    grad_tokens, mix_sum, small_sum = run_end(
        dp_count,
        mp_count,
        grad_hidden_one,
        first_row,
        tokens,
        spread_row(vectors[0]),
        grad_residual,
        grad_mix_weight,
        grad_pack,
    )
    gate_sum, out_sum, mix_sum = lax.optimization_barrier((gate_sum, out_sum, mix_sum))
    return (
        mixed,
        grad_tokens,
        run_update(mix_state, mix_sum, width, total_tokens),
        run_update(out_state, out_sum, width, total_tokens),
        run_update(key_state, key_sum, width, total_tokens),
        run_update(value_state, value_sum, FF, total_tokens),
        run_update(gate_state, gate_sum, width, total_tokens),
        update(down_state, small_sum[:, :down_cols], width, total_tokens),
        update(up_state, small_sum[:, WINDOW : WINDOW + down_cols].T, TM_RANK, total_tokens),
        update(vector_state, small_sum[:, down_cols : down_cols + 16].T, 1, total_tokens),
    )


def solution(mesh):
    return jax.shard_map(
        body,
        mesh=mesh,
        in_specs=(
            P(("dp", "mp"), None),
            P(("dp", "mp"), None),
            P(),
            P(None, None, "dp", "mp"),
            P(None, "mp", "dp"),
            P(None, "dp", "mp"),
            P(None, "mp", "dp"),
            P(None, "dp", "mp"),
            P(None, ("dp", "mp"), None),
            P(None, None, ("dp", "mp")),
            P(None, None, ("dp", "mp")),
        ),
        out_specs=(
            P(("dp", "mp"), None),
            P(("dp", "mp"), None),
            P(None, None, "dp", "mp"),
            P(None, "mp", "dp"),
            P(None, "dp", "mp"),
            P(None, "mp", "dp"),
            P(None, "dp", "mp"),
            P(None, ("dp", "mp"), None),
            P(None, None, ("dp", "mp")),
            P(None, None, ("dp", "mp")),
        ),
        check_vma=False,
    )
```

```python
import functools

import jax
import jax.numpy as jnp
import numpy as np
from jax import lax
from jax.experimental import pallas as pl
from jax.experimental.pallas import tpu as pltpu
from jax.sharding import PartitionSpec as P

LANE_SPAN = 64
FF = 7168
TM_RANK = 32
DECAY_RANK = 64


momentum_rate = 0.9
average_rate = 0.9
norm_epsilon = 1e-05
group_epsilon = 0.00064
CHUNK = 128
LEVELS = 7
PAIR = 2 * LANE_SPAN
MESH = pl.DeviceIdType.MESH
PIECES = 2
WINDOW = 256
ROW_BLOCK = 256


def half_dot(left, right):
    return jnp.dot(left, right, preferred_element_type=jnp.float32)


def half_left(left, right):
    return lax.dot_general(
        left, right, (((0,), (0,)), ((), ())), preferred_element_type=jnp.float32
    )


def half_right(left, right):
    return lax.dot_general(
        left, right, (((1,), (1,)), ((), ())), preferred_element_type=jnp.float32
    )


def split_pair(value):
    upper_part = value.astype(jnp.bfloat16)
    lower_part = (value - upper_part.astype(jnp.float32)).astype(jnp.bfloat16)
    return (upper_part, lower_part)


def norm_forward(value, gain, bias, epsilon):
    centre = value - jnp.mean(value, -1, keepdims=True)
    inverse = lax.rsqrt(jnp.mean(centre * centre, -1, keepdims=True) + epsilon)
    normal_hat = centre * inverse
    return (normal_hat * gain + bias, normal_hat, inverse)


def norm_backward(grad_out, normal_hat, inverse, gain):
    scaled = grad_out * gain
    return inverse * (
        scaled
        - jnp.mean(scaled, -1, keepdims=True)
        - normal_hat * jnp.mean(scaled * normal_hat, -1, keepdims=True)
    )


def level_tables():
    row = np.arange(CHUNK)
    later, earlier = row[:, None], row[None, :]
    level = np.full((CHUNK, CHUNK), -1.0, np.float32)
    sums = []
    for bit in range(LEVELS):
        block = (later >> (bit + 1)) == (earlier >> (bit + 1))
        level[block & ((later >> bit) % 2 == 1) & ((earlier >> bit) % 2 == 0)] = bit
        middle = ((later >> (bit + 1)) << (bit + 1)) + (1 << bit)
        upper = (later >> bit) % 2 == 1
        between = np.where(
            upper, (earlier >= middle) & (earlier < later), (earlier > later) & (earlier < middle)
        )
        if bit:
            sums.append(between)
    sums += [earlier < later, earlier > later]
    sums = np.concatenate(sums, 0).astype(np.float32)
    return np.concatenate([level, level], 1), np.concatenate([sums, sums], 1), sums.T


def dot_nn(left, right):
    return lax.dot_general(
        left, right, (((1,), (0,)), ((), ())), preferred_element_type=jnp.float32
    )


def dot_nt(left, right):
    return lax.dot_general(
        left, right, (((1,), (1,)), ((), ())), preferred_element_type=jnp.float32
    )


def dot_tn(left, right):
    return lax.dot_general(
        left, right, (((0,), (0,)), ((), ())), preferred_element_type=jnp.float32
    )


def first_head(shape):
    return lax.broadcasted_iota(jnp.int32, shape, len(shape) - 1) < LANE_SPAN


def stack_heads(value):
    first = first_head(value.shape)
    none = jnp.zeros_like(value)
    return jnp.concatenate([jnp.where(first, value, none), jnp.where(first, none, value)], 0)


def merge_heads(value):
    half = value.shape[0] // 2
    return jnp.where(first_head((half, value.shape[1])), value[:half], value[half:])


def own_blocks(value):
    upper = lax.broadcasted_iota(jnp.int32, value.shape, 0) < LANE_SPAN
    return jnp.where(upper == first_head(value.shape), value, 0.0)


def head_mean(value):
    row = lax.broadcasted_iota(jnp.int32, (PAIR, PAIR), 0) < LANE_SPAN
    ones = jnp.where(row == first_head((PAIR, PAIR)), 1.0 / LANE_SPAN, 0.0).astype(jnp.bfloat16)
    upper, lower = split_pair(value)
    return dot_nn(upper, ones) + dot_nn(lower, ones)


def head_sum(value):
    return head_mean(value) * float(LANE_SPAN)


def exact_pieces(left, right, axis_left, axis_right):
    upper, lower = split_pair(left)
    right_upper, right_lower = split_pair(right)
    return (
        jnp.concatenate([upper, lower, upper], axis_left),
        jnp.concatenate([right_upper, right_upper, right_lower], axis_right),
    )


def exact_nn(left, right):
    return dot_nn(*exact_pieces(left, right, 1, 0))


def exact_nt(left, right):
    return dot_nt(*exact_pieces(left, right, 1, 1))


def exact_tn(left, right):
    return dot_tn(*exact_pieces(left, right, 0, 0))


def packed_state(state):
    return jnp.concatenate(split_pair(state[:LANE_SPAN] + state[LANE_SPAN:]), 0)


def unpacked_state(piece):
    piece = piece.astype(jnp.float32)
    return piece[:LANE_SPAN] + piece[LANE_SPAN:]


def rows_of(chunk):
    return pl.ds(pl.multiple_of(chunk * CHUNK, CHUNK), CHUNK)


def lanes_of(pair):
    return pl.ds(pl.multiple_of(pair * PAIR, PAIR), PAIR)


def marks_of(chunk):
    return pl.ds(pl.multiple_of(chunk * 8, 8), 8)


def everyone(dp_count, mp_count):
    me, mine = lax.axis_index("dp"), lax.axis_index("mp")
    return [(lax.rem(me + step, dp_count), mine) for step in range(1, dp_count)] + [
        (me, lax.rem(mine + step, mp_count)) for step in range(1, mp_count)
    ]


def swap_copies(count, source, target, send_sems, recv_sems):
    me, mine = lax.axis_index("dp"), lax.axis_index("mp")
    copies = []
    for step in range(1, count):
        other = lax.rem(mine + step, count)
        copies.append(
            pltpu.make_async_remote_copy(
                src_ref=source(other),
                dst_ref=target(mine),
                send_sem=send_sems.at[step - 1],
                recv_sem=recv_sems.at[step - 1],
                device_id=(me, other),
                device_id_type=MESH,
            )
        )
    return copies


def state_copies(other, me, sends, lands, send_sems, recv_sems, to):
    return [
        pltpu.make_async_remote_copy(
            src_ref=send,
            dst_ref=land.at[me],
            send_sem=send_sems.at[number, other],
            recv_sem=recv_sems.at[number, me],
            device_id=(to, lax.axis_index("mp")),
            device_id_type=MESH,
        )
        for number, (send, land) in enumerate(zip(sends, lands))
    ]


def send_states(count, sends, lands, send_sems, recv_sems, ahead):
    me = lax.axis_index("dp")
    for other in range(count):

        @pl.when((other > me) if ahead else (other < me))
        def _():
            for copy in state_copies(other, me, sends, lands, send_sems, recv_sems, other):
                copy.start()


def wait_states(count, sends, lands, send_sems, recv_sems, ahead):
    me = lax.axis_index("dp")
    for other in range(count):

        @pl.when((other > me) if ahead else (other < me))
        def _():
            for copy in state_copies(other, me, sends, lands, send_sems, recv_sems, other):
                copy.wait_send()

        @pl.when((other < me) if ahead else (other > me))
        def _():
            for copy in state_copies(other, other, sends, lands, send_sems, recv_sems, me):
                copy.wait_recv()


def decay_factors(fading, sums):
    upper, lower = split_pair(fading)
    return jnp.exp(dot_nn(sums, jnp.concatenate([upper, lower], 0)))


def table(at):
    return slice(at * CHUNK, (at + 1) * CHUNK)


def level_inputs(level, acceptor, lookup, factors):
    if level == 0:
        return None, acceptor, lookup
    factor = factors[table(level - 1), :]
    return factor, acceptor * factor, lookup * factor


def recurrence_forward(
    count, mp_count, chunks, pairs,
    rec, key, val, gpre, logw, vec, seg_col, seg_row, valid, ending, whole, level, sums, cotangent,
    tokens, out_weight, key_low,
    gated, wkv, states, kept, columns, residual, residual_all, before, key_all,
    factors, pre_a, pre_b, start_b, send_a, send_b, land_a, land_b, send_sems, recv_sems,
    swap_send, swap_recv,
    part, moving, land, total, sum_send, sum_recv, line_send, line_recv, halo_send, halo_recv,
    key_sem, cube_send, cube_recv,
):
    bfloat = jnp.bfloat16
    halo = Halo(count, mp_count, halo_send, halo_recv)
    greet_all(everyone(count, mp_count), halo.partners())
    mine, own_rows, features = lax.axis_index("mp"), cotangent.shape[0], columns.shape[1]

    def own_columns(other):
        return cotangent.at[:, pl.ds(pl.multiple_of(other * features, 128), features)]

    def landing(other):
        return columns.at[pl.ds(pl.multiple_of(other * own_rows, 16), own_rows)]

    key_rows = key_low.shape[0]
    half = key_rows // 2
    me = lax.axis_index("dp")
    key_own = pltpu.make_async_copy(
        key_low, key_all.at[pl.ds(pl.multiple_of(me * key_rows, 16), key_rows)], key_sem
    )
    key_own.start()
    cube = CubeGather(count, cube_send, cube_recv)

    def key_view(side):
        def view(index):
            return key_all.at[pl.ds(pl.multiple_of(index * key_rows + side * half, 16), half)]

        return view

    key_stages = list(range(cube.stages + 1))

    def gather_key():
        if key_stages:
            stage = key_stages.pop(0)
            for side in range(2):
                cube.stage(side, side, key_view(side), stage)

    swaps = swap_copies(mp_count, own_columns, landing, swap_send, swap_recv)
    for copy in swaps:
        copy.start()
    landing(mine)[...] = own_columns(mine)[...]

    def summary(pair, carry):
        lanes = lanes_of(pair)

        def step(chunk, before):
            before_a, before_b = before
            rows, slot = rows_of(chunk), pair * chunks + chunk
            fading = logw[rows, lanes]
            factor = decay_factors(fading, sums[...])
            factors[slot] = factor
            faded = key[rows, lanes] * factor[table(LEVELS)] * ending[rows, :]
            chunk_b = own_blocks(exact_tn(val[rows, lanes], faded))
            chunk_a = jnp.exp(jnp.sum(fading, 0, keepdims=True)) * whole[marks_of(chunk), :][:1]
            pre_a[slot] = jnp.broadcast_to(before_a, (8, PAIR))
            pre_b[slot] = before_b
            return before_a * chunk_a, before_b * chunk_a + chunk_b

        last_a, last_b = lax.fori_loop(
            0, chunks, step, (jnp.ones((1, PAIR), jnp.float32), jnp.zeros((PAIR, PAIR), jnp.float32))
        )
        send_a[:, lanes] = jnp.broadcast_to(last_a, (8, PAIR))
        send_b[:, lanes] = packed_state(last_b)
        return carry

    lax.fori_loop(0, pairs, summary, 0)
    exchange = (count, (send_a, send_b), (land_a, land_b), send_sems, recv_sems, True)
    send_states(*exchange)
    key_own.wait()
    gather_key()

    def inside(slot, carry):
        pair, chunk = slot // chunks, slot % chunks
        rows, lanes = rows_of(chunk), lanes_of(pair)
        acceptor, lookup, payload = rec[rows, lanes], key[rows, lanes], val[rows, lanes]
        place = jnp.where(seg_col[rows, :] == seg_row[marks_of(chunk), :][:1], level[...], -1.0)
        scores = jnp.zeros((CHUNK, 2 * CHUNK), jnp.float32)
        for at in range(LEVELS):
            _, left, right = level_inputs(at, acceptor, lookup, factors.at[slot])
            part = exact_nt(left, stack_heads(right))
            scores = jnp.where(place == float(at), part, scores)
        bonus = head_sum(acceptor * vec[0:1, lanes] * lookup) * payload
        wkv[rows, lanes] = bonus + exact_nn(scores, stack_heads(payload))
        kept[slot] = scores.astype(bfloat)
        return carry

    lax.fori_loop(0, pairs * chunks, inside, 0)
    wait_states(*exchange)
    gather_key()
    start_b[...] = lax.fori_loop(
        0,
        lax.axis_index("dp"),
        lambda other, state: state * land_a[other][:1] + unpacked_state(land_b[other]),
        jnp.zeros(start_b.shape, jnp.float32),
    )

    def finish(chunk, pair):
        slot = pair * chunks + chunk
        rows, lanes = rows_of(chunk), lanes_of(pair)
        state = pre_b[slot] + pre_a[slot][:1] * stack_heads(start_b[:, lanes])
        states[slot] = state
        reader = rec[rows, lanes] * factors[slot, table(LEVELS - 1), :] * valid[rows, :]
        out = wkv[rows, lanes] + exact_nt(reader, state)
        wkv[rows, lanes] = out
        centre = out - head_mean(out)
        inverse = lax.rsqrt(head_mean(centre * centre) + group_epsilon)
        normed = centre * inverse * vec[1:2, lanes] + vec[2:3, lanes]
        pre = gpre[rows, lanes]
        gated[rows, lanes] = (normed * pre * jax.nn.sigmoid(pre)).astype(bfloat)

    def project(block):
        def pair_step(pair, carry):
            for chunk in range(block * own_rows // CHUNK, (block + 1) * own_rows // CHUNK):
                finish(chunk, pair)
            return carry

        lax.fori_loop(0, pairs, pair_step, 0)
        at = slice(block * own_rows, (block + 1) * own_rows)
        width = 512

        def columns_step(number, carry):
            lanes = pl.ds(pl.multiple_of(number * width, width), width)
            part[at, lanes] = dot_nn(gated[at, :], out_weight[:, lanes]).astype(bfloat)
            return carry

        lax.fori_loop(0, part.shape[1] // width, columns_step, 0)

    adder = LineSum(mp_count, own_rows, sum_send, sum_recv)
    line = LineGather(mp_count, own_rows, line_send, line_recv)
    edge = residual_all.at[pl.ds(mp_count * own_rows - 16, 16)]
    project(mp_count - 1)
    project(0)
    adder.begin(part, None, moving, land, 0)
    for block in range(mp_count - 2, 0, -1):
        project(block)
    for number in range(mp_count - 1):
        if number:
            adder.begin(part, None, moving, land, number)
        adder.step(part, None, moving, land, number)
    gather_key()
    for piece in range(PIECES):
        at = adder.total(part, None, moving, land, total, piece)
        value = total[at] + tokens[at].astype(jnp.float32)
        residual[at] = value
        residual_all[line.at(line.me, piece)] = value.astype(bfloat)
        line.send(residual_all, 0, piece)
    halo.start(edge, before)
    for distance in range(1, mp_count):
        for piece in range(PIECES):
            line.send(residual_all, distance, piece)
    while key_stages:
        gather_key()
    for side in range(2):
        cube.finish(side, side, key_view(side))
    adder.finish(moving, land)
    line.finish(residual_all)
    halo.finish(edge, before)
    for copy in swaps:
        copy.wait()


def recurrence_backward(
    count, mp_count, chunks, pairs,
    dgated, wkv, states, kept, rec, key, val, gpre, logw, vec, seg_col, seg_row, valid, ending, whole,
    level, sums, sums_back, change, residual,
    drec, dkey, dval, dgpre, draw, dvec, mixed,
    factors, local, end_b, dout, drec_part, dkey_part, dval_part, dlog_part, steps,
    send_a, send_b, land_a, land_b, send_sems, recv_sems,
    swapped, swap_send, swap_recv,
):
    bfloat = jnp.bfloat16
    greet_all(everyone(count, mp_count))
    mine, own_rows, features = lax.axis_index("mp"), residual.shape[0], change.shape[1]

    def rows_for(other):
        return change.at[pl.ds(pl.multiple_of(other * own_rows, 16), own_rows)]

    swaps = swap_copies(mp_count, rows_for, lambda other: swapped.at[other], swap_send, swap_recv)
    for copy in swaps:
        copy.start()
    swapped[mine] = rows_for(mine)[...]
    dvec[...] = jnp.zeros(dvec.shape, jnp.float32)

    def chunk_decay(chunk, lanes):
        fading = logw[rows_of(chunk), lanes]
        return jnp.exp(jnp.sum(fading, 0, keepdims=True)) * whole[marks_of(chunk), :][:1]

    def summary(pair, carry):
        lanes = lanes_of(pair)

        def step(back, after):
            after_a, after_b = after
            chunk = chunks - 1 - back
            rows, slot = rows_of(chunk), pair * chunks + chunk
            factor = decay_factors(logw[rows, lanes], sums[...])
            factors[slot] = factor
            out = wkv[rows, lanes]
            centre = out - head_mean(out)
            inverse = lax.rsqrt(head_mean(centre * centre) + group_epsilon)
            hat = centre * inverse
            gain = vec[1:2, lanes]
            normed = hat * gain + vec[2:3, lanes]
            pre = gpre[rows, lanes]
            sig = jax.nn.sigmoid(pre)
            grad = dgated[rows, lanes]
            grad_normed = grad * pre * sig
            dgpre[rows, lanes] = (grad * normed * sig * (1.0 + pre * (1.0 - sig))).astype(bfloat)
            dvec[2:3, lanes] += jnp.sum(grad_normed * hat, 0, keepdims=True)
            dvec[3:4, lanes] += jnp.sum(grad_normed, 0, keepdims=True)
            scaled = grad_normed * gain
            grad_out = inverse * (scaled - head_mean(scaled) - hat * head_mean(scaled * hat))
            dout[rows, lanes] = grad_out
            reader = rec[rows, lanes] * factor[table(LEVELS - 1)] * valid[rows, :]
            inner = own_blocks(exact_tn(grad_out, reader))
            local[slot] = inner
            chunk_a = chunk_decay(chunk, lanes)
            return after_a * chunk_a, after_b * chunk_a + inner

        last_a, last_b = lax.fori_loop(
            0, chunks, step, (jnp.ones((1, PAIR), jnp.float32), jnp.zeros((PAIR, PAIR), jnp.float32))
        )
        send_a[:, lanes] = jnp.broadcast_to(last_a, (8, PAIR))
        send_b[:, lanes] = packed_state(last_b)
        return carry

    lax.fori_loop(0, pairs, summary, 0)
    exchange = (count, (send_a, send_b), (land_a, land_b), send_sems, recv_sems, False)
    send_states(*exchange)

    def inside(slot, carry):
        pair, chunk = slot // chunks, slot % chunks
        rows, lanes = rows_of(chunk), lanes_of(pair)
        acceptor, lookup, payload = rec[rows, lanes], key[rows, lanes], val[rows, lanes]
        reward = vec[0:1, lanes]
        grad_exact = dout[rows, lanes]
        grad_out = grad_exact.astype(bfloat)
        place = jnp.where(seg_col[rows, :] == seg_row[marks_of(chunk), :][:1], level[...], -1.0)
        grad_scores = exact_nt(grad_exact, stack_heads(payload))
        grad_bonus = head_sum(grad_exact * payload)
        dvec[1:2, lanes] += jnp.sum(acceptor * lookup * grad_bonus, 0, keepdims=True)
        grad_acceptor = reward * lookup * grad_bonus
        grad_lookup = reward * acceptor * grad_bonus
        for at in range(LEVELS):
            factor, left, right = level_inputs(at, acceptor, lookup, factors.at[slot])
            left_low, right_low = left.astype(bfloat), stack_heads(right.astype(bfloat))
            here = place == float(at)
            grad_part = jnp.where(here, grad_scores, 0.0).astype(bfloat)
            grad_left = dot_nn(grad_part, right_low)
            grad_right = merge_heads(dot_tn(grad_part, left_low))
            if at:
                grad_left = grad_left * factor
                grad_right = grad_right * factor
                steps[table(at - 1), :] = acceptor * grad_left + lookup * grad_right
            grad_acceptor += grad_left
            grad_lookup += grad_right
        drec_part[rows, lanes] = grad_acceptor
        dkey_part[rows, lanes] = grad_lookup
        bonus = head_sum(acceptor * reward * lookup)
        dval_part[rows, lanes] = bonus * grad_exact + merge_heads(
            dot_tn(kept[slot], grad_out)
        )
        inner = (LEVELS - 1) * CHUNK
        dlog_part[rows, lanes] = dot_nn(sums_back[:, :inner], steps[...].astype(bfloat))
        return carry

    lax.fori_loop(0, pairs * chunks, inside, 0)
    wait_states(*exchange)
    me = lax.axis_index("dp")

    def later(step, state):
        other = count - 1 - step
        return state * land_a[other][:1] + unpacked_state(land_b[other])

    end_b[...] = lax.fori_loop(0, count - 1 - me, later, jnp.zeros(end_b.shape, jnp.float32))

    def finish(pair, carry):
        lanes = lanes_of(pair)

        def step(back, after):
            chunk = chunks - 1 - back
            rows, slot = rows_of(chunk), pair * chunks + chunk
            state = states[slot]
            after_low = after.astype(bfloat)
            reach = factors[slot, table(LEVELS - 1), :] * valid[rows, :]
            tail = factors[slot, table(LEVELS), :] * ending[rows, :]
            acceptor, lookup = rec[rows, lanes], key[rows, lanes]
            grad_reader = exact_nn(dout[rows, lanes], state) * reach
            grad_faded = exact_nn(val[rows, lanes], after) * tail
            faded = (lookup * tail).astype(bfloat)
            chunk_a = chunk_decay(chunk, lanes)
            total = chunk_a * jnp.sum(after * state, 0, keepdims=True)
            drec[rows, lanes] = (drec_part[rows, lanes] + grad_reader).astype(bfloat)
            dkey[rows, lanes] = (dkey_part[rows, lanes] + grad_faded).astype(bfloat)
            dval[rows, lanes] = (dval_part[rows, lanes] + dot_nt(faded, after_low)).astype(bfloat)
            inner = (LEVELS - 1) * CHUNK
            moves = jnp.concatenate([acceptor * grad_reader, lookup * grad_faded], 0)
            grad_log = dlog_part[rows, lanes] + total + dot_nn(
                sums_back[:, inner:], moves.astype(bfloat)
            )
            raw = grad_log * logw[rows, lanes]
            draw[rows, lanes] = raw
            dvec[0:1, lanes] += jnp.sum(raw, 0, keepdims=True)
            return after * chunk_a + local[slot]

        lax.fori_loop(0, chunks, step, stack_heads(end_b[:, lanes]))
        return carry

    lax.fori_loop(0, pairs, finish, 0)
    for copy in swaps:
        copy.wait()
    for other in range(mp_count):
        lanes = slice(other * features, (other + 1) * features)
        mixed[:, lanes] = (residual[:, lanes] + swapped[other].astype(jnp.float32)).astype(bfloat)


def exchange_scratch(count, features):
    return [
        pltpu.VMEM((8, features), jnp.float32),
        pltpu.VMEM((2 * LANE_SPAN, features), jnp.bfloat16),
        pltpu.VMEM((count, 8, features), jnp.float32),
        pltpu.VMEM((count, 2 * LANE_SPAN, features), jnp.bfloat16),
        pltpu.SemaphoreType.DMA((2, count)),
        pltpu.SemaphoreType.DMA((2, count)),
    ]


def run_forward(
    count, mp_count, rec, key, val, gpre, logw, vec, marks, tables, cotangent, tokens, out_weight,
    key_low,
):
    rows, features = rec.shape
    width = tokens.shape[1]
    chunks, pairs = rows // CHUNK, features // PAIR
    slots = chunks * pairs
    whole_array = pl.BlockSpec(memory_space=pltpu.VMEM)
    level, sums, _ = tables
    return pl.pallas_call(
        functools.partial(recurrence_forward, count, mp_count, chunks, pairs),
        out_shape=(
            jax.ShapeDtypeStruct((rows, features), jnp.bfloat16),
            jax.ShapeDtypeStruct((rows, features), jnp.float32),
            jax.ShapeDtypeStruct((slots, PAIR, PAIR), jnp.float32),
            jax.ShapeDtypeStruct((slots, CHUNK, 2 * CHUNK), jnp.bfloat16),
            jax.ShapeDtypeStruct((rows, features), jnp.bfloat16),
            jax.ShapeDtypeStruct(tokens.shape, jnp.float32),
            jax.ShapeDtypeStruct((rows, width), jnp.bfloat16),
            jax.ShapeDtypeStruct((16, width), jnp.bfloat16),
            jax.ShapeDtypeStruct((count * key_low.shape[0], key_low.shape[1]), jnp.bfloat16),
        ),
        in_specs=[whole_array] * 17,
        out_specs=(whole_array,) * 8 + (pl.BlockSpec(memory_space=pl.ANY),),
        scratch_shapes=[
            pltpu.VMEM((slots, sums.shape[0], PAIR), jnp.float32),
            pltpu.VMEM((slots, 8, PAIR), jnp.float32),
            pltpu.VMEM((slots, PAIR, PAIR), jnp.float32),
            pltpu.VMEM((LANE_SPAN, features), jnp.float32),
        ]
        + exchange_scratch(count, features)
        + [
            pltpu.SemaphoreType.DMA((mp_count - 1,)),
            pltpu.SemaphoreType.DMA((mp_count - 1,)),
            pltpu.VMEM((rows, width), jnp.bfloat16),
            pltpu.VMEM((rows, width), jnp.bfloat16),
            pltpu.VMEM((2, rows, width), jnp.bfloat16),
            pltpu.VMEM(tokens.shape, jnp.float32),
            *line_sems(mp_count),
            *line_sems(mp_count),
            pltpu.SemaphoreType.DMA((mp_count,)),
            pltpu.SemaphoreType.DMA,
            pltpu.SemaphoreType.DMA,
            *cube_sems(2, count),
        ],
        compiler_params=pltpu.CompilerParams(
            collective_id=1, has_side_effects=True, vmem_limit_bytes=58 << 20
        ),
        name="recurrence_forward",
    )(rec, key, val, gpre, logw, vec, *marks, level, sums, cotangent, tokens, out_weight, key_low)


def run_backward(
    count, mp_count, dgated, wkv, states, kept, rec, key, val, gpre, logw, vec, marks, tables,
    change, residual,
):
    rows, features = rec.shape
    chunks, pairs = rows // CHUNK, features // PAIR
    slots = chunks * pairs
    whole_array = pl.BlockSpec(memory_space=pltpu.VMEM)
    level, sums, sums_back = tables
    low = jax.ShapeDtypeStruct((rows, features), jnp.bfloat16)
    full = pltpu.VMEM((rows, features), jnp.float32)
    return pl.pallas_call(
        functools.partial(recurrence_backward, count, mp_count, chunks, pairs),
        out_shape=(
            low,
            low,
            low,
            low,
            jax.ShapeDtypeStruct((rows, features), jnp.float32),
            jax.ShapeDtypeStruct((8, features), jnp.float32),
            jax.ShapeDtypeStruct(residual.shape, jnp.bfloat16),
        ),
        in_specs=[whole_array] * 20,
        out_specs=(whole_array,) * 7,
        scratch_shapes=[
            pltpu.VMEM((slots, sums.shape[0], PAIR), jnp.float32),
            pltpu.VMEM((slots, PAIR, PAIR), jnp.float32),
            pltpu.VMEM((LANE_SPAN, features), jnp.float32),
            full,
            full,
            full,
            full,
            full,
            pltpu.VMEM(((LEVELS - 1) * CHUNK, PAIR), jnp.float32),
        ]
        + exchange_scratch(count, features)
        + [pltpu.VMEM((mp_count,) + residual.shape[:1] + (features,), jnp.bfloat16)]
        + [
            pltpu.SemaphoreType.DMA((mp_count - 1,)),
            pltpu.SemaphoreType.DMA((mp_count - 1,)),
        ],
        compiler_params=pltpu.CompilerParams(
            collective_id=2, has_side_effects=True, vmem_limit_bytes=52 << 20
        ),
        name="recurrence_backward",
    )(
        dgated, wkv, states, kept, rec, key, val, gpre, logw, vec, *marks, level, sums, sums_back,
        change, residual,
    )


def flipped(index, mask):
    for bit in range(mask.bit_length()):
        size = 1 << bit
        if mask & size:
            index = index + size - 2 * size * lax.rem(index // size, 2)
    return index


def masks_over(bits):
    masks = [0]
    for bit in bits:
        masks = masks + [mask | (1 << bit) for mask in masks]
    return masks


def paths(count):
    higher = list(range(1, count.bit_length() - 1))
    return higher + [0], higher[::-1] + [0]


def remote(source, target, send_sem, recv_sem, dp, mp):
    return pltpu.make_async_remote_copy(
        src_ref=source,
        dst_ref=target,
        send_sem=send_sem,
        recv_sem=recv_sem,
        device_id=(dp, mp),
        device_id_type=MESH,
    )


def greet_all(partners, some=()):
    barrier = pltpu.get_barrier_semaphore()
    count = len(partners)
    for dp, mp in partners:
        pl.semaphore_signal(barrier, inc=1, device_id=(dp, mp), device_id_type=MESH)
    for present, dp, mp in some:

        @pl.when(present)
        def _():
            pl.semaphore_signal(barrier, inc=1, device_id=(dp, mp), device_id_type=MESH)

        count = count + jnp.where(present, 1, 0)
    pl.semaphore_wait(barrier, count)


class Halo:
    def __init__(self, dp_count, mp_count, send_sems, recv_sem):
        self.dp, self.mp = lax.axis_index("dp"), lax.axis_index("mp")
        self.count, self.lines = dp_count, mp_count
        self.send_sems, self.recv_sem = send_sems, recv_sem
        self.after = lax.rem(self.dp + 1, dp_count)
        self.previous = lax.rem(self.dp + dp_count - 1, dp_count)
        self.takes = self.dp > 0
        self.gives = jnp.logical_and(self.mp == mp_count - 1, self.dp < dp_count - 1)

    def partners(self):
        return [(self.takes, self.previous, self.lines - 1)] + [
            (self.gives, self.after, line) for line in range(self.lines)
        ]

    def copy(self, source, target, line):
        return remote(source, target, self.send_sems.at[line], self.recv_sem, self.after, line)

    def start(self, source, target):
        @pl.when(self.dp == 0)
        def _():
            target[...] = jnp.zeros(target.shape, target.dtype)

        @pl.when(self.gives)
        def _():
            for line in range(self.lines):
                self.copy(source, target, line).start()

    def finish(self, source, target):
        @pl.when(self.takes)
        def _():
            self.copy(source, target, 0).wait_recv()

        @pl.when(self.gives)
        def _():
            for line in range(self.lines):
                self.copy(source, target, line).wait_send()


class Arrival:
    def __init__(self, dp_count, send_sem, recv_sem):
        self.dp, self.mp = lax.axis_index("dp"), lax.axis_index("mp")
        self.send_sem, self.recv_sem = send_sem, recv_sem
        self.after = lax.rem(self.dp + 1, dp_count)
        self.previous = lax.rem(self.dp + dp_count - 1, dp_count)
        self.gives, self.takes = self.dp > 0, self.dp < dp_count - 1

    def partners(self):
        return [(self.gives, self.previous, self.mp), (self.takes, self.after, self.mp)]

    def copy(self, row, land):
        return remote(row, land, self.send_sem, self.recv_sem, self.previous, self.mp)

    def start(self, row, land):
        @pl.when(self.gives)
        def _():
            self.copy(row, land).start()

        @pl.when(jnp.logical_not(self.takes))
        def _():
            land[...] = jnp.zeros(land.shape, land.dtype)

    def wait(self, row, land):
        @pl.when(self.takes)
        def _():
            self.copy(row, land).wait_recv()

    def finish(self, row, land):
        @pl.when(self.gives)
        def _():
            self.copy(row, land).wait_send()


def line_partners(count):
    dp, mp = lax.axis_index("dp"), lax.axis_index("mp")
    return [(dp, lax.rem(mp + step, count)) for step in sorted({1, count - 1})]


def cube_partners(count):
    dp, mp = lax.axis_index("dp"), lax.axis_index("mp")
    return [(flipped(dp, 1 << bit), mp) for bit in range(count.bit_length() - 1)]


class Line:
    def __init__(self, count, rows, send_sems, recv_sems):
        self.count, self.rows = count, rows
        self.send_sems, self.recv_sems = send_sems, recv_sems
        self.dp, self.me = lax.axis_index("dp"), lax.axis_index("mp")
        self.piece = rows // PIECES

    def at(self, block, piece):
        return pl.ds(pl.multiple_of(block * self.rows + piece * self.piece, 16), self.piece)

    def copy(self, source, target, right, slot, piece):
        side = 0 if right else 1
        return remote(
            source,
            target,
            self.send_sems.at[side, slot, piece],
            self.recv_sems.at[side, slot, piece],
            self.dp,
            lax.rem(self.me + (1 if right else self.count - 1), self.count),
        )


class LineGather(Line):
    def hop(self, target, distance, piece, right):
        block = self.me - distance if right else self.me + distance
        ref = target.at[self.at(block, piece)]
        return self.copy(ref, ref, right, distance, piece)

    def holds(self, distance, right):
        return self.me >= distance if right else self.me + distance < self.count

    def passes(self, distance, right):
        onward = self.me < self.count - 1 if right else self.me > 0
        return jnp.logical_and(self.holds(distance, right), onward)

    def send(self, target, distance, piece):
        for right in (True, False):
            if distance:

                @pl.when(self.holds(distance, right))
                def _():
                    block = self.me - distance if right else self.me + distance
                    ref = target.at[self.at(block, piece)]
                    self.copy(ref, ref, right, distance - 1, piece).wait_recv()

            if distance < self.count - 1:

                @pl.when(self.passes(distance, right))
                def _():
                    self.hop(target, distance, piece, right).start()

    def finish(self, target):
        for distance in range(self.count - 1):
            for piece in range(PIECES):
                for right in (True, False):

                    @pl.when(self.passes(distance, right))
                    def _():
                        self.hop(target, distance, piece, right).wait_send()


class LineSum(Line):
    def hop(self, source, land, block, piece, right):
        return self.copy(
            source.at[self.at(block, piece)],
            land.at[0 if right else 1, self.at(block, piece)],
            right,
            block,
            piece,
        )

    def own(self, part, extra, block, piece):
        value = part[self.at(block, piece)].astype(jnp.float32)
        if extra is not None and piece == PIECES - 1:
            row = lax.broadcasted_iota(jnp.int32, value.shape, 0)
            last = jnp.logical_and(row == self.piece - 1, block == self.count - 1)
            value = value + jnp.where(last, extra[:1], 0.0)
        return value

    def begin(self, part, extra, moving, land, number, ready=None):
        for piece in range(PIECES):
            if ready is not None and piece == PIECES - 1:
                ready()
            for right in (True, False):
                block = self.count - 1 - number if right else number
                at = self.at(block, piece)

                @pl.when(self.me == (0 if right else self.count - 1))
                def _():
                    moving[at] = self.own(part, extra, block, piece).astype(jnp.bfloat16)
                    if number:
                        before = block + 1 if right else block - 1
                        self.hop(moving, land, before, piece, right).wait_send()
                    self.hop(moving, land, block, piece, right).start()

    def forward(self, part, extra, moving, land, block, piece, right):
        side = 0 if right else 1
        at = self.at(block, piece)
        inside = jnp.logical_and(self.me > 0, self.me < self.count - 1)

        @pl.when(jnp.logical_and(inside, self.me < block if right else self.me > block))
        def _():
            self.hop(moving, land, block, piece, right).wait_recv()
            moving[at] = (
                self.own(part, extra, block, piece) + land[side, at].astype(jnp.float32)
            ).astype(jnp.bfloat16)
            self.hop(moving, land, block, piece, right).start()

    def step(self, part, extra, moving, land, number):
        for piece in range(PIECES):
            self.forward(part, extra, moving, land, self.count - 1 - number, piece, True)
            self.forward(part, extra, moving, land, number, piece, False)

    def total(self, part, extra, moving, land, total, piece):
        at = self.at(self.me, piece)
        own = slice(piece * self.piece, (piece + 1) * self.piece)
        total[own] = self.own(part, extra, self.me, piece)
        for right in (True, False):

            @pl.when(self.me > 0 if right else self.me < self.count - 1)
            def _():
                self.hop(moving, land, self.me, piece, right).wait_recv()
                total[own] += land[0 if right else 1, at].astype(jnp.float32)

        return own

    def finish(self, moving, land):
        inside = jnp.logical_and(self.me > 0, self.me < self.count - 1)
        for number in range(self.count - 1):
            for piece in range(PIECES):
                for right in (True, False):
                    block = self.count - 1 - number if right else number
                    sent = jnp.logical_and(inside, self.me < block if right else self.me > block)
                    if number == self.count - 2:
                        sent = jnp.logical_or(sent, self.me == (0 if right else self.count - 1))

                    @pl.when(sent)
                    def _():
                        self.hop(moving, land, block, piece, right).wait_send()


class Cube:
    def __init__(self, count, send_sems, recv_sems):
        self.count, self.send_sems, self.recv_sems = count, send_sems, recv_sems
        self.dp, self.mp = lax.axis_index("dp"), lax.axis_index("mp")
        self.stages = count.bit_length() - 1

    def copy(self, source, target, unit, mask, bit):
        return remote(
            source,
            target,
            self.send_sems.at[unit, mask],
            self.recv_sems.at[unit, mask],
            flipped(self.dp, 1 << bit),
            self.mp,
        )


class CubeGather(Cube):
    def hop(self, unit, view, mask, bit):
        ref = view(flipped(self.dp, mask))
        return self.copy(ref, ref, unit, mask | (1 << bit), bit)

    def arrived(self, unit, view, mask, bit):
        ref = view(flipped(self.dp, mask))
        self.copy(ref, ref, unit, mask, bit).wait_recv()

    def stage(self, unit, path, view, stage):
        order = paths(self.count)[path]
        last = self.stages - 1
        if stage > last:
            for mask in masks_over(order[:last]):
                self.arrived(unit, view, mask | (1 << order[last]), order[last])
            return
        new = [0]
        if stage:
            new = [mask | (1 << order[stage - 1]) for mask in masks_over(order[: stage - 1])]
            for mask in new:
                self.arrived(unit, view, mask, order[stage - 1])
        if stage < last:
            for mask in masks_over(order[:stage]):
                self.hop(unit, view, mask, order[stage]).start()
        for mask in new:
            self.hop(unit, view, mask, order[last]).start()

    def finish(self, unit, path, view):
        order = paths(self.count)[path]
        for stage in range(self.stages):
            for mask in masks_over(order[:stage]):
                self.hop(unit, view, mask, order[stage]).wait_send()


class CubeSum(Cube):
    def slot(self, order, stage, mask):
        base = self.count - (self.count >> stage)
        return base + masks_over(order[stage + 1 :]).index(mask)

    def source(self, unit, order, view, land, stage, mask):
        if stage == 0:
            return view(flipped(self.dp, mask))
        return land.at[self.slot(order, stage - 1, mask)]

    def sends(self, unit, path, view, land, stage):
        order = paths(self.count)[path][::-1]
        bit = order[stage]
        return [
            self.copy(
                self.source(unit, order, view, land, stage, mask | (1 << bit)),
                land.at[self.slot(order, stage, mask)],
                unit,
                mask | (1 << bit),
                bit,
            )
            for mask in masks_over(order[stage + 1 :])
        ]

    def start(self, unit, path, view, land, stage):
        for copy in self.sends(unit, path, view, land, stage):
            copy.start()

    def absorb(self, unit, path, view, land, stage, out=None):
        order = paths(self.count)[path][::-1]
        for copy, mask in zip(
            self.sends(unit, path, view, land, stage), masks_over(order[stage + 1 :])
        ):
            copy.wait_recv()
            before = self.source(unit, order, view, land, stage, mask)
            here = land.at[self.slot(order, stage, mask)]
            step = 16

            def add(number, carry):
                at = pl.ds(pl.multiple_of(number * step, step), step)
                both = before[at].astype(jnp.float32) + here[at].astype(jnp.float32)
                if out is None:
                    here[at] = both.astype(jnp.bfloat16)
                else:
                    out[at] = both
                return carry

            lax.fori_loop(0, here.shape[0] // step, add, 0)

    def finish(self, unit, path, view, land):
        for stage in range(self.stages):
            for copy in self.sends(unit, path, view, land, stage):
                copy.wait_send()


def line_sems(count):
    return [pltpu.SemaphoreType.DMA((2, count, PIECES)), pltpu.SemaphoreType.DMA((2, count, PIECES))]


def cube_sems(units, count):
    return [pltpu.SemaphoreType.DMA((units, count)), pltpu.SemaphoreType.DMA((units, count))]


def start_kernel(
    dp_count, mp_count, tokens, pack, mix_state, out_state, gate_state, key_state, value_state,
    tokens_all, small, mix_all, out_low, gate_low, key_low, value_low, before,
    mix, mix_full, out_full, gate_full, key_full, value_full,
    load_sems, own_sems, line_send, line_recv, pack_send, pack_recv, cube_send, cube_recv,
    halo_send, halo_recv,
):
    dp, mp = lax.axis_index("dp"), lax.axis_index("mp")
    rows = tokens.shape[0]
    halo = Halo(dp_count, mp_count, halo_send, halo_recv)
    edge = tokens.at[pl.ds(rows - 16, 16)]
    matrices, block = mix.shape[0], mix.shape[1]
    pack_rows, group = pack.shape[0], pack.shape[0] * mp_count
    half = group // 2
    states = (mix_state, out_state, gate_state, key_state, value_state)
    fulls = (mix_full, out_full, gate_full, key_full, value_full)
    loads = [
        pltpu.make_async_copy(state.at[0], full, load_sems.at[number])
        for number, (state, full) in enumerate(zip(states, fulls))
    ]
    for load in loads:
        load.start()
    others = [lax.rem(mp + step, mp_count) for step in range(1, mp_count)]
    greet_all([(dp, other) for other in others] + cube_partners(dp_count), halo.partners())
    halo.start(edge, before)
    line = LineGather(mp_count, rows, line_send, line_recv)
    cube = CubeGather(dp_count, cube_send, cube_recv)

    pack_at = small.at[pl.ds(pl.multiple_of(dp * group + mp * pack_rows, 16), pack_rows)]
    own = [
        pltpu.make_async_copy(pack, pack_at, own_sems.at[0]),
        pltpu.make_async_copy(
            tokens, tokens_all.at[pl.ds(pl.multiple_of(mp * rows, 16), rows)], own_sems.at[1]
        ),
    ]
    pack_copies = [
        remote(pack, pack_at, pack_send.at[step], pack_recv.at[step], dp, other)
        for step, other in enumerate(others)
    ]
    for copy in pack_copies + own:
        copy.start()
    loads[0].wait()
    for number in range(matrices):
        mix[number] = mix_full[number].astype(jnp.bfloat16)
    own_mix = [
        pltpu.make_async_copy(
            mix.at[number],
            mix_all.at[number, pl.ds(pl.multiple_of(dp * block, 16), block)],
            own_sems.at[2 + number],
        )
        for number in range(matrices)
    ]
    for copy in own_mix:
        copy.start()

    def small_view(part):
        def view(index):
            return small.at[pl.ds(pl.multiple_of(index * group + part * half, 16), half)]

        return view

    def mix_view(number):
        def view(index):
            return mix_all.at[number, pl.ds(pl.multiple_of(index * block, 16), block)]

        return view

    mix_units = [
        (2 + number, 0 if 2 * number < matrices else 1, mix_view(number))
        for number in range(matrices)
    ]
    small_units = [(part, part, small_view(part)) for part in range(2)]
    for copy in own + own_mix:
        copy.wait()
    for unit in mix_units:
        cube.stage(*unit, 0)
    for piece in range(PIECES):
        line.send(tokens_all, 0, piece)
    for load, full, low in zip(loads[1:], fulls[1:], (out_low, gate_low, key_low, value_low)):
        load.wait()
        step = 64

        def convert(number, carry):
            at = pl.ds(pl.multiple_of(number * step, step), step)
            low[at] = full[at].astype(jnp.bfloat16)
            return carry

        lax.fori_loop(0, full.shape[0] // step, convert, 0)
    for copy in pack_copies:
        copy.wait()
    for unit in small_units:
        cube.stage(*unit, 0)
    for distance in range(1, mp_count):
        for piece in range(PIECES):
            line.send(tokens_all, distance, piece)
        if distance < dp_count.bit_length() - 1:
            for unit in mix_units + small_units:
                cube.stage(*unit, distance)
    for stage in range(min(mp_count, dp_count.bit_length() - 1), dp_count.bit_length()):
        for unit in mix_units + small_units:
            cube.stage(*unit, stage)
    line.finish(tokens_all)
    halo.finish(edge, before)
    for unit in mix_units + small_units:
        cube.finish(*unit)


def run_start(dp_count, mp_count, tokens, pack, states):
    rows, width = tokens.shape
    matrices, block, features = states[0].shape[1:]
    anywhere = pl.BlockSpec(memory_space=pl.ANY)
    vmem = pl.BlockSpec(memory_space=pltpu.VMEM)
    bfloat = jnp.bfloat16
    return pl.pallas_call(
        functools.partial(start_kernel, dp_count, mp_count),
        out_shape=(
            jax.ShapeDtypeStruct((rows * mp_count, width), bfloat),
            jax.ShapeDtypeStruct((pack.shape[0] * mp_count * dp_count, pack.shape[1]), bfloat),
            jax.ShapeDtypeStruct((matrices, block * dp_count, features), bfloat),
            *[jax.ShapeDtypeStruct(state.shape[1:], bfloat) for state in states[1:]],
            jax.ShapeDtypeStruct((16, width), bfloat),
        ),
        in_specs=[vmem, vmem] + [anywhere] * 5,
        out_specs=(anywhere,) * 3 + (vmem,) * 5,
        scratch_shapes=[
            pltpu.VMEM(states[0].shape[1:], bfloat),
            *[pltpu.VMEM(state.shape[1:], jnp.float32) for state in states],
            pltpu.SemaphoreType.DMA((5,)),
            pltpu.SemaphoreType.DMA((2 + matrices,)),
            *line_sems(mp_count),
            pltpu.SemaphoreType.DMA((mp_count - 1,)),
            pltpu.SemaphoreType.DMA((mp_count - 1,)),
            *cube_sems(2 + matrices, dp_count),
            pltpu.SemaphoreType.DMA((mp_count,)),
            pltpu.SemaphoreType.DMA,
        ],
        compiler_params=pltpu.CompilerParams(
            collective_id=3, has_side_effects=True, vmem_limit_bytes=60 << 20
        ),
        name="gather_start",
    )(tokens, pack, *states)


def backward_rows(total, rows, source, gain, skip):
    value = source[rows].astype(jnp.float32)
    centre = value - jnp.mean(value, -1, keepdims=True)
    inverse = lax.rsqrt(jnp.mean(centre * centre, -1, keepdims=True) + norm_epsilon)
    return skip[rows].astype(jnp.float32) + norm_backward(total, centre * inverse, inverse, gain[:1])


def exchange_kernel(
    dp_count, count, part, first, source, gain, skip,
    own, gathered,
    moving, land, total, edge,
    sum_send, sum_recv, line_send, line_recv, row_send, row_recv,
):
    rows = own.shape[0]
    arrival = Arrival(dp_count, row_send, row_recv)
    greet_all(line_partners(count), arrival.partners())
    arrival.start(first, edge)
    adder = LineSum(count, rows, sum_send, sum_recv)
    line = LineGather(count, rows, line_send, line_recv)
    for number in range(count - 1):
        ready = None if number else lambda: arrival.wait(first, edge)
        adder.begin(part, edge, moving, land, number, ready)
        adder.step(part, edge, moving, land, number)
    for piece in range(PIECES):
        at = adder.total(part, edge, moving, land, total, piece)
        value = backward_rows(total[at], at, source, gain, skip)
        own[at] = value
        gathered[line.at(line.me, piece)] = value.astype(jnp.bfloat16)
        line.send(gathered, 0, piece)
    for distance in range(1, count):
        for piece in range(PIECES):
            line.send(gathered, distance, piece)
    adder.finish(moving, land)
    line.finish(gathered)
    arrival.finish(first, edge)


def run_exchange(dp_count, count, part, first, source, gain, skip):
    rows, width = part.shape[0] // count, part.shape[1]
    vmem = pl.BlockSpec(memory_space=pltpu.VMEM)
    return pl.pallas_call(
        functools.partial(exchange_kernel, dp_count, count),
        out_shape=(
            jax.ShapeDtypeStruct((rows, width), jnp.float32),
            jax.ShapeDtypeStruct(part.shape, jnp.bfloat16),
        ),
        in_specs=[vmem] * 5,
        out_specs=(vmem, vmem),
        scratch_shapes=[
            pltpu.VMEM(part.shape, jnp.bfloat16),
            pltpu.VMEM((2,) + part.shape, jnp.bfloat16),
            pltpu.VMEM((rows, width), jnp.float32),
            pltpu.VMEM((8, width), jnp.float32),
            *line_sems(count),
            *line_sems(count),
            pltpu.SemaphoreType.DMA,
            pltpu.SemaphoreType.DMA,
        ],
        compiler_params=pltpu.CompilerParams(
            collective_id=5, has_side_effects=True, vmem_limit_bytes=40 << 20
        ),
        name="sum_and_gather",
    )(part, first, source, gain, skip)


def end_kernel(
    dp_count, mp_count, part, first, source, gain, skip, mix_a, mix_b, mix_c, mix_d, pack,
    own, mix_sum, pack_sum,
    moving, land, total, mix_land, pack_land, pack_own, pack_out, small_land,
    edge, sum_send, sum_recv, cube_send, cube_recv, small_send, small_recv, row_send, row_recv,
):
    dp, mp = lax.axis_index("dp"), lax.axis_index("mp")
    mix = (mix_a, mix_b, mix_c, mix_d)
    rows, matrices = own.shape[0], len(mix)
    block, group = mix_sum.shape[1], pack_own.shape[0]
    half, pack_rows = group // 2, pack_sum.shape[0]
    others = [lax.rem(mp + step, mp_count) for step in range(1, mp_count)]
    arrival = Arrival(dp_count, row_send, row_recv)
    greet_all([(dp, other) for other in others] + cube_partners(dp_count), arrival.partners())
    arrival.start(first, edge)
    adder = LineSum(mp_count, rows, sum_send, sum_recv)
    cube = CubeSum(dp_count, cube_send, cube_recv)

    def mix_view(number):
        def view(index):
            return mix[number].at[pl.ds(pl.multiple_of(index * block, 16), block)]

        return view

    def pack_view(side):
        def view(index):
            return pack.at[pl.ds(pl.multiple_of(index * group + side * half, 16), half)]

        return view

    units = [(side, side, pack_view(side), pack_land.at[side]) for side in range(2)] + [
        (2 + number, 0 if 2 * number < matrices else 1, mix_view(number), mix_land.at[number])
        for number in range(matrices)
    ]
    outs = [pack_own.at[pl.ds(side * half, half)] for side in range(2)] + [
        mix_sum.at[number] for number in range(matrices)
    ]
    for unit in units:
        cube.start(*unit, 0)
    adder.begin(part, edge, moving, land, 0, lambda: arrival.wait(first, edge))
    last = cube.stages - 1
    for unit in units:
        cube.absorb(*unit, 0)
        cube.start(*unit, 1)
    for number in range(1, mp_count - 1):
        adder.begin(part, edge, moving, land, number)
        adder.step(part, edge, moving, land, number - 1)
    adder.step(part, edge, moving, land, mp_count - 2)
    for piece in range(PIECES):
        at = adder.total(part, edge, moving, land, total, piece)
        own[at] = backward_rows(total[at], at, source, gain, skip)
    for stage in range(1, last):
        for unit in units:
            cube.absorb(*unit, stage)
            cube.start(*unit, stage + 1)
    for unit, out in zip(units[:2], outs[:2]):
        cube.absorb(*unit, last, out)
    pack_out[...] = pack_own[...].astype(jnp.bfloat16)
    small_copies = [
        remote(
            pack_out.at[pl.ds(pl.multiple_of(other * pack_rows, 16), pack_rows)],
            small_land.at[step],
            small_send.at[step],
            small_recv.at[step],
            dp,
            other,
        )
        for step, other in enumerate(others)
    ]
    for copy in small_copies:
        copy.start()
    for unit, out in zip(units[2:], outs[2:]):
        cube.absorb(*unit, last, out)
    pack_sum[...] = pack_own[pl.ds(pl.multiple_of(mp * pack_rows, 16), pack_rows), :]
    for step, copy in enumerate(small_copies):
        copy.wait()
        pack_sum[...] += small_land[step].astype(jnp.float32)
    adder.finish(moving, land)
    arrival.finish(first, edge)
    for unit in units:
        cube.finish(*unit)


def run_end(dp_count, mp_count, part, first, source, gain, skip, mix, pack):
    rows, width = source.shape
    matrices, features = len(mix), mix[0].shape[1]
    block, group = mix[0].shape[0] // dp_count, pack.shape[0] // dp_count
    lanes = pack.shape[1]
    vmem = pl.BlockSpec(memory_space=pltpu.VMEM)
    return pl.pallas_call(
        functools.partial(end_kernel, dp_count, mp_count),
        out_shape=(
            jax.ShapeDtypeStruct((rows, width), jnp.float32),
            jax.ShapeDtypeStruct((matrices, block, features), jnp.float32),
            jax.ShapeDtypeStruct((group // mp_count, lanes), jnp.float32),
        ),
        in_specs=[vmem] * 10,
        out_specs=(vmem,) * 3,
        scratch_shapes=[
            pltpu.VMEM(part.shape, jnp.bfloat16),
            pltpu.VMEM((2,) + part.shape, jnp.bfloat16),
            pltpu.VMEM((rows, width), jnp.float32),
            pltpu.VMEM((matrices, dp_count - 1, block, features), jnp.bfloat16),
            pltpu.VMEM((2, dp_count - 1, group // 2, lanes), jnp.bfloat16),
            pltpu.VMEM((group, lanes), jnp.float32),
            pltpu.VMEM((group, lanes), jnp.bfloat16),
            pltpu.VMEM((mp_count - 1, group // mp_count, lanes), jnp.bfloat16),
            pltpu.VMEM((8, width), jnp.float32),
            *line_sems(mp_count),
            *cube_sems(2 + matrices, dp_count),
            pltpu.SemaphoreType.DMA((mp_count - 1,)),
            pltpu.SemaphoreType.DMA((mp_count - 1,)),
            pltpu.SemaphoreType.DMA,
            pltpu.SemaphoreType.DMA,
        ],
        compiler_params=pltpu.CompilerParams(
            collective_id=6, has_side_effects=True, vmem_limit_bytes=56 << 20
        ),
        name="sum_end",
    )(part, first, source, gain, skip, *mix, pack)


def update_rows(rate, state, grad, new):
    scaled = rate * grad[...].astype(jnp.float32)
    velocity = momentum_rate * state[1] + scaled
    weight = state[0] - (scaled + momentum_rate * velocity)
    new[0] = velocity
    new[1] = weight
    new[2] = average_rate * state[2] + (1.0 - average_rate) * weight


def run_update(state, grad, fan, total_tokens):
    shape = state.shape
    lanes = shape[-1]
    flat = state.reshape(3, -1, lanes)
    grad = grad.reshape(-1, lanes)
    block = 128
    while grad.shape[0] % (2 * block) == 0 and 2 * block * lanes <= 1 << 18:
        block *= 2
    triple = pl.BlockSpec((3, block, lanes), lambda i: (0, i, 0))
    return pl.pallas_call(
        functools.partial(update_rows, (total_tokens * fan) ** (-0.5)),
        grid=(grad.shape[0] // block,),
        out_shape=jax.ShapeDtypeStruct(flat.shape, jnp.float32),
        in_specs=[triple, pl.BlockSpec((block, lanes), lambda i: (i, 0))],
        out_specs=triple,
        compiler_params=pltpu.CompilerParams(vmem_limit_bytes=24 << 20),
        name="momentum_update",
    )(flat, grad).reshape(shape)


def lane_mask(shape, low, high):
    lane = lax.broadcasted_iota(jnp.int32, shape, len(shape) - 1)
    return jnp.logical_and(lane >= low, lane < high)


def masked(value, low, high):
    return jnp.where(lane_mask(value.shape, low, high), value, jnp.zeros_like(value))


def block_norm(value, vectors):
    hidden, hat, _ = norm_forward(value.astype(jnp.float32), vectors[0:1], vectors[1:2], norm_epsilon)
    return hidden, hat


def block_delta(hidden, before, keep):
    row = lax.broadcasted_iota(jnp.int32, hidden.shape, 0)
    behind = jnp.where(row == 0, before, pltpu.roll(hidden, 1, 0))
    return behind * keep - hidden


def mixing_forward(
    tokens, heads, keep, small, vectors, decay_row, up_own, mix, inputs, rec, key, val, gpre, logw, acts
):
    bfloat = jnp.bfloat16
    maa_cols = 5 * TM_RANK
    down_cols = maa_cols + DECAY_RANK
    hidden, _ = block_norm(tokens[...], vectors)
    before, _ = block_norm(heads[0], vectors)
    delta = block_delta(hidden, before[:1], keep[:, :1])
    base = (hidden + delta * vectors[2:3]).astype(bfloat)
    act = jnp.tanh(dot_nn(base, small[:, :WINDOW]))
    act_low = act.astype(bfloat)
    for number in range(5):
        mine = masked(act_low, TM_RANK * number, TM_RANK * (number + 1))
        scale = vectors[3 + number : 4 + number] + dot_nt(mine, small[:, WINDOW:])
        value = (hidden + delta * scale).astype(bfloat)
        inputs[number] = value
        if number:
            place = {1: 1, 2: 2, 3: 0, 4: 3}[number]
            (rec, key, val, gpre)[place][...] = dot_nn(value, mix[place])
        else:
            decay = masked(jnp.tanh(dot_nn(value, small[:, :WINDOW])), maa_cols, down_cols)
            logw[...] = -jnp.exp(decay_row[:1] + dot_nt(decay.astype(bfloat), up_own[...]))
    acts[...] = masked(act, 0, maa_cols) + decay


def run_mixing_forward(tokens, heads, keep, small, vectors, decay_row, up_own, mix):
    rows, width = tokens.shape
    features = mix.shape[2]
    block = lambda lanes: pl.BlockSpec((ROW_BLOCK, lanes), lambda i: (i, 0))
    fixed = lambda value: pl.BlockSpec(
        value.shape, lambda i: (0,) * value.ndim, pipeline_mode=pl.Buffered(1)
    )
    stack = lambda count, lanes: pl.BlockSpec((count, ROW_BLOCK, lanes), lambda i: (0, i, 0))
    return pl.pallas_call(
        mixing_forward,
        grid=(rows // ROW_BLOCK,),
        out_shape=(
            jax.ShapeDtypeStruct((5, rows, width), jnp.bfloat16),
            *[jax.ShapeDtypeStruct((rows, features), jnp.float32)] * 5,
            jax.ShapeDtypeStruct((rows, WINDOW), jnp.float32),
        ),
        in_specs=[
            block(width),
            pl.BlockSpec((1,) + heads.shape[1:], lambda i: (i, 0, 0)),
            block(keep.shape[1]),
            fixed(small),
            fixed(vectors),
            fixed(decay_row),
            fixed(up_own),
            fixed(mix),
        ],
        out_specs=(stack(5, width), *[block(features)] * 5, block(WINDOW)),
        compiler_params=pltpu.CompilerParams(vmem_limit_bytes=58 << 20),
        name="mixing_forward",
    )(tokens, heads, keep, small, vectors, decay_row, up_own, mix)


def mixing_backward(
    tokens, heads, keep, acts, drec, dkey, dval, dgate, draw,
    small, vectors, up_own, mix, given,
    grad_hidden, grad_pack, first_row,
    grad_down, grad_up, grad_vec, carried,
):
    bfloat = jnp.bfloat16
    step, last = pl.program_id(0), pl.num_programs(0) - 1
    maa_cols = 5 * TM_RANK
    down_cols = maa_cols + DECAY_RANK
    features = mix.shape[2]
    col_start = pl.multiple_of(lax.axis_index("mp") * features, 128)

    @pl.when(step == 0)
    def _():
        grad_down[...] = jnp.zeros(grad_down.shape, jnp.float32)
        grad_up[...] = jnp.zeros(grad_up.shape, jnp.float32)
        grad_vec[...] = given[...]
        carried[...] = jnp.zeros(carried.shape, jnp.float32)

    down, upper = small.at[:, :WINDOW], small.at[:, WINDOW:]
    hidden, hat = block_norm(tokens[...], vectors)
    before, before_hat = block_norm(heads[0], vectors)
    delta = block_delta(hidden, before[:1], keep[:, :1])
    act = acts[...]
    act_low = act.astype(bfloat)
    slope = 1.0 - act * act
    raw = draw[...].astype(bfloat)
    grad_decay = masked(dot_nn(raw, up_own[...]) * slope, maa_cols, down_cols).astype(bfloat)
    grad_up[pl.ds(col_start, features), :] += dot_tn(raw, masked(act_low, maa_cols, down_cols))

    def add_row(row, value):
        grad_vec[row : row + 1, :] += jnp.sum(value, 0, keepdims=True)

    total = jnp.zeros(hidden.shape, jnp.float32)
    grad_delta = jnp.zeros(hidden.shape, jnp.float32)
    grad_act = jnp.zeros(act.shape, jnp.float32)
    for number in range(5):
        low, high = TM_RANK * number, TM_RANK * (number + 1)
        mine = masked(act_low, low, high)
        scale = vectors[3 + number : 4 + number] + dot_nt(mine, upper[...])
        if number:
            source = {1: dkey, 2: dval, 3: drec, 4: dgate}[number]
            grad_input = dot_nt(source[...], mix[{1: 1, 2: 2, 3: 0, 4: 3}[number]])
        else:
            grad_input = dot_nt(grad_decay, down[...])
            value = (hidden + delta * scale).astype(bfloat)
            grad_down[...] += dot_tn(value, grad_decay)
        moved = grad_input * delta
        add_row(3 + number, moved)
        moved_low = moved.astype(bfloat)
        grad_up[...] += dot_tn(moved_low, mine)
        grad_act += masked(dot_nn(moved_low, upper[...]), low, high)
        grad_delta += grad_input * scale
        total += grad_input
    grad_pre = (grad_act * slope).astype(bfloat)
    base = (hidden + delta * vectors[2:3]).astype(bfloat)
    grad_down[...] += dot_tn(base, grad_pre)
    grad_base = dot_nt(grad_pre, down[...])
    add_row(2, grad_base * delta)
    grad_delta += grad_base * vectors[2:3]
    shifted_grad = grad_delta * keep[:, :1]
    row = lax.broadcasted_iota(jnp.int32, hidden.shape, 0)
    back = jnp.where(
        row == ROW_BLOCK - 1, carried[:1], pltpu.roll(shifted_grad, ROW_BLOCK - 1, 0)
    )
    carried[...] = jnp.broadcast_to(shifted_grad[:1], carried.shape)
    total += grad_base - grad_delta + back
    add_row(0, total * hat)
    add_row(1, total)
    grad_hidden[...] = total.astype(bfloat)

    @pl.when(step == last)
    def _():
        first_row[...] = carried[...]
        add_row(0, carried[:1] * before_hat[:1])
        add_row(1, carried[:1])
        spot = lax.broadcasted_iota(jnp.int32, (16, WINDOW), 0) + down_cols
        lane = lax.broadcasted_iota(jnp.int32, (16, WINDOW), 1)
        one = jnp.where(spot == lane, 1.0, 0.0).astype(bfloat)
        placed = dot_tn(grad_vec[...].astype(bfloat), one)
        grad_pack[:, :WINDOW] = (grad_down[...] + placed).astype(bfloat)
        grad_pack[:, WINDOW:] = grad_up[...].astype(bfloat)


def run_mixing_backward(
    tokens, heads, keep, acts, drec, dkey, dval, dgate, draw, small, vectors, up_own, mix, given
):
    rows, width = tokens.shape
    features = mix.shape[2]
    count = rows // ROW_BLOCK
    block = lambda lanes: pl.BlockSpec((ROW_BLOCK, lanes), lambda i: (count - 1 - i, 0))
    fixed = lambda value: pl.BlockSpec(
        value.shape, lambda i: (0,) * len(value.shape), pipeline_mode=pl.Buffered(1)
    )
    first = jax.ShapeDtypeStruct((8, width), jnp.float32)
    pack = jax.ShapeDtypeStruct((width, 2 * WINDOW), jnp.bfloat16)
    return pl.pallas_call(
        mixing_backward,
        grid=(count,),
        out_shape=(jax.ShapeDtypeStruct((rows, width), jnp.bfloat16), pack, first),
        in_specs=[
            block(width),
            pl.BlockSpec((1,) + heads.shape[1:], lambda i: (count - 1 - i, 0, 0)),
            block(keep.shape[1]),
            block(WINDOW),
            block(features),
            block(features),
            block(features),
            block(features),
            block(features),
            fixed(small),
            fixed(vectors),
            fixed(up_own),
            fixed(mix),
            fixed(given),
        ],
        out_specs=(block(width), fixed(pack), fixed(first)),
        scratch_shapes=[
            pltpu.VMEM((width, WINDOW), jnp.float32),
            pltpu.VMEM((width, WINDOW), jnp.float32),
            pltpu.VMEM((16, width), jnp.float32),
            pltpu.VMEM((8, width), jnp.float32),
        ],
        compiler_params=pltpu.CompilerParams(vmem_limit_bytes=60 << 20),
        name="mixing_backward",
    )(tokens, heads, keep, acts, drec, dkey, dval, dgate, draw, small, vectors, up_own, mix, given)


def channel_forward(
    source, heads, keep, vectors, gate, cotangent, key_in, recv_in, recv_gate, grad_kv
):
    def norm(value):
        return norm_forward(
            value.astype(jnp.float32), vectors[12:13], vectors[13:14], norm_epsilon
        )[0]

    hidden = norm(source[...])
    delta = block_delta(hidden, norm(heads[0])[:1], keep[:, :1])
    key_in[...] = (hidden + delta * vectors[14:15]).astype(jnp.bfloat16)
    recv = (hidden + delta * vectors[15:16]).astype(jnp.bfloat16)
    recv_in[...] = recv
    opened = jax.nn.sigmoid(dot_nn(recv, gate[...]))
    recv_gate[...] = opened
    grad_kv[...] = (cotangent[...].astype(jnp.float32) * opened).astype(jnp.bfloat16)


def run_channel_forward(source, heads, keep, vectors, gate, cotangent):
    rows, width = source.shape
    features = gate.shape[1]
    block = lambda lanes: pl.BlockSpec((ROW_BLOCK, lanes), lambda i: (i, 0))
    fixed = lambda value: pl.BlockSpec(
        value.shape, lambda i: (0,) * len(value.shape), pipeline_mode=pl.Buffered(1)
    )
    low = lambda lanes: jax.ShapeDtypeStruct((rows, lanes), jnp.bfloat16)
    return pl.pallas_call(
        channel_forward,
        grid=(rows // ROW_BLOCK,),
        out_shape=(
            low(width),
            low(width),
            jax.ShapeDtypeStruct((rows, features), jnp.float32),
            low(features),
        ),
        in_specs=[
            block(width),
            pl.BlockSpec((1,) + heads.shape[1:], lambda i: (i, 0, 0)),
            block(keep.shape[1]),
            fixed(vectors),
            fixed(gate),
            block(features),
        ],
        out_specs=(block(width), block(width), block(features), block(features)),
        compiler_params=pltpu.CompilerParams(vmem_limit_bytes=40 << 20),
        name="channel_forward",
    )(source, heads, keep, vectors, gate, cotangent)


def channel_backward(
    source, heads, keep, grad_key, grad_recv, vectors, gate,
    grad_hidden, sums, first_row,
    carried,
):
    step, last = pl.program_id(0), pl.num_programs(0) - 1

    @pl.when(step == 0)
    def _():
        sums[...] = jnp.zeros(sums.shape, jnp.float32)
        carried[...] = jnp.zeros(carried.shape, jnp.float32)

    def norm(value):
        return norm_forward(
            value.astype(jnp.float32), vectors[12:13], vectors[13:14], norm_epsilon
        )[:2]

    def add_row(row, value):
        sums[row : row + 1, :] += jnp.sum(value, 0, keepdims=True)

    hidden, hat = norm(source[...])
    before, before_hat = norm(heads[0])
    delta = block_delta(hidden, before[:1], keep[:, :1])
    grad_recv_in = dot_nt(grad_recv[...], gate[...])
    grad_key_in = grad_key[...]
    grad_delta = grad_key_in * vectors[14:15] + grad_recv_in * vectors[15:16]
    add_row(2, grad_key_in * delta)
    add_row(3, grad_recv_in * delta)
    shifted_grad = grad_delta * keep[:, :1]
    row = lax.broadcasted_iota(jnp.int32, hidden.shape, 0)
    back = jnp.where(
        row == ROW_BLOCK - 1, carried[:1], pltpu.roll(shifted_grad, ROW_BLOCK - 1, 0)
    )
    carried[...] = jnp.broadcast_to(shifted_grad[:1], carried.shape)
    total = grad_key_in + grad_recv_in - grad_delta + back
    add_row(0, total * hat)
    add_row(1, total)
    grad_hidden[...] = total.astype(jnp.bfloat16)

    @pl.when(step == last)
    def _():
        first_row[...] = carried[...]
        add_row(0, carried[:1] * before_hat[:1])
        add_row(1, carried[:1])


def run_channel_backward(source, heads, keep, grad_key, grad_recv, vectors, gate):
    rows, width = source.shape
    count = rows // ROW_BLOCK
    block = lambda lanes: pl.BlockSpec((ROW_BLOCK, lanes), lambda i: (count - 1 - i, 0))
    fixed = lambda value: pl.BlockSpec(
        value.shape, lambda i: (0,) * len(value.shape), pipeline_mode=pl.Buffered(1)
    )
    first = jax.ShapeDtypeStruct((8, width), jnp.float32)
    return pl.pallas_call(
        channel_backward,
        grid=(count,),
        out_shape=(jax.ShapeDtypeStruct((rows, width), jnp.bfloat16), first, first),
        in_specs=[
            block(width),
            pl.BlockSpec((1,) + heads.shape[1:], lambda i: (count - 1 - i, 0, 0)),
            block(keep.shape[1]),
            block(width),
            block(grad_recv.shape[1]),
            fixed(vectors),
            fixed(gate),
        ],
        out_specs=(block(width), fixed(first), fixed(first)),
        scratch_shapes=[pltpu.VMEM((8, width), jnp.float32)],
        compiler_params=pltpu.CompilerParams(vmem_limit_bytes=48 << 20),
        name="channel_backward",
    )(source, heads, keep, grad_key, grad_recv, vectors, gate)


def update(carried_memory, grad, fan, total_tokens):
    rate = (total_tokens * fan) ** (-0.5)
    scaled = rate * grad
    velocity = momentum_rate * carried_memory[1] + scaled
    weight = carried_memory[0] - (scaled + momentum_rate * velocity)
    average = average_rate * carried_memory[2] + (1.0 - average_rate) * weight
    return jnp.stack([velocity, weight, average])


def split_three(value):
    pieces = []
    for _ in range(3):
        pieces.append(lax.reduce_precision(value, 8, 7))
        value = value - pieces[-1]
    return [piece.astype(jnp.bfloat16) for piece in pieces]


def block_heads(before, rows):
    width = rows.shape[1]
    ends = rows.reshape(-1, ROW_BLOCK, width)[:-1, -1]
    heads = jnp.concatenate([before, ends], 0)
    return jnp.broadcast_to(heads[:, None], (heads.shape[0], 16, width))


def body(
    tokens,
    cotangent,
    lengths,
    mix_state,
    out_state,
    key_state,
    value_state,
    gate_state,
    down_state,
    up_state,
    vector_state,
):
    bfloat = jnp.bfloat16
    single = jnp.float32
    dp_count = lax.axis_size("dp")
    mp_count = lax.axis_size("mp")
    dp_index = lax.axis_index("dp")
    mp_index = lax.axis_index("mp")
    own_rows = tokens.shape[0]
    width = tokens.shape[1]
    group_rows = own_rows * mp_count
    total_tokens = group_rows * dp_count
    features = mix_state.shape[3]
    maa_cols = 5 * TM_RANK
    down_cols = maa_cols + DECAY_RANK
    col_start = mp_index * features

    upper, middle, lower = split_three(vector_state[0].T)
    pack = jnp.concatenate(
        [
            down_state[0].astype(bfloat),
            upper,
            middle,
            up_state[0].T.astype(bfloat),
            lower,
            jnp.zeros_like(lower),
        ],
        1,
    )
    states = (mix_state, out_state, gate_state, key_state, value_state)
    tokens_all, small, mix_weight, out_low, gate_low, key_low, value_low, before_one = run_start(
        dp_count, mp_count, tokens, pack, states
    )
    out_weight = lax.all_gather(out_low, "dp", axis=1, tiled=True)
    gate_weight = lax.all_gather(gate_low, "dp", axis=0, tiled=True)
    chosen = np.zeros((16, small.shape[1]), np.float32)
    for start in (down_cols, down_cols + 16, WINDOW + down_cols):
        chosen[np.arange(16), start + np.arange(16)] = 1.0
    vectors = half_right(jnp.asarray(chosen, bfloat), small)

    seq_ends = jnp.cumsum(lengths)
    offsets = seq_ends - lengths
    positions = dp_index * group_rows + jnp.arange(group_rows, dtype=jnp.int32)
    opening = jnp.any(positions[:, None] == offsets[None, :], 1).astype(single)
    segment = jnp.sum((offsets[None, :] <= positions[:, None]).astype(single), 1)
    keep = 1.0 - opening
    chunks = group_rows // CHUNK
    parts = segment.reshape(chunks, CHUNK)
    first = parts[:, :1] - opening.reshape(chunks, CHUNK)[:, :1]

    def spread(value, lanes):
        return jnp.broadcast_to(value.astype(single).reshape(-1, 1), (value.size, lanes))

    marks = (
        spread(parts, 2 * CHUNK),
        jnp.repeat(jnp.concatenate([parts, parts], 1), 8, 0),
        spread(parts == first, PAIR),
        spread(parts == parts[:, -1:], PAIR),
        spread(jnp.repeat(parts[:, -1:] == first, 8, 0), PAIR),
    )
    level, sums, sums_back = level_tables()
    tables = (jnp.asarray(level), jnp.asarray(sums, bfloat), jnp.asarray(sums_back, bfloat))

    def local_share(row_number):
        return lax.dynamic_slice_in_dim(vectors[row_number], col_start, features, 0)

    def spread_row(value):
        return jnp.broadcast_to(value[None], (8, width))

    heads = block_heads(before_one[-1:], tokens_all)
    keep_lanes = spread(keep, PAIR)
    up_own = lax.dynamic_slice_in_dim(small[:, WINDOW:], col_start, features, 0)
    decay_row = jnp.broadcast_to(local_share(8)[None], (8, features))
    inputs_low, *branch, acts = run_mixing_forward(
        tokens_all, heads, keep_lanes, small, vectors, decay_row, up_own, mix_weight
    )
    value_low, branch = lax.optimization_barrier((value_low, branch))
    value_weight = lax.all_gather(value_low, "dp", axis=1, tiled=True)
    local_vectors = jnp.concatenate(
        [jnp.stack([local_share(9), local_share(10), local_share(11)]), jnp.zeros((5, features))], 0
    )
    outcome = run_forward(
        dp_count,
        mp_count,
        *branch,
        local_vectors,
        marks,
        tables,
        cotangent,
        tokens,
        out_weight,
        key_low,
    )
    gated_low, wkv, states, kept, cotangent_cols, residual, *outcome = outcome
    residual_all, before_second, key_weight = outcome
    before_second = before_second[-1:]
    heads_two = block_heads(before_second, residual_all)
    key_in_low, recv_in_low, recv_gate, grad_kv = run_channel_forward(
        residual_all, heads_two, keep_lanes, vectors, gate_weight, cotangent_cols
    )
    cotangent_cols = cotangent_cols.astype(single)
    key_pre = half_dot(key_in_low, key_weight)
    key_act_low = jnp.square(jnp.maximum(key_pre, 0.0)).astype(bfloat)
    grad_kv_all = lax.all_gather(grad_kv, "mp", axis=1, tiled=True)
    channel_sum = lax.psum_scatter(
        half_dot(key_act_low, value_weight).astype(bfloat), "mp", scatter_dimension=1, tiled=True
    ).astype(single)
    gated_sum = recv_gate * channel_sum
    grad_recv_pre = (cotangent_cols * gated_sum * (1.0 - recv_gate)).astype(bfloat)
    grad_key_act = half_right(grad_kv_all, value_weight)
    grad_key_pre = (grad_key_act * 2.0 * jnp.maximum(key_pre, 0.0)).astype(bfloat)
    grad_key_in = half_right(grad_key_pre, key_weight)
    grad_value_weight = half_left(key_act_low, grad_kv_all).astype(bfloat)
    grad_key_weight = half_left(key_in_low, grad_key_pre).astype(bfloat)
    grad_gate_weight = half_left(recv_in_low, grad_recv_pre).astype(bfloat)
    grad_hidden_two, channel_sums, first_row_two = run_channel_backward(
        residual_all,
        heads_two,
        keep_lanes,
        grad_key_in,
        grad_recv_pre,
        vectors,
        gate_weight,
    )
    def summed(value, axis):
        return lax.psum_scatter(value, "dp", scatter_dimension=axis, tiled=True)

    value_sum = summed(grad_value_weight, 1)
    key_sum = summed(grad_key_weight, 0)
    gate_sum = summed(grad_gate_weight, 0)
    grad_residual, grad_attn_all = run_exchange(
        dp_count,
        mp_count,
        grad_hidden_two,
        first_row_two,
        residual.astype(bfloat),
        spread_row(vectors[12]),
        cotangent,
    )
    grad_out_weight = half_left(gated_low, grad_attn_all)
    out_sum = summed(grad_out_weight.astype(bfloat), 1)
    grad_gated = half_right(grad_attn_all, out_weight)
    grad_recept, grad_keys, grad_values, grad_gate_pre, grad_raw, grad_local, mixed = run_backward(
        dp_count,
        mp_count,
        grad_gated,
        wkv,
        states,
        kept,
        *branch,
        local_vectors,
        marks,
        tables,
        gated_sum.astype(bfloat),
        residual,
    )

    value_sum, key_sum, grad_raw = lax.optimization_barrier((value_sum, key_sum, grad_raw))
    grad_mix_weight = [
        half_left(inputs_low[number], value).astype(bfloat)
        for number, value in (
            (3, grad_recept),
            (1, grad_keys),
            (2, grad_values),
            (4, grad_gate_pre),
        )
    ]
    given = jnp.concatenate(
        [
            jnp.zeros((8, width), single),
            lax.dynamic_update_slice_in_dim(
                jnp.zeros((4, width), single), grad_local[:4], col_start, 1
            ),
            channel_sums[:4],
        ],
        0,
    )
    grad_hidden_one, grad_pack, first_row = run_mixing_backward(
        tokens_all,
        heads,
        keep_lanes,
        acts,
        grad_recept,
        grad_keys,
        grad_values,
        grad_gate_pre,
        grad_raw,
        small,
        vectors,
        up_own,
        mix_weight,
        given,
    )
    grad_tokens, mix_sum, small_sum = run_end(
        dp_count,
        mp_count,
        grad_hidden_one,
        first_row,
        tokens,
        spread_row(vectors[0]),
        grad_residual,
        grad_mix_weight,
        grad_pack,
    )
    gate_sum, out_sum, mix_sum = lax.optimization_barrier((gate_sum, out_sum, mix_sum))
    return (
        mixed,
        grad_tokens,
        run_update(mix_state, mix_sum, width, total_tokens),
        run_update(out_state, out_sum, width, total_tokens),
        run_update(key_state, key_sum, width, total_tokens),
        run_update(value_state, value_sum, FF, total_tokens),
        run_update(gate_state, gate_sum, width, total_tokens),
        update(down_state, small_sum[:, :down_cols], width, total_tokens),
        update(up_state, small_sum[:, WINDOW : WINDOW + down_cols].T, TM_RANK, total_tokens),
        update(vector_state, small_sum[:, down_cols : down_cols + 16].T, 1, total_tokens),
    )


def solution(mesh):
    return jax.shard_map(
        body,
        mesh=mesh,
        in_specs=(
            P(("dp", "mp"), None),
            P(("dp", "mp"), None),
            P(),
            P(None, None, "dp", "mp"),
            P(None, "mp", "dp"),
            P(None, "dp", "mp"),
            P(None, "mp", "dp"),
            P(None, "dp", "mp"),
            P(None, ("dp", "mp"), None),
            P(None, None, ("dp", "mp")),
            P(None, None, ("dp", "mp")),
        ),
        out_specs=(
            P(("dp", "mp"), None),
            P(("dp", "mp"), None),
            P(None, None, "dp", "mp"),
            P(None, "mp", "dp"),
            P(None, "dp", "mp"),
            P(None, "mp", "dp"),
            P(None, "dp", "mp"),
            P(None, ("dp", "mp"), None),
            P(None, None, ("dp", "mp")),
            P(None, None, ("dp", "mp")),
        ),
        check_vma=False,
    )
```

```python
import functools

import jax
import jax.numpy as jnp
import numpy as np
from jax import lax
from jax.experimental import pallas as pl
from jax.experimental.pallas import tpu as pltpu
from jax.sharding import PartitionSpec as P

LANE_SPAN = 64
FF = 7168
TM_RANK = 32
DECAY_RANK = 64


momentum_rate = 0.9
average_rate = 0.9
norm_epsilon = 1e-05
group_epsilon = 0.00064
CHUNK = 128
LEVELS = 7
PAIR = 2 * LANE_SPAN
MESH = pl.DeviceIdType.MESH
PIECES = 2
WINDOW = 256
ROW_BLOCK = 256


def half_dot(left, right):
    return jnp.dot(left, right, preferred_element_type=jnp.float32)


def half_left(left, right):
    return lax.dot_general(
        left, right, (((0,), (0,)), ((), ())), preferred_element_type=jnp.float32
    )


def half_right(left, right):
    return lax.dot_general(
        left, right, (((1,), (1,)), ((), ())), preferred_element_type=jnp.float32
    )


def split_pair(value):
    upper_part = value.astype(jnp.bfloat16)
    lower_part = (value - upper_part.astype(jnp.float32)).astype(jnp.bfloat16)
    return (upper_part, lower_part)


def norm_forward(value, gain, bias, epsilon):
    centre = value - jnp.mean(value, -1, keepdims=True)
    inverse = lax.rsqrt(jnp.mean(centre * centre, -1, keepdims=True) + epsilon)
    normal_hat = centre * inverse
    return (normal_hat * gain + bias, normal_hat, inverse)


def norm_backward(grad_out, normal_hat, inverse, gain):
    scaled = grad_out * gain
    return inverse * (
        scaled
        - jnp.mean(scaled, -1, keepdims=True)
        - normal_hat * jnp.mean(scaled * normal_hat, -1, keepdims=True)
    )


def level_tables():
    row = np.arange(CHUNK)
    later, earlier = row[:, None], row[None, :]
    level = np.full((CHUNK, CHUNK), -1.0, np.float32)
    sums = []
    for bit in range(LEVELS):
        block = (later >> (bit + 1)) == (earlier >> (bit + 1))
        level[block & ((later >> bit) % 2 == 1) & ((earlier >> bit) % 2 == 0)] = bit
        middle = ((later >> (bit + 1)) << (bit + 1)) + (1 << bit)
        upper = (later >> bit) % 2 == 1
        between = np.where(
            upper, (earlier >= middle) & (earlier < later), (earlier > later) & (earlier < middle)
        )
        if bit:
            sums.append(between)
    sums += [earlier < later, earlier > later]
    sums = np.concatenate(sums, 0).astype(np.float32)
    return np.concatenate([level, level], 1), np.concatenate([sums, sums], 1), sums.T


def dot_nn(left, right):
    return lax.dot_general(
        left, right, (((1,), (0,)), ((), ())), preferred_element_type=jnp.float32
    )


def dot_nt(left, right):
    return lax.dot_general(
        left, right, (((1,), (1,)), ((), ())), preferred_element_type=jnp.float32
    )


def dot_tn(left, right):
    return lax.dot_general(
        left, right, (((0,), (0,)), ((), ())), preferred_element_type=jnp.float32
    )


def first_head(shape):
    return lax.broadcasted_iota(jnp.int32, shape, len(shape) - 1) < LANE_SPAN


def stack_heads(value):
    first = first_head(value.shape)
    none = jnp.zeros_like(value)
    return jnp.concatenate([jnp.where(first, value, none), jnp.where(first, none, value)], 0)


def merge_heads(value):
    half = value.shape[0] // 2
    return jnp.where(first_head((half, value.shape[1])), value[:half], value[half:])


def own_blocks(value):
    upper = lax.broadcasted_iota(jnp.int32, value.shape, 0) < LANE_SPAN
    return jnp.where(upper == first_head(value.shape), value, 0.0)


def head_mean(value):
    row = lax.broadcasted_iota(jnp.int32, (PAIR, PAIR), 0) < LANE_SPAN
    ones = jnp.where(row == first_head((PAIR, PAIR)), 1.0 / LANE_SPAN, 0.0).astype(jnp.bfloat16)
    upper, lower = split_pair(value)
    return dot_nn(upper, ones) + dot_nn(lower, ones)


def head_sum(value):
    return head_mean(value) * float(LANE_SPAN)


def exact_pieces(left, right, axis_left, axis_right):
    upper, lower = split_pair(left)
    right_upper, right_lower = split_pair(right)
    return (
        jnp.concatenate([upper, lower, upper], axis_left),
        jnp.concatenate([right_upper, right_upper, right_lower], axis_right),
    )


def exact_nn(left, right):
    return dot_nn(*exact_pieces(left, right, 1, 0))


def exact_nt(left, right):
    return dot_nt(*exact_pieces(left, right, 1, 1))


def exact_tn(left, right):
    return dot_tn(*exact_pieces(left, right, 0, 0))


def packed_state(state):
    return jnp.concatenate(split_pair(state[:LANE_SPAN] + state[LANE_SPAN:]), 0)


def unpacked_state(piece):
    piece = piece.astype(jnp.float32)
    return piece[:LANE_SPAN] + piece[LANE_SPAN:]


def rows_of(chunk):
    return pl.ds(pl.multiple_of(chunk * CHUNK, CHUNK), CHUNK)


def lanes_of(pair):
    return pl.ds(pl.multiple_of(pair * PAIR, PAIR), PAIR)


def marks_of(chunk):
    return pl.ds(pl.multiple_of(chunk * 8, 8), 8)


def everyone(dp_count, mp_count):
    me, mine = lax.axis_index("dp"), lax.axis_index("mp")
    return [(lax.rem(me + step, dp_count), mine) for step in range(1, dp_count)] + [
        (me, lax.rem(mine + step, mp_count)) for step in range(1, mp_count)
    ]


def swap_copies(count, source, target, send_sems, recv_sems):
    me, mine = lax.axis_index("dp"), lax.axis_index("mp")
    copies = []
    for step in range(1, count):
        other = lax.rem(mine + step, count)
        copies.append(
            pltpu.make_async_remote_copy(
                src_ref=source(other),
                dst_ref=target(mine),
                send_sem=send_sems.at[step - 1],
                recv_sem=recv_sems.at[step - 1],
                device_id=(me, other),
                device_id_type=MESH,
            )
        )
    return copies


def state_copies(other, me, sends, lands, send_sems, recv_sems, to):
    return [
        pltpu.make_async_remote_copy(
            src_ref=send,
            dst_ref=land.at[me],
            send_sem=send_sems.at[number, other],
            recv_sem=recv_sems.at[number, me],
            device_id=(to, lax.axis_index("mp")),
            device_id_type=MESH,
        )
        for number, (send, land) in enumerate(zip(sends, lands))
    ]


def send_states(count, sends, lands, send_sems, recv_sems, ahead):
    me = lax.axis_index("dp")
    for other in range(count):

        @pl.when((other > me) if ahead else (other < me))
        def _():
            for copy in state_copies(other, me, sends, lands, send_sems, recv_sems, other):
                copy.start()


def wait_states(count, sends, lands, send_sems, recv_sems, ahead):
    me = lax.axis_index("dp")
    for other in range(count):

        @pl.when((other > me) if ahead else (other < me))
        def _():
            for copy in state_copies(other, me, sends, lands, send_sems, recv_sems, other):
                copy.wait_send()

        @pl.when((other < me) if ahead else (other > me))
        def _():
            for copy in state_copies(other, other, sends, lands, send_sems, recv_sems, me):
                copy.wait_recv()


def decay_factors(fading, sums):
    upper, lower = split_pair(fading)
    return jnp.exp(dot_nn(sums, jnp.concatenate([upper, lower], 0)))


def table(at):
    return slice(at * CHUNK, (at + 1) * CHUNK)


def level_inputs(level, acceptor, lookup, factors):
    if level == 0:
        return None, acceptor, lookup
    factor = factors[table(level - 1), :]
    return factor, acceptor * factor, lookup * factor


def recurrence_forward(
    count, mp_count, chunks, pairs,
    rec, key, val, gpre, logw, vec, seg_col, seg_row, valid, ending, whole, level, sums, cotangent,
    tokens, out_weight, key_low,
    gated, wkv, states, kept, columns, residual, residual_all, before, key_all,
    factors, pre_a, pre_b, start_b, send_a, send_b, land_a, land_b, send_sems, recv_sems,
    swap_send, swap_recv,
    part, moving, land, total, sum_send, sum_recv, line_send, line_recv, halo_send, halo_recv,
    key_sem, cube_send, cube_recv,
):
    bfloat = jnp.bfloat16
    halo = Halo(count, mp_count, halo_send, halo_recv)
    greet_all(everyone(count, mp_count), halo.partners())
    mine, own_rows, features = lax.axis_index("mp"), cotangent.shape[0], columns.shape[1]

    def own_columns(other):
        return cotangent.at[:, pl.ds(pl.multiple_of(other * features, 128), features)]

    def landing(other):
        return columns.at[pl.ds(pl.multiple_of(other * own_rows, 16), own_rows)]

    key_rows = key_low.shape[0]
    half = key_rows // 2
    me = lax.axis_index("dp")
    key_own = pltpu.make_async_copy(
        key_low, key_all.at[pl.ds(pl.multiple_of(me * key_rows, 16), key_rows)], key_sem
    )
    key_own.start()
    cube = CubeGather(count, cube_send, cube_recv)

    def key_view(side):
        def view(index):
            return key_all.at[pl.ds(pl.multiple_of(index * key_rows + side * half, 16), half)]

        return view

    key_stages = list(range(cube.stages + 1))

    def gather_key():
        if key_stages:
            stage = key_stages.pop(0)
            for side in range(2):
                cube.stage(side, side, key_view(side), stage)

    swaps = swap_copies(mp_count, own_columns, landing, swap_send, swap_recv)
    for copy in swaps:
        copy.start()
    landing(mine)[...] = own_columns(mine)[...]

    def summary(pair, carry):
        lanes = lanes_of(pair)

        def step(chunk, before):
            before_a, before_b = before
            rows, slot = rows_of(chunk), pair * chunks + chunk
            fading = logw[rows, lanes]
            factor = decay_factors(fading, sums[...])
            factors[slot] = factor
            faded = key[rows, lanes] * factor[table(LEVELS)] * ending[rows, :]
            chunk_b = own_blocks(exact_tn(val[rows, lanes], faded))
            chunk_a = jnp.exp(jnp.sum(fading, 0, keepdims=True)) * whole[marks_of(chunk), :][:1]
            pre_a[slot] = jnp.broadcast_to(before_a, (8, PAIR))
            pre_b[slot] = before_b
            return before_a * chunk_a, before_b * chunk_a + chunk_b

        last_a, last_b = lax.fori_loop(
            0, chunks, step, (jnp.ones((1, PAIR), jnp.float32), jnp.zeros((PAIR, PAIR), jnp.float32))
        )
        send_a[:, lanes] = jnp.broadcast_to(last_a, (8, PAIR))
        send_b[:, lanes] = packed_state(last_b)
        return carry

    lax.fori_loop(0, pairs, summary, 0)
    exchange = (count, (send_a, send_b), (land_a, land_b), send_sems, recv_sems, True)
    send_states(*exchange)
    key_own.wait()
    gather_key()

    def inside(slot, carry):
        pair, chunk = slot // chunks, slot % chunks
        rows, lanes = rows_of(chunk), lanes_of(pair)
        acceptor, lookup, payload = rec[rows, lanes], key[rows, lanes], val[rows, lanes]
        place = jnp.where(seg_col[rows, :] == seg_row[marks_of(chunk), :][:1], level[...], -1.0)
        scores = jnp.zeros((CHUNK, 2 * CHUNK), jnp.float32)
        for at in range(LEVELS):
            _, left, right = level_inputs(at, acceptor, lookup, factors.at[slot])
            part = exact_nt(left, stack_heads(right))
            scores = jnp.where(place == float(at), part, scores)
        bonus = head_sum(acceptor * vec[0:1, lanes] * lookup) * payload
        wkv[rows, lanes] = bonus + exact_nn(scores, stack_heads(payload))
        kept[slot] = scores.astype(bfloat)
        return carry

    lax.fori_loop(0, pairs * chunks, inside, 0)
    wait_states(*exchange)
    gather_key()
    start_b[...] = lax.fori_loop(
        0,
        lax.axis_index("dp"),
        lambda other, state: state * land_a[other][:1] + unpacked_state(land_b[other]),
        jnp.zeros(start_b.shape, jnp.float32),
    )

    def finish(chunk, pair):
        slot = pair * chunks + chunk
        rows, lanes = rows_of(chunk), lanes_of(pair)
        state = pre_b[slot] + pre_a[slot][:1] * stack_heads(start_b[:, lanes])
        states[slot] = state
        reader = rec[rows, lanes] * factors[slot, table(LEVELS - 1), :] * valid[rows, :]
        out = wkv[rows, lanes] + exact_nt(reader, state)
        wkv[rows, lanes] = out
        centre = out - head_mean(out)
        inverse = lax.rsqrt(head_mean(centre * centre) + group_epsilon)
        normed = centre * inverse * vec[1:2, lanes] + vec[2:3, lanes]
        pre = gpre[rows, lanes]
        gated[rows, lanes] = (normed * pre * jax.nn.sigmoid(pre)).astype(bfloat)

    def project(block):
        def pair_step(pair, carry):
            for chunk in range(block * own_rows // CHUNK, (block + 1) * own_rows // CHUNK):
                finish(chunk, pair)
            return carry

        lax.fori_loop(0, pairs, pair_step, 0)
        at = slice(block * own_rows, (block + 1) * own_rows)
        width = 512

        def columns_step(number, carry):
            lanes = pl.ds(pl.multiple_of(number * width, width), width)
            part[at, lanes] = dot_nn(gated[at, :], out_weight[:, lanes]).astype(bfloat)
            return carry

        lax.fori_loop(0, part.shape[1] // width, columns_step, 0)

    adder = LineSum(mp_count, own_rows, sum_send, sum_recv)
    line = LineGather(mp_count, own_rows, line_send, line_recv)
    edge = residual_all.at[pl.ds(mp_count * own_rows - 16, 16)]
    project(mp_count - 1)
    project(0)
    adder.begin(part, None, moving, land, 0)
    for block in range(mp_count - 2, 0, -1):
        project(block)
    for number in range(mp_count - 1):
        if number:
            adder.begin(part, None, moving, land, number)
        adder.step(part, None, moving, land, number)
    gather_key()
    for piece in range(PIECES):
        at = adder.total(part, None, moving, land, total, piece)
        value = total[at] + tokens[at].astype(jnp.float32)
        residual[at] = value
        residual_all[line.at(line.me, piece)] = value.astype(bfloat)
        line.send(residual_all, 0, piece)
    halo.start(edge, before)
    for distance in range(1, mp_count):
        for piece in range(PIECES):
            line.send(residual_all, distance, piece)
    while key_stages:
        gather_key()
    for side in range(2):
        cube.finish(side, side, key_view(side))
    adder.finish(moving, land)
    line.finish(residual_all)
    halo.finish(edge, before)
    for copy in swaps:
        copy.wait()


def recurrence_backward(
    count, mp_count, chunks, pairs,
    dgated, wkv, states, kept, rec, key, val, gpre, logw, vec, seg_col, seg_row, valid, ending, whole,
    level, sums, sums_back, change, residual,
    drec, dkey, dval, dgpre, draw, dvec, mixed,
    factors, local, end_b, dout, drec_part, dkey_part, dval_part, dlog_part, steps,
    send_a, send_b, land_a, land_b, send_sems, recv_sems,
    swapped, swap_send, swap_recv,
):
    bfloat = jnp.bfloat16
    greet_all(everyone(count, mp_count))
    mine, own_rows, features = lax.axis_index("mp"), residual.shape[0], change.shape[1]

    def rows_for(other):
        return change.at[pl.ds(pl.multiple_of(other * own_rows, 16), own_rows)]

    swaps = swap_copies(mp_count, rows_for, lambda other: swapped.at[other], swap_send, swap_recv)
    for copy in swaps:
        copy.start()
    swapped[mine] = rows_for(mine)[...]
    dvec[...] = jnp.zeros(dvec.shape, jnp.float32)

    def chunk_decay(chunk, lanes):
        fading = logw[rows_of(chunk), lanes]
        return jnp.exp(jnp.sum(fading, 0, keepdims=True)) * whole[marks_of(chunk), :][:1]

    def summary(pair, carry):
        lanes = lanes_of(pair)

        def step(back, after):
            after_a, after_b = after
            chunk = chunks - 1 - back
            rows, slot = rows_of(chunk), pair * chunks + chunk
            factor = decay_factors(logw[rows, lanes], sums[...])
            factors[slot] = factor
            out = wkv[rows, lanes]
            centre = out - head_mean(out)
            inverse = lax.rsqrt(head_mean(centre * centre) + group_epsilon)
            hat = centre * inverse
            gain = vec[1:2, lanes]
            normed = hat * gain + vec[2:3, lanes]
            pre = gpre[rows, lanes]
            sig = jax.nn.sigmoid(pre)
            grad = dgated[rows, lanes]
            grad_normed = grad * pre * sig
            dgpre[rows, lanes] = (grad * normed * sig * (1.0 + pre * (1.0 - sig))).astype(bfloat)
            dvec[2:3, lanes] += jnp.sum(grad_normed * hat, 0, keepdims=True)
            dvec[3:4, lanes] += jnp.sum(grad_normed, 0, keepdims=True)
            scaled = grad_normed * gain
            grad_out = inverse * (scaled - head_mean(scaled) - hat * head_mean(scaled * hat))
            dout[rows, lanes] = grad_out
            reader = rec[rows, lanes] * factor[table(LEVELS - 1)] * valid[rows, :]
            inner = own_blocks(exact_tn(grad_out, reader))
            local[slot] = inner
            chunk_a = chunk_decay(chunk, lanes)
            return after_a * chunk_a, after_b * chunk_a + inner

        last_a, last_b = lax.fori_loop(
            0, chunks, step, (jnp.ones((1, PAIR), jnp.float32), jnp.zeros((PAIR, PAIR), jnp.float32))
        )
        send_a[:, lanes] = jnp.broadcast_to(last_a, (8, PAIR))
        send_b[:, lanes] = packed_state(last_b)
        return carry

    lax.fori_loop(0, pairs, summary, 0)
    exchange = (count, (send_a, send_b), (land_a, land_b), send_sems, recv_sems, False)
    send_states(*exchange)

    def inside(slot, carry):
        pair, chunk = slot // chunks, slot % chunks
        rows, lanes = rows_of(chunk), lanes_of(pair)
        acceptor, lookup, payload = rec[rows, lanes], key[rows, lanes], val[rows, lanes]
        reward = vec[0:1, lanes]
        grad_exact = dout[rows, lanes]
        grad_out = grad_exact.astype(bfloat)
        place = jnp.where(seg_col[rows, :] == seg_row[marks_of(chunk), :][:1], level[...], -1.0)
        grad_scores = exact_nt(grad_exact, stack_heads(payload))
        grad_bonus = head_sum(grad_exact * payload)
        dvec[1:2, lanes] += jnp.sum(acceptor * lookup * grad_bonus, 0, keepdims=True)
        grad_acceptor = reward * lookup * grad_bonus
        grad_lookup = reward * acceptor * grad_bonus
        for at in range(LEVELS):
            factor, left, right = level_inputs(at, acceptor, lookup, factors.at[slot])
            left_low, right_low = left.astype(bfloat), stack_heads(right.astype(bfloat))
            here = place == float(at)
            grad_part = jnp.where(here, grad_scores, 0.0).astype(bfloat)
            grad_left = dot_nn(grad_part, right_low)
            grad_right = merge_heads(dot_tn(grad_part, left_low))
            if at:
                grad_left = grad_left * factor
                grad_right = grad_right * factor
                steps[table(at - 1), :] = acceptor * grad_left + lookup * grad_right
            grad_acceptor += grad_left
            grad_lookup += grad_right
        drec_part[rows, lanes] = grad_acceptor
        dkey_part[rows, lanes] = grad_lookup
        bonus = head_sum(acceptor * reward * lookup)
        dval_part[rows, lanes] = bonus * grad_exact + merge_heads(
            dot_tn(kept[slot], grad_out)
        )
        inner = (LEVELS - 1) * CHUNK
        dlog_part[rows, lanes] = dot_nn(sums_back[:, :inner], steps[...].astype(bfloat))
        return carry

    lax.fori_loop(0, pairs * chunks, inside, 0)
    wait_states(*exchange)
    me = lax.axis_index("dp")

    def later(step, state):
        other = count - 1 - step
        return state * land_a[other][:1] + unpacked_state(land_b[other])

    end_b[...] = lax.fori_loop(0, count - 1 - me, later, jnp.zeros(end_b.shape, jnp.float32))

    def finish(pair, carry):
        lanes = lanes_of(pair)

        def step(back, after):
            chunk = chunks - 1 - back
            rows, slot = rows_of(chunk), pair * chunks + chunk
            state = states[slot]
            after_low = after.astype(bfloat)
            reach = factors[slot, table(LEVELS - 1), :] * valid[rows, :]
            tail = factors[slot, table(LEVELS), :] * ending[rows, :]
            acceptor, lookup = rec[rows, lanes], key[rows, lanes]
            grad_reader = exact_nn(dout[rows, lanes], state) * reach
            grad_faded = exact_nn(val[rows, lanes], after) * tail
            faded = (lookup * tail).astype(bfloat)
            chunk_a = chunk_decay(chunk, lanes)
            total = chunk_a * jnp.sum(after * state, 0, keepdims=True)
            drec[rows, lanes] = (drec_part[rows, lanes] + grad_reader).astype(bfloat)
            dkey[rows, lanes] = (dkey_part[rows, lanes] + grad_faded).astype(bfloat)
            dval[rows, lanes] = (dval_part[rows, lanes] + dot_nt(faded, after_low)).astype(bfloat)
            inner = (LEVELS - 1) * CHUNK
            moves = jnp.concatenate([acceptor * grad_reader, lookup * grad_faded], 0)
            grad_log = dlog_part[rows, lanes] + total + dot_nn(
                sums_back[:, inner:], moves.astype(bfloat)
            )
            raw = grad_log * logw[rows, lanes]
            draw[rows, lanes] = raw
            dvec[0:1, lanes] += jnp.sum(raw, 0, keepdims=True)
            return after * chunk_a + local[slot]

        lax.fori_loop(0, chunks, step, stack_heads(end_b[:, lanes]))
        return carry

    lax.fori_loop(0, pairs, finish, 0)
    for copy in swaps:
        copy.wait()
    for other in range(mp_count):
        lanes = slice(other * features, (other + 1) * features)
        mixed[:, lanes] = (residual[:, lanes] + swapped[other].astype(jnp.float32)).astype(bfloat)


def exchange_scratch(count, features):
    return [
        pltpu.VMEM((8, features), jnp.float32),
        pltpu.VMEM((2 * LANE_SPAN, features), jnp.bfloat16),
        pltpu.VMEM((count, 8, features), jnp.float32),
        pltpu.VMEM((count, 2 * LANE_SPAN, features), jnp.bfloat16),
        pltpu.SemaphoreType.DMA((2, count)),
        pltpu.SemaphoreType.DMA((2, count)),
    ]


def run_forward(
    count, mp_count, rec, key, val, gpre, logw, vec, marks, tables, cotangent, tokens, out_weight,
    key_low,
):
    rows, features = rec.shape
    width = tokens.shape[1]
    chunks, pairs = rows // CHUNK, features // PAIR
    slots = chunks * pairs
    whole_array = pl.BlockSpec(memory_space=pltpu.VMEM)
    level, sums, _ = tables
    return pl.pallas_call(
        functools.partial(recurrence_forward, count, mp_count, chunks, pairs),
        out_shape=(
            jax.ShapeDtypeStruct((rows, features), jnp.bfloat16),
            jax.ShapeDtypeStruct((rows, features), jnp.float32),
            jax.ShapeDtypeStruct((slots, PAIR, PAIR), jnp.float32),
            jax.ShapeDtypeStruct((slots, CHUNK, 2 * CHUNK), jnp.bfloat16),
            jax.ShapeDtypeStruct((rows, features), jnp.bfloat16),
            jax.ShapeDtypeStruct(tokens.shape, jnp.float32),
            jax.ShapeDtypeStruct((rows, width), jnp.bfloat16),
            jax.ShapeDtypeStruct((16, width), jnp.bfloat16),
            jax.ShapeDtypeStruct((count * key_low.shape[0], key_low.shape[1]), jnp.bfloat16),
        ),
        in_specs=[whole_array] * 17,
        out_specs=(whole_array,) * 8 + (pl.BlockSpec(memory_space=pl.ANY),),
        scratch_shapes=[
            pltpu.VMEM((slots, sums.shape[0], PAIR), jnp.float32),
            pltpu.VMEM((slots, 8, PAIR), jnp.float32),
            pltpu.VMEM((slots, PAIR, PAIR), jnp.float32),
            pltpu.VMEM((LANE_SPAN, features), jnp.float32),
        ]
        + exchange_scratch(count, features)
        + [
            pltpu.SemaphoreType.DMA((mp_count - 1,)),
            pltpu.SemaphoreType.DMA((mp_count - 1,)),
            pltpu.VMEM((rows, width), jnp.bfloat16),
            pltpu.VMEM((rows, width), jnp.bfloat16),
            pltpu.VMEM((2, rows, width), jnp.bfloat16),
            pltpu.VMEM(tokens.shape, jnp.float32),
            *line_sems(mp_count),
            *line_sems(mp_count),
            pltpu.SemaphoreType.DMA((mp_count,)),
            pltpu.SemaphoreType.DMA,
            pltpu.SemaphoreType.DMA,
            *cube_sems(2, count),
        ],
        compiler_params=pltpu.CompilerParams(
            collective_id=1, has_side_effects=True, vmem_limit_bytes=58 << 20
        ),
        name="recurrence_forward",
    )(rec, key, val, gpre, logw, vec, *marks, level, sums, cotangent, tokens, out_weight, key_low)


def run_backward(
    count, mp_count, dgated, wkv, states, kept, rec, key, val, gpre, logw, vec, marks, tables,
    change, residual,
):
    rows, features = rec.shape
    chunks, pairs = rows // CHUNK, features // PAIR
    slots = chunks * pairs
    whole_array = pl.BlockSpec(memory_space=pltpu.VMEM)
    level, sums, sums_back = tables
    low = jax.ShapeDtypeStruct((rows, features), jnp.bfloat16)
    full = pltpu.VMEM((rows, features), jnp.float32)
    return pl.pallas_call(
        functools.partial(recurrence_backward, count, mp_count, chunks, pairs),
        out_shape=(
            low,
            low,
            low,
            low,
            jax.ShapeDtypeStruct((rows, features), jnp.float32),
            jax.ShapeDtypeStruct((8, features), jnp.float32),
            jax.ShapeDtypeStruct(residual.shape, jnp.bfloat16),
        ),
        in_specs=[whole_array] * 20,
        out_specs=(whole_array,) * 7,
        scratch_shapes=[
            pltpu.VMEM((slots, sums.shape[0], PAIR), jnp.float32),
            pltpu.VMEM((slots, PAIR, PAIR), jnp.float32),
            pltpu.VMEM((LANE_SPAN, features), jnp.float32),
            full,
            full,
            full,
            full,
            full,
            pltpu.VMEM(((LEVELS - 1) * CHUNK, PAIR), jnp.float32),
        ]
        + exchange_scratch(count, features)
        + [pltpu.VMEM((mp_count,) + residual.shape[:1] + (features,), jnp.bfloat16)]
        + [
            pltpu.SemaphoreType.DMA((mp_count - 1,)),
            pltpu.SemaphoreType.DMA((mp_count - 1,)),
        ],
        compiler_params=pltpu.CompilerParams(
            collective_id=2, has_side_effects=True, vmem_limit_bytes=44 << 20
        ),
        name="recurrence_backward",
    )(
        dgated, wkv, states, kept, rec, key, val, gpre, logw, vec, *marks, level, sums, sums_back,
        change, residual,
    )


def flipped(index, mask):
    for bit in range(mask.bit_length()):
        size = 1 << bit
        if mask & size:
            index = index + size - 2 * size * lax.rem(index // size, 2)
    return index


def masks_over(bits):
    masks = [0]
    for bit in bits:
        masks = masks + [mask | (1 << bit) for mask in masks]
    return masks


def paths(count):
    higher = list(range(1, count.bit_length() - 1))
    return higher + [0], higher[::-1] + [0]


def remote(source, target, send_sem, recv_sem, dp, mp):
    return pltpu.make_async_remote_copy(
        src_ref=source,
        dst_ref=target,
        send_sem=send_sem,
        recv_sem=recv_sem,
        device_id=(dp, mp),
        device_id_type=MESH,
    )


def greet_all(partners, some=()):
    barrier = pltpu.get_barrier_semaphore()
    count = len(partners)
    for dp, mp in partners:
        pl.semaphore_signal(barrier, inc=1, device_id=(dp, mp), device_id_type=MESH)
    for present, dp, mp in some:

        @pl.when(present)
        def _():
            pl.semaphore_signal(barrier, inc=1, device_id=(dp, mp), device_id_type=MESH)

        count = count + jnp.where(present, 1, 0)
    pl.semaphore_wait(barrier, count)


class Halo:
    def __init__(self, dp_count, mp_count, send_sems, recv_sem):
        self.dp, self.mp = lax.axis_index("dp"), lax.axis_index("mp")
        self.count, self.lines = dp_count, mp_count
        self.send_sems, self.recv_sem = send_sems, recv_sem
        self.after = lax.rem(self.dp + 1, dp_count)
        self.previous = lax.rem(self.dp + dp_count - 1, dp_count)
        self.takes = self.dp > 0
        self.gives = jnp.logical_and(self.mp == mp_count - 1, self.dp < dp_count - 1)

    def partners(self):
        return [(self.takes, self.previous, self.lines - 1)] + [
            (self.gives, self.after, line) for line in range(self.lines)
        ]

    def copy(self, source, target, line):
        return remote(source, target, self.send_sems.at[line], self.recv_sem, self.after, line)

    def start(self, source, target):
        @pl.when(self.dp == 0)
        def _():
            target[...] = jnp.zeros(target.shape, target.dtype)

        @pl.when(self.gives)
        def _():
            for line in range(self.lines):
                self.copy(source, target, line).start()

    def finish(self, source, target):
        @pl.when(self.takes)
        def _():
            self.copy(source, target, 0).wait_recv()

        @pl.when(self.gives)
        def _():
            for line in range(self.lines):
                self.copy(source, target, line).wait_send()


class Arrival:
    def __init__(self, dp_count, send_sem, recv_sem):
        self.dp, self.mp = lax.axis_index("dp"), lax.axis_index("mp")
        self.send_sem, self.recv_sem = send_sem, recv_sem
        self.after = lax.rem(self.dp + 1, dp_count)
        self.previous = lax.rem(self.dp + dp_count - 1, dp_count)
        self.gives, self.takes = self.dp > 0, self.dp < dp_count - 1

    def partners(self):
        return [(self.gives, self.previous, self.mp), (self.takes, self.after, self.mp)]

    def copy(self, row, land):
        return remote(row, land, self.send_sem, self.recv_sem, self.previous, self.mp)

    def start(self, row, land):
        @pl.when(self.gives)
        def _():
            self.copy(row, land).start()

        @pl.when(jnp.logical_not(self.takes))
        def _():
            land[...] = jnp.zeros(land.shape, land.dtype)

    def wait(self, row, land):
        @pl.when(self.takes)
        def _():
            self.copy(row, land).wait_recv()

    def finish(self, row, land):
        @pl.when(self.gives)
        def _():
            self.copy(row, land).wait_send()


def line_partners(count):
    dp, mp = lax.axis_index("dp"), lax.axis_index("mp")
    return [(dp, lax.rem(mp + step, count)) for step in sorted({1, count - 1})]


def cube_partners(count):
    dp, mp = lax.axis_index("dp"), lax.axis_index("mp")
    return [(flipped(dp, 1 << bit), mp) for bit in range(count.bit_length() - 1)]


class Line:
    def __init__(self, count, rows, send_sems, recv_sems):
        self.count, self.rows = count, rows
        self.send_sems, self.recv_sems = send_sems, recv_sems
        self.dp, self.me = lax.axis_index("dp"), lax.axis_index("mp")
        self.piece = rows // PIECES

    def at(self, block, piece):
        return pl.ds(pl.multiple_of(block * self.rows + piece * self.piece, 16), self.piece)

    def copy(self, source, target, right, slot, piece):
        side = 0 if right else 1
        return remote(
            source,
            target,
            self.send_sems.at[side, slot, piece],
            self.recv_sems.at[side, slot, piece],
            self.dp,
            lax.rem(self.me + (1 if right else self.count - 1), self.count),
        )


class LineGather(Line):
    def hop(self, target, distance, piece, right):
        block = self.me - distance if right else self.me + distance
        ref = target.at[self.at(block, piece)]
        return self.copy(ref, ref, right, distance, piece)

    def holds(self, distance, right):
        return self.me >= distance if right else self.me + distance < self.count

    def passes(self, distance, right):
        onward = self.me < self.count - 1 if right else self.me > 0
        return jnp.logical_and(self.holds(distance, right), onward)

    def send(self, target, distance, piece):
        for right in (True, False):
            if distance:

                @pl.when(self.holds(distance, right))
                def _():
                    block = self.me - distance if right else self.me + distance
                    ref = target.at[self.at(block, piece)]
                    self.copy(ref, ref, right, distance - 1, piece).wait_recv()

            if distance < self.count - 1:

                @pl.when(self.passes(distance, right))
                def _():
                    self.hop(target, distance, piece, right).start()

    def finish(self, target):
        for distance in range(self.count - 1):
            for piece in range(PIECES):
                for right in (True, False):

                    @pl.when(self.passes(distance, right))
                    def _():
                        self.hop(target, distance, piece, right).wait_send()


class LineSum(Line):
    def hop(self, source, land, block, piece, right):
        return self.copy(
            source.at[self.at(block, piece)],
            land.at[0 if right else 1, self.at(block, piece)],
            right,
            block,
            piece,
        )

    def own(self, part, extra, block, piece):
        value = part[self.at(block, piece)].astype(jnp.float32)
        if extra is not None and piece == PIECES - 1:
            row = lax.broadcasted_iota(jnp.int32, value.shape, 0)
            last = jnp.logical_and(row == self.piece - 1, block == self.count - 1)
            value = value + jnp.where(last, extra[:1], 0.0)
        return value

    def begin(self, part, extra, moving, land, number, ready=None):
        for piece in range(PIECES):
            if ready is not None and piece == PIECES - 1:
                ready()
            for right in (True, False):
                block = self.count - 1 - number if right else number
                at = self.at(block, piece)

                @pl.when(self.me == (0 if right else self.count - 1))
                def _():
                    moving[at] = self.own(part, extra, block, piece).astype(jnp.bfloat16)
                    if number:
                        before = block + 1 if right else block - 1
                        self.hop(moving, land, before, piece, right).wait_send()
                    self.hop(moving, land, block, piece, right).start()

    def forward(self, part, extra, moving, land, block, piece, right):
        side = 0 if right else 1
        at = self.at(block, piece)
        inside = jnp.logical_and(self.me > 0, self.me < self.count - 1)

        @pl.when(jnp.logical_and(inside, self.me < block if right else self.me > block))
        def _():
            self.hop(moving, land, block, piece, right).wait_recv()
            moving[at] = (
                self.own(part, extra, block, piece) + land[side, at].astype(jnp.float32)
            ).astype(jnp.bfloat16)
            self.hop(moving, land, block, piece, right).start()

    def step(self, part, extra, moving, land, number):
        for piece in range(PIECES):
            self.forward(part, extra, moving, land, self.count - 1 - number, piece, True)
            self.forward(part, extra, moving, land, number, piece, False)

    def total(self, part, extra, moving, land, total, piece):
        at = self.at(self.me, piece)
        own = slice(piece * self.piece, (piece + 1) * self.piece)
        total[own] = self.own(part, extra, self.me, piece)
        for right in (True, False):

            @pl.when(self.me > 0 if right else self.me < self.count - 1)
            def _():
                self.hop(moving, land, self.me, piece, right).wait_recv()
                total[own] += land[0 if right else 1, at].astype(jnp.float32)

        return own

    def finish(self, moving, land):
        inside = jnp.logical_and(self.me > 0, self.me < self.count - 1)
        for number in range(self.count - 1):
            for piece in range(PIECES):
                for right in (True, False):
                    block = self.count - 1 - number if right else number
                    sent = jnp.logical_and(inside, self.me < block if right else self.me > block)
                    if number == self.count - 2:
                        sent = jnp.logical_or(sent, self.me == (0 if right else self.count - 1))

                    @pl.when(sent)
                    def _():
                        self.hop(moving, land, block, piece, right).wait_send()


class Cube:
    def __init__(self, count, send_sems, recv_sems):
        self.count, self.send_sems, self.recv_sems = count, send_sems, recv_sems
        self.dp, self.mp = lax.axis_index("dp"), lax.axis_index("mp")
        self.stages = count.bit_length() - 1

    def copy(self, source, target, unit, mask, bit):
        return remote(
            source,
            target,
            self.send_sems.at[unit, mask],
            self.recv_sems.at[unit, mask],
            flipped(self.dp, 1 << bit),
            self.mp,
        )


class CubeGather(Cube):
    def hop(self, unit, view, mask, bit):
        ref = view(flipped(self.dp, mask))
        return self.copy(ref, ref, unit, mask | (1 << bit), bit)

    def arrived(self, unit, view, mask, bit):
        ref = view(flipped(self.dp, mask))
        self.copy(ref, ref, unit, mask, bit).wait_recv()

    def stage(self, unit, path, view, stage):
        order = paths(self.count)[path]
        last = self.stages - 1
        if stage > last:
            for mask in masks_over(order[:last]):
                self.arrived(unit, view, mask | (1 << order[last]), order[last])
            return
        new = [0]
        if stage:
            new = [mask | (1 << order[stage - 1]) for mask in masks_over(order[: stage - 1])]
            for mask in new:
                self.arrived(unit, view, mask, order[stage - 1])
        if stage < last:
            for mask in masks_over(order[:stage]):
                self.hop(unit, view, mask, order[stage]).start()
        for mask in new:
            self.hop(unit, view, mask, order[last]).start()

    def finish(self, unit, path, view):
        order = paths(self.count)[path]
        for stage in range(self.stages):
            for mask in masks_over(order[:stage]):
                self.hop(unit, view, mask, order[stage]).wait_send()


class CubeSum(Cube):
    def slot(self, order, stage, mask):
        base = self.count - (self.count >> stage)
        return base + masks_over(order[stage + 1 :]).index(mask)

    def source(self, unit, order, view, land, stage, mask):
        if stage == 0:
            return view(flipped(self.dp, mask))
        return land.at[self.slot(order, stage - 1, mask)]

    def sends(self, unit, path, view, land, stage):
        order = paths(self.count)[path][::-1]
        bit = order[stage]
        return [
            self.copy(
                self.source(unit, order, view, land, stage, mask | (1 << bit)),
                land.at[self.slot(order, stage, mask)],
                unit,
                mask | (1 << bit),
                bit,
            )
            for mask in masks_over(order[stage + 1 :])
        ]

    def start(self, unit, path, view, land, stage):
        for copy in self.sends(unit, path, view, land, stage):
            copy.start()

    def absorb(self, unit, path, view, land, stage, out=None):
        order = paths(self.count)[path][::-1]
        for copy, mask in zip(
            self.sends(unit, path, view, land, stage), masks_over(order[stage + 1 :])
        ):
            copy.wait_recv()
            before = self.source(unit, order, view, land, stage, mask)
            here = land.at[self.slot(order, stage, mask)]
            step = 16

            def add(number, carry):
                at = pl.ds(pl.multiple_of(number * step, step), step)
                both = before[at].astype(jnp.float32) + here[at].astype(jnp.float32)
                if out is None:
                    here[at] = both.astype(jnp.bfloat16)
                else:
                    out[at] = both
                return carry

            lax.fori_loop(0, here.shape[0] // step, add, 0)

    def finish(self, unit, path, view, land):
        for stage in range(self.stages):
            for copy in self.sends(unit, path, view, land, stage):
                copy.wait_send()


def line_sems(count):
    return [pltpu.SemaphoreType.DMA((2, count, PIECES)), pltpu.SemaphoreType.DMA((2, count, PIECES))]


def cube_sems(units, count):
    return [pltpu.SemaphoreType.DMA((units, count)), pltpu.SemaphoreType.DMA((units, count))]


def start_kernel(
    dp_count, mp_count, tokens, pack, mix_state, out_state, gate_state, key_state, value_state,
    tokens_all, small, mix_all, out_low, gate_low, key_low, value_low, before,
    mix, mix_full, out_full, gate_full, key_full, value_full,
    load_sems, own_sems, line_send, line_recv, pack_send, pack_recv, cube_send, cube_recv,
    halo_send, halo_recv,
):
    dp, mp = lax.axis_index("dp"), lax.axis_index("mp")
    rows = tokens.shape[0]
    halo = Halo(dp_count, mp_count, halo_send, halo_recv)
    edge = tokens.at[pl.ds(rows - 16, 16)]
    matrices, block = mix.shape[0], mix.shape[1]
    pack_rows, group = pack.shape[0], pack.shape[0] * mp_count
    half = group // 2
    states = (mix_state, out_state, gate_state, key_state, value_state)
    fulls = (mix_full, out_full, gate_full, key_full, value_full)
    loads = [
        pltpu.make_async_copy(state.at[0], full, load_sems.at[number])
        for number, (state, full) in enumerate(zip(states, fulls))
    ]
    for load in loads:
        load.start()
    others = [lax.rem(mp + step, mp_count) for step in range(1, mp_count)]
    greet_all([(dp, other) for other in others] + cube_partners(dp_count), halo.partners())
    halo.start(edge, before)
    line = LineGather(mp_count, rows, line_send, line_recv)
    cube = CubeGather(dp_count, cube_send, cube_recv)

    pack_at = small.at[pl.ds(pl.multiple_of(dp * group + mp * pack_rows, 16), pack_rows)]
    own = [
        pltpu.make_async_copy(pack, pack_at, own_sems.at[0]),
        pltpu.make_async_copy(
            tokens, tokens_all.at[pl.ds(pl.multiple_of(mp * rows, 16), rows)], own_sems.at[1]
        ),
    ]
    pack_copies = [
        remote(pack, pack_at, pack_send.at[step], pack_recv.at[step], dp, other)
        for step, other in enumerate(others)
    ]
    for copy in pack_copies + own:
        copy.start()
    loads[0].wait()
    for number in range(matrices):
        mix[number] = mix_full[number].astype(jnp.bfloat16)
    own_mix = [
        pltpu.make_async_copy(
            mix.at[number],
            mix_all.at[number, pl.ds(pl.multiple_of(dp * block, 16), block)],
            own_sems.at[2 + number],
        )
        for number in range(matrices)
    ]
    for copy in own_mix:
        copy.start()

    def small_view(part):
        def view(index):
            return small.at[pl.ds(pl.multiple_of(index * group + part * half, 16), half)]

        return view

    def mix_view(number):
        def view(index):
            return mix_all.at[number, pl.ds(pl.multiple_of(index * block, 16), block)]

        return view

    mix_units = [
        (2 + number, 0 if 2 * number < matrices else 1, mix_view(number))
        for number in range(matrices)
    ]
    small_units = [(part, part, small_view(part)) for part in range(2)]
    for copy in own + own_mix:
        copy.wait()
    for unit in mix_units:
        cube.stage(*unit, 0)
    for piece in range(PIECES):
        line.send(tokens_all, 0, piece)
    for load, full, low in zip(loads[1:], fulls[1:], (out_low, gate_low, key_low, value_low)):
        load.wait()
        step = 64

        def convert(number, carry):
            at = pl.ds(pl.multiple_of(number * step, step), step)
            low[at] = full[at].astype(jnp.bfloat16)
            return carry

        lax.fori_loop(0, full.shape[0] // step, convert, 0)
    for copy in pack_copies:
        copy.wait()
    for unit in small_units:
        cube.stage(*unit, 0)
    for distance in range(1, mp_count):
        for piece in range(PIECES):
            line.send(tokens_all, distance, piece)
        if distance < dp_count.bit_length() - 1:
            for unit in mix_units + small_units:
                cube.stage(*unit, distance)
    for stage in range(min(mp_count, dp_count.bit_length() - 1), dp_count.bit_length()):
        for unit in mix_units + small_units:
            cube.stage(*unit, stage)
    line.finish(tokens_all)
    halo.finish(edge, before)
    for unit in mix_units + small_units:
        cube.finish(*unit)


def run_start(dp_count, mp_count, tokens, pack, states):
    rows, width = tokens.shape
    matrices, block, features = states[0].shape[1:]
    anywhere = pl.BlockSpec(memory_space=pl.ANY)
    vmem = pl.BlockSpec(memory_space=pltpu.VMEM)
    bfloat = jnp.bfloat16
    return pl.pallas_call(
        functools.partial(start_kernel, dp_count, mp_count),
        out_shape=(
            jax.ShapeDtypeStruct((rows * mp_count, width), bfloat),
            jax.ShapeDtypeStruct((pack.shape[0] * mp_count * dp_count, pack.shape[1]), bfloat),
            jax.ShapeDtypeStruct((matrices, block * dp_count, features), bfloat),
            *[jax.ShapeDtypeStruct(state.shape[1:], bfloat) for state in states[1:]],
            jax.ShapeDtypeStruct((16, width), bfloat),
        ),
        in_specs=[vmem, vmem] + [anywhere] * 5,
        out_specs=(anywhere,) * 3 + (vmem,) * 5,
        scratch_shapes=[
            pltpu.VMEM(states[0].shape[1:], bfloat),
            *[pltpu.VMEM(state.shape[1:], jnp.float32) for state in states],
            pltpu.SemaphoreType.DMA((5,)),
            pltpu.SemaphoreType.DMA((2 + matrices,)),
            *line_sems(mp_count),
            pltpu.SemaphoreType.DMA((mp_count - 1,)),
            pltpu.SemaphoreType.DMA((mp_count - 1,)),
            *cube_sems(2 + matrices, dp_count),
            pltpu.SemaphoreType.DMA((mp_count,)),
            pltpu.SemaphoreType.DMA,
        ],
        compiler_params=pltpu.CompilerParams(
            collective_id=3, has_side_effects=True, vmem_limit_bytes=60 << 20
        ),
        name="gather_start",
    )(tokens, pack, *states)


def backward_rows(total, rows, source, gain, skip):
    value = source[rows].astype(jnp.float32)
    centre = value - jnp.mean(value, -1, keepdims=True)
    inverse = lax.rsqrt(jnp.mean(centre * centre, -1, keepdims=True) + norm_epsilon)
    return skip[rows].astype(jnp.float32) + norm_backward(total, centre * inverse, inverse, gain[:1])


def exchange_kernel(
    dp_count, count, part, first, source, gain, skip,
    own, gathered,
    moving, land, total, edge,
    sum_send, sum_recv, line_send, line_recv, row_send, row_recv,
):
    rows = own.shape[0]
    arrival = Arrival(dp_count, row_send, row_recv)
    greet_all(line_partners(count), arrival.partners())
    arrival.start(first, edge)
    adder = LineSum(count, rows, sum_send, sum_recv)
    line = LineGather(count, rows, line_send, line_recv)
    for number in range(count - 1):
        ready = None if number else lambda: arrival.wait(first, edge)
        adder.begin(part, edge, moving, land, number, ready)
        adder.step(part, edge, moving, land, number)
    for piece in range(PIECES):
        at = adder.total(part, edge, moving, land, total, piece)
        value = backward_rows(total[at], at, source, gain, skip)
        own[at] = value
        gathered[line.at(line.me, piece)] = value.astype(jnp.bfloat16)
        line.send(gathered, 0, piece)
    for distance in range(1, count):
        for piece in range(PIECES):
            line.send(gathered, distance, piece)
    adder.finish(moving, land)
    line.finish(gathered)
    arrival.finish(first, edge)


def run_exchange(dp_count, count, part, first, source, gain, skip):
    rows, width = part.shape[0] // count, part.shape[1]
    vmem = pl.BlockSpec(memory_space=pltpu.VMEM)
    return pl.pallas_call(
        functools.partial(exchange_kernel, dp_count, count),
        out_shape=(
            jax.ShapeDtypeStruct((rows, width), jnp.float32),
            jax.ShapeDtypeStruct(part.shape, jnp.bfloat16),
        ),
        in_specs=[vmem] * 5,
        out_specs=(vmem, vmem),
        scratch_shapes=[
            pltpu.VMEM(part.shape, jnp.bfloat16),
            pltpu.VMEM((2,) + part.shape, jnp.bfloat16),
            pltpu.VMEM((rows, width), jnp.float32),
            pltpu.VMEM((8, width), jnp.float32),
            *line_sems(count),
            *line_sems(count),
            pltpu.SemaphoreType.DMA,
            pltpu.SemaphoreType.DMA,
        ],
        compiler_params=pltpu.CompilerParams(
            collective_id=5, has_side_effects=True, vmem_limit_bytes=20 << 20
        ),
        name="sum_and_gather",
    )(part, first, source, gain, skip)


def end_kernel(
    dp_count, mp_count, part, first, source, gain, skip, mix_a, mix_b, mix_c, mix_d, pack,
    own, mix_sum, pack_sum,
    moving, land, total, mix_land, pack_land, pack_own, pack_out, small_land,
    edge, sum_send, sum_recv, cube_send, cube_recv, small_send, small_recv, row_send, row_recv,
):
    dp, mp = lax.axis_index("dp"), lax.axis_index("mp")
    mix = (mix_a, mix_b, mix_c, mix_d)
    rows, matrices = own.shape[0], len(mix)
    block, group = mix_sum.shape[1], pack_own.shape[0]
    half, pack_rows = group // 2, pack_sum.shape[0]
    others = [lax.rem(mp + step, mp_count) for step in range(1, mp_count)]
    arrival = Arrival(dp_count, row_send, row_recv)
    greet_all([(dp, other) for other in others] + cube_partners(dp_count), arrival.partners())
    arrival.start(first, edge)
    adder = LineSum(mp_count, rows, sum_send, sum_recv)
    cube = CubeSum(dp_count, cube_send, cube_recv)

    def mix_view(number):
        def view(index):
            return mix[number].at[pl.ds(pl.multiple_of(index * block, 16), block)]

        return view

    def pack_view(side):
        def view(index):
            return pack.at[pl.ds(pl.multiple_of(index * group + side * half, 16), half)]

        return view

    units = [(side, side, pack_view(side), pack_land.at[side]) for side in range(2)] + [
        (2 + number, 0 if 2 * number < matrices else 1, mix_view(number), mix_land.at[number])
        for number in range(matrices)
    ]
    outs = [pack_own.at[pl.ds(side * half, half)] for side in range(2)] + [
        mix_sum.at[number] for number in range(matrices)
    ]
    for unit in units:
        cube.start(*unit, 0)
    adder.begin(part, edge, moving, land, 0, lambda: arrival.wait(first, edge))
    last = cube.stages - 1
    for unit in units:
        cube.absorb(*unit, 0)
        cube.start(*unit, 1)
    for number in range(1, mp_count - 1):
        adder.begin(part, edge, moving, land, number)
        adder.step(part, edge, moving, land, number - 1)
    adder.step(part, edge, moving, land, mp_count - 2)
    for piece in range(PIECES):
        at = adder.total(part, edge, moving, land, total, piece)
        own[at] = backward_rows(total[at], at, source, gain, skip)
    for stage in range(1, last):
        for unit in units:
            cube.absorb(*unit, stage)
            cube.start(*unit, stage + 1)
    for unit, out in zip(units[:2], outs[:2]):
        cube.absorb(*unit, last, out)
    pack_out[...] = pack_own[...].astype(jnp.bfloat16)
    small_copies = [
        remote(
            pack_out.at[pl.ds(pl.multiple_of(other * pack_rows, 16), pack_rows)],
            small_land.at[step],
            small_send.at[step],
            small_recv.at[step],
            dp,
            other,
        )
        for step, other in enumerate(others)
    ]
    for copy in small_copies:
        copy.start()
    for unit, out in zip(units[2:], outs[2:]):
        cube.absorb(*unit, last, out)
    pack_sum[...] = pack_own[pl.ds(pl.multiple_of(mp * pack_rows, 16), pack_rows), :]
    for step, copy in enumerate(small_copies):
        copy.wait()
        pack_sum[...] += small_land[step].astype(jnp.float32)
    adder.finish(moving, land)
    arrival.finish(first, edge)
    for unit in units:
        cube.finish(*unit)


def run_end(dp_count, mp_count, part, first, source, gain, skip, mix, pack):
    rows, width = source.shape
    matrices, features = len(mix), mix[0].shape[1]
    block, group = mix[0].shape[0] // dp_count, pack.shape[0] // dp_count
    lanes = pack.shape[1]
    vmem = pl.BlockSpec(memory_space=pltpu.VMEM)
    return pl.pallas_call(
        functools.partial(end_kernel, dp_count, mp_count),
        out_shape=(
            jax.ShapeDtypeStruct((rows, width), jnp.float32),
            jax.ShapeDtypeStruct((matrices, block, features), jnp.float32),
            jax.ShapeDtypeStruct((group // mp_count, lanes), jnp.float32),
        ),
        in_specs=[vmem] * 10,
        out_specs=(vmem,) * 3,
        scratch_shapes=[
            pltpu.VMEM(part.shape, jnp.bfloat16),
            pltpu.VMEM((2,) + part.shape, jnp.bfloat16),
            pltpu.VMEM((rows, width), jnp.float32),
            pltpu.VMEM((matrices, dp_count - 1, block, features), jnp.bfloat16),
            pltpu.VMEM((2, dp_count - 1, group // 2, lanes), jnp.bfloat16),
            pltpu.VMEM((group, lanes), jnp.float32),
            pltpu.VMEM((group, lanes), jnp.bfloat16),
            pltpu.VMEM((mp_count - 1, group // mp_count, lanes), jnp.bfloat16),
            pltpu.VMEM((8, width), jnp.float32),
            *line_sems(mp_count),
            *cube_sems(2 + matrices, dp_count),
            pltpu.SemaphoreType.DMA((mp_count - 1,)),
            pltpu.SemaphoreType.DMA((mp_count - 1,)),
            pltpu.SemaphoreType.DMA,
            pltpu.SemaphoreType.DMA,
        ],
        compiler_params=pltpu.CompilerParams(
            collective_id=6, has_side_effects=True, vmem_limit_bytes=56 << 20
        ),
        name="sum_end",
    )(part, first, source, gain, skip, *mix, pack)


def update_rows(rate, state, grad, new):
    scaled = rate * grad[...].astype(jnp.float32)
    velocity = momentum_rate * state[1] + scaled
    weight = state[0] - (scaled + momentum_rate * velocity)
    new[0] = velocity
    new[1] = weight
    new[2] = average_rate * state[2] + (1.0 - average_rate) * weight


def run_update(state, grad, fan, total_tokens):
    shape = state.shape
    lanes = shape[-1]
    flat = state.reshape(3, -1, lanes)
    grad = grad.reshape(-1, lanes)
    block = 128
    while grad.shape[0] % (2 * block) == 0 and 2 * block * lanes <= 1 << 18:
        block *= 2
    triple = pl.BlockSpec((3, block, lanes), lambda i: (0, i, 0))
    return pl.pallas_call(
        functools.partial(update_rows, (total_tokens * fan) ** (-0.5)),
        grid=(grad.shape[0] // block,),
        out_shape=jax.ShapeDtypeStruct(flat.shape, jnp.float32),
        in_specs=[triple, pl.BlockSpec((block, lanes), lambda i: (i, 0))],
        out_specs=triple,
        compiler_params=pltpu.CompilerParams(vmem_limit_bytes=24 << 20),
        name="momentum_update",
    )(flat, grad).reshape(shape)


def lane_mask(shape, low, high):
    lane = lax.broadcasted_iota(jnp.int32, shape, len(shape) - 1)
    return jnp.logical_and(lane >= low, lane < high)


def masked(value, low, high):
    return jnp.where(lane_mask(value.shape, low, high), value, jnp.zeros_like(value))


def block_norm(value, vectors):
    hidden, hat, _ = norm_forward(value.astype(jnp.float32), vectors[0:1], vectors[1:2], norm_epsilon)
    return hidden, hat


def block_delta(hidden, before, keep):
    row = lax.broadcasted_iota(jnp.int32, hidden.shape, 0)
    behind = jnp.where(row == 0, before, pltpu.roll(hidden, 1, 0))
    return behind * keep - hidden


def mixing_forward(
    tokens, heads, keep, small, vectors, decay_row, up_own, mix, inputs, rec, key, val, gpre, logw, acts
):
    bfloat = jnp.bfloat16
    maa_cols = 5 * TM_RANK
    down_cols = maa_cols + DECAY_RANK
    hidden, _ = block_norm(tokens[...], vectors)
    before, _ = block_norm(heads[0], vectors)
    delta = block_delta(hidden, before[:1], keep[:, :1])
    base = (hidden + delta * vectors[2:3]).astype(bfloat)
    act = jnp.tanh(dot_nn(base, small[:, :WINDOW]))
    act_low = act.astype(bfloat)
    for number in range(5):
        mine = masked(act_low, TM_RANK * number, TM_RANK * (number + 1))
        scale = vectors[3 + number : 4 + number] + dot_nt(mine, small[:, WINDOW:])
        value = (hidden + delta * scale).astype(bfloat)
        inputs[number] = value
        if number:
            place = {1: 1, 2: 2, 3: 0, 4: 3}[number]
            (rec, key, val, gpre)[place][...] = dot_nn(value, mix[place])
        else:
            decay = masked(jnp.tanh(dot_nn(value, small[:, :WINDOW])), maa_cols, down_cols)
            logw[...] = -jnp.exp(decay_row[:1] + dot_nt(decay.astype(bfloat), up_own[...]))
    acts[...] = masked(act, 0, maa_cols) + decay


def run_mixing_forward(tokens, heads, keep, small, vectors, decay_row, up_own, mix):
    rows, width = tokens.shape
    features = mix.shape[2]
    block = lambda lanes: pl.BlockSpec((ROW_BLOCK, lanes), lambda i: (i, 0))
    fixed = lambda value: pl.BlockSpec(
        value.shape, lambda i: (0,) * value.ndim, pipeline_mode=pl.Buffered(1)
    )
    stack = lambda count, lanes: pl.BlockSpec((count, ROW_BLOCK, lanes), lambda i: (0, i, 0))
    return pl.pallas_call(
        mixing_forward,
        grid=(rows // ROW_BLOCK,),
        out_shape=(
            jax.ShapeDtypeStruct((5, rows, width), jnp.bfloat16),
            *[jax.ShapeDtypeStruct((rows, features), jnp.float32)] * 5,
            jax.ShapeDtypeStruct((rows, WINDOW), jnp.float32),
        ),
        in_specs=[
            block(width),
            pl.BlockSpec((1,) + heads.shape[1:], lambda i: (i, 0, 0)),
            block(keep.shape[1]),
            fixed(small),
            fixed(vectors),
            fixed(decay_row),
            fixed(up_own),
            fixed(mix),
        ],
        out_specs=(stack(5, width), *[block(features)] * 5, block(WINDOW)),
        compiler_params=pltpu.CompilerParams(vmem_limit_bytes=58 << 20),
        name="mixing_forward",
    )(tokens, heads, keep, small, vectors, decay_row, up_own, mix)


def mixing_backward(
    tokens, heads, keep, acts, drec, dkey, dval, dgate, draw,
    small, vectors, up_own, mix, given,
    grad_hidden, grad_pack, first_row,
    grad_down, grad_up, grad_vec, carried,
):
    bfloat = jnp.bfloat16
    step, last = pl.program_id(0), pl.num_programs(0) - 1
    maa_cols = 5 * TM_RANK
    down_cols = maa_cols + DECAY_RANK
    features = mix.shape[2]
    col_start = pl.multiple_of(lax.axis_index("mp") * features, 128)

    @pl.when(step == 0)
    def _():
        grad_down[...] = jnp.zeros(grad_down.shape, jnp.float32)
        grad_up[...] = jnp.zeros(grad_up.shape, jnp.float32)
        grad_vec[...] = given[...]
        carried[...] = jnp.zeros(carried.shape, jnp.float32)

    down, upper = small.at[:, :WINDOW], small.at[:, WINDOW:]
    hidden, hat = block_norm(tokens[...], vectors)
    before, before_hat = block_norm(heads[0], vectors)
    delta = block_delta(hidden, before[:1], keep[:, :1])
    act = acts[...]
    act_low = act.astype(bfloat)
    slope = 1.0 - act * act
    raw = draw[...].astype(bfloat)
    grad_decay = masked(dot_nn(raw, up_own[...]) * slope, maa_cols, down_cols).astype(bfloat)
    grad_up[pl.ds(col_start, features), :] += dot_tn(raw, masked(act_low, maa_cols, down_cols))

    def add_row(row, value):
        grad_vec[row : row + 1, :] += jnp.sum(value, 0, keepdims=True)

    total = jnp.zeros(hidden.shape, jnp.float32)
    grad_delta = jnp.zeros(hidden.shape, jnp.float32)
    grad_act = jnp.zeros(act.shape, jnp.float32)
    for number in range(5):
        low, high = TM_RANK * number, TM_RANK * (number + 1)
        mine = masked(act_low, low, high)
        scale = vectors[3 + number : 4 + number] + dot_nt(mine, upper[...])
        if number:
            source = {1: dkey, 2: dval, 3: drec, 4: dgate}[number]
            grad_input = dot_nt(source[...], mix[{1: 1, 2: 2, 3: 0, 4: 3}[number]])
        else:
            grad_input = dot_nt(grad_decay, down[...])
            value = (hidden + delta * scale).astype(bfloat)
            grad_down[...] += dot_tn(value, grad_decay)
        moved = grad_input * delta
        add_row(3 + number, moved)
        moved_low = moved.astype(bfloat)
        grad_up[...] += dot_tn(moved_low, mine)
        grad_act += masked(dot_nn(moved_low, upper[...]), low, high)
        grad_delta += grad_input * scale
        total += grad_input
    grad_pre = (grad_act * slope).astype(bfloat)
    base = (hidden + delta * vectors[2:3]).astype(bfloat)
    grad_down[...] += dot_tn(base, grad_pre)
    grad_base = dot_nt(grad_pre, down[...])
    add_row(2, grad_base * delta)
    grad_delta += grad_base * vectors[2:3]
    shifted_grad = grad_delta * keep[:, :1]
    row = lax.broadcasted_iota(jnp.int32, hidden.shape, 0)
    back = jnp.where(
        row == ROW_BLOCK - 1, carried[:1], pltpu.roll(shifted_grad, ROW_BLOCK - 1, 0)
    )
    carried[...] = jnp.broadcast_to(shifted_grad[:1], carried.shape)
    total += grad_base - grad_delta + back
    add_row(0, total * hat)
    add_row(1, total)
    grad_hidden[...] = total.astype(bfloat)

    @pl.when(step == last)
    def _():
        first_row[...] = carried[...]
        add_row(0, carried[:1] * before_hat[:1])
        add_row(1, carried[:1])
        spot = lax.broadcasted_iota(jnp.int32, (16, WINDOW), 0) + down_cols
        lane = lax.broadcasted_iota(jnp.int32, (16, WINDOW), 1)
        one = jnp.where(spot == lane, 1.0, 0.0).astype(bfloat)
        placed = dot_tn(grad_vec[...].astype(bfloat), one)
        grad_pack[:, :WINDOW] = (grad_down[...] + placed).astype(bfloat)
        grad_pack[:, WINDOW:] = grad_up[...].astype(bfloat)


def run_mixing_backward(
    tokens, heads, keep, acts, drec, dkey, dval, dgate, draw, small, vectors, up_own, mix, given
):
    rows, width = tokens.shape
    features = mix.shape[2]
    count = rows // ROW_BLOCK
    block = lambda lanes: pl.BlockSpec((ROW_BLOCK, lanes), lambda i: (count - 1 - i, 0))
    fixed = lambda value: pl.BlockSpec(
        value.shape, lambda i: (0,) * len(value.shape), pipeline_mode=pl.Buffered(1)
    )
    first = jax.ShapeDtypeStruct((8, width), jnp.float32)
    pack = jax.ShapeDtypeStruct((width, 2 * WINDOW), jnp.bfloat16)
    return pl.pallas_call(
        mixing_backward,
        grid=(count,),
        out_shape=(jax.ShapeDtypeStruct((rows, width), jnp.bfloat16), pack, first),
        in_specs=[
            block(width),
            pl.BlockSpec((1,) + heads.shape[1:], lambda i: (count - 1 - i, 0, 0)),
            block(keep.shape[1]),
            block(WINDOW),
            block(features),
            block(features),
            block(features),
            block(features),
            block(features),
            fixed(small),
            fixed(vectors),
            fixed(up_own),
            fixed(mix),
            fixed(given),
        ],
        out_specs=(block(width), fixed(pack), fixed(first)),
        scratch_shapes=[
            pltpu.VMEM((width, WINDOW), jnp.float32),
            pltpu.VMEM((width, WINDOW), jnp.float32),
            pltpu.VMEM((16, width), jnp.float32),
            pltpu.VMEM((8, width), jnp.float32),
        ],
        compiler_params=pltpu.CompilerParams(vmem_limit_bytes=60 << 20),
        name="mixing_backward",
    )(tokens, heads, keep, acts, drec, dkey, dval, dgate, draw, small, vectors, up_own, mix, given)


def channel_forward(
    source, heads, keep, vectors, gate, cotangent, key_in, recv_in, recv_gate, grad_kv
):
    def norm(value):
        return norm_forward(
            value.astype(jnp.float32), vectors[12:13], vectors[13:14], norm_epsilon
        )[0]

    hidden = norm(source[...])
    delta = block_delta(hidden, norm(heads[0])[:1], keep[:, :1])
    key_in[...] = (hidden + delta * vectors[14:15]).astype(jnp.bfloat16)
    recv = (hidden + delta * vectors[15:16]).astype(jnp.bfloat16)
    recv_in[...] = recv
    opened = jax.nn.sigmoid(dot_nn(recv, gate[...]))
    recv_gate[...] = opened
    grad_kv[...] = (cotangent[...].astype(jnp.float32) * opened).astype(jnp.bfloat16)


def run_channel_forward(source, heads, keep, vectors, gate, cotangent):
    rows, width = source.shape
    features = gate.shape[1]
    block = lambda lanes: pl.BlockSpec((ROW_BLOCK, lanes), lambda i: (i, 0))
    fixed = lambda value: pl.BlockSpec(
        value.shape, lambda i: (0,) * len(value.shape), pipeline_mode=pl.Buffered(1)
    )
    low = lambda lanes: jax.ShapeDtypeStruct((rows, lanes), jnp.bfloat16)
    return pl.pallas_call(
        channel_forward,
        grid=(rows // ROW_BLOCK,),
        out_shape=(
            low(width),
            low(width),
            jax.ShapeDtypeStruct((rows, features), jnp.float32),
            low(features),
        ),
        in_specs=[
            block(width),
            pl.BlockSpec((1,) + heads.shape[1:], lambda i: (i, 0, 0)),
            block(keep.shape[1]),
            fixed(vectors),
            fixed(gate),
            block(features),
        ],
        out_specs=(block(width), block(width), block(features), block(features)),
        compiler_params=pltpu.CompilerParams(vmem_limit_bytes=60 << 20),
        name="channel_forward",
    )(source, heads, keep, vectors, gate, cotangent)


def channel_backward(
    source, heads, keep, grad_key, grad_recv, vectors, gate,
    grad_hidden, sums, first_row,
    carried,
):
    step, last = pl.program_id(0), pl.num_programs(0) - 1

    @pl.when(step == 0)
    def _():
        sums[...] = jnp.zeros(sums.shape, jnp.float32)
        carried[...] = jnp.zeros(carried.shape, jnp.float32)

    def norm(value):
        return norm_forward(
            value.astype(jnp.float32), vectors[12:13], vectors[13:14], norm_epsilon
        )[:2]

    def add_row(row, value):
        sums[row : row + 1, :] += jnp.sum(value, 0, keepdims=True)

    hidden, hat = norm(source[...])
    before, before_hat = norm(heads[0])
    delta = block_delta(hidden, before[:1], keep[:, :1])
    grad_recv_in = dot_nt(grad_recv[...], gate[...])
    grad_key_in = grad_key[...]
    grad_delta = grad_key_in * vectors[14:15] + grad_recv_in * vectors[15:16]
    add_row(2, grad_key_in * delta)
    add_row(3, grad_recv_in * delta)
    shifted_grad = grad_delta * keep[:, :1]
    row = lax.broadcasted_iota(jnp.int32, hidden.shape, 0)
    back = jnp.where(
        row == ROW_BLOCK - 1, carried[:1], pltpu.roll(shifted_grad, ROW_BLOCK - 1, 0)
    )
    carried[...] = jnp.broadcast_to(shifted_grad[:1], carried.shape)
    total = grad_key_in + grad_recv_in - grad_delta + back
    add_row(0, total * hat)
    add_row(1, total)
    grad_hidden[...] = total.astype(jnp.bfloat16)

    @pl.when(step == last)
    def _():
        first_row[...] = carried[...]
        add_row(0, carried[:1] * before_hat[:1])
        add_row(1, carried[:1])


def run_channel_backward(source, heads, keep, grad_key, grad_recv, vectors, gate):
    rows, width = source.shape
    count = rows // ROW_BLOCK
    block = lambda lanes: pl.BlockSpec((ROW_BLOCK, lanes), lambda i: (count - 1 - i, 0))
    fixed = lambda value: pl.BlockSpec(
        value.shape, lambda i: (0,) * len(value.shape), pipeline_mode=pl.Buffered(1)
    )
    first = jax.ShapeDtypeStruct((8, width), jnp.float32)
    return pl.pallas_call(
        channel_backward,
        grid=(count,),
        out_shape=(jax.ShapeDtypeStruct((rows, width), jnp.bfloat16), first, first),
        in_specs=[
            block(width),
            pl.BlockSpec((1,) + heads.shape[1:], lambda i: (count - 1 - i, 0, 0)),
            block(keep.shape[1]),
            block(width),
            block(grad_recv.shape[1]),
            fixed(vectors),
            fixed(gate),
        ],
        out_specs=(block(width), fixed(first), fixed(first)),
        scratch_shapes=[pltpu.VMEM((8, width), jnp.float32)],
        compiler_params=pltpu.CompilerParams(vmem_limit_bytes=48 << 20),
        name="channel_backward",
    )(source, heads, keep, grad_key, grad_recv, vectors, gate)


def update(carried_memory, grad, fan, total_tokens):
    rate = (total_tokens * fan) ** (-0.5)
    scaled = rate * grad
    velocity = momentum_rate * carried_memory[1] + scaled
    weight = carried_memory[0] - (scaled + momentum_rate * velocity)
    average = average_rate * carried_memory[2] + (1.0 - average_rate) * weight
    return jnp.stack([velocity, weight, average])


def split_three(value):
    pieces = []
    for _ in range(3):
        pieces.append(lax.reduce_precision(value, 8, 7))
        value = value - pieces[-1]
    return [piece.astype(jnp.bfloat16) for piece in pieces]


def block_heads(before, rows):
    width = rows.shape[1]
    ends = rows.reshape(-1, ROW_BLOCK, width)[:-1, -1]
    heads = jnp.concatenate([before, ends], 0)
    return jnp.broadcast_to(heads[:, None], (heads.shape[0], 16, width))


def body(
    tokens,
    cotangent,
    lengths,
    mix_state,
    out_state,
    key_state,
    value_state,
    gate_state,
    down_state,
    up_state,
    vector_state,
):
    bfloat = jnp.bfloat16
    single = jnp.float32
    dp_count = lax.axis_size("dp")
    mp_count = lax.axis_size("mp")
    dp_index = lax.axis_index("dp")
    mp_index = lax.axis_index("mp")
    own_rows = tokens.shape[0]
    width = tokens.shape[1]
    group_rows = own_rows * mp_count
    total_tokens = group_rows * dp_count
    features = mix_state.shape[3]
    maa_cols = 5 * TM_RANK
    down_cols = maa_cols + DECAY_RANK
    col_start = mp_index * features

    upper, middle, lower = split_three(vector_state[0].T)
    pack = jnp.concatenate(
        [
            down_state[0].astype(bfloat),
            upper,
            middle,
            up_state[0].T.astype(bfloat),
            lower,
            jnp.zeros_like(lower),
        ],
        1,
    )
    states = (mix_state, out_state, gate_state, key_state, value_state)
    tokens_all, small, mix_weight, out_low, gate_low, key_low, value_low, before_one = run_start(
        dp_count, mp_count, tokens, pack, states
    )
    out_weight = lax.all_gather(out_low, "dp", axis=1, tiled=True)
    gate_weight = lax.all_gather(gate_low, "dp", axis=0, tiled=True)
    chosen = np.zeros((16, small.shape[1]), np.float32)
    for start in (down_cols, down_cols + 16, WINDOW + down_cols):
        chosen[np.arange(16), start + np.arange(16)] = 1.0
    vectors = half_right(jnp.asarray(chosen, bfloat), small)

    seq_ends = jnp.cumsum(lengths)
    offsets = seq_ends - lengths
    positions = dp_index * group_rows + jnp.arange(group_rows, dtype=jnp.int32)
    opening = jnp.any(positions[:, None] == offsets[None, :], 1).astype(single)
    segment = jnp.sum((offsets[None, :] <= positions[:, None]).astype(single), 1)
    keep = 1.0 - opening
    chunks = group_rows // CHUNK
    parts = segment.reshape(chunks, CHUNK)
    first = parts[:, :1] - opening.reshape(chunks, CHUNK)[:, :1]

    def spread(value, lanes):
        return jnp.broadcast_to(value.astype(single).reshape(-1, 1), (value.size, lanes))

    marks = (
        spread(parts, 2 * CHUNK),
        jnp.repeat(jnp.concatenate([parts, parts], 1), 8, 0),
        spread(parts == first, PAIR),
        spread(parts == parts[:, -1:], PAIR),
        spread(jnp.repeat(parts[:, -1:] == first, 8, 0), PAIR),
    )
    level, sums, sums_back = level_tables()
    tables = (jnp.asarray(level), jnp.asarray(sums, bfloat), jnp.asarray(sums_back, bfloat))

    def local_share(row_number):
        return lax.dynamic_slice_in_dim(vectors[row_number], col_start, features, 0)

    def spread_row(value):
        return jnp.broadcast_to(value[None], (8, width))

    heads = block_heads(before_one[-1:], tokens_all)
    keep_lanes = spread(keep, PAIR)
    up_own = lax.dynamic_slice_in_dim(small[:, WINDOW:], col_start, features, 0)
    decay_row = jnp.broadcast_to(local_share(8)[None], (8, features))
    inputs_low, *branch, acts = run_mixing_forward(
        tokens_all, heads, keep_lanes, small, vectors, decay_row, up_own, mix_weight
    )
    value_low, branch = lax.optimization_barrier((value_low, branch))
    value_weight = lax.all_gather(value_low, "dp", axis=1, tiled=True)
    local_vectors = jnp.concatenate(
        [jnp.stack([local_share(9), local_share(10), local_share(11)]), jnp.zeros((5, features))], 0
    )
    outcome = run_forward(
        dp_count,
        mp_count,
        *branch,
        local_vectors,
        marks,
        tables,
        cotangent,
        tokens,
        out_weight,
        key_low,
    )
    gated_low, wkv, states, kept, cotangent_cols, residual, *outcome = outcome
    residual_all, before_second, key_weight = outcome
    before_second = before_second[-1:]
    heads_two = block_heads(before_second, residual_all)
    key_in_low, recv_in_low, recv_gate, grad_kv = run_channel_forward(
        residual_all, heads_two, keep_lanes, vectors, gate_weight, cotangent_cols
    )
    cotangent_cols = cotangent_cols.astype(single)
    key_pre = half_dot(key_in_low, key_weight)
    key_act_low = jnp.square(jnp.maximum(key_pre, 0.0)).astype(bfloat)
    grad_kv_all = lax.all_gather(grad_kv, "mp", axis=1, tiled=True)
    channel_sum = lax.psum_scatter(
        half_dot(key_act_low, value_weight).astype(bfloat), "mp", scatter_dimension=1, tiled=True
    ).astype(single)
    gated_sum = recv_gate * channel_sum
    grad_recv_pre = (cotangent_cols * gated_sum * (1.0 - recv_gate)).astype(bfloat)
    grad_key_act = half_right(grad_kv_all, value_weight)
    grad_key_pre = (grad_key_act * 2.0 * jnp.maximum(key_pre, 0.0)).astype(bfloat)
    grad_key_in = half_right(grad_key_pre, key_weight)
    grad_value_weight = half_left(key_act_low, grad_kv_all).astype(bfloat)
    grad_key_weight = half_left(key_in_low, grad_key_pre).astype(bfloat)
    grad_gate_weight = half_left(recv_in_low, grad_recv_pre).astype(bfloat)
    grad_hidden_two, channel_sums, first_row_two = run_channel_backward(
        residual_all,
        heads_two,
        keep_lanes,
        grad_key_in,
        grad_recv_pre,
        vectors,
        gate_weight,
    )
    def summed(value, axis):
        return lax.psum_scatter(value, "dp", scatter_dimension=axis, tiled=True)

    value_sum = summed(grad_value_weight, 1)
    key_sum = summed(grad_key_weight, 0)
    gate_sum = summed(grad_gate_weight, 0)
    grad_residual, grad_attn_all = run_exchange(
        dp_count,
        mp_count,
        grad_hidden_two,
        first_row_two,
        residual.astype(bfloat),
        spread_row(vectors[12]),
        cotangent,
    )
    grad_out_weight = half_left(gated_low, grad_attn_all)
    out_sum = summed(grad_out_weight.astype(bfloat), 1)
    grad_gated = half_right(grad_attn_all, out_weight)
    grad_recept, grad_keys, grad_values, grad_gate_pre, grad_raw, grad_local, mixed = run_backward(
        dp_count,
        mp_count,
        grad_gated,
        wkv,
        states,
        kept,
        *branch,
        local_vectors,
        marks,
        tables,
        gated_sum.astype(bfloat),
        residual,
    )

    value_sum, key_sum, grad_raw = lax.optimization_barrier((value_sum, key_sum, grad_raw))
    grad_mix_weight = [
        half_left(inputs_low[number], value).astype(bfloat)
        for number, value in (
            (3, grad_recept),
            (1, grad_keys),
            (2, grad_values),
            (4, grad_gate_pre),
        )
    ]
    given = jnp.concatenate(
        [
            jnp.zeros((8, width), single),
            lax.dynamic_update_slice_in_dim(
                jnp.zeros((4, width), single), grad_local[:4], col_start, 1
            ),
            channel_sums[:4],
        ],
        0,
    )
    grad_hidden_one, grad_pack, first_row = run_mixing_backward(
        tokens_all,
        heads,
        keep_lanes,
        acts,
        grad_recept,
        grad_keys,
        grad_values,
        grad_gate_pre,
        grad_raw,
        small,
        vectors,
        up_own,
        mix_weight,
        given,
    )
    grad_tokens, mix_sum, small_sum = run_end(
        dp_count,
        mp_count,
        grad_hidden_one,
        first_row,
        tokens,
        spread_row(vectors[0]),
        grad_residual,
        grad_mix_weight,
        grad_pack,
    )
    gate_sum, out_sum, mix_sum = lax.optimization_barrier((gate_sum, out_sum, mix_sum))
    return (
        mixed,
        grad_tokens,
        run_update(mix_state, mix_sum, width, total_tokens),
        run_update(out_state, out_sum, width, total_tokens),
        run_update(key_state, key_sum, width, total_tokens),
        run_update(value_state, value_sum, FF, total_tokens),
        run_update(gate_state, gate_sum, width, total_tokens),
        update(down_state, small_sum[:, :down_cols], width, total_tokens),
        update(up_state, small_sum[:, WINDOW : WINDOW + down_cols].T, TM_RANK, total_tokens),
        update(vector_state, small_sum[:, down_cols : down_cols + 16].T, 1, total_tokens),
    )


def solution(mesh):
    return jax.shard_map(
        body,
        mesh=mesh,
        in_specs=(
            P(("dp", "mp"), None),
            P(("dp", "mp"), None),
            P(),
            P(None, None, "dp", "mp"),
            P(None, "mp", "dp"),
            P(None, "dp", "mp"),
            P(None, "mp", "dp"),
            P(None, "dp", "mp"),
            P(None, ("dp", "mp"), None),
            P(None, None, ("dp", "mp")),
            P(None, None, ("dp", "mp")),
        ),
        out_specs=(
            P(("dp", "mp"), None),
            P(("dp", "mp"), None),
            P(None, None, "dp", "mp"),
            P(None, "mp", "dp"),
            P(None, "dp", "mp"),
            P(None, "mp", "dp"),
            P(None, "dp", "mp"),
            P(None, ("dp", "mp"), None),
            P(None, None, ("dp", "mp")),
            P(None, None, ("dp", "mp")),
        ),
        check_vma=False,
    )
```

```python
import functools

import jax
import jax.numpy as jnp
import numpy as np
from jax import lax
from jax.experimental import pallas as pl
from jax.experimental.pallas import tpu as pltpu
from jax.sharding import PartitionSpec as P

LANE_SPAN = 64
FF = 7168
TM_RANK = 32
DECAY_RANK = 64


momentum_rate = 0.9
average_rate = 0.9
norm_epsilon = 1e-05
group_epsilon = 0.00064
CHUNK = 128
LEVELS = 7
PAIR = 2 * LANE_SPAN
MESH = pl.DeviceIdType.MESH
PIECES = 2
WINDOW = 256
ROW_BLOCK = 256


def half_dot(left, right):
    return jnp.dot(left, right, preferred_element_type=jnp.float32)


def half_left(left, right):
    return lax.dot_general(
        left, right, (((0,), (0,)), ((), ())), preferred_element_type=jnp.float32
    )


def half_right(left, right):
    return lax.dot_general(
        left, right, (((1,), (1,)), ((), ())), preferred_element_type=jnp.float32
    )


def split_pair(value):
    upper_part = value.astype(jnp.bfloat16)
    lower_part = (value - upper_part.astype(jnp.float32)).astype(jnp.bfloat16)
    return (upper_part, lower_part)


def norm_forward(value, gain, bias, epsilon):
    centre = value - jnp.mean(value, -1, keepdims=True)
    inverse = lax.rsqrt(jnp.mean(centre * centre, -1, keepdims=True) + epsilon)
    normal_hat = centre * inverse
    return (normal_hat * gain + bias, normal_hat, inverse)


def norm_backward(grad_out, normal_hat, inverse, gain):
    scaled = grad_out * gain
    return inverse * (
        scaled
        - jnp.mean(scaled, -1, keepdims=True)
        - normal_hat * jnp.mean(scaled * normal_hat, -1, keepdims=True)
    )


def level_tables():
    row = np.arange(CHUNK)
    later, earlier = row[:, None], row[None, :]
    level = np.full((CHUNK, CHUNK), -1.0, np.float32)
    sums = []
    for bit in range(LEVELS):
        block = (later >> (bit + 1)) == (earlier >> (bit + 1))
        level[block & ((later >> bit) % 2 == 1) & ((earlier >> bit) % 2 == 0)] = bit
        middle = ((later >> (bit + 1)) << (bit + 1)) + (1 << bit)
        upper = (later >> bit) % 2 == 1
        between = np.where(
            upper, (earlier >= middle) & (earlier < later), (earlier > later) & (earlier < middle)
        )
        if bit:
            sums.append(between)
    sums += [earlier < later, earlier > later]
    sums = np.concatenate(sums, 0).astype(np.float32)
    return np.concatenate([level, level], 1), np.concatenate([sums, sums], 1), sums.T


def dot_nn(left, right):
    return lax.dot_general(
        left, right, (((1,), (0,)), ((), ())), preferred_element_type=jnp.float32
    )


def dot_nt(left, right):
    return lax.dot_general(
        left, right, (((1,), (1,)), ((), ())), preferred_element_type=jnp.float32
    )


def dot_tn(left, right):
    return lax.dot_general(
        left, right, (((0,), (0,)), ((), ())), preferred_element_type=jnp.float32
    )


def first_head(shape):
    return lax.broadcasted_iota(jnp.int32, shape, len(shape) - 1) < LANE_SPAN


def stack_heads(value):
    first = first_head(value.shape)
    none = jnp.zeros_like(value)
    return jnp.concatenate([jnp.where(first, value, none), jnp.where(first, none, value)], 0)


def merge_heads(value):
    half = value.shape[0] // 2
    return jnp.where(first_head((half, value.shape[1])), value[:half], value[half:])


def own_blocks(value):
    upper = lax.broadcasted_iota(jnp.int32, value.shape, 0) < LANE_SPAN
    return jnp.where(upper == first_head(value.shape), value, 0.0)


def head_mean(value):
    row = lax.broadcasted_iota(jnp.int32, (PAIR, PAIR), 0) < LANE_SPAN
    ones = jnp.where(row == first_head((PAIR, PAIR)), 1.0 / LANE_SPAN, 0.0).astype(jnp.bfloat16)
    upper, lower = split_pair(value)
    return dot_nn(upper, ones) + dot_nn(lower, ones)


def head_sum(value):
    return head_mean(value) * float(LANE_SPAN)


def exact_pieces(left, right, axis_left, axis_right):
    upper, lower = split_pair(left)
    right_upper, right_lower = split_pair(right)
    return (
        jnp.concatenate([upper, lower, upper], axis_left),
        jnp.concatenate([right_upper, right_upper, right_lower], axis_right),
    )


def exact_nn(left, right):
    return dot_nn(*exact_pieces(left, right, 1, 0))


def exact_nt(left, right):
    return dot_nt(*exact_pieces(left, right, 1, 1))


def exact_tn(left, right):
    return dot_tn(*exact_pieces(left, right, 0, 0))


def packed_state(state):
    return jnp.concatenate(split_pair(state[:LANE_SPAN] + state[LANE_SPAN:]), 0)


def unpacked_state(piece):
    piece = piece.astype(jnp.float32)
    return piece[:LANE_SPAN] + piece[LANE_SPAN:]


def rows_of(chunk):
    return pl.ds(pl.multiple_of(chunk * CHUNK, CHUNK), CHUNK)


def lanes_of(pair):
    return pl.ds(pl.multiple_of(pair * PAIR, PAIR), PAIR)


def marks_of(chunk):
    return pl.ds(pl.multiple_of(chunk * 8, 8), 8)


def everyone(dp_count, mp_count):
    me, mine = lax.axis_index("dp"), lax.axis_index("mp")
    return [(lax.rem(me + step, dp_count), mine) for step in range(1, dp_count)] + [
        (me, lax.rem(mine + step, mp_count)) for step in range(1, mp_count)
    ]


def swap_copies(count, source, target, send_sems, recv_sems):
    me, mine = lax.axis_index("dp"), lax.axis_index("mp")
    copies = []
    for step in range(1, count):
        other = lax.rem(mine + step, count)
        copies.append(
            pltpu.make_async_remote_copy(
                src_ref=source(other),
                dst_ref=target(mine),
                send_sem=send_sems.at[step - 1],
                recv_sem=recv_sems.at[step - 1],
                device_id=(me, other),
                device_id_type=MESH,
            )
        )
    return copies


def state_copies(other, me, sends, lands, send_sems, recv_sems, to):
    return [
        pltpu.make_async_remote_copy(
            src_ref=send,
            dst_ref=land.at[me],
            send_sem=send_sems.at[number, other],
            recv_sem=recv_sems.at[number, me],
            device_id=(to, lax.axis_index("mp")),
            device_id_type=MESH,
        )
        for number, (send, land) in enumerate(zip(sends, lands))
    ]


def send_states(count, sends, lands, send_sems, recv_sems, ahead):
    me = lax.axis_index("dp")
    for other in range(count):

        @pl.when((other > me) if ahead else (other < me))
        def _():
            for copy in state_copies(other, me, sends, lands, send_sems, recv_sems, other):
                copy.start()


def wait_states(count, sends, lands, send_sems, recv_sems, ahead):
    me = lax.axis_index("dp")
    for other in range(count):

        @pl.when((other > me) if ahead else (other < me))
        def _():
            for copy in state_copies(other, me, sends, lands, send_sems, recv_sems, other):
                copy.wait_send()

        @pl.when((other < me) if ahead else (other > me))
        def _():
            for copy in state_copies(other, other, sends, lands, send_sems, recv_sems, me):
                copy.wait_recv()


def decay_factors(fading, sums):
    upper, lower = split_pair(fading)
    return jnp.exp(dot_nn(sums, jnp.concatenate([upper, lower], 0)))


def table(at):
    return slice(at * CHUNK, (at + 1) * CHUNK)


def level_inputs(level, acceptor, lookup, factors):
    if level == 0:
        return None, acceptor, lookup
    factor = factors[table(level - 1), :]
    return factor, acceptor * factor, lookup * factor


def recurrence_forward(
    count, mp_count, chunks, pairs,
    rec, key, val, gpre, logw, vec, seg_col, seg_row, valid, ending, whole, level, sums, cotangent,
    tokens, out_weight, key_low,
    gated, wkv, states, kept, columns, residual, residual_all, before, key_all,
    factors, pre_a, pre_b, start_b, send_a, send_b, land_a, land_b, send_sems, recv_sems,
    swap_send, swap_recv,
    part, moving, land, total, sum_send, sum_recv, line_send, line_recv, halo_send, halo_recv,
    key_sem, cube_send, cube_recv,
):
    bfloat = jnp.bfloat16
    halo = Halo(count, mp_count, halo_send, halo_recv)
    greet_all(everyone(count, mp_count), halo.partners())
    mine, own_rows, features = lax.axis_index("mp"), cotangent.shape[0], columns.shape[1]

    def own_columns(other):
        return cotangent.at[:, pl.ds(pl.multiple_of(other * features, 128), features)]

    def landing(other):
        return columns.at[pl.ds(pl.multiple_of(other * own_rows, 16), own_rows)]

    key_rows = key_low.shape[0]
    half = key_rows // 2
    me = lax.axis_index("dp")
    key_own = pltpu.make_async_copy(
        key_low, key_all.at[pl.ds(pl.multiple_of(me * key_rows, 16), key_rows)], key_sem
    )
    key_own.start()
    cube = CubeGather(count, cube_send, cube_recv)

    def key_view(side):
        def view(index):
            return key_all.at[pl.ds(pl.multiple_of(index * key_rows + side * half, 16), half)]

        return view

    key_stages = list(range(cube.stages + 1))

    def gather_key():
        if key_stages:
            stage = key_stages.pop(0)
            for side in range(2):
                cube.stage(side, side, key_view(side), stage)

    swaps = swap_copies(mp_count, own_columns, landing, swap_send, swap_recv)
    for copy in swaps:
        copy.start()
    landing(mine)[...] = own_columns(mine)[...]

    def summary(pair, carry):
        lanes = lanes_of(pair)

        def step(chunk, before):
            before_a, before_b = before
            rows, slot = rows_of(chunk), pair * chunks + chunk
            fading = logw[rows, lanes]
            factor = decay_factors(fading, sums[...])
            factors[slot] = factor
            faded = key[rows, lanes] * factor[table(LEVELS)] * ending[rows, :]
            chunk_b = own_blocks(exact_tn(val[rows, lanes], faded))
            chunk_a = jnp.exp(jnp.sum(fading, 0, keepdims=True)) * whole[marks_of(chunk), :][:1]
            pre_a[slot] = jnp.broadcast_to(before_a, (8, PAIR))
            pre_b[slot] = before_b
            return before_a * chunk_a, before_b * chunk_a + chunk_b

        last_a, last_b = lax.fori_loop(
            0, chunks, step, (jnp.ones((1, PAIR), jnp.float32), jnp.zeros((PAIR, PAIR), jnp.float32))
        )
        send_a[:, lanes] = jnp.broadcast_to(last_a, (8, PAIR))
        send_b[:, lanes] = packed_state(last_b)
        return carry

    lax.fori_loop(0, pairs, summary, 0)
    exchange = (count, (send_a, send_b), (land_a, land_b), send_sems, recv_sems, True)
    send_states(*exchange)
    key_own.wait()
    gather_key()

    def inside(slot, carry):
        pair, chunk = slot // chunks, slot % chunks
        rows, lanes = rows_of(chunk), lanes_of(pair)
        acceptor, lookup, payload = rec[rows, lanes], key[rows, lanes], val[rows, lanes]
        place = jnp.where(seg_col[rows, :] == seg_row[marks_of(chunk), :][:1], level[...], -1.0)
        scores = jnp.zeros((CHUNK, 2 * CHUNK), jnp.float32)
        for at in range(LEVELS):
            _, left, right = level_inputs(at, acceptor, lookup, factors.at[slot])
            part = exact_nt(left, stack_heads(right))
            scores = jnp.where(place == float(at), part, scores)
        bonus = head_sum(acceptor * vec[0:1, lanes] * lookup) * payload
        wkv[rows, lanes] = bonus + exact_nn(scores, stack_heads(payload))
        kept[slot] = scores.astype(bfloat)
        return carry

    lax.fori_loop(0, pairs * chunks, inside, 0)
    wait_states(*exchange)
    gather_key()
    start_b[...] = lax.fori_loop(
        0,
        lax.axis_index("dp"),
        lambda other, state: state * land_a[other][:1] + unpacked_state(land_b[other]),
        jnp.zeros(start_b.shape, jnp.float32),
    )

    def finish(chunk, pair):
        slot = pair * chunks + chunk
        rows, lanes = rows_of(chunk), lanes_of(pair)
        state = pre_b[slot] + pre_a[slot][:1] * stack_heads(start_b[:, lanes])
        states[slot] = state
        reader = rec[rows, lanes] * factors[slot, table(LEVELS - 1), :] * valid[rows, :]
        out = wkv[rows, lanes] + exact_nt(reader, state)
        wkv[rows, lanes] = out
        centre = out - head_mean(out)
        inverse = lax.rsqrt(head_mean(centre * centre) + group_epsilon)
        normed = centre * inverse * vec[1:2, lanes] + vec[2:3, lanes]
        pre = gpre[rows, lanes]
        gated[rows, lanes] = (normed * pre * jax.nn.sigmoid(pre)).astype(bfloat)

    def project(block):
        def pair_step(pair, carry):
            for chunk in range(block * own_rows // CHUNK, (block + 1) * own_rows // CHUNK):
                finish(chunk, pair)
            return carry

        lax.fori_loop(0, pairs, pair_step, 0)
        at = slice(block * own_rows, (block + 1) * own_rows)
        width = 512

        def columns_step(number, carry):
            lanes = pl.ds(pl.multiple_of(number * width, width), width)
            part[at, lanes] = dot_nn(gated[at, :], out_weight[:, lanes]).astype(bfloat)
            return carry

        lax.fori_loop(0, part.shape[1] // width, columns_step, 0)

    adder = LineSum(mp_count, own_rows, sum_send, sum_recv)
    line = LineGather(mp_count, own_rows, line_send, line_recv)
    edge = residual_all.at[pl.ds(mp_count * own_rows - 16, 16)]
    project(mp_count - 1)
    project(0)
    adder.begin(part, None, moving, land, 0)
    for block in range(mp_count - 2, 0, -1):
        project(block)
    for number in range(mp_count - 1):
        if number:
            adder.begin(part, None, moving, land, number)
        adder.step(part, None, moving, land, number)
    gather_key()
    for piece in range(PIECES):
        at = adder.total(part, None, moving, land, total, piece)
        value = total[at] + tokens[at].astype(jnp.float32)
        residual[at] = value
        residual_all[line.at(line.me, piece)] = value.astype(bfloat)
        line.send(residual_all, 0, piece)
    halo.start(edge, before)
    for distance in range(1, mp_count):
        for piece in range(PIECES):
            line.send(residual_all, distance, piece)
    while key_stages:
        gather_key()
    for side in range(2):
        cube.finish(side, side, key_view(side))
    adder.finish(moving, land)
    line.finish(residual_all)
    halo.finish(edge, before)
    for copy in swaps:
        copy.wait()


def recurrence_backward(
    count, mp_count, chunks, pairs,
    dgated, wkv, states, kept, rec, key, val, gpre, logw, vec, seg_col, seg_row, valid, ending, whole,
    level, sums, sums_back, change, residual,
    drec, dkey, dval, dgpre, draw, dvec, mixed,
    factors, local, end_b, dout, drec_part, dkey_part, dval_part, dlog_part, steps,
    send_a, send_b, land_a, land_b, send_sems, recv_sems,
    swapped, swap_send, swap_recv,
):
    bfloat = jnp.bfloat16
    greet_all(everyone(count, mp_count))
    mine, own_rows, features = lax.axis_index("mp"), residual.shape[0], change.shape[1]

    def rows_for(other):
        return change.at[pl.ds(pl.multiple_of(other * own_rows, 16), own_rows)]

    swaps = swap_copies(mp_count, rows_for, lambda other: swapped.at[other], swap_send, swap_recv)
    for copy in swaps:
        copy.start()
    swapped[mine] = rows_for(mine)[...]
    dvec[...] = jnp.zeros(dvec.shape, jnp.float32)

    def chunk_decay(chunk, lanes):
        fading = logw[rows_of(chunk), lanes]
        return jnp.exp(jnp.sum(fading, 0, keepdims=True)) * whole[marks_of(chunk), :][:1]

    def summary(pair, carry):
        lanes = lanes_of(pair)

        def step(back, after):
            after_a, after_b = after
            chunk = chunks - 1 - back
            rows, slot = rows_of(chunk), pair * chunks + chunk
            factor = decay_factors(logw[rows, lanes], sums[...])
            factors[slot] = factor
            out = wkv[rows, lanes]
            centre = out - head_mean(out)
            inverse = lax.rsqrt(head_mean(centre * centre) + group_epsilon)
            hat = centre * inverse
            gain = vec[1:2, lanes]
            normed = hat * gain + vec[2:3, lanes]
            pre = gpre[rows, lanes]
            sig = jax.nn.sigmoid(pre)
            grad = dgated[rows, lanes]
            grad_normed = grad * pre * sig
            dgpre[rows, lanes] = (grad * normed * sig * (1.0 + pre * (1.0 - sig))).astype(bfloat)
            dvec[2:3, lanes] += jnp.sum(grad_normed * hat, 0, keepdims=True)
            dvec[3:4, lanes] += jnp.sum(grad_normed, 0, keepdims=True)
            scaled = grad_normed * gain
            grad_out = inverse * (scaled - head_mean(scaled) - hat * head_mean(scaled * hat))
            dout[rows, lanes] = grad_out
            reader = rec[rows, lanes] * factor[table(LEVELS - 1)] * valid[rows, :]
            inner = own_blocks(exact_tn(grad_out, reader))
            local[slot] = inner
            chunk_a = chunk_decay(chunk, lanes)
            return after_a * chunk_a, after_b * chunk_a + inner

        last_a, last_b = lax.fori_loop(
            0, chunks, step, (jnp.ones((1, PAIR), jnp.float32), jnp.zeros((PAIR, PAIR), jnp.float32))
        )
        send_a[:, lanes] = jnp.broadcast_to(last_a, (8, PAIR))
        send_b[:, lanes] = packed_state(last_b)
        return carry

    lax.fori_loop(0, pairs, summary, 0)
    exchange = (count, (send_a, send_b), (land_a, land_b), send_sems, recv_sems, False)
    send_states(*exchange)

    def inside(slot, carry):
        pair, chunk = slot // chunks, slot % chunks
        rows, lanes = rows_of(chunk), lanes_of(pair)
        acceptor, lookup, payload = rec[rows, lanes], key[rows, lanes], val[rows, lanes]
        reward = vec[0:1, lanes]
        grad_exact = dout[rows, lanes]
        grad_out = grad_exact.astype(bfloat)
        place = jnp.where(seg_col[rows, :] == seg_row[marks_of(chunk), :][:1], level[...], -1.0)
        grad_scores = exact_nt(grad_exact, stack_heads(payload))
        grad_bonus = head_sum(grad_exact * payload)
        dvec[1:2, lanes] += jnp.sum(acceptor * lookup * grad_bonus, 0, keepdims=True)
        grad_acceptor = reward * lookup * grad_bonus
        grad_lookup = reward * acceptor * grad_bonus
        for at in range(LEVELS):
            factor, left, right = level_inputs(at, acceptor, lookup, factors.at[slot])
            left_low, right_low = left.astype(bfloat), stack_heads(right.astype(bfloat))
            here = place == float(at)
            grad_part = jnp.where(here, grad_scores, 0.0).astype(bfloat)
            grad_left = dot_nn(grad_part, right_low)
            grad_right = merge_heads(dot_tn(grad_part, left_low))
            if at:
                grad_left = grad_left * factor
                grad_right = grad_right * factor
                steps[table(at - 1), :] = acceptor * grad_left + lookup * grad_right
            grad_acceptor += grad_left
            grad_lookup += grad_right
        drec_part[rows, lanes] = grad_acceptor
        dkey_part[rows, lanes] = grad_lookup
        bonus = head_sum(acceptor * reward * lookup)
        dval_part[rows, lanes] = bonus * grad_exact + merge_heads(
            dot_tn(kept[slot], grad_out)
        )
        inner = (LEVELS - 1) * CHUNK
        dlog_part[rows, lanes] = dot_nn(sums_back[:, :inner], steps[...].astype(bfloat))
        return carry

    lax.fori_loop(0, pairs * chunks, inside, 0)
    wait_states(*exchange)
    me = lax.axis_index("dp")

    def later(step, state):
        other = count - 1 - step
        return state * land_a[other][:1] + unpacked_state(land_b[other])

    end_b[...] = lax.fori_loop(0, count - 1 - me, later, jnp.zeros(end_b.shape, jnp.float32))

    def finish(pair, carry):
        lanes = lanes_of(pair)

        def step(back, after):
            chunk = chunks - 1 - back
            rows, slot = rows_of(chunk), pair * chunks + chunk
            state = states[slot]
            after_low = after.astype(bfloat)
            reach = factors[slot, table(LEVELS - 1), :] * valid[rows, :]
            tail = factors[slot, table(LEVELS), :] * ending[rows, :]
            acceptor, lookup = rec[rows, lanes], key[rows, lanes]
            grad_reader = exact_nn(dout[rows, lanes], state) * reach
            grad_faded = exact_nn(val[rows, lanes], after) * tail
            faded = (lookup * tail).astype(bfloat)
            chunk_a = chunk_decay(chunk, lanes)
            total = chunk_a * jnp.sum(after * state, 0, keepdims=True)
            drec[rows, lanes] = (drec_part[rows, lanes] + grad_reader).astype(bfloat)
            dkey[rows, lanes] = (dkey_part[rows, lanes] + grad_faded).astype(bfloat)
            dval[rows, lanes] = (dval_part[rows, lanes] + dot_nt(faded, after_low)).astype(bfloat)
            inner = (LEVELS - 1) * CHUNK
            moves = jnp.concatenate([acceptor * grad_reader, lookup * grad_faded], 0)
            grad_log = dlog_part[rows, lanes] + total + dot_nn(
                sums_back[:, inner:], moves.astype(bfloat)
            )
            raw = grad_log * logw[rows, lanes]
            draw[rows, lanes] = raw
            dvec[0:1, lanes] += jnp.sum(raw, 0, keepdims=True)
            return after * chunk_a + local[slot]

        lax.fori_loop(0, chunks, step, stack_heads(end_b[:, lanes]))
        return carry

    lax.fori_loop(0, pairs, finish, 0)
    for copy in swaps:
        copy.wait()
    for other in range(mp_count):
        lanes = slice(other * features, (other + 1) * features)
        mixed[:, lanes] = (residual[:, lanes] + swapped[other].astype(jnp.float32)).astype(bfloat)


def exchange_scratch(count, features):
    return [
        pltpu.VMEM((8, features), jnp.float32),
        pltpu.VMEM((2 * LANE_SPAN, features), jnp.bfloat16),
        pltpu.VMEM((count, 8, features), jnp.float32),
        pltpu.VMEM((count, 2 * LANE_SPAN, features), jnp.bfloat16),
        pltpu.SemaphoreType.DMA((2, count)),
        pltpu.SemaphoreType.DMA((2, count)),
    ]


def run_forward(
    count, mp_count, rec, key, val, gpre, logw, vec, marks, tables, cotangent, tokens, out_weight,
    key_low,
):
    rows, features = rec.shape
    width = tokens.shape[1]
    chunks, pairs = rows // CHUNK, features // PAIR
    slots = chunks * pairs
    whole_array = pl.BlockSpec(memory_space=pltpu.VMEM)
    level, sums, _ = tables
    return pl.pallas_call(
        functools.partial(recurrence_forward, count, mp_count, chunks, pairs),
        out_shape=(
            jax.ShapeDtypeStruct((rows, features), jnp.bfloat16),
            jax.ShapeDtypeStruct((rows, features), jnp.float32),
            jax.ShapeDtypeStruct((slots, PAIR, PAIR), jnp.float32),
            jax.ShapeDtypeStruct((slots, CHUNK, 2 * CHUNK), jnp.bfloat16),
            jax.ShapeDtypeStruct((rows, features), jnp.bfloat16),
            jax.ShapeDtypeStruct(tokens.shape, jnp.float32),
            jax.ShapeDtypeStruct((rows, width), jnp.bfloat16),
            jax.ShapeDtypeStruct((16, width), jnp.bfloat16),
            jax.ShapeDtypeStruct((count * key_low.shape[0], key_low.shape[1]), jnp.bfloat16),
        ),
        in_specs=[whole_array] * 17,
        out_specs=(whole_array,) * 8 + (pl.BlockSpec(memory_space=pl.ANY),),
        scratch_shapes=[
            pltpu.VMEM((slots, sums.shape[0], PAIR), jnp.float32),
            pltpu.VMEM((slots, 8, PAIR), jnp.float32),
            pltpu.VMEM((slots, PAIR, PAIR), jnp.float32),
            pltpu.VMEM((LANE_SPAN, features), jnp.float32),
        ]
        + exchange_scratch(count, features)
        + [
            pltpu.SemaphoreType.DMA((mp_count - 1,)),
            pltpu.SemaphoreType.DMA((mp_count - 1,)),
            pltpu.VMEM((rows, width), jnp.bfloat16),
            pltpu.VMEM((rows, width), jnp.bfloat16),
            pltpu.VMEM((2, rows, width), jnp.bfloat16),
            pltpu.VMEM(tokens.shape, jnp.float32),
            *line_sems(mp_count),
            *line_sems(mp_count),
            pltpu.SemaphoreType.DMA((mp_count,)),
            pltpu.SemaphoreType.DMA,
            pltpu.SemaphoreType.DMA,
            *cube_sems(2, count),
        ],
        compiler_params=pltpu.CompilerParams(
            collective_id=1, has_side_effects=True, vmem_limit_bytes=44 << 20
        ),
        name="recurrence_forward",
    )(rec, key, val, gpre, logw, vec, *marks, level, sums, cotangent, tokens, out_weight, key_low)


def run_backward(
    count, mp_count, dgated, wkv, states, kept, rec, key, val, gpre, logw, vec, marks, tables,
    change, residual,
):
    rows, features = rec.shape
    chunks, pairs = rows // CHUNK, features // PAIR
    slots = chunks * pairs
    whole_array = pl.BlockSpec(memory_space=pltpu.VMEM)
    level, sums, sums_back = tables
    low = jax.ShapeDtypeStruct((rows, features), jnp.bfloat16)
    full = pltpu.VMEM((rows, features), jnp.float32)
    return pl.pallas_call(
        functools.partial(recurrence_backward, count, mp_count, chunks, pairs),
        out_shape=(
            low,
            low,
            low,
            low,
            jax.ShapeDtypeStruct((rows, features), jnp.float32),
            jax.ShapeDtypeStruct((8, features), jnp.float32),
            jax.ShapeDtypeStruct(residual.shape, jnp.bfloat16),
        ),
        in_specs=[whole_array] * 20,
        out_specs=(whole_array,) * 7,
        scratch_shapes=[
            pltpu.VMEM((slots, sums.shape[0], PAIR), jnp.float32),
            pltpu.VMEM((slots, PAIR, PAIR), jnp.float32),
            pltpu.VMEM((LANE_SPAN, features), jnp.float32),
            full,
            full,
            full,
            full,
            full,
            pltpu.VMEM(((LEVELS - 1) * CHUNK, PAIR), jnp.float32),
        ]
        + exchange_scratch(count, features)
        + [pltpu.VMEM((mp_count,) + residual.shape[:1] + (features,), jnp.bfloat16)]
        + [
            pltpu.SemaphoreType.DMA((mp_count - 1,)),
            pltpu.SemaphoreType.DMA((mp_count - 1,)),
        ],
        compiler_params=pltpu.CompilerParams(
            collective_id=2, has_side_effects=True, vmem_limit_bytes=44 << 20
        ),
        name="recurrence_backward",
    )(
        dgated, wkv, states, kept, rec, key, val, gpre, logw, vec, *marks, level, sums, sums_back,
        change, residual,
    )


def flipped(index, mask):
    for bit in range(mask.bit_length()):
        size = 1 << bit
        if mask & size:
            index = index + size - 2 * size * lax.rem(index // size, 2)
    return index


def masks_over(bits):
    masks = [0]
    for bit in bits:
        masks = masks + [mask | (1 << bit) for mask in masks]
    return masks


def paths(count):
    higher = list(range(1, count.bit_length() - 1))
    return higher + [0], higher[::-1] + [0]


def remote(source, target, send_sem, recv_sem, dp, mp):
    return pltpu.make_async_remote_copy(
        src_ref=source,
        dst_ref=target,
        send_sem=send_sem,
        recv_sem=recv_sem,
        device_id=(dp, mp),
        device_id_type=MESH,
    )


def greet_all(partners, some=()):
    barrier = pltpu.get_barrier_semaphore()
    count = len(partners)
    for dp, mp in partners:
        pl.semaphore_signal(barrier, inc=1, device_id=(dp, mp), device_id_type=MESH)
    for present, dp, mp in some:

        @pl.when(present)
        def _():
            pl.semaphore_signal(barrier, inc=1, device_id=(dp, mp), device_id_type=MESH)

        count = count + jnp.where(present, 1, 0)
    pl.semaphore_wait(barrier, count)


class Halo:
    def __init__(self, dp_count, mp_count, send_sems, recv_sem):
        self.dp, self.mp = lax.axis_index("dp"), lax.axis_index("mp")
        self.count, self.lines = dp_count, mp_count
        self.send_sems, self.recv_sem = send_sems, recv_sem
        self.after = lax.rem(self.dp + 1, dp_count)
        self.previous = lax.rem(self.dp + dp_count - 1, dp_count)
        self.takes = self.dp > 0
        self.gives = jnp.logical_and(self.mp == mp_count - 1, self.dp < dp_count - 1)

    def partners(self):
        return [(self.takes, self.previous, self.lines - 1)] + [
            (self.gives, self.after, line) for line in range(self.lines)
        ]

    def copy(self, source, target, line):
        return remote(source, target, self.send_sems.at[line], self.recv_sem, self.after, line)

    def start(self, source, target):
        @pl.when(self.dp == 0)
        def _():
            target[...] = jnp.zeros(target.shape, target.dtype)

        @pl.when(self.gives)
        def _():
            for line in range(self.lines):
                self.copy(source, target, line).start()

    def finish(self, source, target):
        @pl.when(self.takes)
        def _():
            self.copy(source, target, 0).wait_recv()

        @pl.when(self.gives)
        def _():
            for line in range(self.lines):
                self.copy(source, target, line).wait_send()


class Arrival:
    def __init__(self, dp_count, send_sem, recv_sem):
        self.dp, self.mp = lax.axis_index("dp"), lax.axis_index("mp")
        self.send_sem, self.recv_sem = send_sem, recv_sem
        self.after = lax.rem(self.dp + 1, dp_count)
        self.previous = lax.rem(self.dp + dp_count - 1, dp_count)
        self.gives, self.takes = self.dp > 0, self.dp < dp_count - 1

    def partners(self):
        return [(self.gives, self.previous, self.mp), (self.takes, self.after, self.mp)]

    def copy(self, row, land):
        return remote(row, land, self.send_sem, self.recv_sem, self.previous, self.mp)

    def start(self, row, land):
        @pl.when(self.gives)
        def _():
            self.copy(row, land).start()

        @pl.when(jnp.logical_not(self.takes))
        def _():
            land[...] = jnp.zeros(land.shape, land.dtype)

    def wait(self, row, land):
        @pl.when(self.takes)
        def _():
            self.copy(row, land).wait_recv()

    def finish(self, row, land):
        @pl.when(self.gives)
        def _():
            self.copy(row, land).wait_send()


def line_partners(count):
    dp, mp = lax.axis_index("dp"), lax.axis_index("mp")
    return [(dp, lax.rem(mp + step, count)) for step in sorted({1, count - 1})]


def cube_partners(count):
    dp, mp = lax.axis_index("dp"), lax.axis_index("mp")
    return [(flipped(dp, 1 << bit), mp) for bit in range(count.bit_length() - 1)]


class Line:
    def __init__(self, count, rows, send_sems, recv_sems):
        self.count, self.rows = count, rows
        self.send_sems, self.recv_sems = send_sems, recv_sems
        self.dp, self.me = lax.axis_index("dp"), lax.axis_index("mp")
        self.piece = rows // PIECES

    def at(self, block, piece):
        return pl.ds(pl.multiple_of(block * self.rows + piece * self.piece, 16), self.piece)

    def copy(self, source, target, right, slot, piece):
        side = 0 if right else 1
        return remote(
            source,
            target,
            self.send_sems.at[side, slot, piece],
            self.recv_sems.at[side, slot, piece],
            self.dp,
            lax.rem(self.me + (1 if right else self.count - 1), self.count),
        )


class LineGather(Line):
    def hop(self, target, distance, piece, right):
        block = self.me - distance if right else self.me + distance
        ref = target.at[self.at(block, piece)]
        return self.copy(ref, ref, right, distance, piece)

    def holds(self, distance, right):
        return self.me >= distance if right else self.me + distance < self.count

    def passes(self, distance, right):
        onward = self.me < self.count - 1 if right else self.me > 0
        return jnp.logical_and(self.holds(distance, right), onward)

    def send(self, target, distance, piece):
        for right in (True, False):
            if distance:

                @pl.when(self.holds(distance, right))
                def _():
                    block = self.me - distance if right else self.me + distance
                    ref = target.at[self.at(block, piece)]
                    self.copy(ref, ref, right, distance - 1, piece).wait_recv()

            if distance < self.count - 1:

                @pl.when(self.passes(distance, right))
                def _():
                    self.hop(target, distance, piece, right).start()

    def finish(self, target):
        for distance in range(self.count - 1):
            for piece in range(PIECES):
                for right in (True, False):

                    @pl.when(self.passes(distance, right))
                    def _():
                        self.hop(target, distance, piece, right).wait_send()


class LineSum(Line):
    def hop(self, source, land, block, piece, right):
        return self.copy(
            source.at[self.at(block, piece)],
            land.at[0 if right else 1, self.at(block, piece)],
            right,
            block,
            piece,
        )

    def own(self, part, extra, block, piece):
        value = part[self.at(block, piece)].astype(jnp.float32)
        if extra is not None and piece == PIECES - 1:
            row = lax.broadcasted_iota(jnp.int32, value.shape, 0)
            last = jnp.logical_and(row == self.piece - 1, block == self.count - 1)
            value = value + jnp.where(last, extra[:1], 0.0)
        return value

    def begin(self, part, extra, moving, land, number, ready=None):
        for piece in range(PIECES):
            if ready is not None and piece == PIECES - 1:
                ready()
            for right in (True, False):
                block = self.count - 1 - number if right else number
                at = self.at(block, piece)

                @pl.when(self.me == (0 if right else self.count - 1))
                def _():
                    moving[at] = self.own(part, extra, block, piece).astype(jnp.bfloat16)
                    if number:
                        before = block + 1 if right else block - 1
                        self.hop(moving, land, before, piece, right).wait_send()
                    self.hop(moving, land, block, piece, right).start()

    def forward(self, part, extra, moving, land, block, piece, right):
        side = 0 if right else 1
        at = self.at(block, piece)
        inside = jnp.logical_and(self.me > 0, self.me < self.count - 1)

        @pl.when(jnp.logical_and(inside, self.me < block if right else self.me > block))
        def _():
            self.hop(moving, land, block, piece, right).wait_recv()
            moving[at] = (
                self.own(part, extra, block, piece) + land[side, at].astype(jnp.float32)
            ).astype(jnp.bfloat16)
            self.hop(moving, land, block, piece, right).start()

    def step(self, part, extra, moving, land, number):
        for piece in range(PIECES):
            self.forward(part, extra, moving, land, self.count - 1 - number, piece, True)
            self.forward(part, extra, moving, land, number, piece, False)

    def total(self, part, extra, moving, land, total, piece):
        at = self.at(self.me, piece)
        own = slice(piece * self.piece, (piece + 1) * self.piece)
        total[own] = self.own(part, extra, self.me, piece)
        for right in (True, False):

            @pl.when(self.me > 0 if right else self.me < self.count - 1)
            def _():
                self.hop(moving, land, self.me, piece, right).wait_recv()
                total[own] += land[0 if right else 1, at].astype(jnp.float32)

        return own

    def finish(self, moving, land):
        inside = jnp.logical_and(self.me > 0, self.me < self.count - 1)
        for number in range(self.count - 1):
            for piece in range(PIECES):
                for right in (True, False):
                    block = self.count - 1 - number if right else number
                    sent = jnp.logical_and(inside, self.me < block if right else self.me > block)
                    if number == self.count - 2:
                        sent = jnp.logical_or(sent, self.me == (0 if right else self.count - 1))

                    @pl.when(sent)
                    def _():
                        self.hop(moving, land, block, piece, right).wait_send()


class Cube:
    def __init__(self, count, send_sems, recv_sems):
        self.count, self.send_sems, self.recv_sems = count, send_sems, recv_sems
        self.dp, self.mp = lax.axis_index("dp"), lax.axis_index("mp")
        self.stages = count.bit_length() - 1

    def copy(self, source, target, unit, mask, bit):
        return remote(
            source,
            target,
            self.send_sems.at[unit, mask],
            self.recv_sems.at[unit, mask],
            flipped(self.dp, 1 << bit),
            self.mp,
        )


class CubeGather(Cube):
    def hop(self, unit, view, mask, bit):
        ref = view(flipped(self.dp, mask))
        return self.copy(ref, ref, unit, mask | (1 << bit), bit)

    def arrived(self, unit, view, mask, bit):
        ref = view(flipped(self.dp, mask))
        self.copy(ref, ref, unit, mask, bit).wait_recv()

    def stage(self, unit, path, view, stage):
        order = paths(self.count)[path]
        last = self.stages - 1
        if stage > last:
            for mask in masks_over(order[:last]):
                self.arrived(unit, view, mask | (1 << order[last]), order[last])
            return
        new = [0]
        if stage:
            new = [mask | (1 << order[stage - 1]) for mask in masks_over(order[: stage - 1])]
            for mask in new:
                self.arrived(unit, view, mask, order[stage - 1])
        if stage < last:
            for mask in masks_over(order[:stage]):
                self.hop(unit, view, mask, order[stage]).start()
        for mask in new:
            self.hop(unit, view, mask, order[last]).start()

    def finish(self, unit, path, view):
        order = paths(self.count)[path]
        for stage in range(self.stages):
            for mask in masks_over(order[:stage]):
                self.hop(unit, view, mask, order[stage]).wait_send()


class CubeSum(Cube):
    def slot(self, order, stage, mask):
        base = self.count - (self.count >> stage)
        return base + masks_over(order[stage + 1 :]).index(mask)

    def source(self, unit, order, view, land, stage, mask):
        if stage == 0:
            return view(flipped(self.dp, mask))
        return land.at[self.slot(order, stage - 1, mask)]

    def sends(self, unit, path, view, land, stage):
        order = paths(self.count)[path][::-1]
        bit = order[stage]
        return [
            self.copy(
                self.source(unit, order, view, land, stage, mask | (1 << bit)),
                land.at[self.slot(order, stage, mask)],
                unit,
                mask | (1 << bit),
                bit,
            )
            for mask in masks_over(order[stage + 1 :])
        ]

    def start(self, unit, path, view, land, stage):
        for copy in self.sends(unit, path, view, land, stage):
            copy.start()

    def absorb(self, unit, path, view, land, stage, out=None):
        order = paths(self.count)[path][::-1]
        for copy, mask in zip(
            self.sends(unit, path, view, land, stage), masks_over(order[stage + 1 :])
        ):
            copy.wait_recv()
            before = self.source(unit, order, view, land, stage, mask)
            here = land.at[self.slot(order, stage, mask)]
            step = 16

            def add(number, carry):
                at = pl.ds(pl.multiple_of(number * step, step), step)
                both = before[at].astype(jnp.float32) + here[at].astype(jnp.float32)
                if out is None:
                    here[at] = both.astype(jnp.bfloat16)
                else:
                    out[at] = both
                return carry

            lax.fori_loop(0, here.shape[0] // step, add, 0)

    def finish(self, unit, path, view, land):
        for stage in range(self.stages):
            for copy in self.sends(unit, path, view, land, stage):
                copy.wait_send()


def line_sems(count):
    return [pltpu.SemaphoreType.DMA((2, count, PIECES)), pltpu.SemaphoreType.DMA((2, count, PIECES))]


def cube_sems(units, count):
    return [pltpu.SemaphoreType.DMA((units, count)), pltpu.SemaphoreType.DMA((units, count))]


def start_kernel(
    dp_count, mp_count, tokens, pack, mix_state, out_state, gate_state, key_state, value_state,
    tokens_all, small, mix_all, out_low, gate_low, key_low, value_low, before,
    mix, mix_full, out_full, gate_full, key_full, value_full,
    load_sems, own_sems, line_send, line_recv, pack_send, pack_recv, cube_send, cube_recv,
    halo_send, halo_recv,
):
    dp, mp = lax.axis_index("dp"), lax.axis_index("mp")
    rows = tokens.shape[0]
    halo = Halo(dp_count, mp_count, halo_send, halo_recv)
    edge = tokens.at[pl.ds(rows - 16, 16)]
    matrices, block = mix.shape[0], mix.shape[1]
    pack_rows, group = pack.shape[0], pack.shape[0] * mp_count
    half = group // 2
    states = (mix_state, out_state, gate_state, key_state, value_state)
    fulls = (mix_full, out_full, gate_full, key_full, value_full)
    loads = [
        pltpu.make_async_copy(state.at[0], full, load_sems.at[number])
        for number, (state, full) in enumerate(zip(states, fulls))
    ]
    for load in loads:
        load.start()
    others = [lax.rem(mp + step, mp_count) for step in range(1, mp_count)]
    greet_all([(dp, other) for other in others] + cube_partners(dp_count), halo.partners())
    halo.start(edge, before)
    line = LineGather(mp_count, rows, line_send, line_recv)
    cube = CubeGather(dp_count, cube_send, cube_recv)

    pack_at = small.at[pl.ds(pl.multiple_of(dp * group + mp * pack_rows, 16), pack_rows)]
    own = [
        pltpu.make_async_copy(pack, pack_at, own_sems.at[0]),
        pltpu.make_async_copy(
            tokens, tokens_all.at[pl.ds(pl.multiple_of(mp * rows, 16), rows)], own_sems.at[1]
        ),
    ]
    pack_copies = [
        remote(pack, pack_at, pack_send.at[step], pack_recv.at[step], dp, other)
        for step, other in enumerate(others)
    ]
    for copy in pack_copies + own:
        copy.start()
    loads[0].wait()
    for number in range(matrices):
        mix[number] = mix_full[number].astype(jnp.bfloat16)
    own_mix = [
        pltpu.make_async_copy(
            mix.at[number],
            mix_all.at[number, pl.ds(pl.multiple_of(dp * block, 16), block)],
            own_sems.at[2 + number],
        )
        for number in range(matrices)
    ]
    for copy in own_mix:
        copy.start()

    def small_view(part):
        def view(index):
            return small.at[pl.ds(pl.multiple_of(index * group + part * half, 16), half)]

        return view

    def mix_view(number):
        def view(index):
            return mix_all.at[number, pl.ds(pl.multiple_of(index * block, 16), block)]

        return view

    mix_units = [
        (2 + number, 0 if 2 * number < matrices else 1, mix_view(number))
        for number in range(matrices)
    ]
    small_units = [(part, part, small_view(part)) for part in range(2)]
    for copy in own + own_mix:
        copy.wait()
    for unit in mix_units:
        cube.stage(*unit, 0)
    for piece in range(PIECES):
        line.send(tokens_all, 0, piece)
    for load, full, low in zip(loads[1:], fulls[1:], (out_low, gate_low, key_low, value_low)):
        load.wait()
        step = 64

        def convert(number, carry):
            at = pl.ds(pl.multiple_of(number * step, step), step)
            low[at] = full[at].astype(jnp.bfloat16)
            return carry

        lax.fori_loop(0, full.shape[0] // step, convert, 0)
    for copy in pack_copies:
        copy.wait()
    for unit in small_units:
        cube.stage(*unit, 0)
    for distance in range(1, mp_count):
        for piece in range(PIECES):
            line.send(tokens_all, distance, piece)
        if distance < dp_count.bit_length() - 1:
            for unit in mix_units + small_units:
                cube.stage(*unit, distance)
    for stage in range(min(mp_count, dp_count.bit_length() - 1), dp_count.bit_length()):
        for unit in mix_units + small_units:
            cube.stage(*unit, stage)
    line.finish(tokens_all)
    halo.finish(edge, before)
    for unit in mix_units + small_units:
        cube.finish(*unit)


def run_start(dp_count, mp_count, tokens, pack, states):
    rows, width = tokens.shape
    matrices, block, features = states[0].shape[1:]
    anywhere = pl.BlockSpec(memory_space=pl.ANY)
    vmem = pl.BlockSpec(memory_space=pltpu.VMEM)
    bfloat = jnp.bfloat16
    return pl.pallas_call(
        functools.partial(start_kernel, dp_count, mp_count),
        out_shape=(
            jax.ShapeDtypeStruct((rows * mp_count, width), bfloat),
            jax.ShapeDtypeStruct((pack.shape[0] * mp_count * dp_count, pack.shape[1]), bfloat),
            jax.ShapeDtypeStruct((matrices, block * dp_count, features), bfloat),
            *[jax.ShapeDtypeStruct(state.shape[1:], bfloat) for state in states[1:]],
            jax.ShapeDtypeStruct((16, width), bfloat),
        ),
        in_specs=[vmem, vmem] + [anywhere] * 5,
        out_specs=(anywhere,) * 3 + (vmem,) * 5,
        scratch_shapes=[
            pltpu.VMEM(states[0].shape[1:], bfloat),
            *[pltpu.VMEM(state.shape[1:], jnp.float32) for state in states],
            pltpu.SemaphoreType.DMA((5,)),
            pltpu.SemaphoreType.DMA((2 + matrices,)),
            *line_sems(mp_count),
            pltpu.SemaphoreType.DMA((mp_count - 1,)),
            pltpu.SemaphoreType.DMA((mp_count - 1,)),
            *cube_sems(2 + matrices, dp_count),
            pltpu.SemaphoreType.DMA((mp_count,)),
            pltpu.SemaphoreType.DMA,
        ],
        compiler_params=pltpu.CompilerParams(
            collective_id=3, has_side_effects=True, vmem_limit_bytes=60 << 20
        ),
        name="gather_start",
    )(tokens, pack, *states)


def backward_rows(total, rows, source, gain, skip):
    value = source[rows].astype(jnp.float32)
    centre = value - jnp.mean(value, -1, keepdims=True)
    inverse = lax.rsqrt(jnp.mean(centre * centre, -1, keepdims=True) + norm_epsilon)
    return skip[rows].astype(jnp.float32) + norm_backward(total, centre * inverse, inverse, gain[:1])


def exchange_kernel(
    dp_count, count, part, first, source, gain, skip,
    own, gathered,
    moving, land, total, edge,
    sum_send, sum_recv, line_send, line_recv, row_send, row_recv,
):
    rows = own.shape[0]
    arrival = Arrival(dp_count, row_send, row_recv)
    greet_all(line_partners(count), arrival.partners())
    arrival.start(first, edge)
    adder = LineSum(count, rows, sum_send, sum_recv)
    line = LineGather(count, rows, line_send, line_recv)
    for number in range(count - 1):
        ready = None if number else lambda: arrival.wait(first, edge)
        adder.begin(part, edge, moving, land, number, ready)
        adder.step(part, edge, moving, land, number)
    for piece in range(PIECES):
        at = adder.total(part, edge, moving, land, total, piece)
        value = backward_rows(total[at], at, source, gain, skip)
        own[at] = value
        gathered[line.at(line.me, piece)] = value.astype(jnp.bfloat16)
        line.send(gathered, 0, piece)
    for distance in range(1, count):
        for piece in range(PIECES):
            line.send(gathered, distance, piece)
    adder.finish(moving, land)
    line.finish(gathered)
    arrival.finish(first, edge)


def run_exchange(dp_count, count, part, first, source, gain, skip):
    rows, width = part.shape[0] // count, part.shape[1]
    vmem = pl.BlockSpec(memory_space=pltpu.VMEM)
    return pl.pallas_call(
        functools.partial(exchange_kernel, dp_count, count),
        out_shape=(
            jax.ShapeDtypeStruct((rows, width), jnp.float32),
            jax.ShapeDtypeStruct(part.shape, jnp.bfloat16),
        ),
        in_specs=[vmem] * 5,
        out_specs=(vmem, vmem),
        scratch_shapes=[
            pltpu.VMEM(part.shape, jnp.bfloat16),
            pltpu.VMEM((2,) + part.shape, jnp.bfloat16),
            pltpu.VMEM((rows, width), jnp.float32),
            pltpu.VMEM((8, width), jnp.float32),
            *line_sems(count),
            *line_sems(count),
            pltpu.SemaphoreType.DMA,
            pltpu.SemaphoreType.DMA,
        ],
        compiler_params=pltpu.CompilerParams(
            collective_id=5, has_side_effects=True, vmem_limit_bytes=20 << 20
        ),
        name="sum_and_gather",
    )(part, first, source, gain, skip)


def end_kernel(
    dp_count, mp_count, part, first, source, gain, skip, mix_a, mix_b, mix_c, mix_d, pack,
    own, mix_sum, pack_sum,
    moving, land, total, mix_land, pack_land, pack_own, pack_out, small_land,
    edge, sum_send, sum_recv, cube_send, cube_recv, small_send, small_recv, row_send, row_recv,
):
    dp, mp = lax.axis_index("dp"), lax.axis_index("mp")
    mix = (mix_a, mix_b, mix_c, mix_d)
    rows, matrices = own.shape[0], len(mix)
    block, group = mix_sum.shape[1], pack_own.shape[0]
    half, pack_rows = group // 2, pack_sum.shape[0]
    others = [lax.rem(mp + step, mp_count) for step in range(1, mp_count)]
    arrival = Arrival(dp_count, row_send, row_recv)
    greet_all([(dp, other) for other in others] + cube_partners(dp_count), arrival.partners())
    arrival.start(first, edge)
    adder = LineSum(mp_count, rows, sum_send, sum_recv)
    cube = CubeSum(dp_count, cube_send, cube_recv)

    def mix_view(number):
        def view(index):
            return mix[number].at[pl.ds(pl.multiple_of(index * block, 16), block)]

        return view

    def pack_view(side):
        def view(index):
            return pack.at[pl.ds(pl.multiple_of(index * group + side * half, 16), half)]

        return view

    units = [(side, side, pack_view(side), pack_land.at[side]) for side in range(2)] + [
        (2 + number, 0 if 2 * number < matrices else 1, mix_view(number), mix_land.at[number])
        for number in range(matrices)
    ]
    outs = [pack_own.at[pl.ds(side * half, half)] for side in range(2)] + [
        mix_sum.at[number] for number in range(matrices)
    ]
    for unit in units:
        cube.start(*unit, 0)
    adder.begin(part, edge, moving, land, 0, lambda: arrival.wait(first, edge))
    last = cube.stages - 1
    for unit in units:
        cube.absorb(*unit, 0)
        cube.start(*unit, 1)
    for number in range(1, mp_count - 1):
        adder.begin(part, edge, moving, land, number)
        adder.step(part, edge, moving, land, number - 1)
    adder.step(part, edge, moving, land, mp_count - 2)
    for piece in range(PIECES):
        at = adder.total(part, edge, moving, land, total, piece)
        own[at] = backward_rows(total[at], at, source, gain, skip)
    for stage in range(1, last):
        for unit in units:
            cube.absorb(*unit, stage)
            cube.start(*unit, stage + 1)
    for unit, out in zip(units[:2], outs[:2]):
        cube.absorb(*unit, last, out)
    pack_out[...] = pack_own[...].astype(jnp.bfloat16)
    small_copies = [
        remote(
            pack_out.at[pl.ds(pl.multiple_of(other * pack_rows, 16), pack_rows)],
            small_land.at[step],
            small_send.at[step],
            small_recv.at[step],
            dp,
            other,
        )
        for step, other in enumerate(others)
    ]
    for copy in small_copies:
        copy.start()
    for unit, out in zip(units[2:], outs[2:]):
        cube.absorb(*unit, last, out)
    pack_sum[...] = pack_own[pl.ds(pl.multiple_of(mp * pack_rows, 16), pack_rows), :]
    for step, copy in enumerate(small_copies):
        copy.wait()
        pack_sum[...] += small_land[step].astype(jnp.float32)
    adder.finish(moving, land)
    arrival.finish(first, edge)
    for unit in units:
        cube.finish(*unit)


def run_end(dp_count, mp_count, part, first, source, gain, skip, mix, pack):
    rows, width = source.shape
    matrices, features = len(mix), mix[0].shape[1]
    block, group = mix[0].shape[0] // dp_count, pack.shape[0] // dp_count
    lanes = pack.shape[1]
    vmem = pl.BlockSpec(memory_space=pltpu.VMEM)
    return pl.pallas_call(
        functools.partial(end_kernel, dp_count, mp_count),
        out_shape=(
            jax.ShapeDtypeStruct((rows, width), jnp.float32),
            jax.ShapeDtypeStruct((matrices, block, features), jnp.float32),
            jax.ShapeDtypeStruct((group // mp_count, lanes), jnp.float32),
        ),
        in_specs=[vmem] * 10,
        out_specs=(vmem,) * 3,
        scratch_shapes=[
            pltpu.VMEM(part.shape, jnp.bfloat16),
            pltpu.VMEM((2,) + part.shape, jnp.bfloat16),
            pltpu.VMEM((rows, width), jnp.float32),
            pltpu.VMEM((matrices, dp_count - 1, block, features), jnp.bfloat16),
            pltpu.VMEM((2, dp_count - 1, group // 2, lanes), jnp.bfloat16),
            pltpu.VMEM((group, lanes), jnp.float32),
            pltpu.VMEM((group, lanes), jnp.bfloat16),
            pltpu.VMEM((mp_count - 1, group // mp_count, lanes), jnp.bfloat16),
            pltpu.VMEM((8, width), jnp.float32),
            *line_sems(mp_count),
            *cube_sems(2 + matrices, dp_count),
            pltpu.SemaphoreType.DMA((mp_count - 1,)),
            pltpu.SemaphoreType.DMA((mp_count - 1,)),
            pltpu.SemaphoreType.DMA,
            pltpu.SemaphoreType.DMA,
        ],
        compiler_params=pltpu.CompilerParams(
            collective_id=6, has_side_effects=True, vmem_limit_bytes=56 << 20
        ),
        name="sum_end",
    )(part, first, source, gain, skip, *mix, pack)


def update_rows(rate, state, grad, new):
    scaled = rate * grad[...].astype(jnp.float32)
    velocity = momentum_rate * state[1] + scaled
    weight = state[0] - (scaled + momentum_rate * velocity)
    new[0] = velocity
    new[1] = weight
    new[2] = average_rate * state[2] + (1.0 - average_rate) * weight


def run_update(state, grad, fan, total_tokens):
    shape = state.shape
    lanes = shape[-1]
    flat = state.reshape(3, -1, lanes)
    grad = grad.reshape(-1, lanes)
    block = 128
    while grad.shape[0] % (2 * block) == 0 and 2 * block * lanes <= 1 << 18:
        block *= 2
    triple = pl.BlockSpec((3, block, lanes), lambda i: (0, i, 0))
    return pl.pallas_call(
        functools.partial(update_rows, (total_tokens * fan) ** (-0.5)),
        grid=(grad.shape[0] // block,),
        out_shape=jax.ShapeDtypeStruct(flat.shape, jnp.float32),
        in_specs=[triple, pl.BlockSpec((block, lanes), lambda i: (i, 0))],
        out_specs=triple,
        compiler_params=pltpu.CompilerParams(vmem_limit_bytes=24 << 20),
        name="momentum_update",
    )(flat, grad).reshape(shape)


def lane_mask(shape, low, high):
    lane = lax.broadcasted_iota(jnp.int32, shape, len(shape) - 1)
    return jnp.logical_and(lane >= low, lane < high)


def masked(value, low, high):
    return jnp.where(lane_mask(value.shape, low, high), value, jnp.zeros_like(value))


def block_norm(value, vectors):
    hidden, hat, _ = norm_forward(value.astype(jnp.float32), vectors[0:1], vectors[1:2], norm_epsilon)
    return hidden, hat


def block_delta(hidden, before, keep):
    row = lax.broadcasted_iota(jnp.int32, hidden.shape, 0)
    behind = jnp.where(row == 0, before, pltpu.roll(hidden, 1, 0))
    return behind * keep - hidden


def mixing_forward(
    tokens, heads, keep, small, vectors, decay_row, up_own, mix, inputs, rec, key, val, gpre, logw, acts
):
    bfloat = jnp.bfloat16
    maa_cols = 5 * TM_RANK
    down_cols = maa_cols + DECAY_RANK
    hidden, _ = block_norm(tokens[...], vectors)
    before, _ = block_norm(heads[0], vectors)
    delta = block_delta(hidden, before[:1], keep[:, :1])
    base = (hidden + delta * vectors[2:3]).astype(bfloat)
    act = jnp.tanh(dot_nn(base, small[:, :WINDOW]))
    act_low = act.astype(bfloat)
    for number in range(5):
        mine = masked(act_low, TM_RANK * number, TM_RANK * (number + 1))
        scale = vectors[3 + number : 4 + number] + dot_nt(mine, small[:, WINDOW:])
        value = (hidden + delta * scale).astype(bfloat)
        inputs[number] = value
        if number:
            place = {1: 1, 2: 2, 3: 0, 4: 3}[number]
            (rec, key, val, gpre)[place][...] = dot_nn(value, mix[place])
        else:
            decay = masked(jnp.tanh(dot_nn(value, small[:, :WINDOW])), maa_cols, down_cols)
            logw[...] = -jnp.exp(decay_row[:1] + dot_nt(decay.astype(bfloat), up_own[...]))
    acts[...] = masked(act, 0, maa_cols) + decay


def run_mixing_forward(tokens, heads, keep, small, vectors, decay_row, up_own, mix):
    rows, width = tokens.shape
    features = mix.shape[2]
    block = lambda lanes: pl.BlockSpec((ROW_BLOCK, lanes), lambda i: (i, 0))
    fixed = lambda value: pl.BlockSpec(
        value.shape, lambda i: (0,) * value.ndim, pipeline_mode=pl.Buffered(1)
    )
    stack = lambda count, lanes: pl.BlockSpec((count, ROW_BLOCK, lanes), lambda i: (0, i, 0))
    return pl.pallas_call(
        mixing_forward,
        grid=(rows // ROW_BLOCK,),
        out_shape=(
            jax.ShapeDtypeStruct((5, rows, width), jnp.bfloat16),
            *[jax.ShapeDtypeStruct((rows, features), jnp.float32)] * 5,
            jax.ShapeDtypeStruct((rows, WINDOW), jnp.float32),
        ),
        in_specs=[
            block(width),
            pl.BlockSpec((1,) + heads.shape[1:], lambda i: (i, 0, 0)),
            block(keep.shape[1]),
            fixed(small),
            fixed(vectors),
            fixed(decay_row),
            fixed(up_own),
            fixed(mix),
        ],
        out_specs=(stack(5, width), *[block(features)] * 5, block(WINDOW)),
        compiler_params=pltpu.CompilerParams(vmem_limit_bytes=58 << 20),
        name="mixing_forward",
    )(tokens, heads, keep, small, vectors, decay_row, up_own, mix)


def mixing_backward(
    tokens, heads, keep, acts, drec, dkey, dval, dgate, draw,
    small, vectors, up_own, mix, given,
    grad_hidden, grad_pack, first_row,
    grad_down, grad_up, grad_vec, carried,
):
    bfloat = jnp.bfloat16
    step, last = pl.program_id(0), pl.num_programs(0) - 1
    maa_cols = 5 * TM_RANK
    down_cols = maa_cols + DECAY_RANK
    features = mix.shape[2]
    col_start = pl.multiple_of(lax.axis_index("mp") * features, 128)

    @pl.when(step == 0)
    def _():
        grad_down[...] = jnp.zeros(grad_down.shape, jnp.float32)
        grad_up[...] = jnp.zeros(grad_up.shape, jnp.float32)
        grad_vec[...] = given[...]
        carried[...] = jnp.zeros(carried.shape, jnp.float32)

    down, upper = small.at[:, :WINDOW], small.at[:, WINDOW:]
    hidden, hat = block_norm(tokens[...], vectors)
    before, before_hat = block_norm(heads[0], vectors)
    delta = block_delta(hidden, before[:1], keep[:, :1])
    act = acts[...]
    act_low = act.astype(bfloat)
    slope = 1.0 - act * act
    raw = draw[...].astype(bfloat)
    grad_decay = masked(dot_nn(raw, up_own[...]) * slope, maa_cols, down_cols).astype(bfloat)
    grad_up[pl.ds(col_start, features), :] += dot_tn(raw, masked(act_low, maa_cols, down_cols))

    def add_row(row, value):
        grad_vec[row : row + 1, :] += jnp.sum(value, 0, keepdims=True)

    total = jnp.zeros(hidden.shape, jnp.float32)
    grad_delta = jnp.zeros(hidden.shape, jnp.float32)
    grad_act = jnp.zeros(act.shape, jnp.float32)
    for number in range(5):
        low, high = TM_RANK * number, TM_RANK * (number + 1)
        mine = masked(act_low, low, high)
        scale = vectors[3 + number : 4 + number] + dot_nt(mine, upper[...])
        if number:
            source = {1: dkey, 2: dval, 3: drec, 4: dgate}[number]
            grad_input = dot_nt(source[...], mix[{1: 1, 2: 2, 3: 0, 4: 3}[number]])
        else:
            grad_input = dot_nt(grad_decay, down[...])
            value = (hidden + delta * scale).astype(bfloat)
            grad_down[...] += dot_tn(value, grad_decay)
        moved = grad_input * delta
        add_row(3 + number, moved)
        moved_low = moved.astype(bfloat)
        grad_up[...] += dot_tn(moved_low, mine)
        grad_act += masked(dot_nn(moved_low, upper[...]), low, high)
        grad_delta += grad_input * scale
        total += grad_input
    grad_pre = (grad_act * slope).astype(bfloat)
    base = (hidden + delta * vectors[2:3]).astype(bfloat)
    grad_down[...] += dot_tn(base, grad_pre)
    grad_base = dot_nt(grad_pre, down[...])
    add_row(2, grad_base * delta)
    grad_delta += grad_base * vectors[2:3]
    shifted_grad = grad_delta * keep[:, :1]
    row = lax.broadcasted_iota(jnp.int32, hidden.shape, 0)
    back = jnp.where(
        row == ROW_BLOCK - 1, carried[:1], pltpu.roll(shifted_grad, ROW_BLOCK - 1, 0)
    )
    carried[...] = jnp.broadcast_to(shifted_grad[:1], carried.shape)
    total += grad_base - grad_delta + back
    add_row(0, total * hat)
    add_row(1, total)
    grad_hidden[...] = total.astype(bfloat)

    @pl.when(step == last)
    def _():
        first_row[...] = carried[...]
        add_row(0, carried[:1] * before_hat[:1])
        add_row(1, carried[:1])
        spot = lax.broadcasted_iota(jnp.int32, (16, WINDOW), 0) + down_cols
        lane = lax.broadcasted_iota(jnp.int32, (16, WINDOW), 1)
        one = jnp.where(spot == lane, 1.0, 0.0).astype(bfloat)
        placed = dot_tn(grad_vec[...].astype(bfloat), one)
        grad_pack[:, :WINDOW] = (grad_down[...] + placed).astype(bfloat)
        grad_pack[:, WINDOW:] = grad_up[...].astype(bfloat)


def run_mixing_backward(
    tokens, heads, keep, acts, drec, dkey, dval, dgate, draw, small, vectors, up_own, mix, given
):
    rows, width = tokens.shape
    features = mix.shape[2]
    count = rows // ROW_BLOCK
    block = lambda lanes: pl.BlockSpec((ROW_BLOCK, lanes), lambda i: (count - 1 - i, 0))
    fixed = lambda value: pl.BlockSpec(
        value.shape, lambda i: (0,) * len(value.shape), pipeline_mode=pl.Buffered(1)
    )
    first = jax.ShapeDtypeStruct((8, width), jnp.float32)
    pack = jax.ShapeDtypeStruct((width, 2 * WINDOW), jnp.bfloat16)
    return pl.pallas_call(
        mixing_backward,
        grid=(count,),
        out_shape=(jax.ShapeDtypeStruct((rows, width), jnp.bfloat16), pack, first),
        in_specs=[
            block(width),
            pl.BlockSpec((1,) + heads.shape[1:], lambda i: (count - 1 - i, 0, 0)),
            block(keep.shape[1]),
            block(WINDOW),
            block(features),
            block(features),
            block(features),
            block(features),
            block(features),
            fixed(small),
            fixed(vectors),
            fixed(up_own),
            fixed(mix),
            fixed(given),
        ],
        out_specs=(block(width), fixed(pack), fixed(first)),
        scratch_shapes=[
            pltpu.VMEM((width, WINDOW), jnp.float32),
            pltpu.VMEM((width, WINDOW), jnp.float32),
            pltpu.VMEM((16, width), jnp.float32),
            pltpu.VMEM((8, width), jnp.float32),
        ],
        compiler_params=pltpu.CompilerParams(vmem_limit_bytes=60 << 20),
        name="mixing_backward",
    )(tokens, heads, keep, acts, drec, dkey, dval, dgate, draw, small, vectors, up_own, mix, given)


def channel_forward(
    source, heads, keep, vectors, gate, cotangent, key_in, recv_in, recv_gate, grad_kv
):
    def norm(value):
        return norm_forward(
            value.astype(jnp.float32), vectors[12:13], vectors[13:14], norm_epsilon
        )[0]

    hidden = norm(source[...])
    delta = block_delta(hidden, norm(heads[0])[:1], keep[:, :1])
    key_in[...] = (hidden + delta * vectors[14:15]).astype(jnp.bfloat16)
    recv = (hidden + delta * vectors[15:16]).astype(jnp.bfloat16)
    recv_in[...] = recv
    opened = jax.nn.sigmoid(dot_nn(recv, gate[...]))
    recv_gate[...] = opened
    grad_kv[...] = (cotangent[...].astype(jnp.float32) * opened).astype(jnp.bfloat16)


def run_channel_forward(source, heads, keep, vectors, gate, cotangent):
    rows, width = source.shape
    features = gate.shape[1]
    block = lambda lanes: pl.BlockSpec((ROW_BLOCK, lanes), lambda i: (i, 0))
    fixed = lambda value: pl.BlockSpec(
        value.shape, lambda i: (0,) * len(value.shape), pipeline_mode=pl.Buffered(1)
    )
    low = lambda lanes: jax.ShapeDtypeStruct((rows, lanes), jnp.bfloat16)
    return pl.pallas_call(
        channel_forward,
        grid=(rows // ROW_BLOCK,),
        out_shape=(
            low(width),
            low(width),
            jax.ShapeDtypeStruct((rows, features), jnp.float32),
            low(features),
        ),
        in_specs=[
            block(width),
            pl.BlockSpec((1,) + heads.shape[1:], lambda i: (i, 0, 0)),
            block(keep.shape[1]),
            fixed(vectors),
            fixed(gate),
            block(features),
        ],
        out_specs=(block(width), block(width), block(features), block(features)),
        compiler_params=pltpu.CompilerParams(vmem_limit_bytes=60 << 20),
        name="channel_forward",
    )(source, heads, keep, vectors, gate, cotangent)


def channel_backward(
    source, heads, keep, grad_key, grad_recv, vectors, gate,
    grad_hidden, sums, first_row,
    carried,
):
    step, last = pl.program_id(0), pl.num_programs(0) - 1

    @pl.when(step == 0)
    def _():
        sums[...] = jnp.zeros(sums.shape, jnp.float32)
        carried[...] = jnp.zeros(carried.shape, jnp.float32)

    def norm(value):
        return norm_forward(
            value.astype(jnp.float32), vectors[12:13], vectors[13:14], norm_epsilon
        )[:2]

    def add_row(row, value):
        sums[row : row + 1, :] += jnp.sum(value, 0, keepdims=True)

    hidden, hat = norm(source[...])
    before, before_hat = norm(heads[0])
    delta = block_delta(hidden, before[:1], keep[:, :1])
    grad_recv_in = dot_nt(grad_recv[...], gate[...])
    grad_key_in = grad_key[...]
    grad_delta = grad_key_in * vectors[14:15] + grad_recv_in * vectors[15:16]
    add_row(2, grad_key_in * delta)
    add_row(3, grad_recv_in * delta)
    shifted_grad = grad_delta * keep[:, :1]
    row = lax.broadcasted_iota(jnp.int32, hidden.shape, 0)
    back = jnp.where(
        row == ROW_BLOCK - 1, carried[:1], pltpu.roll(shifted_grad, ROW_BLOCK - 1, 0)
    )
    carried[...] = jnp.broadcast_to(shifted_grad[:1], carried.shape)
    total = grad_key_in + grad_recv_in - grad_delta + back
    add_row(0, total * hat)
    add_row(1, total)
    grad_hidden[...] = total.astype(jnp.bfloat16)

    @pl.when(step == last)
    def _():
        first_row[...] = carried[...]
        add_row(0, carried[:1] * before_hat[:1])
        add_row(1, carried[:1])


def run_channel_backward(source, heads, keep, grad_key, grad_recv, vectors, gate):
    rows, width = source.shape
    count = rows // ROW_BLOCK
    block = lambda lanes: pl.BlockSpec((ROW_BLOCK, lanes), lambda i: (count - 1 - i, 0))
    fixed = lambda value: pl.BlockSpec(
        value.shape, lambda i: (0,) * len(value.shape), pipeline_mode=pl.Buffered(1)
    )
    first = jax.ShapeDtypeStruct((8, width), jnp.float32)
    return pl.pallas_call(
        channel_backward,
        grid=(count,),
        out_shape=(jax.ShapeDtypeStruct((rows, width), jnp.bfloat16), first, first),
        in_specs=[
            block(width),
            pl.BlockSpec((1,) + heads.shape[1:], lambda i: (count - 1 - i, 0, 0)),
            block(keep.shape[1]),
            block(width),
            block(grad_recv.shape[1]),
            fixed(vectors),
            fixed(gate),
        ],
        out_specs=(block(width), fixed(first), fixed(first)),
        scratch_shapes=[pltpu.VMEM((8, width), jnp.float32)],
        compiler_params=pltpu.CompilerParams(vmem_limit_bytes=48 << 20),
        name="channel_backward",
    )(source, heads, keep, grad_key, grad_recv, vectors, gate)


def update(carried_memory, grad, fan, total_tokens):
    rate = (total_tokens * fan) ** (-0.5)
    scaled = rate * grad
    velocity = momentum_rate * carried_memory[1] + scaled
    weight = carried_memory[0] - (scaled + momentum_rate * velocity)
    average = average_rate * carried_memory[2] + (1.0 - average_rate) * weight
    return jnp.stack([velocity, weight, average])


def split_three(value):
    pieces = []
    for _ in range(3):
        pieces.append(lax.reduce_precision(value, 8, 7))
        value = value - pieces[-1]
    return [piece.astype(jnp.bfloat16) for piece in pieces]


def block_heads(before, rows):
    width = rows.shape[1]
    ends = rows.reshape(-1, ROW_BLOCK, width)[:-1, -1]
    heads = jnp.concatenate([before, ends], 0)
    return jnp.broadcast_to(heads[:, None], (heads.shape[0], 16, width))


def body(
    tokens,
    cotangent,
    lengths,
    mix_state,
    out_state,
    key_state,
    value_state,
    gate_state,
    down_state,
    up_state,
    vector_state,
):
    bfloat = jnp.bfloat16
    single = jnp.float32
    dp_count = lax.axis_size("dp")
    mp_count = lax.axis_size("mp")
    dp_index = lax.axis_index("dp")
    mp_index = lax.axis_index("mp")
    own_rows = tokens.shape[0]
    width = tokens.shape[1]
    group_rows = own_rows * mp_count
    total_tokens = group_rows * dp_count
    features = mix_state.shape[3]
    maa_cols = 5 * TM_RANK
    down_cols = maa_cols + DECAY_RANK
    col_start = mp_index * features

    upper, middle, lower = split_three(vector_state[0].T)
    pack = jnp.concatenate(
        [
            down_state[0].astype(bfloat),
            upper,
            middle,
            up_state[0].T.astype(bfloat),
            lower,
            jnp.zeros_like(lower),
        ],
        1,
    )
    states = (mix_state, out_state, gate_state, key_state, value_state)
    tokens_all, small, mix_weight, out_low, gate_low, key_low, value_low, before_one = run_start(
        dp_count, mp_count, tokens, pack, states
    )
    out_weight = lax.all_gather(out_low, "dp", axis=1, tiled=True)
    gate_weight = lax.all_gather(gate_low, "dp", axis=0, tiled=True)
    chosen = np.zeros((16, small.shape[1]), np.float32)
    for start in (down_cols, down_cols + 16, WINDOW + down_cols):
        chosen[np.arange(16), start + np.arange(16)] = 1.0
    vectors = half_right(jnp.asarray(chosen, bfloat), small)

    seq_ends = jnp.cumsum(lengths)
    offsets = seq_ends - lengths
    positions = dp_index * group_rows + jnp.arange(group_rows, dtype=jnp.int32)
    opening = jnp.any(positions[:, None] == offsets[None, :], 1).astype(single)
    segment = jnp.sum((offsets[None, :] <= positions[:, None]).astype(single), 1)
    keep = 1.0 - opening
    chunks = group_rows // CHUNK
    parts = segment.reshape(chunks, CHUNK)
    first = parts[:, :1] - opening.reshape(chunks, CHUNK)[:, :1]

    def spread(value, lanes):
        return jnp.broadcast_to(value.astype(single).reshape(-1, 1), (value.size, lanes))

    marks = (
        spread(parts, 2 * CHUNK),
        jnp.repeat(jnp.concatenate([parts, parts], 1), 8, 0),
        spread(parts == first, PAIR),
        spread(parts == parts[:, -1:], PAIR),
        spread(jnp.repeat(parts[:, -1:] == first, 8, 0), PAIR),
    )
    level, sums, sums_back = level_tables()
    tables = (jnp.asarray(level), jnp.asarray(sums, bfloat), jnp.asarray(sums_back, bfloat))

    def local_share(row_number):
        return lax.dynamic_slice_in_dim(vectors[row_number], col_start, features, 0)

    def spread_row(value):
        return jnp.broadcast_to(value[None], (8, width))

    heads = block_heads(before_one[-1:], tokens_all)
    keep_lanes = spread(keep, PAIR)
    up_own = lax.dynamic_slice_in_dim(small[:, WINDOW:], col_start, features, 0)
    decay_row = jnp.broadcast_to(local_share(8)[None], (8, features))
    inputs_low, *branch, acts = run_mixing_forward(
        tokens_all, heads, keep_lanes, small, vectors, decay_row, up_own, mix_weight
    )
    value_low, branch = lax.optimization_barrier((value_low, branch))
    value_weight = lax.all_gather(value_low, "dp", axis=1, tiled=True)
    local_vectors = jnp.concatenate(
        [jnp.stack([local_share(9), local_share(10), local_share(11)]), jnp.zeros((5, features))], 0
    )
    outcome = run_forward(
        dp_count,
        mp_count,
        *branch,
        local_vectors,
        marks,
        tables,
        cotangent,
        tokens,
        out_weight,
        key_low,
    )
    gated_low, wkv, states, kept, cotangent_cols, residual, *outcome = outcome
    residual_all, before_second, key_weight = outcome
    before_second = before_second[-1:]
    heads_two = block_heads(before_second, residual_all)
    key_in_low, recv_in_low, recv_gate, grad_kv = run_channel_forward(
        residual_all, heads_two, keep_lanes, vectors, gate_weight, cotangent_cols
    )
    cotangent_cols = cotangent_cols.astype(single)
    key_pre = half_dot(key_in_low, key_weight)
    key_act_low = jnp.square(jnp.maximum(key_pre, 0.0)).astype(bfloat)
    grad_kv_all = lax.all_gather(grad_kv, "mp", axis=1, tiled=True)
    channel_sum = lax.psum_scatter(
        half_dot(key_act_low, value_weight).astype(bfloat), "mp", scatter_dimension=1, tiled=True
    ).astype(single)
    gated_sum = recv_gate * channel_sum
    grad_recv_pre = (cotangent_cols * gated_sum * (1.0 - recv_gate)).astype(bfloat)
    grad_key_act = half_right(grad_kv_all, value_weight)
    grad_key_pre = (grad_key_act * 2.0 * jnp.maximum(key_pre, 0.0)).astype(bfloat)
    grad_key_in = half_right(grad_key_pre, key_weight)
    grad_value_weight = half_left(key_act_low, grad_kv_all).astype(bfloat)
    grad_key_weight = half_left(key_in_low, grad_key_pre).astype(bfloat)
    grad_gate_weight = half_left(recv_in_low, grad_recv_pre).astype(bfloat)
    grad_hidden_two, channel_sums, first_row_two = run_channel_backward(
        residual_all,
        heads_two,
        keep_lanes,
        grad_key_in,
        grad_recv_pre,
        vectors,
        gate_weight,
    )
    def summed(value, axis):
        return lax.psum_scatter(value, "dp", scatter_dimension=axis, tiled=True)

    value_sum = summed(grad_value_weight, 1)
    key_sum = summed(grad_key_weight, 0)
    gate_sum = summed(grad_gate_weight, 0)
    grad_residual, grad_attn_all = run_exchange(
        dp_count,
        mp_count,
        grad_hidden_two,
        first_row_two,
        residual.astype(bfloat),
        spread_row(vectors[12]),
        cotangent,
    )
    grad_out_weight = half_left(gated_low, grad_attn_all)
    out_sum = summed(grad_out_weight.astype(bfloat), 1)
    grad_gated = half_right(grad_attn_all, out_weight)
    grad_recept, grad_keys, grad_values, grad_gate_pre, grad_raw, grad_local, mixed = run_backward(
        dp_count,
        mp_count,
        grad_gated,
        wkv,
        states,
        kept,
        *branch,
        local_vectors,
        marks,
        tables,
        gated_sum.astype(bfloat),
        residual,
    )

    value_sum, key_sum, grad_raw = lax.optimization_barrier((value_sum, key_sum, grad_raw))
    grad_mix_weight = [
        half_left(inputs_low[number], value).astype(bfloat)
        for number, value in (
            (3, grad_recept),
            (1, grad_keys),
            (2, grad_values),
            (4, grad_gate_pre),
        )
    ]
    given = jnp.concatenate(
        [
            jnp.zeros((8, width), single),
            lax.dynamic_update_slice_in_dim(
                jnp.zeros((4, width), single), grad_local[:4], col_start, 1
            ),
            channel_sums[:4],
        ],
        0,
    )
    grad_hidden_one, grad_pack, first_row = run_mixing_backward(
        tokens_all,
        heads,
        keep_lanes,
        acts,
        grad_recept,
        grad_keys,
        grad_values,
        grad_gate_pre,
        grad_raw,
        small,
        vectors,
        up_own,
        mix_weight,
        given,
    )
    grad_tokens, mix_sum, small_sum = run_end(
        dp_count,
        mp_count,
        grad_hidden_one,
        first_row,
        tokens,
        spread_row(vectors[0]),
        grad_residual,
        grad_mix_weight,
        grad_pack,
    )
    gate_sum, out_sum, mix_sum = lax.optimization_barrier((gate_sum, out_sum, mix_sum))
    return (
        mixed,
        grad_tokens,
        run_update(mix_state, mix_sum, width, total_tokens),
        run_update(out_state, out_sum, width, total_tokens),
        run_update(key_state, key_sum, width, total_tokens),
        run_update(value_state, value_sum, FF, total_tokens),
        run_update(gate_state, gate_sum, width, total_tokens),
        update(down_state, small_sum[:, :down_cols], width, total_tokens),
        update(up_state, small_sum[:, WINDOW : WINDOW + down_cols].T, TM_RANK, total_tokens),
        update(vector_state, small_sum[:, down_cols : down_cols + 16].T, 1, total_tokens),
    )


def solution(mesh):
    return jax.shard_map(
        body,
        mesh=mesh,
        in_specs=(
            P(("dp", "mp"), None),
            P(("dp", "mp"), None),
            P(),
            P(None, None, "dp", "mp"),
            P(None, "mp", "dp"),
            P(None, "dp", "mp"),
            P(None, "mp", "dp"),
            P(None, "dp", "mp"),
            P(None, ("dp", "mp"), None),
            P(None, None, ("dp", "mp")),
            P(None, None, ("dp", "mp")),
        ),
        out_specs=(
            P(("dp", "mp"), None),
            P(("dp", "mp"), None),
            P(None, None, "dp", "mp"),
            P(None, "mp", "dp"),
            P(None, "dp", "mp"),
            P(None, "mp", "dp"),
            P(None, "dp", "mp"),
            P(None, ("dp", "mp"), None),
            P(None, None, ("dp", "mp")),
            P(None, None, ("dp", "mp")),
        ),
        check_vma=False,
    )
```
